128 devices in a mesh: ctx: 32 (over z, y, core), wsh: 4 (over x).
Axes of the slice: x: 4, y: 4, z: 4, core: 2. Of those that a mesh axis runs over, the one named last changes fastest.
Arguments:
- layer_input: bfloat16 [8, 2048, 1600], P('wsh', 'ctx'), may hold values from -6 to 6
- block_order: int32 [8, 64], P('wsh'), may hold values from 0 to 63, each once within a row
- norm_gains: bfloat16 [2, 1600], P(None, 'wsh'), may hold values from 0.25 to 1.75
- norm_shifts: bfloat16 [2, 1600], P(None, 'wsh'), may hold values from -1.5 to 1.5
- qkv_weight: bfloat16 [1600, 4800], P('wsh'), may hold values from -0.15625 to 0.15625
- attn_bias: bfloat16 [2, 1600], P(None, 'wsh'), may hold values from -2.5 to 2.5
- out_weight: bfloat16 [1600, 1600], P('wsh'), may hold values from -0.625 to 0.625
- out_bias: bfloat16 [1600], P('wsh'), may hold values from -1.5 to 1.5
- fc_weight: bfloat16 [1600, 6400], P('wsh'), may hold values from -0.15625 to 0.15625
- fc_bias: bfloat16 [6400], P('wsh'), may hold values from -2.5 to 2.5
- proj_weight: bfloat16 [6400, 1600], P('wsh'), may hold values from -0.078125 to 0.078125
- proj_bias: bfloat16 [1600], P('wsh'), may hold values from -1.5 to 1.5
- output_grad: bfloat16 [8, 2048, 1600], P('wsh', 'ctx'), may hold values from -6 to 6
Outputs:
- layer_output: bfloat16 [8, 2048, 1600], P('wsh', 'ctx')
- input_grad: float32 [8, 2048, 1600], P('wsh', 'ctx')
- gains_grad: float32 [2, 1600], P(None, 'wsh')
- shifts_grad: float32 [2, 1600], P(None, 'wsh')
- qkv_grad: float32 [1600, 4800], P('wsh')
- attn_bias_grad: float32 [2, 1600], P(None, 'wsh')
- out_weight_grad: float32 [1600, 1600], P('wsh')
- out_bias_grad: float32 [1600], P('wsh')
- fc_weight_grad: float32 [1600, 6400], P('wsh')
- fc_bias_grad: float32 [6400], P('wsh')
- proj_weight_grad: float32 [6400, 1600], P('wsh')
- proj_bias_grad: float32 [1600], P('wsh')
The draws below stay inside these ranges and needn't reach their ends.
Inputs may be any that keep to these rules, and one draw needn't show every extreme that they name: Each row of block_order names every half-block number of a sequence exactly once.
All inputs are finite; a program needn't handle non-finite values.
Results may differ from the reference program's by a relative error of at most 0.023.
Values may be sent and summed in bfloat16 or wider, within the bound.
No kernel may reach another device: no remote copies, remote signals or barrier semaphores. Data moves between devices by JAX's collectives and lax.ppermute only.
A program may use at most 384 MiB of HBM per device.

```python
import jax
import jax.numpy as jnp
from jax import lax

D = 1600
HEADS = 25
HD = 64
FF = 6400
SEQ_LEN = 2048
SEQS = 8
HALVES = 64


def level_of(own_key, extent, shards, smallest, top_value):
    def one(axis_at, blocks):
        heights = jax.random.uniform(jax.random.fold_in(jax.random.fold_in(own_key, 6), axis_at), (blocks,), jnp.float32, smallest / len(shards), top_value / len(shards))
        return jnp.repeat(jnp.exp(heights), extent[axis_at] // blocks).reshape((-1,) + (1,) * (len(extent) - axis_at - 1))

    factor_of = one(*shards[0])
    for cut in shards[1:]:
        factor_of = factor_of * one(*cut)
    return factor_of


def scatter_about(rng, extent, deviation, reach, cuts=(), kind=jnp.bfloat16):
    factor_of = level_of(rng, extent, cuts, -0.22, 0.18) if cuts else 1.0
    entries = jax.random.normal(rng, extent, jnp.float32) * deviation * factor_of
    return jnp.minimum(jnp.maximum(entries, -reach), reach).astype(kind)


def setup_inputs(seed: int = 0) -> dict:
    splits = jax.random.split(jax.random.key(seed), 14)
    layer_input = scatter_about(splits[0], (SEQS, SEQ_LEN, D), 1.0, 6.0, ((0, 4), (1, 32)))
    block_order = jax.vmap(lambda own: jax.random.permutation(own, HALVES))(jax.random.split(splits[1], SEQS)).reshape((SEQS, HALVES)).astype(jnp.int32)
    norm_gains = jnp.clip(1.0 + 0.15 * jax.random.normal(splits[2], (2, D), jnp.float32), 0.25, 1.75).astype(jnp.bfloat16)
    norm_shifts = scatter_about(splits[3], (2, D), 0.3, 1.5, ((1, 4),))
    qkv_weight = scatter_about(splits[4], (D, 3 * D), D ** -0.5, 0.15625, ((0, 4),))
    attn_bias = scatter_about(splits[5], (2, D), 0.5, 2.5, ((1, 4),))
    out_weight = scatter_about(splits[6], (D, D), (D // 16) ** -0.5, 0.625, ((0, 4),))
    out_bias = scatter_about(splits[7], (D,), 0.3, 1.5, ((0, 4),))
    fc_weight = scatter_about(splits[8], (D, FF), D ** -0.5, 0.15625, ((0, 4),))
    fc_bias = scatter_about(splits[9], (FF,), 0.5, 2.5, ((0, 4),))
    proj_weight = scatter_about(splits[10], (FF, D), FF ** -0.5, 0.078125, ((0, 4),))
    proj_bias = scatter_about(splits[11], (D,), 0.3, 1.5, ((0, 4),))
    output_grad = scatter_about(splits[12], (SEQS, SEQ_LEN, D), 1.0, 6.0, ((0, 4), (1, 32)))
    return dict(layer_input=layer_input, block_order=block_order, norm_gains=norm_gains, norm_shifts=norm_shifts, qkv_weight=qkv_weight, attn_bias=attn_bias, out_weight=out_weight, out_bias=out_bias, fc_weight=fc_weight, fc_bias=fc_bias, proj_weight=proj_weight, proj_bias=proj_bias, output_grad=output_grad)


@jax.custom_vjp
def low(v):
    return lax.optimization_barrier(v.astype(jnp.bfloat16)).astype(jnp.float32)

@jax.custom_vjp
def low_back(v):
    return v

def low_keep(v):
    return (low(v), None)

def low_pass(kept, grad):
    return (grad,)

def back_keep(v):
    return (v, None)

def back_low(kept, grad):
    return (low(grad),)
low.defvjp(low_keep, low_pass)
low_back.defvjp(back_keep, back_low)

def product(left, right):
    return jnp.dot(left, right, precision=lax.Precision.HIGHEST)

def layer_norm(hidden, gain_row, shift_row):
    mean_value = lax.optimization_barrier(jnp.mean(hidden, axis=-1, keepdims=True))
    centered = hidden - mean_value
    variance = lax.optimization_barrier(jnp.mean(centered * centered, axis=-1, keepdims=True))
    return centered * lax.rsqrt(variance + 1e-05) * gain_row + shift_row

def gelu_tanh(pre_gelu):
    return 0.5 * pre_gelu * (1.0 + jnp.tanh(0.7978845608028654 * (pre_gelu + 0.044715 * pre_gelu * pre_gelu * pre_gelu)))

def attention(queries, keys_all, values_all, places):
    length = queries.shape[0]
    stride = min(512, length)
    query_blocks = queries.reshape(length // stride, stride, HEADS, HD)
    query_places = places.reshape(length // stride, stride)
    key_heads = keys_all.reshape(length, HEADS, HD)
    value_heads = values_all.reshape(length, HEADS, HD)

    @jax.checkpoint
    def one_block(member):
        block_rows, block_places = member
        scores = jnp.einsum('qhd,khd->hqk', block_rows, key_heads, precision=lax.Precision.HIGHEST) * 0.125
        scores = low_back(scores)
        allowed = places[None, None, :] <= block_places[None, :, None]
        scores = jnp.where(allowed, scores, -1e+30)
        top_score = lax.optimization_barrier(jnp.max(scores, axis=-1, keepdims=True))
        expo = jnp.where(allowed, jnp.exp(scores - top_score), 0.0)
        probs = low(expo / lax.optimization_barrier(jnp.sum(expo, axis=-1, keepdims=True)))
        mixed = jnp.einsum('hqk,khd->qhd', probs, value_heads, precision=lax.Precision.HIGHEST)
        return mixed.reshape(stride, HEADS * HD)
    return lax.map(one_block, (query_blocks, query_places)).reshape(length, HEADS * HD)

def block_forward(params, hidden, places):
    gains, shifts, qkv_w, attn_b, out_w, out_b, fc_w, fc_b, proj_w, proj_b = params
    input_one = low(layer_norm(hidden, gains[0], shifts[0]))
    projected = product(input_one, qkv_w)
    queries = low(low_back(projected[:, :D] + attn_b[0]))
    keys_all = low(low_back(projected[:, D:2 * D]))
    values_all = low(low_back(projected[:, 2 * D:] + attn_b[1]))
    attended = low(low_back(attention(queries, keys_all, values_all, places)))
    middle = hidden + low_back(product(attended, out_w) + out_b)
    input_two = low(layer_norm(middle, gains[1], shifts[1]))
    pre_gelu = low_back(product(input_two, fc_w) + fc_b)
    activated = low(gelu_tanh(pre_gelu))
    return middle + low_back(product(activated, proj_w) + proj_b)

def widen(array):
    return array.astype(jnp.float32)

def reference(layer_input, block_order, norm_gains, norm_shifts, qkv_weight, attn_bias, out_weight, out_bias, fc_weight, fc_bias, proj_weight, proj_bias, output_grad):
    length = layer_input.shape[1]
    half_rows = length // block_order.shape[1]
    row_index = jnp.arange(length, dtype=jnp.int32)
    places = jnp.take(block_order, row_index // half_rows, axis=1).astype(jnp.int32) * half_rows + row_index % half_rows
    params = (widen(norm_gains), widen(norm_shifts), widen(qkv_weight), widen(attn_bias), widen(out_weight), widen(out_bias), widen(fc_weight), widen(fc_bias), widen(proj_weight), widen(proj_bias))

    def forward(inputs, weights):

        def step(carried, member):
            return (carried, block_forward(weights, member[0], member[1]))
        return lax.scan(step, jnp.zeros((), jnp.float32), (inputs, places))[1]
    outputs, pullback = jax.vjp(forward, widen(layer_input), params)
    input_grad, grads = pullback(widen(output_grad))
    return (outputs.astype(jnp.bfloat16), input_grad, grads[0], grads[1], grads[2], grads[3], grads[4], grads[5], grads[6], grads[7], grads[8], grads[9])
```

```python
import functools

import jax
import jax.numpy as jnp
from jax import lax
from jax.experimental import pallas as pl
from jax.experimental.pallas import tpu as pltpu
from jax.sharding import PartitionSpec as P

HEADS = 25
HD = 64
QB = 256
BF = jnp.bfloat16
F32 = jnp.float32
NN = (((1,), (0,)), ((), ()))
NT = (((1,), (1,)), ((), ()))
TN = (((0,), (0,)), ((), ()))


def mm(left, right, dims=NN):
    return lax.dot_general(left, right, dims, preferred_element_type=F32)


def layer_norm(hidden, gain_row, shift_row):
    centered = hidden - jnp.mean(hidden, axis=-1, keepdims=True)
    inverse = lax.rsqrt(jnp.mean(centered * centered, axis=-1, keepdims=True) + 1e-05)
    scaled = centered * inverse
    return scaled * gain_row + shift_row, scaled, inverse


def norm_back(gradient, scaled, inverse, gain_row):
    weighted = gradient * gain_row
    first_mean = jnp.mean(weighted, axis=-1, keepdims=True)
    second_mean = jnp.mean(weighted * scaled, axis=-1, keepdims=True)
    result = inverse * (weighted - first_mean - scaled * second_mean)
    return result, jnp.sum(gradient * scaled, axis=0), jnp.sum(gradient, axis=0)


def gelu_pair(pre_gelu):
    squared = pre_gelu * pre_gelu
    tangent = jnp.tanh(0.7978845608028654 * (pre_gelu + 0.044715 * squared * pre_gelu))
    result = 0.5 * pre_gelu * (1.0 + tangent)
    derivative = 0.5 * (1.0 + tangent) + 0.5 * pre_gelu * (
        1.0 - tangent * tangent
    ) * 0.7978845608028654 * (1.0 + 3.0 * 0.044715 * squared)
    return result, derivative


def attend_kernel(halves, half, order_ref, qkv_ref, sorted_ref, out_ref, mixed_ref, log_ref, rows_ref):
    seq = pl.program_id(0)
    length = halves * half
    for b in range(halves):
        at = pl.multiple_of(order_ref[seq, b] * half, half)
        sorted_ref[0, pl.ds(at, half), :] = qkv_ref[0, b * half : (b + 1) * half, :]
    k_all = sorted_ref[0, :, HD : 2 * HD]
    v_turned = sorted_ref[0, :, 2 * HD :].T
    below = lax.broadcasted_iota(jnp.int32, (QB, QB), 0) <= lax.broadcasted_iota(
        jnp.int32, (QB, QB), 1
    )
    for i in range(length // QB):
        lo, hi = i * QB, (i + 1) * QB
        q_rows = sorted_ref[0, lo:hi, :HD] * 0.125
        scores = mm(k_all[:hi], q_rows, NT)
        last = jnp.where(below, scores[lo:], -1e30)
        best = jnp.max(last, axis=0, keepdims=True)
        if i:
            best = jnp.maximum(best, jnp.max(scores[:lo], axis=0, keepdims=True))
        tail = jnp.exp(last - best)
        total = jnp.sum(tail, axis=0, keepdims=True)
        mixed = mm(v_turned[:, lo:hi], tail.astype(BF))
        if i:
            head = jnp.exp(scores[:lo] - best)
            total = total + jnp.sum(head, axis=0, keepdims=True)
            mixed = mixed + mm(v_turned[:, :lo], head.astype(BF))
        mixed = mixed / total
        mixed_ref[0, :, lo:hi] = mixed
        log_ref[0, :, lo:hi] = best + jnp.log(total)
        rows_ref[lo:hi, :] = mixed.T
    for b in range(halves):
        at = pl.multiple_of(order_ref[seq, b] * half, half)
        out_ref[0, b * half : (b + 1) * half, :] = rows_ref[pl.ds(at, half), :].astype(BF)


def attend(order, qkv):
    seqs, length, width = qkv.shape
    halves = order.shape[1]
    return pl.pallas_call(
        functools.partial(attend_kernel, halves, length // halves),
        grid=(seqs,),
        in_specs=[
            pl.BlockSpec(memory_space=pltpu.SMEM),
            pl.BlockSpec((1, length, width), lambda s: (s, 0, 0)),
        ],
        out_specs=[
            pl.BlockSpec((1, length, width), lambda s: (s, 0, 0)),
            pl.BlockSpec((1, length, HD), lambda s: (s, 0, 0)),
            pl.BlockSpec((1, HD, length), lambda s: (s, 0, 0)),
            pl.BlockSpec((1, 1, length), lambda s: (s, 0, 0)),
        ],
        out_shape=[
            jax.ShapeDtypeStruct((seqs, length, width), BF),
            jax.ShapeDtypeStruct((seqs, length, HD), BF),
            jax.ShapeDtypeStruct((seqs, HD, length), F32),
            jax.ShapeDtypeStruct((seqs, 1, length), F32),
        ],
        scratch_shapes=[pltpu.VMEM((length, HD), F32)],
        compiler_params=pltpu.CompilerParams(vmem_limit_bytes=48 << 20),
        cost_estimate=pl.CostEstimate(
            flops=seqs * length * length * HD * 8, bytes_accessed=seqs * length * 2048, transcendentals=0
        ),
        name="attend",
    )(order, qkv)


def attend_back_kernel(
    halves, half, order_ref, sorted_ref, mixed_ref, log_ref, grad_ref, out_ref, rows_ref, key_ref, value_ref, all_ref
):
    seq = pl.program_id(0)
    length = halves * half
    for b in range(halves):
        at = pl.multiple_of(order_ref[seq, b] * half, half)
        rows_ref[pl.ds(at, half), :] = grad_ref[0, b * half : (b + 1) * half, :]
    k_all = sorted_ref[0, :, HD : 2 * HD]
    v_all = sorted_ref[0, :, 2 * HD :]
    k_turned = k_all.T
    delta = jnp.sum(rows_ref[...].T.astype(F32) * mixed_ref[0], axis=0, keepdims=True)
    key_ref[...] = jnp.zeros_like(key_ref)
    value_ref[...] = jnp.zeros_like(value_ref)
    below = lax.broadcasted_iota(jnp.int32, (QB, QB), 0) <= lax.broadcasted_iota(
        jnp.int32, (QB, QB), 1
    )
    for i in range(length // QB):
        lo, hi = i * QB, (i + 1) * QB
        q_rows = sorted_ref[0, lo:hi, :HD] * 0.125
        g_rows = rows_ref[lo:hi, :]
        log_row = log_ref[0, :, lo:hi]
        delta_row = delta[:, lo:hi]
        query = jnp.zeros((HD, QB), F32)
        for first, end in ((0, lo), (lo, hi)):
            if first == end:
                continue
            scores = mm(k_all[first:end], q_rows, NT)
            probs = jnp.exp(scores - log_row)
            if end == hi:
                probs = jnp.where(below, probs, 0.0)
            slopes = mm(v_all[first:end], g_rows, NT)
            pulled = (probs * (slopes - delta_row)).astype(BF)
            value_ref[first:end, :] += mm(probs.astype(BF), g_rows)
            key_ref[first:end, :] += mm(pulled, q_rows)
            query = query + mm(k_turned[:, first:end], pulled)
        all_ref[lo:hi, :HD] = (query * 0.125).T
    all_ref[:, HD : 2 * HD] = key_ref[...]
    all_ref[:, 2 * HD :] = value_ref[...]
    for b in range(halves):
        at = pl.multiple_of(order_ref[seq, b] * half, half)
        out_ref[0, b * half : (b + 1) * half, :] = all_ref[pl.ds(at, half), :].astype(BF)


def attend_back(order, ordered, mixed, logs, grads):
    seqs, length, width = ordered.shape
    halves = order.shape[1]
    return pl.pallas_call(
        functools.partial(attend_back_kernel, halves, length // halves),
        grid=(seqs,),
        in_specs=[
            pl.BlockSpec(memory_space=pltpu.SMEM),
            pl.BlockSpec((1, length, width), lambda s: (s, 0, 0)),
            pl.BlockSpec((1, HD, length), lambda s: (s, 0, 0)),
            pl.BlockSpec((1, 1, length), lambda s: (s, 0, 0)),
            pl.BlockSpec((1, length, HD), lambda s: (s, 0, 0)),
        ],
        out_specs=pl.BlockSpec((1, length, width), lambda s: (s, 0, 0)),
        out_shape=jax.ShapeDtypeStruct((seqs, length, width), BF),
        scratch_shapes=[
            pltpu.VMEM((length, HD), BF),
            pltpu.VMEM((length, HD), F32),
            pltpu.VMEM((length, HD), F32),
            pltpu.VMEM((length, width), F32),
        ],
        compiler_params=pltpu.CompilerParams(vmem_limit_bytes=48 << 20),
        cost_estimate=pl.CostEstimate(
            flops=seqs * length * length * HD * 16, bytes_accessed=seqs * length * 2048, transcendentals=0
        ),
        name="attend_back",
    )(order, ordered, mixed, logs, grads)


def on_device(
    layer_input,
    block_order,
    norm_gains,
    norm_shifts,
    qkv_weight,
    attn_bias,
    out_weight,
    out_bias,
    fc_weight,
    fc_bias,
    proj_weight,
    proj_bias,
    output_grad,
):
    seqs, rows, width = layer_input.shape
    tokens = seqs * rows
    n_ctx, n_w = lax.axis_size("ctx"), lax.axis_size("wsh")
    length = rows * n_ctx
    ctx, wsh = lax.axis_index("ctx"), lax.axis_index("wsh")
    core = ctx % 2
    own = width // n_w
    ff = fc_weight.shape[1] // n_w

    def to_right(array, k):
        return lax.ppermute(array, "wsh", [(i, (i + k) % n_w) for i in range(n_w)])

    def to_partner(array):
        return lax.ppermute(array, "ctx", [(i, i ^ 1) for i in range(n_ctx)])

    def around(array):
        return [array] + [to_right(array, k) for k in range(1, n_w)]

    def deal(choose):
        return [choose(0)] + [to_right(choose(k), k) for k in range(1, n_w)]

    def send_back(pieces):
        total = pieces[0]
        for k in range(1, n_w):
            total = total + to_right(pieces[k].astype(BF), n_w - k).astype(F32)
        return total

    def whole_rows(choose, half_rows):
        whole = choose(0, None)
        total = jnp.zeros((n_w * 2 * half_rows, whole.shape[1]), whole.dtype)
        total = lax.dynamic_update_slice(total, whole, (wsh * 2 * half_rows, 0))
        for k in range(1, n_w):
            mine = to_right(choose(k, core * half_rows), k)
            other = to_partner(mine)
            base = (wsh - k) % n_w * 2 * half_rows
            total = lax.dynamic_update_slice(total, mine, (base + core * half_rows, 0))
            total = lax.dynamic_update_slice(total, other, (base + (1 - core) * half_rows, 0))
        return total

    packed = jnp.concatenate(
        [norm_gains, norm_shifts, attn_bias, out_bias[None], proj_bias[None]], axis=0
    )
    vectors = lax.all_gather(packed, "wsh", axis=1, tiled=True).astype(F32)
    gains, shifts, bias_pair = vectors[0:2], vectors[2:4], vectors[4:6]
    out_bias_row, proj_bias_row = vectors[6], vectors[7]

    head = jnp.minimum(ctx, HEADS - 1)
    head_cols = lax.dynamic_slice(
        qkv_weight.reshape(own, 3, HEADS, HD), (0, 0, head, 0), (own, 3, 1, HD)
    ).reshape(own, 3 * HD)
    head_weight = lax.all_gather(head_cols, "wsh", axis=0, tiled=True)
    head_bias = lax.dynamic_slice(bias_pair.reshape(2, HEADS, HD), (0, head, 0), (2, 1, HD))
    head_bias = jnp.concatenate([head_bias[0], jnp.zeros((1, HD), F32), head_bias[1]], axis=1)

    residual = layer_input.reshape(tokens, width).astype(F32)
    normed_one, scaled_one, inverse_one = layer_norm(residual, gains[0], shifts[0])
    input_one = lax.all_gather(
        normed_one.astype(BF).reshape(seqs, rows, width), "ctx", axis=1, tiled=True
    ).reshape(seqs * length, width)

    grad_low = output_grad.reshape(tokens, width)
    grad_group = jnp.concatenate(around(grad_low), axis=0)
    out_all = whole_rows(
        lambda k, start: out_weight
        if start is None
        else lax.dynamic_slice(out_weight, (start, 0), (own // 2, width)),
        own // 2,
    )
    fc_blocks = jnp.moveaxis(fc_weight.reshape(own, n_w, ff), 1, 0)

    def fc_choose(k, start):
        block = (wsh + k) % n_w
        if start is None:
            return lax.dynamic_slice(fc_blocks, (block, 0, 0), (1, own, ff))[0]
        return lax.dynamic_slice(fc_blocks, (block, start, 0), (1, own // 2, ff))[0]

    fc_cols = whole_rows(fc_choose, own // 2)
    qkv_half = lax.dynamic_slice(qkv_weight, (core * (own // 2), 0), (own // 2, 3 * width))
    qkv_half = lax.optimization_barrier((qkv_half, input_one))[0]
    qkv_mine = lax.all_gather(qkv_half, "wsh", axis=0, tiled=True)
    qkv_other = to_partner(qkv_mine)

    head_qkv = (mm(input_one, head_weight) + head_bias).astype(BF).reshape(seqs, length, 3 * HD)
    ordered, mixed_rows, mixed, logs = attend(block_order, head_qkv)

    def to_tokens(array):
        f = array.shape[2]
        parts = array.reshape(seqs, n_ctx, rows, f).transpose(1, 0, 2, 3).reshape(n_ctx, tokens, f)
        return lax.all_to_all(parts, "ctx", 0, 0)

    attended = to_tokens(mixed_rows)[:HEADS].transpose(1, 0, 2).reshape(tokens, width)
    middle = residual + mm(attended, out_all) + out_bias_row
    normed_two, scaled_two, inverse_two = layer_norm(middle, gains[1], shifts[1])
    input_two = jnp.concatenate(around(normed_two.astype(BF)), axis=0)

    pre_gelu = mm(input_two, fc_cols) + fc_bias.astype(F32)
    activated, derivative = gelu_pair(pre_gelu)
    activated = activated.astype(BF)
    grad_active = mm(grad_group, proj_weight, NT)
    grad_pre = (grad_active * derivative).astype(BF)
    grad_two = mm(grad_pre, fc_cols, NT).reshape(n_w, tokens, width)
    grad_two = send_back([grad_two[k] for k in range(n_w)])
    branch = mm(activated, proj_weight).reshape(n_w, tokens, width)
    branch = send_back([branch[k] for k in range(n_w)])
    layer_output = (middle + branch + proj_bias_row).astype(BF)
    grad_proj = mm(activated, grad_group, TN)
    grad_fc_cols = mm(input_two, grad_pre, TN).astype(BF)
    grad_fc = jnp.zeros((n_w, own, ff), BF)
    fc_pieces = deal(
        lambda k: lax.dynamic_slice(grad_fc_cols, ((wsh + k) % n_w * own, 0), (own, ff))
    )
    for k, piece in enumerate(fc_pieces):
        grad_fc = lax.dynamic_update_slice(grad_fc, piece[None], ((wsh - k) % n_w, 0, 0))

    grad_norm_two, gain_two, shift_two = norm_back(grad_two, scaled_two, inverse_two, gains[1])
    grad_middle = grad_low.astype(F32) + grad_norm_two
    grad_branch = grad_middle.astype(BF)
    grad_attended = mm(grad_branch, out_all, NT).astype(BF)
    grad_heads = jnp.pad(
        grad_attended.reshape(tokens, HEADS, HD).transpose(1, 0, 2),
        ((0, n_ctx - HEADS), (0, 0), (0, 0)),
    )
    grad_rows = lax.all_to_all(grad_heads, "ctx", 0, 0)
    grad_rows = (
        grad_rows.reshape(n_ctx, seqs, rows, HD).transpose(1, 0, 2, 3).reshape(seqs, length, HD)
    )

    branch_group = jnp.concatenate(around(grad_branch), axis=0)
    attended_cols = jnp.concatenate(
        deal(lambda k: lax.dynamic_slice(attended, (0, (wsh + k) % n_w * own), (tokens, own))),
        axis=0,
    )
    grad_out = mm(attended_cols, branch_group, TN)

    column = lambda array: lax.dynamic_slice(
        jnp.sum(array.astype(F32), axis=0), (wsh * own,), (own,)
    )
    side = jnp.concatenate(
        [jnp.sum(grad_pre.astype(F32), axis=0), column(grad_group), column(branch_group)]
    ).reshape(-1, own)
    share_proj, share_fc, share_out, share_side = lax.psum(
        (grad_proj.astype(BF), grad_fc, grad_out.astype(BF), side.astype(BF)), "ctx"
    )
    fc_out = share_fc.transpose(1, 0, 2).reshape(own, n_w * ff).astype(F32)
    share_side = share_side.astype(F32).reshape(-1)

    grad_qkv = attend_back(block_order, ordered, mixed, logs, grad_rows)
    grad_cols = mm(input_one, grad_qkv.reshape(seqs * length, 3 * HD), TN).reshape(
        n_w, own, 3 * HD
    )
    grad_cols_sum = None
    for k in range(n_w):
        piece = lax.dynamic_slice(grad_cols, ((wsh + k) % n_w, 0, 0), (1, own, 3 * HD))[0]
        piece = piece if k == 0 else to_right(piece.astype(BF), k).astype(F32)
        grad_cols_sum = piece if k == 0 else grad_cols_sum + piece
    qkv_out = lax.all_gather(grad_cols_sum.astype(BF), "ctx", axis=0)
    qkv_out = (
        qkv_out[:HEADS]
        .reshape(HEADS, own, 3, HD)
        .transpose(1, 2, 0, 3)
        .reshape(own, 3 * width)
        .astype(F32)
    )

    grad_tokens = to_tokens(grad_qkv)[:HEADS].reshape(HEADS, tokens, 3, HD)
    grad_tokens = grad_tokens.transpose(1, 2, 0, 3).reshape(tokens, 3 * width)
    one_mine = mm(grad_tokens, qkv_mine, NT).reshape(tokens, n_w, 1, own // 2)
    one_other = mm(grad_tokens, qkv_other, NT).reshape(tokens, n_w, 1, own // 2)
    grad_one = jnp.where(
        core == 0,
        jnp.concatenate([one_mine, one_other], axis=2),
        jnp.concatenate([one_other, one_mine], axis=2),
    ).reshape(tokens, width)
    grad_norm_one, gain_one, shift_one = norm_back(grad_one, scaled_one, inverse_one, gains[0])
    input_grad = grad_middle + grad_norm_one

    wide = grad_tokens.astype(F32)
    vector_grads = jnp.stack(
        [
            gain_one,
            gain_two,
            shift_one,
            shift_two,
            jnp.sum(wide[:, :width], axis=0),
            jnp.sum(wide[:, 2 * width :], axis=0),
        ]
    )
    vector_grads = vector_grads.reshape(6, n_w, own).transpose(1, 0, 2).reshape(n_w, 6 * own)
    pieces = deal(
        lambda k: lax.dynamic_slice(vector_grads, ((wsh + k) % n_w, 0), (1, 6 * own))
    )
    vector_sum = (pieces[0] + pieces[1]) + (pieces[2] + pieces[3])
    padded = jnp.pad(vector_sum.reshape(-1), (0, -6 * own % 1024)).reshape(1, 8, -1)
    everyone = lax.all_to_all(
        jnp.broadcast_to(padded, (n_ctx,) + padded.shape[1:]), "ctx", 0, 0
    )
    vector_out = jnp.sum(everyone, axis=0).reshape(-1)[: 6 * own].reshape(6, own)
    return (
        layer_output.reshape(seqs, rows, width),
        input_grad.reshape(seqs, rows, width),
        vector_out[0:2],
        vector_out[2:4],
        qkv_out,
        vector_out[4:6],
        share_out.astype(F32),
        share_side[ff + own :],
        fc_out,
        share_side[:ff],
        share_proj.astype(F32),
        share_side[ff : ff + own],
    )


def solution(mesh):
    return jax.shard_map(
        on_device,
        mesh=mesh,
        in_specs=(
            P("wsh", "ctx", None),
            P("wsh", None),
            P(None, "wsh"),
            P(None, "wsh"),
            P("wsh", None),
            P(None, "wsh"),
            P("wsh", None),
            P("wsh"),
            P("wsh", None),
            P("wsh"),
            P("wsh", None),
            P("wsh"),
            P("wsh", "ctx", None),
        ),
        out_specs=(
            P("wsh", "ctx", None),
            P("wsh", "ctx", None),
            P(None, "wsh"),
            P(None, "wsh"),
            P("wsh", None),
            P(None, "wsh"),
            P("wsh", None),
            P("wsh"),
            P("wsh", None),
            P("wsh"),
            P("wsh", None),
            P("wsh"),
        ),
        check_vma=False,
    )
```

```python
import functools

import jax
import jax.numpy as jnp
from jax import lax
from jax.experimental import pallas as pl
from jax.experimental.pallas import tpu as pltpu
from jax.sharding import PartitionSpec as P

HEADS = 25
HD = 64
QB = 256
BF = jnp.bfloat16
F32 = jnp.float32
NN = (((1,), (0,)), ((), ()))
NT = (((1,), (1,)), ((), ()))
TN = (((0,), (0,)), ((), ()))


def mm(left, right, dims=NN):
    return lax.dot_general(left, right, dims, preferred_element_type=F32)


def layer_norm(hidden, gain_row, shift_row):
    centered = hidden - jnp.mean(hidden, axis=-1, keepdims=True)
    inverse = lax.rsqrt(jnp.mean(centered * centered, axis=-1, keepdims=True) + 1e-05)
    scaled = centered * inverse
    return scaled * gain_row + shift_row, scaled, inverse


def norm_back(gradient, scaled, inverse, gain_row):
    weighted = gradient * gain_row
    first_mean = jnp.mean(weighted, axis=-1, keepdims=True)
    second_mean = jnp.mean(weighted * scaled, axis=-1, keepdims=True)
    result = inverse * (weighted - first_mean - scaled * second_mean)
    return result, jnp.sum(gradient * scaled, axis=0), jnp.sum(gradient, axis=0)


def gelu_pair(pre_gelu):
    squared = pre_gelu * pre_gelu
    tangent = jnp.tanh(0.7978845608028654 * (pre_gelu + 0.044715 * squared * pre_gelu))
    result = 0.5 * pre_gelu * (1.0 + tangent)
    derivative = 0.5 * (1.0 + tangent) + 0.5 * pre_gelu * (
        1.0 - tangent * tangent
    ) * 0.7978845608028654 * (1.0 + 3.0 * 0.044715 * squared)
    return result, derivative


def ordered_rows(order_ref, seq, block, half, length):
    return pl.multiple_of(seq * length + order_ref[seq, block] * half, half)


def below_mask():
    return lax.broadcasted_iota(jnp.int32, (QB, QB), 0) <= lax.broadcasted_iota(
        jnp.int32, (QB, QB), 1
    )


def attend_kernel(
    seqs, rows, half, order_ref, in_ref, weight_ref, bias_ref, sorted_ref, out_ref, mixed_ref, log_ref, rows_ref
):
    step = pl.program_id(0)
    group, tokens, width = in_ref.shape
    length = mixed_ref.shape[2]
    per = rows // half
    made = mm(in_ref[...].reshape(group * tokens, width), weight_ref[...], NT) + bias_ref[...]
    made = made.astype(BF)
    for g in range(group):
        for s in range(seqs):
            for b in range(per):
                at = ordered_rows(order_ref, s, (step * group + g) * per + b, half, length)
                first = g * tokens + s * rows + b * half
                sorted_ref[pl.ds(at, half), :] = made[first : first + half]

    @pl.when(step == pl.num_programs(0) - 1)
    def _():
        below = below_mask()

        def one_seq(s, carry):
            base = pl.multiple_of(s * length, length)
            k_all = sorted_ref[pl.ds(base, length), HD : 2 * HD]
            v_turned = sorted_ref[pl.ds(base, length), 2 * HD :].T
            for i in range(length // QB):
                lo, hi = i * QB, (i + 1) * QB
                q_rows = sorted_ref[pl.ds(base + lo, QB), :HD] * 0.125
                scores = mm(k_all[:hi], q_rows, NT)
                last = jnp.where(below, scores[lo:], -1e30)
                best = jnp.max(last, axis=0, keepdims=True)
                if i:
                    best = jnp.maximum(best, jnp.max(scores[:lo], axis=0, keepdims=True))
                tail = jnp.exp(last - best)
                total = jnp.sum(tail, axis=0, keepdims=True)
                mixed = mm(v_turned[:, lo:hi], tail.astype(BF))
                if i:
                    head = jnp.exp(scores[:lo] - best)
                    total = total + jnp.sum(head, axis=0, keepdims=True)
                    mixed = mixed + mm(v_turned[:, :lo], head.astype(BF))
                mixed = mixed / total
                mixed_ref[s, :, lo:hi] = mixed
                log_ref[s, :, lo:hi] = best + jnp.log(total)
                rows_ref[pl.ds(base + lo, QB), :] = mixed.T
            return carry

        lax.fori_loop(0, seqs, one_seq, 0)

        def one_block(c, carry):
            parts = [
                rows_ref[pl.ds(ordered_rows(order_ref, s, c * per + b, half, length), half), :]
                for s in range(seqs)
                for b in range(per)
            ]
            out_ref[c] = jnp.concatenate(parts, axis=0).T.astype(BF)
            return carry

        lax.fori_loop(0, out_ref.shape[0], one_block, 0)


def attend(order, gathered, weight, bias, rows):
    n_ctx, tokens, width = gathered.shape
    seqs, halves = order.shape
    length = rows * n_ctx
    half = length // halves
    group = 4
    whole = lambda *shape: pl.BlockSpec(shape, lambda i: (0,) * len(shape))
    return pl.pallas_call(
        functools.partial(attend_kernel, seqs, rows, half),
        grid=(n_ctx // group,),
        in_specs=[
            pl.BlockSpec(memory_space=pltpu.SMEM),
            pl.BlockSpec((group, tokens, width), lambda i: (i, 0, 0)),
            whole(3 * HD, width),
            whole(1, 3 * HD),
        ],
        out_specs=[
            whole(seqs * length, 3 * HD),
            whole(n_ctx, HD, tokens),
            whole(seqs, HD, length),
            whole(seqs, 1, length),
        ],
        out_shape=[
            jax.ShapeDtypeStruct((seqs * length, 3 * HD), BF),
            jax.ShapeDtypeStruct((n_ctx, HD, tokens), BF),
            jax.ShapeDtypeStruct((seqs, HD, length), F32),
            jax.ShapeDtypeStruct((seqs, 1, length), F32),
        ],
        scratch_shapes=[pltpu.VMEM((seqs * length, HD), F32)],
        compiler_params=pltpu.CompilerParams(vmem_limit_bytes=48 << 20),
        cost_estimate=pl.CostEstimate(
            flops=20_000_000_000, bytes_accessed=20_000_000, transcendentals=0
        ),
        name="attend",
    )(order, gathered, weight, bias)


def attend_back_kernel(
    seqs, rows, half, order_ref, sorted_ref, mixed_ref, log_ref, grad_ref, out_ref,
    rows_ref, key_ref, value_ref, all_ref,
):
    n_ctx, _, tokens = grad_ref.shape
    length = mixed_ref.shape[2]
    per = rows // half

    def spread(c, carry):
        block = grad_ref[c].T
        for s in range(seqs):
            for b in range(per):
                at = ordered_rows(order_ref, s, c * per + b, half, length)
                first = s * rows + b * half
                rows_ref[pl.ds(at, half), :] = block[first : first + half]
        return carry

    lax.fori_loop(0, n_ctx, spread, 0)
    below = below_mask()

    def one_seq(s, carry):
        base = pl.multiple_of(s * length, length)
        k_all = sorted_ref[pl.ds(base, length), HD : 2 * HD]
        v_all = sorted_ref[pl.ds(base, length), 2 * HD :]
        k_turned = k_all.T
        g_turned = rows_ref[pl.ds(base, length), :].T
        delta = jnp.sum(g_turned.astype(F32) * mixed_ref[s], axis=0, keepdims=True)
        key_ref[...] = jnp.zeros_like(key_ref)
        value_ref[...] = jnp.zeros_like(value_ref)
        for i in range(length // QB):
            lo, hi = i * QB, (i + 1) * QB
            q_rows = sorted_ref[pl.ds(base + lo, QB), :HD] * 0.125
            g_rows = rows_ref[pl.ds(base + lo, QB), :]
            log_row = log_ref[s, :, lo:hi]
            delta_row = delta[:, lo:hi]
            query = jnp.zeros((HD, QB), F32)
            for first, end in ((0, lo), (lo, hi)):
                if first == end:
                    continue
                scores = mm(k_all[first:end], q_rows, NT)
                probs = jnp.exp(scores - log_row)
                if end == hi:
                    probs = jnp.where(below, probs, 0.0)
                slopes = mm(v_all[first:end], g_rows, NT)
                pulled = (probs * (slopes - delta_row)).astype(BF)
                value_ref[first:end, :] += mm(probs.astype(BF), g_rows)
                key_ref[first:end, :] += mm(pulled, q_rows)
                query = query + mm(k_turned[:, first:end], pulled)
            all_ref[pl.ds(base + lo, QB), :HD] = (query * 0.125).T
        all_ref[pl.ds(base, length), HD : 2 * HD] = key_ref[...]
        all_ref[pl.ds(base, length), 2 * HD :] = value_ref[...]
        return carry

    lax.fori_loop(0, seqs, one_seq, 0)

    def one_block(c, carry):
        parts = [
            all_ref[pl.ds(ordered_rows(order_ref, s, c * per + b, half, length), half), :]
            for s in range(seqs)
            for b in range(per)
        ]
        out_ref[c] = jnp.concatenate(parts, axis=0).T.astype(BF)
        return carry

    lax.fori_loop(0, n_ctx, one_block, 0)


def attend_back(order, ordered, mixed, logs, grads, rows):
    n_ctx, _, tokens = grads.shape
    seqs, halves = order.shape
    length = rows * n_ctx
    half = length // halves
    vmem = pl.BlockSpec(memory_space=pltpu.VMEM)
    return pl.pallas_call(
        functools.partial(attend_back_kernel, seqs, rows, half),
        in_specs=[pl.BlockSpec(memory_space=pltpu.SMEM)] + [vmem] * 4,
        out_specs=vmem,
        out_shape=jax.ShapeDtypeStruct((n_ctx, 3 * HD, tokens), BF),
        scratch_shapes=[
            pltpu.VMEM((seqs * length, HD), BF),
            pltpu.VMEM((length, HD), F32),
            pltpu.VMEM((length, HD), F32),
            pltpu.VMEM((seqs * length, 3 * HD), F32),
        ],
        compiler_params=pltpu.CompilerParams(vmem_limit_bytes=48 << 20),
        cost_estimate=pl.CostEstimate(
            flops=20_000_000_000, bytes_accessed=10_000_000, transcendentals=0
        ),
        name="attend_back",
    )(order, ordered, mixed, logs, grads)


def head_grad_kernel(grad_ref, in_ref, out_ref, total_ref):
    step = pl.program_id(0)

    @pl.when(step == 0)
    def _():
        total_ref[...] = jnp.zeros_like(total_ref)

    group, tokens, width = in_ref.shape
    turned = jnp.concatenate([grad_ref[g] for g in range(group)], axis=1)
    total_ref[...] += mm(turned, in_ref[...].reshape(group * tokens, width))

    @pl.when(step == pl.num_programs(0) - 1)
    def _():
        out_ref[...] = total_ref[...].T


def head_grad(grads, gathered):
    n_ctx, tokens, width = gathered.shape
    group = 4
    return pl.pallas_call(
        head_grad_kernel,
        grid=(n_ctx // group,),
        in_specs=[
            pl.BlockSpec((group, 3 * HD, tokens), lambda i: (i, 0, 0)),
            pl.BlockSpec((group, tokens, width), lambda i: (i, 0, 0)),
        ],
        out_specs=pl.BlockSpec((width, 3 * HD), lambda i: (0, 0)),
        out_shape=jax.ShapeDtypeStruct((width, 3 * HD), F32),
        scratch_shapes=[pltpu.VMEM((3 * HD, width), F32)],
        compiler_params=pltpu.CompilerParams(vmem_limit_bytes=32 << 20),
        cost_estimate=pl.CostEstimate(
            flops=5_000_000_000, bytes_accessed=15_000_000, transcendentals=0
        ),
        name="head_grad",
    )(grads, gathered)


def join_rows_kernel(n_w, overlap, at_ref, *refs):
    *pieces, out_ref = refs
    wsh, core = at_ref[0], at_ref[1]
    own = pieces[0].shape[0]
    out_ref[pl.ds(pl.multiple_of(wsh * own, 16), own), :] = pieces[0][...]
    for k in range(1, n_w):
        base = (wsh + k) % n_w * own
        mine, other = pieces[2 * k - 1], pieces[2 * k]
        size = mine.shape[0]
        out_ref[pl.ds(pl.multiple_of(base + core * overlap, 16), size), :] = mine[...]
        out_ref[pl.ds(pl.multiple_of(base + (1 - core) * overlap, 16), size), :] = other[...]


def join_rows(at, pieces, n_w, overlap):
    own, width = pieces[0].shape
    vmem = pl.BlockSpec(memory_space=pltpu.VMEM)
    return pl.pallas_call(
        functools.partial(join_rows_kernel, n_w, overlap),
        in_specs=[pl.BlockSpec(memory_space=pltpu.SMEM)] + [vmem] * len(pieces),
        out_specs=vmem,
        out_shape=jax.ShapeDtypeStruct((n_w * own, width), BF),
        compiler_params=pltpu.CompilerParams(vmem_limit_bytes=32 << 20),
        cost_estimate=pl.CostEstimate(flops=0, bytes_accessed=12_000_000, transcendentals=0),
        name="join_rows",
    )(at, *pieces)


def cut_columns_kernel(n_w, overlap, at_ref, in_ref, *out_refs):
    wsh, core = at_ref[0], at_ref[1]
    cols = out_refs[0].shape[1]
    for k, out_ref in enumerate(out_refs):
        size = out_ref.shape[0]
        start = 0 if k == 0 else pl.multiple_of(core * overlap, 16)
        for b in range(n_w):

            @pl.when((wsh + n_w - k) % n_w == b)
            def _(out_ref=out_ref, start=start, size=size, b=b):
                out_ref[...] = in_ref[pl.ds(start, size), b * cols : (b + 1) * cols]


def cut_columns(at, array, n_w, size, overlap):
    own, cols = array.shape[0], array.shape[1] // n_w
    vmem = pl.BlockSpec(memory_space=pltpu.VMEM)
    return pl.pallas_call(
        functools.partial(cut_columns_kernel, n_w, overlap),
        in_specs=[pl.BlockSpec(memory_space=pltpu.SMEM), vmem],
        out_specs=[vmem] * n_w,
        out_shape=[
            jax.ShapeDtypeStruct((own if k == 0 else size, cols), BF) for k in range(n_w)
        ],
        compiler_params=pltpu.CompilerParams(vmem_limit_bytes=32 << 20),
        cost_estimate=pl.CostEstimate(flops=0, bytes_accessed=10_000_000, transcendentals=0),
        name="cut_columns",
    )(at, array)


def join_columns_kernel(n_w, overlap, at_ref, *refs):
    *pieces, out_ref = refs
    wsh, core = at_ref[0], at_ref[1]
    cols = pieces[0].shape[1]
    for k in range(n_w):
        for b in range(n_w):

            @pl.when((wsh + k) % n_w == b)
            def _(k=k, b=b):
                at = slice(b * cols, (b + 1) * cols)
                if k == 0:
                    out_ref[:, at] = pieces[0][...].astype(F32)
                    return
                mine, other = pieces[2 * k - 1], pieces[2 * k]
                size = mine.shape[0]
                out_ref[pl.ds(pl.multiple_of(core * overlap, 16), size), at] = mine[...].astype(F32)
                out_ref[pl.ds(pl.multiple_of((1 - core) * overlap, 16), size), at] = other[
                    ...
                ].astype(F32)


def join_columns(at, pieces, n_w, overlap):
    own, cols = pieces[0].shape
    vmem = pl.BlockSpec(memory_space=pltpu.VMEM)
    return pl.pallas_call(
        functools.partial(join_columns_kernel, n_w, overlap),
        in_specs=[pl.BlockSpec(memory_space=pltpu.SMEM)] + [vmem] * len(pieces),
        out_specs=vmem,
        out_shape=jax.ShapeDtypeStruct((own, n_w * cols), F32),
        compiler_params=pltpu.CompilerParams(vmem_limit_bytes=40 << 20),
        cost_estimate=pl.CostEstimate(flops=0, bytes_accessed=16_000_000, transcendentals=0),
        name="join_columns",
    )(at, *pieces)


def unpack_kernel(at_ref, own_ref, other_ref, qkv_ref, out_ref, side_ref):
    z, y, core = at_ref[0], at_ref[1], at_ref[2]
    for h in range(HEADS + 1):
        slot = (h // 8 + 4 - z) % 4 * 4 + ((h // 2) % 4 + 4 - y) % 4
        piece = jnp.where(core == h % 2, own_ref[slot], other_ref[slot]).astype(F32)
        if h == HEADS:
            side_ref[...] = piece[:, 3 * HD :]
            break
        for part in range(3):
            at = (part * HEADS + h) * HD
            qkv_ref[:, at : at + HD] = piece[:, part * HD : (part + 1) * HD]
        out_ref[:, h * HD : (h + 1) * HD] = piece[:, 3 * HD :]


def unpack(at, own, other):
    rows = own.shape[1]
    vmem = pl.BlockSpec(memory_space=pltpu.VMEM)
    return pl.pallas_call(
        unpack_kernel,
        in_specs=[pl.BlockSpec(memory_space=pltpu.SMEM), vmem, vmem],
        out_specs=[vmem] * 3,
        out_shape=[
            jax.ShapeDtypeStruct((rows, 3 * HEADS * HD), F32),
            jax.ShapeDtypeStruct((rows, HEADS * HD), F32),
            jax.ShapeDtypeStruct((rows, HD), F32),
        ],
        compiler_params=pltpu.CompilerParams(vmem_limit_bytes=40 << 20),
        cost_estimate=pl.CostEstimate(flops=0, bytes_accessed=18_000_000, transcendentals=0),
        name="unpack",
    )(at, own, other)


def after(array, *others):
    return lax.optimization_barrier((array, *others))[0]


def on_device(
    layer_input,
    block_order,
    norm_gains,
    norm_shifts,
    qkv_weight,
    attn_bias,
    out_weight,
    out_bias,
    fc_weight,
    fc_bias,
    proj_weight,
    proj_bias,
    output_grad,
):
    seqs, rows, width = layer_input.shape
    tokens = seqs * rows
    n_ctx, n_w = lax.axis_size("ctx"), lax.axis_size("wsh")
    ctx, wsh = lax.axis_index("ctx"), lax.axis_index("wsh")
    z, y, core = ctx // 8, ctx // 2 % 4, ctx % 2
    own = width // n_w
    ff = fc_weight.shape[1] // n_w
    size, overlap = 208, 192
    at_x = jnp.stack([wsh, core])

    def x_shift(array, k):
        return lax.ppermute(array, "wsh", [((i + k) % n_w, i) for i in range(n_w)])

    def ctx_shift(array, to):
        return lax.ppermute(array, "ctx", [(to(i), i) for i in range(n_ctx)])

    def partner(array):
        return ctx_shift(array, lambda i: i ^ 1)

    def around(array):
        return [array] + [x_shift(array, k) for k in range(1, n_w)]

    def deal(choose):
        return [choose(0)] + [x_shift(choose(k), k) for k in range(1, n_w)]

    def send_back(pieces):
        total = pieces[0]
        for k in range(1, n_w):
            total = total + x_shift(pieces[k].astype(BF), n_w - k).astype(F32)
        return total

    def with_halves(whole, halves):
        pieces = [whole]
        for k in range(1, n_w):
            mine = x_shift(halves[k - 1], k)
            pieces += [mine, partner(mine)]
        return pieces

    def in_order(pieces):
        twice = jnp.stack(pieces + pieces)
        start = (n_w - wsh) % n_w
        return lax.dynamic_slice(twice, (start,) + (0,) * pieces[0].ndim, (n_w,) + pieces[0].shape)

    packed = jnp.concatenate(
        [norm_gains, norm_shifts, attn_bias, out_bias[None], proj_bias[None]], axis=0
    )
    vectors = in_order(around(packed)).transpose(1, 0, 2).reshape(8, width).astype(F32)
    gains, shifts, bias_pair = vectors[0:2], vectors[2:4], vectors[4:6]
    out_bias_row, proj_bias_row = vectors[6], vectors[7]

    residual = layer_input.reshape(tokens, width).astype(F32)
    normed_one, scaled_one, inverse_one = layer_norm(residual, gains[0], shifts[0])
    gathered = lax.all_gather(normed_one.astype(BF), "ctx", axis=0)

    head = jnp.minimum(ctx, HEADS - 1)
    head_cols = jnp.concatenate(
        [
            lax.dynamic_slice(qkv_weight, (0, part * width + head * HD), (own, HD))
            for part in range(3)
        ],
        axis=1,
    )
    head_weight = in_order(around(head_cols)).reshape(width, 3 * HD).T
    head_bias = lax.dynamic_slice(bias_pair, (0, head * HD), (2, HD))
    head_bias = jnp.concatenate([head_bias[:1], jnp.zeros((1, HD), F32), head_bias[1:]], axis=1)

    grad_low = output_grad.reshape(tokens, width)
    out_half = lax.dynamic_slice(out_weight, (core * overlap, 0), (size, width))
    out_all = join_rows(at_x, with_halves(out_weight, [out_half] * (n_w - 1)), n_w, overlap)
    fc_own, *fc_halves = cut_columns(at_x, fc_weight, n_w, size, overlap)
    fc_cols = join_rows(at_x, with_halves(fc_own, fc_halves), n_w, overlap)
    grad_group = jnp.concatenate(around(grad_low), axis=0)
    grad_active = mm(grad_group, proj_weight, NT)
    weight_all = lax.all_gather(after(head_weight, gathered), "ctx", axis=0)

    ordered, mixed_turned, mixed, logs = attend(block_order, gathered, head_weight, head_bias, rows)
    attended = lax.all_to_all(mixed_turned, "ctx", 0, 0).reshape(n_ctx * HD, tokens)[:width]
    middle = residual + mm(attended, out_all, TN) + out_bias_row
    normed_two, scaled_two, inverse_two = layer_norm(middle, gains[1], shifts[1])
    input_two = jnp.concatenate(around(normed_two.astype(BF)), axis=0)

    pre_gelu = mm(input_two, fc_cols) + fc_bias.astype(F32)
    activated, derivative = gelu_pair(pre_gelu)
    activated = activated.astype(BF)
    grad_pre = (grad_active * derivative).astype(BF)
    grad_parts = mm(grad_pre, fc_cols, NT)
    grad_two = grad_parts.reshape(n_w, tokens, width)
    grad_two = send_back([grad_two[k] for k in range(n_w)])
    activated, grad_pre = lax.optimization_barrier((activated, grad_pre, grad_parts))[:2]
    grad_proj = mm(activated, grad_group, TN).astype(BF)
    grad_fc = mm(input_two, grad_pre, TN).astype(BF)
    share_proj, share_fc = lax.psum((grad_proj, grad_fc), "ctx")

    grad_norm_two, gain_two, shift_two = norm_back(grad_two, scaled_two, inverse_two, gains[1])
    grad_middle = grad_low.astype(F32) + grad_norm_two
    grad_branch = grad_middle.astype(BF)
    grad_attended = mm(out_all, grad_branch, NT).astype(BF)
    grad_heads = jnp.pad(grad_attended, ((0, (n_ctx - HEADS) * HD), (0, 0)))
    grad_heads = lax.all_to_all(grad_heads.reshape(n_ctx, HD, tokens), "ctx", 0, 0)
    branch_group = jnp.concatenate(around(after(grad_branch, grad_attended)), axis=0)
    attended_rows = jnp.concatenate(
        deal(
            lambda k: lax.dynamic_slice(
                after(attended, grad_attended), ((wsh + n_w - k) % n_w * own, 0), (own, tokens)
            )
        ),
        axis=1,
    )

    branch = mm(after(activated, branch_group), proj_weight).reshape(n_w, tokens, width)
    branch = send_back([branch[k] for k in range(n_w)])
    layer_output = (middle + branch + proj_bias_row).astype(BF)

    grad_qkv = attend_back(block_order, ordered, mixed, logs, grad_heads, rows)
    grad_tokens = lax.all_to_all(grad_qkv, "ctx", 0, 0).reshape(n_ctx * 3 * HD, tokens)
    grad_tokens = grad_tokens[: 3 * width]

    grad_out = lax.dot_general(
        after(branch_group, grad_qkv), attended_rows, (((0,), (1,)), ((), ())), preferred_element_type=F32
    )
    column = lambda array: lax.dynamic_slice(
        jnp.sum(array.astype(F32), axis=0, keepdims=True), (0, wsh * own), (1, own)
    )
    side = jnp.concatenate(
        [
            jnp.sum(grad_pre.astype(F32), axis=0).reshape(n_w, own),
            column(grad_group),
            column(branch_group),
        ],
        axis=0,
    )
    chunks = jnp.concatenate([grad_out.astype(BF), side.astype(BF)], axis=0)
    chunks = jnp.pad(chunks, ((0, n_ctx * HD - chunks.shape[0]), (0, 0)))
    chunks = lax.all_to_all(chunks.reshape(n_ctx, HD, own), "ctx", 0, 0)
    out_piece = jnp.sum(chunks.astype(F32), axis=0).T.astype(BF)

    grad_cols = head_grad(grad_qkv, gathered)
    pieces = deal(
        lambda k: lax.dynamic_slice(grad_cols, ((wsh + n_w - k) % n_w * own, 0), (own, 3 * HD))
        if k == 0
        else lax.dynamic_slice(
            grad_cols.astype(BF), ((wsh + n_w - k) % n_w * own, 0), (own, 3 * HD)
        )
    )
    total = pieces[0] + sum(piece.astype(F32) for piece in pieces[1:])
    piece = jnp.concatenate([total.astype(BF), out_piece], axis=1)
    along_y = jnp.stack(
        [piece]
        + [ctx_shift(piece, lambda i, k=k: i // 8 * 8 + (i + 2 * k) % 8) for k in range(1, 4)]
    )
    along_z = jnp.concatenate(
        [along_y] + [ctx_shift(along_y, lambda i, k=k: (i + 8 * k) % 32) for k in range(1, 4)]
    )
    qkv_out, out_out, side_out = unpack(jnp.stack([z, y, core]), along_z, partner(along_z))
    side_out = side_out.T[: n_w + 2]

    grad_one = mm(grad_tokens, weight_all.reshape(n_ctx * 3 * HD, width)[: 3 * width], TN)
    grad_norm_one, gain_one, shift_one = norm_back(grad_one, scaled_one, inverse_one, gains[0])
    input_grad = grad_middle + grad_norm_one

    wide = jnp.sum(grad_tokens.astype(F32), axis=1).reshape(HEADS, 3, HD)
    vector_grads = jnp.stack(
        [
            gain_one,
            gain_two,
            shift_one,
            shift_two,
            wide[:, 0].reshape(width),
            wide[:, 2].reshape(width),
        ]
    )
    vector_grads = vector_grads.reshape(6, n_w, own).transpose(1, 0, 2).reshape(n_w, 6 * own)
    pieces = deal(
        lambda k: lax.dynamic_slice(vector_grads, ((wsh + n_w - k) % n_w, 0), (1, 6 * own))
    )
    vector_sum = (pieces[0] + pieces[1]) + (pieces[2] + pieces[3])
    padded = jnp.pad(vector_sum.reshape(-1), (0, -6 * own % 1024)).reshape(1, 8, -1)
    everyone = lax.all_to_all(
        jnp.broadcast_to(padded, (n_ctx,) + padded.shape[1:]), "ctx", 0, 0
    )
    vector_out = jnp.sum(everyone, axis=0).reshape(-1)[: 6 * own].reshape(6, own)

    rows_for = lambda k, start, count: lax.dynamic_slice(
        share_fc, ((wsh + n_w - k) % n_w * own + start, 0), (count, ff)
    )
    fc_out = join_columns(
        at_x,
        with_halves(
            rows_for(0, 0, own), [rows_for(k, core * overlap, size) for k in range(1, n_w)]
        ),
        n_w,
        overlap,
    )
    return (
        layer_output.reshape(seqs, rows, width),
        input_grad.reshape(seqs, rows, width),
        vector_out[0:2],
        vector_out[2:4],
        qkv_out,
        vector_out[4:6],
        out_out,
        side_out[n_w + 1],
        fc_out,
        side_out[:n_w].reshape(ff),
        share_proj.astype(F32),
        side_out[n_w],
    )


def solution(mesh):
    return jax.shard_map(
        on_device,
        mesh=mesh,
        in_specs=(
            P("wsh", "ctx", None),
            P("wsh", None),
            P(None, "wsh"),
            P(None, "wsh"),
            P("wsh", None),
            P(None, "wsh"),
            P("wsh", None),
            P("wsh"),
            P("wsh", None),
            P("wsh"),
            P("wsh", None),
            P("wsh"),
            P("wsh", "ctx", None),
        ),
        out_specs=(
            P("wsh", "ctx", None),
            P("wsh", "ctx", None),
            P(None, "wsh"),
            P(None, "wsh"),
            P("wsh", None),
            P(None, "wsh"),
            P("wsh", None),
            P("wsh"),
            P("wsh", None),
            P("wsh"),
            P("wsh", None),
            P("wsh"),
        ),
        check_vma=False,
    )
```

```python
import functools

import jax
import jax.numpy as jnp
from jax import lax
from jax.experimental import pallas as pl
from jax.experimental.pallas import tpu as pltpu
from jax.sharding import PartitionSpec as P

HEADS = 25
HD = 64
QB = 256
BF = jnp.bfloat16
F32 = jnp.float32
NN = (((1,), (0,)), ((), ()))
NT = (((1,), (1,)), ((), ()))
TN = (((0,), (0,)), ((), ()))


def mm(left, right, dims=NN):
    return lax.dot_general(left, right, dims, preferred_element_type=F32)


def layer_norm(hidden, gain_row, shift_row):
    centered = hidden - jnp.mean(hidden, axis=-1, keepdims=True)
    inverse = lax.rsqrt(jnp.mean(centered * centered, axis=-1, keepdims=True) + 1e-05)
    scaled = centered * inverse
    return scaled * gain_row + shift_row, scaled, inverse


def norm_back(gradient, scaled, inverse, gain_row):
    weighted = gradient * gain_row
    first_mean = jnp.mean(weighted, axis=-1, keepdims=True)
    second_mean = jnp.mean(weighted * scaled, axis=-1, keepdims=True)
    result = inverse * (weighted - first_mean - scaled * second_mean)
    return result, jnp.sum(gradient * scaled, axis=0), jnp.sum(gradient, axis=0)


def gelu_pair(pre_gelu):
    squared = pre_gelu * pre_gelu
    tangent = jnp.tanh(0.7978845608028654 * (pre_gelu + 0.044715 * squared * pre_gelu))
    result = 0.5 * pre_gelu * (1.0 + tangent)
    derivative = 0.5 * (1.0 + tangent) + 0.5 * pre_gelu * (
        1.0 - tangent * tangent
    ) * 0.7978845608028654 * (1.0 + 3.0 * 0.044715 * squared)
    return result, derivative


def ordered_rows(order_ref, seq, block, half, length):
    return pl.multiple_of(seq * length + order_ref[seq, block] * half, half)


def below_mask():
    return lax.broadcasted_iota(jnp.int32, (QB, QB), 0) <= lax.broadcasted_iota(
        jnp.int32, (QB, QB), 1
    )


def attend_kernel(
    seqs, rows, half, order_ref, in_ref, gain_ref, shift_ref, weight_ref, bias_ref,
    normed_ref, sorted_ref, out_ref, mixed_ref, log_ref, rows_ref,
):
    step = pl.program_id(0)
    tokens = seqs * rows
    group = in_ref.shape[0] // tokens
    length = mixed_ref.shape[2]
    per = rows // half
    normed = layer_norm(in_ref[...].astype(F32), gain_ref[...], shift_ref[...])[0].astype(BF)
    normed_ref[...] = normed
    made = (mm(normed, weight_ref[...], NT) + bias_ref[...]).astype(BF)
    for g in range(group):
        for s in range(seqs):
            for b in range(per):
                at = ordered_rows(order_ref, s, (step * group + g) * per + b, half, length)
                first = g * tokens + s * rows + b * half
                sorted_ref[pl.ds(at, half), :] = made[first : first + half]

    @pl.when(step == pl.num_programs(0) - 1)
    def _():
        below = below_mask()

        def one_seq(s, carry):
            base = pl.multiple_of(s * length, length)
            k_all = sorted_ref[pl.ds(base, length), HD : 2 * HD]
            v_turned = sorted_ref[pl.ds(base, length), 2 * HD :].T
            for i in range(length // QB):
                lo, hi = i * QB, (i + 1) * QB
                q_rows = sorted_ref[pl.ds(base + lo, QB), :HD] * 0.125
                scores = mm(k_all[:hi], q_rows, NT)
                last = jnp.where(below, scores[lo:], -1e30)
                best = jnp.max(last, axis=0, keepdims=True)
                if i:
                    best = jnp.maximum(best, jnp.max(scores[:lo], axis=0, keepdims=True))
                tail = jnp.exp(last - best)
                total = jnp.sum(tail, axis=0, keepdims=True)
                mixed = mm(v_turned[:, lo:hi], tail.astype(BF))
                if i:
                    head = jnp.exp(scores[:lo] - best)
                    total = total + jnp.sum(head, axis=0, keepdims=True)
                    mixed = mixed + mm(v_turned[:, :lo], head.astype(BF))
                mixed = mixed / total
                mixed_ref[s, :, lo:hi] = mixed
                log_ref[s, :, lo:hi] = best + jnp.log(total)
                rows_ref[pl.ds(base + lo, QB), :] = mixed.T
            return carry

        lax.fori_loop(0, seqs, one_seq, 0)

        def one_block(c, carry):
            parts = [
                rows_ref[pl.ds(ordered_rows(order_ref, s, c * per + b, half, length), half), :]
                for s in range(seqs)
                for b in range(per)
            ]
            out_ref[c] = jnp.concatenate(parts, axis=0).T.astype(BF)
            return carry

        lax.fori_loop(0, out_ref.shape[0], one_block, 0)


def attend(order, gathered, gain, shift, weight, bias, rows):
    seqs, halves = order.shape
    tokens, width = seqs * rows, gathered.shape[1]
    n_ctx = gathered.shape[0] // tokens
    length = rows * n_ctx
    half = length // halves
    group = 4
    whole = lambda *shape: pl.BlockSpec(shape, lambda i: (0,) * len(shape))
    return pl.pallas_call(
        functools.partial(attend_kernel, seqs, rows, half),
        grid=(n_ctx // group,),
        in_specs=[
            pl.BlockSpec(memory_space=pltpu.SMEM),
            pl.BlockSpec((group * tokens, width), lambda i: (i, 0)),
            whole(1, width),
            whole(1, width),
            whole(3 * HD, width),
            whole(1, 3 * HD),
        ],
        out_specs=[
            pl.BlockSpec((group * tokens, width), lambda i: (i, 0)),
            whole(seqs * length, 3 * HD),
            whole(n_ctx, HD, tokens),
            whole(seqs, HD, length),
            whole(seqs, 1, length),
        ],
        out_shape=[
            jax.ShapeDtypeStruct(gathered.shape, BF),
            jax.ShapeDtypeStruct((seqs * length, 3 * HD), BF),
            jax.ShapeDtypeStruct((n_ctx, HD, tokens), BF),
            jax.ShapeDtypeStruct((seqs, HD, length), F32),
            jax.ShapeDtypeStruct((seqs, 1, length), F32),
        ],
        scratch_shapes=[pltpu.VMEM((seqs * length, HD), F32)],
        compiler_params=pltpu.CompilerParams(vmem_limit_bytes=48 << 20),
        cost_estimate=pl.CostEstimate(
            flops=20_000_000_000, bytes_accessed=20_000_000, transcendentals=0
        ),
        name="attend",
    )(order, gathered, gain, shift, weight, bias)


def attend_back_kernel(
    seqs, rows, half, order_ref, sorted_ref, mixed_ref, log_ref, grad_ref, out_ref,
    rows_ref, key_ref, value_ref, all_ref,
):
    n_ctx, _, tokens = grad_ref.shape
    length = mixed_ref.shape[2]
    per = rows // half

    def spread(c, carry):
        block = grad_ref[c].T
        for s in range(seqs):
            for b in range(per):
                at = ordered_rows(order_ref, s, c * per + b, half, length)
                first = s * rows + b * half
                rows_ref[pl.ds(at, half), :] = block[first : first + half]
        return carry

    lax.fori_loop(0, n_ctx, spread, 0)
    below = below_mask()

    def one_seq(s, carry):
        base = pl.multiple_of(s * length, length)
        k_all = sorted_ref[pl.ds(base, length), HD : 2 * HD]
        v_all = sorted_ref[pl.ds(base, length), 2 * HD :]
        k_turned = k_all.T
        g_turned = rows_ref[pl.ds(base, length), :].T
        delta = jnp.sum(g_turned.astype(F32) * mixed_ref[s], axis=0, keepdims=True)
        key_ref[...] = jnp.zeros_like(key_ref)
        value_ref[...] = jnp.zeros_like(value_ref)
        for i in range(length // QB):
            lo, hi = i * QB, (i + 1) * QB
            q_rows = sorted_ref[pl.ds(base + lo, QB), :HD] * 0.125
            g_rows = rows_ref[pl.ds(base + lo, QB), :]
            log_row = log_ref[s, :, lo:hi]
            delta_row = delta[:, lo:hi]
            query = jnp.zeros((HD, QB), F32)
            for first, end in ((0, lo), (lo, hi)):
                if first == end:
                    continue
                scores = mm(k_all[first:end], q_rows, NT)
                probs = jnp.exp(scores - log_row)
                if end == hi:
                    probs = jnp.where(below, probs, 0.0)
                slopes = mm(v_all[first:end], g_rows, NT)
                pulled = (probs * (slopes - delta_row)).astype(BF)
                value_ref[first:end, :] += mm(probs.astype(BF), g_rows)
                key_ref[first:end, :] += mm(pulled, q_rows)
                query = query + mm(k_turned[:, first:end], pulled)
            all_ref[pl.ds(base + lo, QB), :HD] = (query * 0.125).T
        all_ref[pl.ds(base, length), HD : 2 * HD] = key_ref[...]
        all_ref[pl.ds(base, length), 2 * HD :] = value_ref[...]
        return carry

    lax.fori_loop(0, seqs, one_seq, 0)

    def one_block(c, carry):
        parts = [
            all_ref[pl.ds(ordered_rows(order_ref, s, c * per + b, half, length), half), :]
            for s in range(seqs)
            for b in range(per)
        ]
        out_ref[c] = jnp.concatenate(parts, axis=0).T.astype(BF)
        return carry

    lax.fori_loop(0, n_ctx, one_block, 0)


def attend_back(order, ordered, mixed, logs, grads, rows):
    n_ctx, _, tokens = grads.shape
    seqs, halves = order.shape
    length = rows * n_ctx
    half = length // halves
    vmem = pl.BlockSpec(memory_space=pltpu.VMEM)
    return pl.pallas_call(
        functools.partial(attend_back_kernel, seqs, rows, half),
        in_specs=[pl.BlockSpec(memory_space=pltpu.SMEM)] + [vmem] * 4,
        out_specs=vmem,
        out_shape=jax.ShapeDtypeStruct((n_ctx, 3 * HD, tokens), BF),
        scratch_shapes=[
            pltpu.VMEM((seqs * length, HD), BF),
            pltpu.VMEM((length, HD), F32),
            pltpu.VMEM((length, HD), F32),
            pltpu.VMEM((seqs * length, 3 * HD), F32),
        ],
        compiler_params=pltpu.CompilerParams(vmem_limit_bytes=48 << 20),
        cost_estimate=pl.CostEstimate(
            flops=20_000_000_000, bytes_accessed=10_000_000, transcendentals=0
        ),
        name="attend_back",
    )(order, ordered, mixed, logs, grads)


def head_grad_kernel(grad_ref, in_ref, out_ref, total_ref):
    step = pl.program_id(0)

    @pl.when(step == 0)
    def _():
        total_ref[...] = jnp.zeros_like(total_ref)

    turned = jnp.concatenate([grad_ref[g] for g in range(grad_ref.shape[0])], axis=1)
    total_ref[...] += mm(turned, in_ref[...])

    @pl.when(step == pl.num_programs(0) - 1)
    def _():
        out_ref[...] = total_ref[...].T


def head_grad(grads, gathered):
    n_ctx, _, tokens = grads.shape
    width = gathered.shape[1]
    group = 4
    return pl.pallas_call(
        head_grad_kernel,
        grid=(n_ctx // group,),
        in_specs=[
            pl.BlockSpec((group, 3 * HD, tokens), lambda i: (i, 0, 0)),
            pl.BlockSpec((group * tokens, width), lambda i: (i, 0)),
        ],
        out_specs=pl.BlockSpec((width, 3 * HD), lambda i: (0, 0)),
        out_shape=jax.ShapeDtypeStruct((width, 3 * HD), F32),
        scratch_shapes=[pltpu.VMEM((3 * HD, width), F32)],
        compiler_params=pltpu.CompilerParams(vmem_limit_bytes=32 << 20),
        cost_estimate=pl.CostEstimate(
            flops=5_000_000_000, bytes_accessed=15_000_000, transcendentals=0
        ),
        name="head_grad",
    )(grads, gathered)


def join_rows_kernel(n_w, overlap, at_ref, *refs):
    *pieces, out_ref = refs
    wsh, core = at_ref[0], at_ref[1]
    own = pieces[0].shape[0]
    out_ref[pl.ds(pl.multiple_of(wsh * own, 16), own), :] = pieces[0][...]
    for k in range(1, n_w):
        base = (wsh + k) % n_w * own
        mine, other = pieces[2 * k - 1], pieces[2 * k]
        size = mine.shape[0]
        out_ref[pl.ds(pl.multiple_of(base + core * overlap, 16), size), :] = mine[...]
        out_ref[pl.ds(pl.multiple_of(base + (1 - core) * overlap, 16), size), :] = other[...]


def join_rows(at, pieces, n_w, overlap):
    own, width = pieces[0].shape
    vmem = pl.BlockSpec(memory_space=pltpu.VMEM)
    return pl.pallas_call(
        functools.partial(join_rows_kernel, n_w, overlap),
        in_specs=[pl.BlockSpec(memory_space=pltpu.SMEM)] + [vmem] * len(pieces),
        out_specs=vmem,
        out_shape=jax.ShapeDtypeStruct((n_w * own, width), BF),
        compiler_params=pltpu.CompilerParams(vmem_limit_bytes=32 << 20),
        cost_estimate=pl.CostEstimate(flops=0, bytes_accessed=12_000_000, transcendentals=0),
        name="join_rows",
    )(at, *pieces)


def cut_columns_kernel(n_w, overlap, at_ref, in_ref, *out_refs):
    wsh, core = at_ref[0], at_ref[1]
    cols = out_refs[0].shape[1]
    for k, out_ref in enumerate(out_refs):
        size = out_ref.shape[0]
        start = 0 if k == 0 else pl.multiple_of(core * overlap, 16)
        for b in range(n_w):

            @pl.when((wsh + n_w - k) % n_w == b)
            def _(out_ref=out_ref, start=start, size=size, b=b):
                out_ref[...] = in_ref[pl.ds(start, size), b * cols : (b + 1) * cols]


def cut_columns(at, array, n_w, size, overlap):
    own, cols = array.shape[0], array.shape[1] // n_w
    vmem = pl.BlockSpec(memory_space=pltpu.VMEM)
    return pl.pallas_call(
        functools.partial(cut_columns_kernel, n_w, overlap),
        in_specs=[pl.BlockSpec(memory_space=pltpu.SMEM), vmem],
        out_specs=[vmem] * n_w,
        out_shape=[
            jax.ShapeDtypeStruct((own if k == 0 else size, cols), BF) for k in range(n_w)
        ],
        compiler_params=pltpu.CompilerParams(vmem_limit_bytes=32 << 20),
        cost_estimate=pl.CostEstimate(flops=0, bytes_accessed=10_000_000, transcendentals=0),
        name="cut_columns",
    )(at, array)


def join_columns_kernel(n_w, overlap, at_ref, *refs):
    *pieces, out_ref = refs
    wsh, core = at_ref[0], at_ref[1]
    cols = pieces[0].shape[1]
    for k in range(n_w):
        for b in range(n_w):

            @pl.when((wsh + k) % n_w == b)
            def _(k=k, b=b):
                at = slice(b * cols, (b + 1) * cols)
                if k == 0:
                    out_ref[:, at] = pieces[0][...].astype(F32)
                    return
                mine, other = pieces[2 * k - 1], pieces[2 * k]
                size = mine.shape[0]
                out_ref[pl.ds(pl.multiple_of(core * overlap, 16), size), at] = mine[...].astype(F32)
                out_ref[pl.ds(pl.multiple_of((1 - core) * overlap, 16), size), at] = other[
                    ...
                ].astype(F32)


def join_columns(at, pieces, n_w, overlap):
    own, cols = pieces[0].shape
    vmem = pl.BlockSpec(memory_space=pltpu.VMEM)
    return pl.pallas_call(
        functools.partial(join_columns_kernel, n_w, overlap),
        in_specs=[pl.BlockSpec(memory_space=pltpu.SMEM)] + [vmem] * len(pieces),
        out_specs=vmem,
        out_shape=jax.ShapeDtypeStruct((own, n_w * cols), F32),
        compiler_params=pltpu.CompilerParams(vmem_limit_bytes=40 << 20),
        cost_estimate=pl.CostEstimate(flops=0, bytes_accessed=16_000_000, transcendentals=0),
        name="join_columns",
    )(at, *pieces)


def out_grad_kernel(n_w, in_ref, grad_ref, side_ref, out_ref):
    made = mm(in_ref[...], grad_ref[...])
    chunks = made.shape[0] // 16
    out_ref[...] = jnp.zeros_like(out_ref)
    for c in range(chunks):
        out_ref[c] = made[c * 16 : (c + 1) * 16].astype(BF)
    out_ref[chunks, :1] = side_ref[...].astype(BF)


def out_grad(rows, grads, side, n_ctx, n_w):
    vmem = pl.BlockSpec(memory_space=pltpu.VMEM)
    return pl.pallas_call(
        functools.partial(out_grad_kernel, n_w),
        in_specs=[vmem] * 3,
        out_specs=vmem,
        out_shape=jax.ShapeDtypeStruct((n_ctx, 16, grads.shape[1]), BF),
        compiler_params=pltpu.CompilerParams(vmem_limit_bytes=24 << 20),
        cost_estimate=pl.CostEstimate(
            flops=1_500_000_000, bytes_accessed=4_000_000, transcendentals=0
        ),
        name="out_grad",
    )(rows, grads, side)


def pack_kernel(chunk_ref, *refs):
    *pieces, left_ref, right_ref = refs
    total = pieces[0][...]
    for piece in pieces[1:]:
        total = total + piece[...].astype(F32)
    left_ref[...] = total[:, : 2 * HD].astype(BF)
    chunk = chunk_ref[0].astype(F32)
    for c in range(1, chunk_ref.shape[0]):
        chunk = chunk + chunk_ref[c].astype(F32)
    turned = jnp.concatenate(
        [chunk[:, q * HD : (q + 1) * HD] for q in range(chunk.shape[1] // HD)], axis=0
    )
    right_ref[...] = jnp.concatenate([total[:, 2 * HD :], turned], axis=1).astype(BF)


def pack(chunks, pieces):
    rows = pieces[0].shape[0]
    vmem = pl.BlockSpec(memory_space=pltpu.VMEM)
    return pl.pallas_call(
        pack_kernel,
        in_specs=[vmem] * (1 + len(pieces)),
        out_specs=[vmem] * 2,
        out_shape=[jax.ShapeDtypeStruct((rows, 2 * HD), BF)] * 2,
        compiler_params=pltpu.CompilerParams(vmem_limit_bytes=24 << 20),
        cost_estimate=pl.CostEstimate(flops=0, bytes_accessed=4_000_000, transcendentals=0),
        name="pack",
    )(chunks, *pieces)


def unpack_kernel(at_ref, left_own, left_other, right_own, right_other, qkv_ref, out_ref, side_ref):
    z, y, core = at_ref[0], at_ref[1], at_ref[2]
    for h in range(HEADS + 1):
        by_z, by_y = (h // 8 + 4 - z) % 4, ((h // 2) % 4 + 4 - y) % 4
        same = core == h % 2
        right_at = by_y * 4 + by_z
        right = jnp.where(same, right_own[right_at], right_other[right_at]).astype(F32)
        if h == HEADS:
            for q in range(HEADS):
                side_ref[:, q * HD : (q + 1) * HD] = right[q * 16 : q * 16 + 8, HD:]
            break
        left_at = by_z * 4 + by_y
        left = jnp.where(same, left_own[left_at], left_other[left_at]).astype(F32)
        for part, piece in enumerate((left[:, :HD], left[:, HD:], right[:, :HD])):
            at = (part * HEADS + h) * HD
            qkv_ref[:, at : at + HD] = piece
        for q in range(HEADS):
            out_ref[h * 16 : (h + 1) * 16, q * HD : (q + 1) * HD] = right[
                q * 16 : (q + 1) * 16, HD:
            ]


def unpack(at, left_own, left_other, right_own, right_other):
    rows = left_own.shape[1]
    vmem = pl.BlockSpec(memory_space=pltpu.VMEM)
    return pl.pallas_call(
        unpack_kernel,
        in_specs=[pl.BlockSpec(memory_space=pltpu.SMEM)] + [vmem] * 4,
        out_specs=[vmem] * 3,
        out_shape=[
            jax.ShapeDtypeStruct((rows, 3 * HEADS * HD), F32),
            jax.ShapeDtypeStruct((rows, HEADS * HD), F32),
            jax.ShapeDtypeStruct((8, HEADS * HD), F32),
        ],
        compiler_params=pltpu.CompilerParams(vmem_limit_bytes=40 << 20),
        cost_estimate=pl.CostEstimate(flops=0, bytes_accessed=18_000_000, transcendentals=0),
        name="unpack",
    )(at, left_own, left_other, right_own, right_other)


def after(array, *others):
    return lax.optimization_barrier((array, *others))[0]


def on_device(
    layer_input,
    block_order,
    norm_gains,
    norm_shifts,
    qkv_weight,
    attn_bias,
    out_weight,
    out_bias,
    fc_weight,
    fc_bias,
    proj_weight,
    proj_bias,
    output_grad,
):
    seqs, rows, width = layer_input.shape
    tokens = seqs * rows
    n_ctx, n_w = lax.axis_size("ctx"), lax.axis_size("wsh")
    ctx, wsh = lax.axis_index("ctx"), lax.axis_index("wsh")
    z, y, core = ctx // 8, ctx // 2 % 4, ctx % 2
    own = width // n_w
    ff = fc_weight.shape[1] // n_w
    size, overlap = 208, 192
    at_x = jnp.stack([wsh, core])

    def x_shift(array, k):
        return lax.ppermute(array, "wsh", [((i + k) % n_w, i) for i in range(n_w)])

    def ctx_shift(array, to):
        return lax.ppermute(array, "ctx", [(to(i), i) for i in range(n_ctx)])

    def partner(array):
        return ctx_shift(array, lambda i: i ^ 1)

    def around(array):
        return [array] + [x_shift(array, k) for k in range(1, n_w)]

    def deal(choose):
        return [choose(0)] + [x_shift(choose(k), k) for k in range(1, n_w)]

    def send_back(pieces):
        total = pieces[0]
        for k in range(1, n_w):
            total = total + x_shift(pieces[k].astype(BF), n_w - k).astype(F32)
        return total

    def with_halves(whole, halves):
        pieces = [whole]
        for k in range(1, n_w):
            mine = x_shift(halves[k - 1], k)
            pieces += [mine, partner(mine)]
        return pieces

    def in_order(pieces):
        twice = jnp.stack(pieces + pieces)
        start = (n_w - wsh) % n_w
        return lax.dynamic_slice(twice, (start,) + (0,) * pieces[0].ndim, (n_w,) + pieces[0].shape)

    low = layer_input.reshape(tokens, width)
    gathered = lax.all_gather(low, "ctx", axis=0, tiled=True)
    packed = jnp.concatenate(
        [norm_gains, norm_shifts, attn_bias, out_bias[None], proj_bias[None]], axis=0
    )
    vectors = in_order(around(packed)).transpose(1, 0, 2).reshape(8, width).astype(F32)
    gains, shifts, bias_pair = vectors[0:2], vectors[2:4], vectors[4:6]
    out_bias_row, proj_bias_row = vectors[6], vectors[7]

    head = jnp.minimum(ctx, HEADS - 1)
    head_cols = jnp.concatenate(
        [
            lax.dynamic_slice(qkv_weight, (0, part * width + head * HD), (own, HD))
            for part in range(3)
        ],
        axis=1,
    )
    head_weight = in_order(around(head_cols)).reshape(width, 3 * HD).T
    head_bias = lax.dynamic_slice(bias_pair, (0, head * HD), (2, HD))
    head_bias = jnp.concatenate([head_bias[:1], jnp.zeros((1, HD), F32), head_bias[1:]], axis=1)

    grad_low = output_grad.reshape(tokens, width)
    grad_group = jnp.concatenate(around(after(grad_low, head_weight)), axis=0)
    grad_active = mm(grad_group, proj_weight, NT)
    out_half = lax.dynamic_slice(
        after(out_weight, head_weight), (core * overlap, 0), (size, width)
    )
    out_all = join_rows(at_x, with_halves(out_weight, [out_half] * (n_w - 1)), n_w, overlap)
    fc_own, *fc_halves = cut_columns(at_x, fc_weight, n_w, size, overlap)
    fc_halves = lax.optimization_barrier((*fc_halves, grad_group))[: n_w - 1]
    fc_cols = join_rows(at_x, with_halves(fc_own, fc_halves), n_w, overlap)

    input_one, ordered, mixed_turned, mixed, logs = attend(
        block_order, gathered, gains[:1], shifts[:1], head_weight, head_bias, rows
    )
    weight_all = lax.all_gather(head_weight, "ctx", axis=0, tiled=True)
    attended = lax.all_to_all(mixed_turned, "ctx", 0, 0).reshape(n_ctx * HD, tokens)[:width]
    residual = low.astype(F32)
    middle = residual + mm(attended, out_all, TN) + out_bias_row
    normed_two, scaled_two, inverse_two = layer_norm(middle, gains[1], shifts[1])
    input_two = jnp.concatenate(around(normed_two.astype(BF)), axis=0)

    pre_gelu = mm(input_two, fc_cols) + fc_bias.astype(F32)
    activated, derivative = gelu_pair(pre_gelu)
    activated = activated.astype(BF)
    grad_pre = (grad_active * derivative).astype(BF)
    grad_two = mm(grad_pre, fc_cols, NT).reshape(n_w, tokens, width)
    came = [x_shift(grad_two[k].astype(BF), n_w - k) for k in range(1, n_w)]
    activated, grad_pre = lax.optimization_barrier((activated, grad_pre, came[0], weight_all))[:2]
    grad_proj = mm(activated, grad_group, TN).astype(BF)
    grad_fc = mm(input_two, grad_pre, TN).astype(BF)
    came = lax.optimization_barrier((*came, grad_proj, grad_fc))[: n_w - 1]
    grad_two = grad_two[0] + sum(piece.astype(F32) for piece in came)
    grad_fc_bias = jnp.sum(grad_pre.astype(F32), axis=0, keepdims=True)
    share_proj, share_fc = lax.psum((grad_proj, grad_fc), "ctx")

    grad_norm_two, gain_two, shift_two = norm_back(grad_two, scaled_two, inverse_two, gains[1])
    grad_middle = grad_low.astype(F32) + grad_norm_two
    grad_branch = grad_middle.astype(BF)
    grad_attended = mm(out_all, grad_branch, NT).astype(BF)
    grad_heads = jnp.pad(grad_attended, ((0, (n_ctx - HEADS) * HD), (0, 0)))
    grad_heads = lax.all_to_all(grad_heads.reshape(n_ctx, HD, tokens), "ctx", 0, 0)
    branch_group = jnp.concatenate(around(after(grad_branch, grad_attended)), axis=0)
    attended_rows = jnp.concatenate(
        deal(
            lambda k: lax.dynamic_slice(
                after(attended, activated), ((wsh + n_w - k) % n_w * own, 0), (own, tokens)
            )
        ),
        axis=1,
    )

    branch = mm(after(activated, grad_attended), proj_weight).reshape(n_w, tokens, width)
    branch = send_back([branch[k] for k in range(n_w)])
    layer_output = (middle + branch + proj_bias_row).astype(BF)

    chunks = out_grad(attended_rows, branch_group, grad_fc_bias, n_ctx, n_w)
    grad_heads = after(grad_heads, chunks)
    chunks = lax.all_to_all(chunks, "ctx", 0, 0)

    grad_qkv = attend_back(block_order, ordered, mixed, logs, grad_heads, rows)
    grad_tokens = lax.all_to_all(grad_qkv, "ctx", 0, 0).reshape(n_ctx * 3 * HD, tokens)

    grad_cols = head_grad(grad_qkv, input_one)
    grad_cols_low = grad_cols.astype(BF)
    pieces = deal(
        lambda k: lax.dynamic_slice(
            grad_cols if k == 0 else grad_cols_low,
            ((wsh + n_w - k) % n_w * own, 0),
            (own, 3 * HD),
        )
    )
    left, right = pack(chunks, pieces)
    from_y = lambda array, k: ctx_shift(array, lambda i: i // 8 * 8 + (i + 2 * k) % 8)
    from_z = lambda array, k: ctx_shift(array, lambda i: (i + 8 * k) % 32)
    left = jnp.stack([left] + [from_y(left, k) for k in range(1, 4)])
    right = jnp.stack([right] + [from_z(right, k) for k in range(1, 4)])
    left = jnp.concatenate([left] + [from_z(left, k) for k in range(1, 4)])
    right = jnp.concatenate([right] + [from_y(right, k) for k in range(1, 4)])
    grad_one = mm(grad_tokens, weight_all, TN)
    _, scaled_one, inverse_one = layer_norm(residual, gains[0], shifts[0])
    grad_norm_one, gain_one, shift_one = norm_back(grad_one, scaled_one, inverse_one, gains[0])
    input_grad = grad_middle + grad_norm_one
    qkv_out, out_out, side_out = unpack(
        jnp.stack([z, y, core]), after(left, grad_one), partner(left), right, partner(right)
    )

    wide = jnp.sum(grad_tokens.astype(F32), axis=1).reshape(n_ctx, 3, HD)[:HEADS]
    vector_grads = jnp.stack(
        [
            gain_one,
            gain_two,
            shift_one,
            shift_two,
            wide[:, 0].reshape(width),
            wide[:, 2].reshape(width),
            jnp.sum(grad_low.astype(F32), axis=0),
            jnp.sum(grad_branch.astype(F32), axis=0),
        ]
    )
    vector_grads = vector_grads.reshape(8, n_w, own).transpose(1, 0, 2)
    pieces = deal(
        lambda k: lax.dynamic_slice(vector_grads, ((wsh + n_w - k) % n_w, 0, 0), (1, 8, own))
    )
    vector_sum = (pieces[0] + pieces[1]) + (pieces[2] + pieces[3])
    everyone = lax.all_to_all(jnp.broadcast_to(vector_sum, (n_ctx, 8, own)), "ctx", 0, 0)
    vector_out = jnp.sum(everyone, axis=0)

    rows_for = lambda k, start, count: lax.dynamic_slice(
        share_fc, ((wsh + n_w - k) % n_w * own + start, 0), (count, ff)
    )
    fc_out = join_columns(
        at_x,
        with_halves(
            rows_for(0, 0, own), [rows_for(k, core * overlap, size) for k in range(1, n_w)]
        ),
        n_w,
        overlap,
    )
    return (
        layer_output.reshape(seqs, rows, width),
        input_grad.reshape(seqs, rows, width),
        vector_out[0:2],
        vector_out[2:4],
        qkv_out,
        vector_out[4:6],
        out_out,
        vector_out[7],
        fc_out,
        side_out[0],
        share_proj.astype(F32),
        vector_out[6],
    )


def solution(mesh):
    return jax.shard_map(
        on_device,
        mesh=mesh,
        in_specs=(
            P("wsh", "ctx", None),
            P("wsh", None),
            P(None, "wsh"),
            P(None, "wsh"),
            P("wsh", None),
            P(None, "wsh"),
            P("wsh", None),
            P("wsh"),
            P("wsh", None),
            P("wsh"),
            P("wsh", None),
            P("wsh"),
            P("wsh", "ctx", None),
        ),
        out_specs=(
            P("wsh", "ctx", None),
            P("wsh", "ctx", None),
            P(None, "wsh"),
            P(None, "wsh"),
            P("wsh", None),
            P(None, "wsh"),
            P("wsh", None),
            P("wsh"),
            P("wsh", None),
            P("wsh"),
            P("wsh", None),
            P("wsh"),
        ),
        check_vma=False,
    )
```

```python
import functools

import jax
import jax.numpy as jnp
from jax import lax
from jax.experimental import pallas as pl
from jax.experimental.pallas import tpu as pltpu
from jax.sharding import PartitionSpec as P

HEADS = 25
HD = 64
QB = 256
BF = jnp.bfloat16
F32 = jnp.float32
NN = (((1,), (0,)), ((), ()))
NT = (((1,), (1,)), ((), ()))
TN = (((0,), (0,)), ((), ()))


def mm(left, right, dims=NN):
    return lax.dot_general(left, right, dims, preferred_element_type=F32)


def layer_norm(hidden, gain_row, shift_row):
    centered = hidden - jnp.mean(hidden, axis=-1, keepdims=True)
    inverse = lax.rsqrt(jnp.mean(centered * centered, axis=-1, keepdims=True) + 1e-05)
    scaled = centered * inverse
    return scaled * gain_row + shift_row, scaled, inverse


def norm_back(gradient, scaled, inverse, gain_row):
    weighted = gradient * gain_row
    first_mean = jnp.mean(weighted, axis=-1, keepdims=True)
    second_mean = jnp.mean(weighted * scaled, axis=-1, keepdims=True)
    result = inverse * (weighted - first_mean - scaled * second_mean)
    return result, jnp.sum(gradient * scaled, axis=0), jnp.sum(gradient, axis=0)


def gelu_pair(pre_gelu):
    squared = pre_gelu * pre_gelu
    tangent = jnp.tanh(0.7978845608028654 * (pre_gelu + 0.044715 * squared * pre_gelu))
    result = 0.5 * pre_gelu * (1.0 + tangent)
    derivative = 0.5 * (1.0 + tangent) + 0.5 * pre_gelu * (
        1.0 - tangent * tangent
    ) * 0.7978845608028654 * (1.0 + 3.0 * 0.044715 * squared)
    return result, derivative


def ordered_rows(order_ref, seq, block, half, length):
    return pl.multiple_of(seq * length + order_ref[seq, block] * half, half)


def below_mask():
    return lax.broadcasted_iota(jnp.int32, (QB, QB), 0) <= lax.broadcasted_iota(
        jnp.int32, (QB, QB), 1
    )


def attend_kernel(
    seqs, rows, half, order_ref, in_ref, gain_ref, shift_ref, weight_ref, bias_ref,
    normed_ref, sorted_ref, out_ref, mixed_ref, log_ref, rows_ref,
):
    step = pl.program_id(0)
    tokens = seqs * rows
    group = in_ref.shape[0] // tokens
    length = mixed_ref.shape[2]
    per = rows // half
    normed = layer_norm(in_ref[...].astype(F32), gain_ref[...], shift_ref[...])[0].astype(BF)
    normed_ref[...] = normed
    made = (mm(normed, weight_ref[...], NT) + bias_ref[...]).astype(BF)
    for g in range(group):
        for s in range(seqs):
            for b in range(per):
                at = ordered_rows(order_ref, s, (step * group + g) * per + b, half, length)
                first = g * tokens + s * rows + b * half
                sorted_ref[pl.ds(at, half), :] = made[first : first + half]

    @pl.when(step == pl.num_programs(0) - 1)
    def _():
        below = below_mask()

        def one_seq(s, carry):
            base = pl.multiple_of(s * length, length)
            k_all = sorted_ref[pl.ds(base, length), HD : 2 * HD]
            v_turned = sorted_ref[pl.ds(base, length), 2 * HD :].T
            for i in range(length // QB):
                lo, hi = i * QB, (i + 1) * QB
                q_rows = sorted_ref[pl.ds(base + lo, QB), :HD] * 0.125
                scores = mm(k_all[:hi], q_rows, NT)
                last = jnp.where(below, scores[lo:], -1e30)
                best = jnp.max(last, axis=0, keepdims=True)
                if i:
                    best = jnp.maximum(best, jnp.max(scores[:lo], axis=0, keepdims=True))
                tail = jnp.exp(last - best)
                total = jnp.sum(tail, axis=0, keepdims=True)
                mixed = mm(v_turned[:, lo:hi], tail.astype(BF))
                if i:
                    head = jnp.exp(scores[:lo] - best)
                    total = total + jnp.sum(head, axis=0, keepdims=True)
                    mixed = mixed + mm(v_turned[:, :lo], head.astype(BF))
                mixed = mixed / total
                mixed_ref[s, :, lo:hi] = mixed
                log_ref[s, :, lo:hi] = best + jnp.log(total)
                rows_ref[pl.ds(base + lo, QB), :] = mixed.T
            return carry

        lax.fori_loop(0, seqs, one_seq, 0)

        def one_block(c, carry):
            parts = [
                rows_ref[pl.ds(ordered_rows(order_ref, s, c * per + b, half, length), half), :]
                for s in range(seqs)
                for b in range(per)
            ]
            out_ref[c] = jnp.concatenate(parts, axis=0).T.astype(BF)
            return carry

        lax.fori_loop(0, out_ref.shape[0], one_block, 0)


def attend(order, gathered, gain, shift, weight, bias, rows):
    seqs, halves = order.shape
    tokens, width = seqs * rows, gathered.shape[1]
    n_ctx = gathered.shape[0] // tokens
    length = rows * n_ctx
    half = length // halves
    group = 4
    whole = lambda *shape: pl.BlockSpec(shape, lambda i: (0,) * len(shape))
    return pl.pallas_call(
        functools.partial(attend_kernel, seqs, rows, half),
        grid=(n_ctx // group,),
        in_specs=[
            pl.BlockSpec(memory_space=pltpu.SMEM),
            pl.BlockSpec((group * tokens, width), lambda i: (i, 0)),
            whole(1, width),
            whole(1, width),
            whole(3 * HD, width),
            whole(1, 3 * HD),
        ],
        out_specs=[
            pl.BlockSpec((group * tokens, width), lambda i: (i, 0)),
            whole(seqs * length, 3 * HD),
            whole(n_ctx, HD, tokens),
            whole(seqs, HD, length),
            whole(seqs, 1, length),
        ],
        out_shape=[
            jax.ShapeDtypeStruct(gathered.shape, BF),
            jax.ShapeDtypeStruct((seqs * length, 3 * HD), BF),
            jax.ShapeDtypeStruct((n_ctx, HD, tokens), BF),
            jax.ShapeDtypeStruct((seqs, HD, length), F32),
            jax.ShapeDtypeStruct((seqs, 1, length), F32),
        ],
        scratch_shapes=[pltpu.VMEM((seqs * length, HD), F32)],
        compiler_params=pltpu.CompilerParams(vmem_limit_bytes=48 << 20),
        cost_estimate=pl.CostEstimate(
            flops=20_000_000_000, bytes_accessed=20_000_000, transcendentals=0
        ),
        name="attend",
    )(order, gathered, gain, shift, weight, bias)


def attend_back_kernel(
    seqs, rows, half, order_ref, sorted_ref, mixed_ref, log_ref, grad_ref, out_ref, bias_ref,
    rows_ref, key_ref, value_ref, all_ref,
):
    n_ctx, _, tokens = grad_ref.shape
    length = mixed_ref.shape[2]
    per = rows // half

    def spread(c, carry):
        block = grad_ref[c].T
        for s in range(seqs):
            for b in range(per):
                at = ordered_rows(order_ref, s, c * per + b, half, length)
                first = s * rows + b * half
                rows_ref[pl.ds(at, half), :] = block[first : first + half]
        return carry

    lax.fori_loop(0, n_ctx, spread, 0)
    below = below_mask()

    def one_seq(s, carry):
        base = pl.multiple_of(s * length, length)
        k_all = sorted_ref[pl.ds(base, length), HD : 2 * HD]
        v_all = sorted_ref[pl.ds(base, length), 2 * HD :]
        k_turned = k_all.T
        g_turned = rows_ref[pl.ds(base, length), :].T
        delta = jnp.sum(g_turned.astype(F32) * mixed_ref[s], axis=0, keepdims=True)
        key_ref[...] = jnp.zeros_like(key_ref)
        value_ref[...] = jnp.zeros_like(value_ref)
        for i in range(length // QB):
            lo, hi = i * QB, (i + 1) * QB
            q_rows = sorted_ref[pl.ds(base + lo, QB), :HD] * 0.125
            g_rows = rows_ref[pl.ds(base + lo, QB), :]
            log_row = log_ref[s, :, lo:hi]
            delta_row = delta[:, lo:hi]
            query = jnp.zeros((HD, QB), F32)
            for first, end in ((0, lo), (lo, hi)):
                if first == end:
                    continue
                scores = mm(k_all[first:end], q_rows, NT)
                probs = jnp.exp(scores - log_row)
                if end == hi:
                    probs = jnp.where(below, probs, 0.0)
                slopes = mm(v_all[first:end], g_rows, NT)
                pulled = (probs * (slopes - delta_row)).astype(BF)
                value_ref[first:end, :] += mm(probs.astype(BF), g_rows)
                key_ref[first:end, :] += mm(pulled, q_rows)
                query = query + mm(k_turned[:, first:end], pulled)
            all_ref[pl.ds(base + lo, QB), :HD] = (query * 0.125).T
        all_ref[pl.ds(base, length), HD : 2 * HD] = key_ref[...]
        all_ref[pl.ds(base, length), 2 * HD :] = value_ref[...]
        return carry

    lax.fori_loop(0, seqs, one_seq, 0)

    def one_block(c, carry):
        parts = [
            all_ref[pl.ds(ordered_rows(order_ref, s, c * per + b, half, length), half), :]
            for s in range(seqs)
            for b in range(per)
        ]
        block = jnp.concatenate(parts, axis=0).astype(BF)
        out_ref[c] = block.T
        return carry + jnp.sum(block.astype(F32), axis=0, keepdims=True)

    bias_ref[...] = lax.fori_loop(0, n_ctx, one_block, jnp.zeros((1, 3 * HD), F32))


def attend_back(order, ordered, mixed, logs, grads, rows):
    n_ctx, _, tokens = grads.shape
    seqs, halves = order.shape
    length = rows * n_ctx
    half = length // halves
    vmem = pl.BlockSpec(memory_space=pltpu.VMEM)
    return pl.pallas_call(
        functools.partial(attend_back_kernel, seqs, rows, half),
        in_specs=[pl.BlockSpec(memory_space=pltpu.SMEM)] + [vmem] * 4,
        out_specs=[vmem] * 2,
        out_shape=[
            jax.ShapeDtypeStruct((n_ctx, 3 * HD, tokens), BF),
            jax.ShapeDtypeStruct((1, 3 * HD), F32),
        ],
        scratch_shapes=[
            pltpu.VMEM((seqs * length, HD), BF),
            pltpu.VMEM((length, HD), F32),
            pltpu.VMEM((length, HD), F32),
            pltpu.VMEM((seqs * length, 3 * HD), F32),
        ],
        compiler_params=pltpu.CompilerParams(vmem_limit_bytes=48 << 20),
        cost_estimate=pl.CostEstimate(
            flops=20_000_000_000, bytes_accessed=10_000_000, transcendentals=0
        ),
        name="attend_back",
    )(order, ordered, mixed, logs, grads)


def head_grad_kernel(n_w, at_ref, grad_ref, bias_ref, in_ref, *refs):
    *out_refs, total_ref, turned_ref = refs
    step = pl.program_id(0)

    @pl.when(step == 0)
    def _():
        total_ref[...] = jnp.zeros_like(total_ref)

    turned = jnp.concatenate([grad_ref[g] for g in range(grad_ref.shape[0])], axis=1)
    total_ref[...] += mm(turned, in_ref[...])

    @pl.when(step == pl.num_programs(0) - 1)
    def _():
        turned_ref[...] = total_ref[...].T
        own = turned_ref.shape[0] // n_w
        for k, out_ref in enumerate(out_refs):
            at = pl.multiple_of((at_ref[0] + n_w - k) % n_w * own, 16)
            out_ref[:own] = turned_ref[pl.ds(at, own), :].astype(out_ref.dtype)
            out_ref[own:] = jnp.broadcast_to(
                bias_ref[...], (out_ref.shape[0] - own, out_ref.shape[1])
            ).astype(out_ref.dtype)


def head_grad(at, grads, bias, gathered, n_w):
    n_ctx, _, tokens = grads.shape
    width = gathered.shape[1]
    group = 4
    rows = width // n_w + 16
    return pl.pallas_call(
        functools.partial(head_grad_kernel, n_w),
        grid=(n_ctx // group,),
        in_specs=[
            pl.BlockSpec(memory_space=pltpu.SMEM),
            pl.BlockSpec((group, 3 * HD, tokens), lambda i: (i, 0, 0)),
            pl.BlockSpec((1, 3 * HD), lambda i: (0, 0)),
            pl.BlockSpec((group * tokens, width), lambda i: (i, 0)),
        ],
        out_specs=[pl.BlockSpec((rows, 3 * HD), lambda i: (0, 0))] * n_w,
        out_shape=[
            jax.ShapeDtypeStruct((rows, 3 * HD), BF if k else F32) for k in range(n_w)
        ],
        scratch_shapes=[pltpu.VMEM((3 * HD, width), F32), pltpu.VMEM((width, 3 * HD), F32)],
        compiler_params=pltpu.CompilerParams(vmem_limit_bytes=32 << 20),
        cost_estimate=pl.CostEstimate(
            flops=5_000_000_000, bytes_accessed=15_000_000, transcendentals=0
        ),
        name="head_grad",
    )(at, grads, bias, gathered)


def finish_kernel(n_w, turned_ref, weight_ref, in_ref, gain_ref, shift_ref, middle_ref, side_ref, out_ref, block_ref, total_ref):
    step = pl.program_id(0)

    @pl.when(step == 0)
    def _():
        total_ref[...] = jnp.zeros_like(total_ref)

    total_ref[...] += mm(turned_ref[...].T, weight_ref[...])

    @pl.when(step == pl.num_programs(0) - 1)
    def _():
        grad = total_ref[...]
        _, scaled, inverse = layer_norm(in_ref[...].astype(F32), gain_ref[...], shift_ref[...])
        result, gain_grad, shift_grad = norm_back(grad, scaled, inverse, gain_ref[...])
        out_ref[...] = middle_ref[...] + result
        own = block_ref.shape[2]
        rows = (gain_grad.reshape(1, -1), side_ref[0:1], shift_grad.reshape(1, -1), side_ref[1:2])
        for w in range(n_w):
            at = slice(w * own, (w + 1) * own)
            for r, row in enumerate(rows):
                block_ref[w, r : r + 1] = row[:, at]
            block_ref[w, len(rows) :] = side_ref[2 : 2 + block_ref.shape[1] - len(rows), at]


def finish(turned, weight, low, gain, shift, middle, side, n_w):
    tokens, width = low.shape
    depth = HEADS * 3 * HD // 5
    whole = lambda *shape: pl.BlockSpec(shape, lambda i: (0,) * len(shape))
    return pl.pallas_call(
        functools.partial(finish_kernel, n_w),
        grid=(5,),
        in_specs=[
            pl.BlockSpec((depth, tokens), lambda i: (i, 0)),
            pl.BlockSpec((depth, width), lambda i: (i, 0)),
            whole(tokens, width),
            whole(1, width),
            whole(1, width),
            whole(tokens, width),
            whole(*side.shape),
        ],
        out_specs=[whole(tokens, width), whole(n_w, 8, width // n_w)],
        out_shape=[
            jax.ShapeDtypeStruct((tokens, width), F32),
            jax.ShapeDtypeStruct((n_w, 8, width // n_w), F32),
        ],
        scratch_shapes=[pltpu.VMEM((tokens, width), F32)],
        compiler_params=pltpu.CompilerParams(vmem_limit_bytes=32 << 20),
        cost_estimate=pl.CostEstimate(
            flops=2_500_000_000, bytes_accessed=20_000_000, transcendentals=0
        ),
        name="finish",
    )(turned, weight, low, gain, shift, middle, side)


def join_rows_kernel(n_w, overlap, at_ref, *refs):
    *pieces, out_ref = refs
    wsh, core = at_ref[0], at_ref[1]
    own = pieces[0].shape[0]
    out_ref[pl.ds(pl.multiple_of(wsh * own, 16), own), :] = pieces[0][...]
    for k in range(1, n_w):
        base = (wsh + k) % n_w * own
        mine, other = pieces[2 * k - 1], pieces[2 * k]
        size = mine.shape[0]
        out_ref[pl.ds(pl.multiple_of(base + core * overlap, 16), size), :] = mine[...]
        out_ref[pl.ds(pl.multiple_of(base + (1 - core) * overlap, 16), size), :] = other[...]


def join_rows(at, pieces, n_w, overlap):
    own, width = pieces[0].shape
    vmem = pl.BlockSpec(memory_space=pltpu.VMEM)
    return pl.pallas_call(
        functools.partial(join_rows_kernel, n_w, overlap),
        in_specs=[pl.BlockSpec(memory_space=pltpu.SMEM)] + [vmem] * len(pieces),
        out_specs=vmem,
        out_shape=jax.ShapeDtypeStruct((n_w * own, width), BF),
        compiler_params=pltpu.CompilerParams(vmem_limit_bytes=32 << 20),
        cost_estimate=pl.CostEstimate(flops=0, bytes_accessed=12_000_000, transcendentals=0),
        name="join_rows",
    )(at, *pieces)


def cut_columns_kernel(n_w, overlap, at_ref, in_ref, *out_refs):
    wsh, core = at_ref[0], at_ref[1]
    cols = out_refs[0].shape[1]
    for k, out_ref in enumerate(out_refs):
        size = out_ref.shape[0]
        start = 0 if k == 0 else pl.multiple_of(core * overlap, 16)
        for b in range(n_w):

            @pl.when((wsh + n_w - k) % n_w == b)
            def _(out_ref=out_ref, start=start, size=size, b=b):
                out_ref[...] = in_ref[pl.ds(start, size), b * cols : (b + 1) * cols]


def cut_columns(at, array, n_w, size, overlap):
    own, cols = array.shape[0], array.shape[1] // n_w
    vmem = pl.BlockSpec(memory_space=pltpu.VMEM)
    return pl.pallas_call(
        functools.partial(cut_columns_kernel, n_w, overlap),
        in_specs=[pl.BlockSpec(memory_space=pltpu.SMEM), vmem],
        out_specs=[vmem] * n_w,
        out_shape=[
            jax.ShapeDtypeStruct((own if k == 0 else size, cols), BF) for k in range(n_w)
        ],
        compiler_params=pltpu.CompilerParams(vmem_limit_bytes=32 << 20),
        cost_estimate=pl.CostEstimate(flops=0, bytes_accessed=10_000_000, transcendentals=0),
        name="cut_columns",
    )(at, array)


def join_columns_kernel(n_w, overlap, at_ref, *refs):
    *pieces, out_ref = refs
    wsh, core = at_ref[0], at_ref[1]
    cols = pieces[0].shape[1]
    for k in range(n_w):
        for b in range(n_w):

            @pl.when((wsh + k) % n_w == b)
            def _(k=k, b=b):
                at = slice(b * cols, (b + 1) * cols)
                if k == 0:
                    out_ref[:, at] = pieces[0][...].astype(F32)
                    return
                mine, other = pieces[2 * k - 1], pieces[2 * k]
                size = mine.shape[0]
                out_ref[pl.ds(pl.multiple_of(core * overlap, 16), size), at] = mine[...].astype(F32)
                out_ref[pl.ds(pl.multiple_of((1 - core) * overlap, 16), size), at] = other[
                    ...
                ].astype(F32)


def join_columns(at, pieces, n_w, overlap):
    own, cols = pieces[0].shape
    vmem = pl.BlockSpec(memory_space=pltpu.VMEM)
    return pl.pallas_call(
        functools.partial(join_columns_kernel, n_w, overlap),
        in_specs=[pl.BlockSpec(memory_space=pltpu.SMEM)] + [vmem] * len(pieces),
        out_specs=vmem,
        out_shape=jax.ShapeDtypeStruct((own, n_w * cols), F32),
        compiler_params=pltpu.CompilerParams(vmem_limit_bytes=40 << 20),
        cost_estimate=pl.CostEstimate(flops=0, bytes_accessed=16_000_000, transcendentals=0),
        name="join_columns",
    )(at, *pieces)


def out_grad_kernel(n_w, in_ref, grad_ref, side_ref, out_ref):
    made = mm(in_ref[...], grad_ref[...])
    chunks = made.shape[0] // 16
    out_ref[...] = jnp.zeros_like(out_ref)
    for c in range(chunks):
        out_ref[c] = made[c * 16 : (c + 1) * 16].astype(BF)
    out_ref[chunks, :1] = side_ref[...].astype(BF)


def out_grad(rows, grads, side, n_ctx, n_w):
    vmem = pl.BlockSpec(memory_space=pltpu.VMEM)
    return pl.pallas_call(
        functools.partial(out_grad_kernel, n_w),
        in_specs=[vmem] * 3,
        out_specs=vmem,
        out_shape=jax.ShapeDtypeStruct((n_ctx, 16, grads.shape[1]), BF),
        compiler_params=pltpu.CompilerParams(vmem_limit_bytes=24 << 20),
        cost_estimate=pl.CostEstimate(
            flops=1_500_000_000, bytes_accessed=4_000_000, transcendentals=0
        ),
        name="out_grad",
    )(rows, grads, side)


def pack_kernel(chunk_ref, *refs):
    *pieces, left_ref, right_ref = refs
    total = pieces[0][...]
    for piece in pieces[1:]:
        total = total + piece[...].astype(F32)
    left_ref[...] = total[:, : 2 * HD].astype(BF)
    chunk = chunk_ref[0].astype(F32)
    for c in range(1, chunk_ref.shape[0]):
        chunk = chunk + chunk_ref[c].astype(F32)
    turned = jnp.concatenate(
        [chunk[:, q * HD : (q + 1) * HD] for q in range(chunk.shape[1] // HD)], axis=0
    )
    turned = jnp.concatenate(
        [turned, jnp.zeros((total.shape[0] - turned.shape[0], HD), F32)], axis=0
    )
    right_ref[...] = jnp.concatenate([total[:, 2 * HD :], turned], axis=1).astype(BF)


def pack(chunks, pieces):
    rows = pieces[0].shape[0]
    vmem = pl.BlockSpec(memory_space=pltpu.VMEM)
    return pl.pallas_call(
        pack_kernel,
        in_specs=[vmem] * (1 + len(pieces)),
        out_specs=[vmem] * 2,
        out_shape=[jax.ShapeDtypeStruct((rows, 2 * HD), BF)] * 2,
        compiler_params=pltpu.CompilerParams(vmem_limit_bytes=24 << 20),
        cost_estimate=pl.CostEstimate(flops=0, bytes_accessed=4_000_000, transcendentals=0),
        name="pack",
    )(chunks, *pieces)


def unpack_kernel(
    at_ref, left_own, left_other, right_own, right_other, qkv_ref, out_ref, bias_ref, side_ref
):
    z, y, core = at_ref[0], at_ref[1], at_ref[2]
    own = qkv_ref.shape[0]
    bias_ref[...] = jnp.zeros_like(bias_ref)
    for h in range(HEADS + 1):
        by_z, by_y = (h // 8 + 4 - z) % 4, ((h // 2) % 4 + 4 - y) % 4
        same = core == h % 2
        right_at = by_y * 4 + by_z
        right = jnp.where(same, right_own[right_at], right_other[right_at]).astype(F32)
        if h == HEADS:
            for q in range(HEADS):
                side_ref[:, q * HD : (q + 1) * HD] = right[q * 16 : q * 16 + 8, HD:]
            break
        left_at = by_z * 4 + by_y
        left = jnp.where(same, left_own[left_at], left_other[left_at]).astype(F32)
        for part, piece in enumerate((left[:, :HD], left[:, HD:], right[:, :HD])):
            at = (part * HEADS + h) * HD
            qkv_ref[:, at : at + HD] = piece[:own]
        bias_ref[0:1, h * HD : (h + 1) * HD] = left[own : own + 1, :HD]
        bias_ref[1:2, h * HD : (h + 1) * HD] = right[own : own + 1, :HD]
        for q in range(HEADS):
            out_ref[h * 16 : (h + 1) * 16, q * HD : (q + 1) * HD] = right[
                q * 16 : (q + 1) * 16, HD:
            ]


def unpack(at, left_own, left_other, right_own, right_other):
    rows = left_own.shape[1] - 16
    vmem = pl.BlockSpec(memory_space=pltpu.VMEM)
    return pl.pallas_call(
        unpack_kernel,
        in_specs=[pl.BlockSpec(memory_space=pltpu.SMEM)] + [vmem] * 4,
        out_specs=[vmem] * 4,
        out_shape=[
            jax.ShapeDtypeStruct((rows, 3 * HEADS * HD), F32),
            jax.ShapeDtypeStruct((rows, HEADS * HD), F32),
            jax.ShapeDtypeStruct((8, HEADS * HD), F32),
            jax.ShapeDtypeStruct((8, HEADS * HD), F32),
        ],
        compiler_params=pltpu.CompilerParams(vmem_limit_bytes=40 << 20),
        cost_estimate=pl.CostEstimate(flops=0, bytes_accessed=18_000_000, transcendentals=0),
        name="unpack",
    )(at, left_own, left_other, right_own, right_other)


def after(array, *others):
    return lax.optimization_barrier((array, *others))[0]


def on_device(
    layer_input,
    block_order,
    norm_gains,
    norm_shifts,
    qkv_weight,
    attn_bias,
    out_weight,
    out_bias,
    fc_weight,
    fc_bias,
    proj_weight,
    proj_bias,
    output_grad,
):
    seqs, rows, width = layer_input.shape
    tokens = seqs * rows
    n_ctx, n_w = lax.axis_size("ctx"), lax.axis_size("wsh")
    ctx, wsh = lax.axis_index("ctx"), lax.axis_index("wsh")
    z, y, core = ctx // 8, ctx // 2 % 4, ctx % 2
    own = width // n_w
    ff = fc_weight.shape[1] // n_w
    size, overlap = 208, 192
    at_x = jnp.stack([wsh, core])

    def x_shift(array, k):
        return lax.ppermute(array, "wsh", [((i + k) % n_w, i) for i in range(n_w)])

    def ctx_shift(array, to):
        return lax.ppermute(array, "ctx", [(to(i), i) for i in range(n_ctx)])

    def partner(array):
        return ctx_shift(array, lambda i: i ^ 1)

    def around(array):
        return [array] + [x_shift(array, k) for k in range(1, n_w)]

    def deal(choose):
        return [choose(0)] + [x_shift(choose(k), k) for k in range(1, n_w)]

    def send_back(pieces):
        total = pieces[0]
        for k in range(1, n_w):
            total = total + x_shift(pieces[k].astype(BF), n_w - k).astype(F32)
        return total

    def with_halves(whole, halves, *before):
        pieces = [whole]
        for k in range(1, n_w):
            mine = x_shift(halves[k - 1], k)
            pieces += [mine, partner(after(mine, *before))]
        return pieces

    def in_order(pieces):
        twice = jnp.stack(pieces + pieces)
        start = (n_w - wsh) % n_w
        return lax.dynamic_slice(twice, (start,) + (0,) * pieces[0].ndim, (n_w,) + pieces[0].shape)

    low = layer_input.reshape(tokens, width)
    gathered = lax.all_gather(low, "ctx", axis=0, tiled=True)
    packed = jnp.concatenate(
        [norm_gains, norm_shifts, attn_bias, out_bias[None], proj_bias[None]], axis=0
    )
    vectors = in_order(around(packed)).transpose(1, 0, 2).reshape(8, width).astype(F32)
    gains, shifts, bias_pair = vectors[0:2], vectors[2:4], vectors[4:6]
    out_bias_row, proj_bias_row = vectors[6], vectors[7]

    head = jnp.minimum(ctx, HEADS - 1)
    head_cols = jnp.concatenate(
        [
            lax.dynamic_slice(qkv_weight, (0, part * width + head * HD), (own, HD))
            for part in range(3)
        ],
        axis=1,
    )
    head_weight = in_order(around(head_cols)).reshape(width, 3 * HD).T
    head_bias = lax.dynamic_slice(bias_pair, (0, head * HD), (2, HD))
    head_bias = jnp.concatenate([head_bias[:1], jnp.zeros((1, HD), F32), head_bias[1:]], axis=1)

    grad_low = output_grad.reshape(tokens, width)
    out_half = lax.dynamic_slice(
        after(out_weight, head_weight), (core * overlap, 0), (size, width)
    )
    out_pieces = with_halves(out_weight, [out_half] * (n_w - 1))
    out_all = join_rows(at_x, out_pieces, n_w, overlap)
    fc_own, *fc_halves = cut_columns(at_x, fc_weight, n_w, size, overlap)
    fc_halves = [after(half, *out_pieces[1::2]) for half in fc_halves]
    gathered = after(gathered, out_all)

    input_one, ordered, mixed_turned, mixed, logs = attend(
        block_order, gathered, gains[:1], shifts[:1], head_weight, head_bias, rows
    )
    weight_all = lax.all_gather(head_weight, "ctx", axis=0, tiled=True)
    grad_group = jnp.concatenate(around(after(grad_low, mixed_turned)), axis=0)
    grad_active = mm(grad_group, proj_weight, NT)
    attended = lax.all_to_all(mixed_turned, "ctx", 0, 0).reshape(n_ctx * HD, tokens)[:width]
    fc_pieces = with_halves(fc_own, fc_halves, mixed_turned)
    fc_cols = join_rows(at_x, [after(fc_pieces[0], attended), *fc_pieces[1:]], n_w, overlap)
    residual = low.astype(F32)
    middle = residual + mm(attended, out_all, TN) + out_bias_row
    normed_two, scaled_two, inverse_two = layer_norm(middle, gains[1], shifts[1])
    input_two = around(normed_two.astype(BF))
    *input_two, grad_active = lax.optimization_barrier((*input_two, grad_active))
    input_two = jnp.concatenate(input_two, axis=0)

    pre_gelu = mm(input_two, fc_cols) + fc_bias.astype(F32)
    activated, derivative = gelu_pair(pre_gelu)
    activated = activated.astype(BF)
    grad_pre = (grad_active * derivative).astype(BF)
    grad_two = mm(grad_pre, fc_cols, NT).reshape(n_w, tokens, width)
    came = [x_shift(grad_two[k].astype(BF), n_w - k) for k in range(1, n_w)]
    activated, grad_pre = lax.optimization_barrier((activated, grad_pre, came[0], weight_all))[:2]
    grad_proj = mm(activated, grad_group, TN).astype(BF)
    grad_fc = mm(input_two, grad_pre, TN).astype(BF)
    came = lax.optimization_barrier((*came, grad_proj, grad_fc))[: n_w - 1]
    grad_two = grad_two[0] + sum(piece.astype(F32) for piece in came)
    grad_fc_bias = jnp.sum(grad_pre.astype(F32), axis=0, keepdims=True)
    share_proj, share_fc = lax.psum((grad_proj, grad_fc), "ctx")

    grad_norm_two, gain_two, shift_two = norm_back(grad_two, scaled_two, inverse_two, gains[1])
    grad_middle = grad_low.astype(F32) + grad_norm_two
    grad_branch = grad_middle.astype(BF)
    grad_attended = mm(out_all, grad_branch, NT).astype(BF)
    grad_heads = jnp.pad(grad_attended, ((0, (n_ctx - HEADS) * HD), (0, 0)))
    grad_heads = lax.all_to_all(grad_heads.reshape(n_ctx, HD, tokens), "ctx", 0, 0)
    branch_group = jnp.concatenate(around(after(grad_branch, grad_attended)), axis=0)
    attended_rows = jnp.concatenate(
        deal(
            lambda k: lax.dynamic_slice(
                after(attended, activated), ((wsh + n_w - k) % n_w * own, 0), (own, tokens)
            )
        ),
        axis=1,
    )

    branch = mm(after(activated, branch_group), proj_weight).reshape(n_w, tokens, width)
    branch = send_back([branch[k] for k in range(n_w)])
    layer_output = (middle + branch + proj_bias_row).astype(BF)

    chunks = out_grad(attended_rows, branch_group, grad_fc_bias, n_ctx, n_w)
    grad_heads = after(grad_heads, chunks)
    chunks = lax.all_to_all(chunks, "ctx", 0, 0)

    grad_qkv, grad_bias = attend_back(block_order, ordered, mixed, logs, grad_heads, rows)
    grad_tokens = lax.all_to_all(grad_qkv, "ctx", 0, 0).reshape(n_ctx * 3 * HD, tokens)

    dealt = head_grad(at_x, grad_qkv, grad_bias, input_one, n_w)
    pieces = deal(lambda k: dealt[k])
    left, right = pack(chunks, pieces)
    from_y = lambda array, k: ctx_shift(array, lambda i: i // 8 * 8 + (i + 2 * k) % 8)
    from_z = lambda array, k: ctx_shift(array, lambda i: (i + 8 * k) % 32)
    left = jnp.stack([left] + [from_y(left, k) for k in range(1, 4)])
    right = jnp.stack([right] + [from_z(right, k) for k in range(1, 4)])
    left = jnp.concatenate([left] + [from_z(left, k) for k in range(1, 4)])
    right = jnp.concatenate([right] + [from_y(right, k) for k in range(1, 4)])
    side = jnp.stack(
        [
            gain_two,
            shift_two,
            jnp.sum(grad_low.astype(F32), axis=0),
            jnp.sum(grad_branch.astype(F32), axis=0),
        ]
    )
    side = jnp.pad(side, ((0, 4), (0, 0)))
    input_grad, blocks = finish(
        grad_tokens, weight_all, low, gains[:1], shifts[:1], grad_middle, side, n_w
    )
    pieces = deal(
        lambda k: lax.dynamic_slice(blocks, ((wsh + n_w - k) % n_w, 0, 0), (1, 8, own))
    )
    vector_sum = (pieces[0] + pieces[1]) + (pieces[2] + pieces[3])
    everyone = lax.all_to_all(jnp.broadcast_to(vector_sum, (n_ctx, 8, own)), "ctx", 0, 0)
    vector_out = jnp.sum(everyone, axis=0)

    qkv_out, out_out, bias_out, side_out = unpack(
        jnp.stack([z, y, core]), after(left, blocks), partner(left), right, partner(right)
    )
    bias_out = lax.dynamic_slice(bias_out, (0, wsh * own), (2, own))

    rows_for = lambda k, start, count: lax.dynamic_slice(
        share_fc, ((wsh + n_w - k) % n_w * own + start, 0), (count, ff)
    )
    fc_out = join_columns(
        at_x,
        with_halves(
            rows_for(0, 0, own),
            [rows_for(k, core * overlap, size) for k in range(1, n_w)],
            qkv_out,
        ),
        n_w,
        overlap,
    )
    return (
        layer_output.reshape(seqs, rows, width),
        input_grad.reshape(seqs, rows, width),
        vector_out[0:2],
        vector_out[2:4],
        qkv_out,
        bias_out,
        out_out,
        vector_out[5],
        fc_out,
        side_out[0],
        share_proj.astype(F32),
        vector_out[4],
    )


def solution(mesh):
    return jax.shard_map(
        on_device,
        mesh=mesh,
        in_specs=(
            P("wsh", "ctx", None),
            P("wsh", None),
            P(None, "wsh"),
            P(None, "wsh"),
            P("wsh", None),
            P(None, "wsh"),
            P("wsh", None),
            P("wsh"),
            P("wsh", None),
            P("wsh"),
            P("wsh", None),
            P("wsh"),
            P("wsh", "ctx", None),
        ),
        out_specs=(
            P("wsh", "ctx", None),
            P("wsh", "ctx", None),
            P(None, "wsh"),
            P(None, "wsh"),
            P("wsh", None),
            P(None, "wsh"),
            P("wsh", None),
            P("wsh"),
            P("wsh", None),
            P("wsh"),
            P("wsh", None),
            P("wsh"),
        ),
        check_vma=False,
    )
```

```python
import functools

import jax
import jax.numpy as jnp
from jax import lax
from jax.experimental import pallas as pl
from jax.experimental.pallas import tpu as pltpu
from jax.sharding import Mesh
from jax.sharding import PartitionSpec as P

HEADS = 25
HD = 64
QB = 256
FB = 512
BF = jnp.bfloat16
F32 = jnp.float32
NN = (((1,), (0,)), ((), ()))
NT = (((1,), (1,)), ((), ()))
TN = (((0,), (0,)), ((), ()))
CTX = ("z", "y", "core")


def mm(left, right, dims=NN):
    return lax.dot_general(left, right, dims, preferred_element_type=F32)


def layer_norm(hidden, gain_row, shift_row):
    centered = hidden - jnp.mean(hidden, axis=-1, keepdims=True)
    inverse = lax.rsqrt(jnp.mean(centered * centered, axis=-1, keepdims=True) + 1e-05)
    scaled = centered * inverse
    return scaled * gain_row + shift_row, scaled, inverse


def norm_back(gradient, scaled, inverse, gain_row):
    weighted = gradient * gain_row
    first_mean = jnp.mean(weighted, axis=-1, keepdims=True)
    second_mean = jnp.mean(weighted * scaled, axis=-1, keepdims=True)
    result = inverse * (weighted - first_mean - scaled * second_mean)
    return result, jnp.sum(gradient * scaled, axis=0), jnp.sum(gradient, axis=0)


def gelu_pair(pre_gelu):
    squared = pre_gelu * pre_gelu
    tangent = jnp.tanh(0.7978845608028654 * (pre_gelu + 0.044715 * squared * pre_gelu))
    result = 0.5 * pre_gelu * (1.0 + tangent)
    derivative = 0.5 * (1.0 + tangent) + 0.5 * pre_gelu * (
        1.0 - tangent * tangent
    ) * 0.7978845608028654 * (1.0 + 3.0 * 0.044715 * squared)
    return result, derivative


def ordered_rows(order_ref, seq, block, half, length):
    return pl.multiple_of(seq * length + order_ref[seq, block] * half, half)


def below_mask(size):
    return lax.broadcasted_iota(jnp.int32, (size, size), 0) <= lax.broadcasted_iota(
        jnp.int32, (size, size), 1
    )


def attend_kernel(
    seqs, rows, half, order_ref, in_ref, gain_ref, shift_ref, weight_ref, bias_ref,
    normed_ref, sorted_ref, out_ref, mixed_ref, log_ref, rows_ref,
):
    step = pl.program_id(0)
    tokens = seqs * rows
    group = in_ref.shape[0] // tokens
    length = mixed_ref.shape[2]
    per = rows // half
    normed = layer_norm(in_ref[...].astype(F32), gain_ref[...], shift_ref[...])[0].astype(BF)
    normed_ref[...] = normed
    made = (mm(normed, weight_ref[...], NT) + bias_ref[...]).astype(BF)
    for g in range(group):
        for s in range(seqs):
            for b in range(per):
                at = ordered_rows(order_ref, s, (step * group + g) * per + b, half, length)
                first = g * tokens + s * rows + b * half
                sorted_ref[pl.ds(at, half), :] = made[first : first + half]

    @pl.when(step == pl.num_programs(0) - 1)
    def _():
        below = below_mask(FB)

        def one_seq(s, carry):
            base = pl.multiple_of(s * length, length)
            k_all = sorted_ref[pl.ds(base, length), HD : 2 * HD]
            v_turned = sorted_ref[pl.ds(base, length), 2 * HD :].T
            for i in range(length // FB):
                lo, hi = i * FB, (i + 1) * FB
                q_rows = sorted_ref[pl.ds(base + lo, FB), :HD] * 0.125
                scores = mm(k_all[:hi], q_rows, NT)
                last = jnp.where(below, scores[lo:], -1e30)
                best = jnp.max(last, axis=0, keepdims=True)
                if i:
                    best = jnp.maximum(best, jnp.max(scores[:lo], axis=0, keepdims=True))
                tail = jnp.exp(last - best)
                total = jnp.sum(tail, axis=0, keepdims=True)
                mixed = mm(v_turned[:, lo:hi], tail.astype(BF))
                if i:
                    head = jnp.exp(scores[:lo] - best)
                    total = total + jnp.sum(head, axis=0, keepdims=True)
                    mixed = mixed + mm(v_turned[:, :lo], head.astype(BF))
                mixed = mixed / total
                mixed_ref[s, :, lo:hi] = mixed
                log_ref[s, :, lo:hi] = best + jnp.log(total)
                rows_ref[pl.ds(base + lo, FB), :] = mixed.T
            return carry

        lax.fori_loop(0, seqs, one_seq, 0)

        def one_block(c, carry):
            parts = [
                rows_ref[pl.ds(ordered_rows(order_ref, s, c * per + b, half, length), half), :]
                for s in range(seqs)
                for b in range(per)
            ]
            out_ref[c] = jnp.concatenate(parts, axis=0).T.astype(BF)
            return carry

        lax.fori_loop(0, out_ref.shape[0], one_block, 0)


def attend(order, gathered, gain, shift, weight, bias, rows):
    seqs, halves = order.shape
    tokens, width = seqs * rows, gathered.shape[1]
    n_ctx = gathered.shape[0] // tokens
    length = rows * n_ctx
    half = length // halves
    group = 8
    whole = lambda *shape: pl.BlockSpec(shape, lambda i: (0,) * len(shape))
    return pl.pallas_call(
        functools.partial(attend_kernel, seqs, rows, half),
        grid=(n_ctx // group,),
        in_specs=[
            pl.BlockSpec(memory_space=pltpu.SMEM),
            pl.BlockSpec((group * tokens, width), lambda i: (i, 0)),
            whole(1, width),
            whole(1, width),
            whole(3 * HD, width),
            whole(1, 3 * HD),
        ],
        out_specs=[
            pl.BlockSpec((group * tokens, width), lambda i: (i, 0)),
            whole(seqs * length, 3 * HD),
            whole(n_ctx, HD, tokens),
            whole(seqs, HD, length),
            whole(seqs, 1, length),
        ],
        out_shape=[
            jax.ShapeDtypeStruct(gathered.shape, BF),
            jax.ShapeDtypeStruct((seqs * length, 3 * HD), BF),
            jax.ShapeDtypeStruct((n_ctx, HD, tokens), BF),
            jax.ShapeDtypeStruct((seqs, HD, length), F32),
            jax.ShapeDtypeStruct((seqs, 1, length), F32),
        ],
        scratch_shapes=[pltpu.VMEM((seqs * length, HD), F32)],
        compiler_params=pltpu.CompilerParams(vmem_limit_bytes=48 << 20),
        cost_estimate=pl.CostEstimate(flops=1, bytes_accessed=1, transcendentals=0),
        name="attend",
    )(order, gathered, gain, shift, weight, bias)


def attend_back_kernel(
    seqs, rows, half, order_ref, sorted_ref, mixed_ref, log_ref, grad_ref, out_ref, bias_ref,
    rows_ref, key_ref, value_ref, all_ref,
):
    n_ctx, _, tokens = grad_ref.shape
    length = mixed_ref.shape[2]
    per = rows // half

    def spread(c, carry):
        block = grad_ref[c].T
        for s in range(seqs):
            for b in range(per):
                at = ordered_rows(order_ref, s, c * per + b, half, length)
                first = s * rows + b * half
                rows_ref[pl.ds(at, half), :] = block[first : first + half]
        return carry

    lax.fori_loop(0, n_ctx, spread, 0)
    below = below_mask(QB)

    def one_seq(s, carry):
        base = pl.multiple_of(s * length, length)
        k_all = sorted_ref[pl.ds(base, length), HD : 2 * HD]
        v_all = sorted_ref[pl.ds(base, length), 2 * HD :]
        k_turned = k_all.T
        g_turned = rows_ref[pl.ds(base, length), :].T
        delta = jnp.sum(g_turned.astype(F32) * mixed_ref[s], axis=0, keepdims=True)
        key_ref[...] = jnp.zeros_like(key_ref)
        value_ref[...] = jnp.zeros_like(value_ref)
        for i in range(length // QB):
            lo, hi = i * QB, (i + 1) * QB
            q_rows = sorted_ref[pl.ds(base + lo, QB), :HD] * 0.125
            g_rows = rows_ref[pl.ds(base + lo, QB), :]
            log_row = log_ref[s, :, lo:hi]
            delta_row = delta[:, lo:hi]
            query = jnp.zeros((HD, QB), F32)
            for first, end in ((0, lo), (lo, hi)):
                if first == end:
                    continue
                scores = mm(k_all[first:end], q_rows, NT)
                probs = jnp.exp(scores - log_row)
                if end == hi:
                    probs = jnp.where(below, probs, 0.0)
                slopes = mm(v_all[first:end], g_rows, NT)
                pulled = (probs * (slopes - delta_row)).astype(BF)
                value_ref[first:end, :] += mm(probs.astype(BF), g_rows)
                key_ref[first:end, :] += mm(pulled, q_rows)
                query = query + mm(k_turned[:, first:end], pulled)
            all_ref[pl.ds(base + lo, QB), :HD] = (query * 0.125).T
        all_ref[pl.ds(base, length), HD : 2 * HD] = key_ref[...]
        all_ref[pl.ds(base, length), 2 * HD :] = value_ref[...]
        return carry

    lax.fori_loop(0, seqs, one_seq, 0)

    def one_block(c, carry):
        parts = [
            all_ref[pl.ds(ordered_rows(order_ref, s, c * per + b, half, length), half), :]
            for s in range(seqs)
            for b in range(per)
        ]
        block = jnp.concatenate(parts, axis=0).astype(BF)
        out_ref[c] = block.T
        return carry + jnp.sum(block.astype(F32), axis=0, keepdims=True)

    bias_ref[...] = lax.fori_loop(0, n_ctx, one_block, jnp.zeros((1, 3 * HD), F32))


def attend_back(order, ordered, mixed, logs, grads, rows):
    n_ctx, _, tokens = grads.shape
    seqs, halves = order.shape
    length = rows * n_ctx
    half = length // halves
    vmem = pl.BlockSpec(memory_space=pltpu.VMEM)
    return pl.pallas_call(
        functools.partial(attend_back_kernel, seqs, rows, half),
        in_specs=[pl.BlockSpec(memory_space=pltpu.SMEM)] + [vmem] * 4,
        out_specs=[vmem] * 2,
        out_shape=[
            jax.ShapeDtypeStruct((n_ctx, 3 * HD, tokens), BF),
            jax.ShapeDtypeStruct((1, 3 * HD), F32),
        ],
        scratch_shapes=[
            pltpu.VMEM((seqs * length, HD), BF),
            pltpu.VMEM((length, HD), F32),
            pltpu.VMEM((length, HD), F32),
            pltpu.VMEM((seqs * length, 3 * HD), F32),
        ],
        compiler_params=pltpu.CompilerParams(vmem_limit_bytes=48 << 20),
        cost_estimate=pl.CostEstimate(flops=1, bytes_accessed=1, transcendentals=0),
        name="attend_back",
    )(order, ordered, mixed, logs, grads)


def head_grad_kernel(n_w, at_ref, grad_ref, bias_ref, in_ref, *refs):
    *out_refs, total_ref, turned_ref = refs
    step = pl.program_id(0)

    @pl.when(step == 0)
    def _():
        total_ref[...] = jnp.zeros_like(total_ref)

    turned = jnp.concatenate([grad_ref[g] for g in range(grad_ref.shape[0])], axis=1)
    total_ref[...] += mm(turned, in_ref[...])

    @pl.when(step == pl.num_programs(0) - 1)
    def _():
        turned_ref[...] = total_ref[...].T
        own = turned_ref.shape[0] // n_w
        for k, out_ref in enumerate(out_refs):
            at = pl.multiple_of((at_ref[0] + n_w - k) % n_w * own, 16)
            out_ref[:own] = turned_ref[pl.ds(at, own), :].astype(out_ref.dtype)
            out_ref[own:] = jnp.broadcast_to(
                bias_ref[...], (out_ref.shape[0] - own, out_ref.shape[1])
            ).astype(out_ref.dtype)


def head_grad(at, grads, bias, gathered, n_w):
    n_ctx, _, tokens = grads.shape
    width = gathered.shape[1]
    group = 4
    rows = width // n_w + 16
    return pl.pallas_call(
        functools.partial(head_grad_kernel, n_w),
        grid=(n_ctx // group,),
        in_specs=[
            pl.BlockSpec(memory_space=pltpu.SMEM),
            pl.BlockSpec((group, 3 * HD, tokens), lambda i: (i, 0, 0)),
            pl.BlockSpec((1, 3 * HD), lambda i: (0, 0)),
            pl.BlockSpec((group * tokens, width), lambda i: (i, 0)),
        ],
        out_specs=[pl.BlockSpec((rows, 3 * HD), lambda i: (0, 0))] * n_w,
        out_shape=[
            jax.ShapeDtypeStruct((rows, 3 * HD), BF if k else F32) for k in range(n_w)
        ],
        scratch_shapes=[pltpu.VMEM((3 * HD, width), F32), pltpu.VMEM((width, 3 * HD), F32)],
        compiler_params=pltpu.CompilerParams(vmem_limit_bytes=32 << 20),
        cost_estimate=pl.CostEstimate(flops=1, bytes_accessed=1, transcendentals=0),
        name="head_grad",
    )(at, grads, bias, gathered)


def finish_kernel(
    n_w, at_ref, turned_ref, weight_own, weight_other, in_ref, gain_ref, shift_ref, middle_ref, side_ref,
    out_ref, block_ref, total_ref,
):
    step = pl.program_id(0)
    core = at_ref[1]

    @pl.when(step == 0)
    def _():
        total_ref[...] = jnp.zeros_like(total_ref)

    for weight_ref, at in ((weight_own, core), (weight_other, 1 - core)):
        turned = jnp.concatenate([turned_ref[g, at] for g in range(turned_ref.shape[0])], axis=0)
        total_ref[...] += mm(turned.T, weight_ref[...])

    @pl.when(step == pl.num_programs(0) - 1)
    def _():
        grad = total_ref[...]
        _, scaled, inverse = layer_norm(in_ref[...].astype(F32), gain_ref[...], shift_ref[...])
        result, gain_grad, shift_grad = norm_back(grad, scaled, inverse, gain_ref[...])
        out_ref[...] = middle_ref[...] + result
        own = block_ref.shape[2]
        rows = (gain_grad.reshape(1, -1), side_ref[0:1], shift_grad.reshape(1, -1), side_ref[1:2])
        for w in range(n_w):
            at = slice(w * own, (w + 1) * own)
            for r, row in enumerate(rows):
                block_ref[w, r : r + 1] = row[:, at]
            block_ref[w, len(rows) :] = side_ref[2 : 2 + block_ref.shape[1] - len(rows), at]


def finish(at, turned, weight_own, weight_other, low, gain, shift, middle, side, n_w):
    tokens, width = low.shape
    turned = turned.reshape(turned.shape[0] // 2, 2, 3 * HD, tokens)
    group = 4
    whole = lambda *shape: pl.BlockSpec(shape, lambda i: (0,) * len(shape))
    weight = pl.BlockSpec((group * 3 * HD, width), lambda i: (i, 0))
    return pl.pallas_call(
        functools.partial(finish_kernel, n_w),
        grid=(turned.shape[0] // group,),
        in_specs=[
            pl.BlockSpec(memory_space=pltpu.SMEM),
            pl.BlockSpec((group, 2, 3 * HD, tokens), lambda i: (i, 0, 0, 0)),
            weight,
            weight,
            whole(tokens, width),
            whole(1, width),
            whole(1, width),
            whole(tokens, width),
            whole(*side.shape),
        ],
        out_specs=[whole(tokens, width), whole(n_w, 8, width // n_w)],
        out_shape=[
            jax.ShapeDtypeStruct((tokens, width), F32),
            jax.ShapeDtypeStruct((n_w, 8, width // n_w), F32),
        ],
        scratch_shapes=[pltpu.VMEM((tokens, width), F32)],
        compiler_params=pltpu.CompilerParams(vmem_limit_bytes=32 << 20),
        cost_estimate=pl.CostEstimate(flops=1, bytes_accessed=1, transcendentals=0),
        name="finish",
    )(at, turned, weight_own, weight_other, low, gain, shift, middle, side)


def join_rows_kernel(n_w, overlap, at_ref, *refs):
    *pieces, out_ref = refs
    wsh, core = at_ref[0], at_ref[1]
    own = pieces[0].shape[0]
    out_ref[pl.ds(pl.multiple_of(wsh * own, 16), own), :] = pieces[0][...]
    for k in range(1, n_w):
        base = (wsh + k) % n_w * own
        mine, other = pieces[2 * k - 1], pieces[2 * k]
        size = mine.shape[0]
        out_ref[pl.ds(pl.multiple_of(base + core * overlap, 16), size), :] = mine[...]
        out_ref[pl.ds(pl.multiple_of(base + (1 - core) * overlap, 16), size), :] = other[...]


def join_rows(at, pieces, n_w, overlap):
    own, width = pieces[0].shape
    vmem = pl.BlockSpec(memory_space=pltpu.VMEM)
    return pl.pallas_call(
        functools.partial(join_rows_kernel, n_w, overlap),
        in_specs=[pl.BlockSpec(memory_space=pltpu.SMEM)] + [vmem] * len(pieces),
        out_specs=vmem,
        out_shape=jax.ShapeDtypeStruct((n_w * own, width), BF),
        compiler_params=pltpu.CompilerParams(vmem_limit_bytes=32 << 20),
        cost_estimate=pl.CostEstimate(flops=1, bytes_accessed=1, transcendentals=0),
        name="join_rows",
    )(at, *pieces)


def cut_columns_kernel(n_w, overlap, at_ref, in_ref, *out_refs):
    wsh, core = at_ref[0], at_ref[1]
    cols = out_refs[0].shape[1]
    for k, out_ref in enumerate(out_refs):
        size = out_ref.shape[0]
        start = 0 if k == 0 else pl.multiple_of(core * overlap, 16)
        for b in range(n_w):

            @pl.when((wsh + n_w - k) % n_w == b)
            def _(out_ref=out_ref, start=start, size=size, b=b):
                out_ref[...] = in_ref[pl.ds(start, size), b * cols : (b + 1) * cols]


def cut_columns(at, array, n_w, size, overlap):
    own, cols = array.shape[0], array.shape[1] // n_w
    vmem = pl.BlockSpec(memory_space=pltpu.VMEM)
    return pl.pallas_call(
        functools.partial(cut_columns_kernel, n_w, overlap),
        in_specs=[pl.BlockSpec(memory_space=pltpu.SMEM), vmem],
        out_specs=[vmem] * n_w,
        out_shape=[
            jax.ShapeDtypeStruct((own if k == 0 else size, cols), BF) for k in range(n_w)
        ],
        compiler_params=pltpu.CompilerParams(vmem_limit_bytes=32 << 20),
        cost_estimate=pl.CostEstimate(flops=1, bytes_accessed=1, transcendentals=0),
        name="cut_columns",
    )(at, array)


def join_columns_kernel(n_w, overlap, at_ref, *refs):
    *pieces, out_ref = refs
    wsh, core = at_ref[0], at_ref[1]
    cols = pieces[0].shape[1]
    for k in range(n_w):
        for b in range(n_w):

            @pl.when((wsh + k) % n_w == b)
            def _(k=k, b=b):
                at = slice(b * cols, (b + 1) * cols)
                if k == 0:
                    out_ref[:, at] = pieces[0][...].astype(F32)
                    return
                mine, other = pieces[2 * k - 1], pieces[2 * k]
                size = mine.shape[0]
                out_ref[pl.ds(pl.multiple_of(core * overlap, 16), size), at] = mine[...].astype(F32)
                out_ref[pl.ds(pl.multiple_of((1 - core) * overlap, 16), size), at] = other[
                    ...
                ].astype(F32)


def join_columns(at, pieces, n_w, overlap):
    own, cols = pieces[0].shape
    vmem = pl.BlockSpec(memory_space=pltpu.VMEM)
    return pl.pallas_call(
        functools.partial(join_columns_kernel, n_w, overlap),
        in_specs=[pl.BlockSpec(memory_space=pltpu.SMEM)] + [vmem] * len(pieces),
        out_specs=vmem,
        out_shape=jax.ShapeDtypeStruct((own, n_w * cols), F32),
        compiler_params=pltpu.CompilerParams(vmem_limit_bytes=40 << 20),
        cost_estimate=pl.CostEstimate(flops=1, bytes_accessed=1, transcendentals=0),
        name="join_columns",
    )(at, *pieces)


def out_grad_kernel(n_w, in_ref, grad_ref, side_ref, out_ref):
    made = mm(in_ref[...], grad_ref[...])
    chunks = made.shape[0] // 16
    out_ref[...] = jnp.zeros_like(out_ref)
    for c in range(chunks):
        out_ref[c] = made[c * 16 : (c + 1) * 16].astype(BF)
    out_ref[chunks, :1] = side_ref[...].astype(BF)


def out_grad(rows, grads, side, n_ctx, n_w):
    vmem = pl.BlockSpec(memory_space=pltpu.VMEM)
    return pl.pallas_call(
        functools.partial(out_grad_kernel, n_w),
        in_specs=[vmem] * 3,
        out_specs=vmem,
        out_shape=jax.ShapeDtypeStruct((n_ctx, 16, grads.shape[1]), BF),
        compiler_params=pltpu.CompilerParams(vmem_limit_bytes=24 << 20),
        cost_estimate=pl.CostEstimate(flops=1, bytes_accessed=1, transcendentals=0),
        name="out_grad",
    )(rows, grads, side)


def pack_kernel(chunk_ref, *refs):
    *pieces, left_ref, right_ref = refs
    total = pieces[0][...]
    for piece in pieces[1:]:
        total = total + piece[...].astype(F32)
    left_ref[...] = total[:, : 2 * HD].astype(BF)
    chunk = chunk_ref[0].astype(F32)
    for c in range(1, chunk_ref.shape[0]):
        chunk = chunk + chunk_ref[c].astype(F32)
    turned = jnp.concatenate(
        [chunk[:, q * HD : (q + 1) * HD] for q in range(chunk.shape[1] // HD)], axis=0
    )
    turned = jnp.concatenate(
        [turned, jnp.zeros((total.shape[0] - turned.shape[0], HD), F32)], axis=0
    )
    right_ref[...] = jnp.concatenate([total[:, 2 * HD :], turned], axis=1).astype(BF)


def pack(chunks, pieces):
    rows = pieces[0].shape[0]
    vmem = pl.BlockSpec(memory_space=pltpu.VMEM)
    return pl.pallas_call(
        pack_kernel,
        in_specs=[vmem] * (1 + len(pieces)),
        out_specs=[vmem] * 2,
        out_shape=[jax.ShapeDtypeStruct((rows, 2 * HD), BF)] * 2,
        compiler_params=pltpu.CompilerParams(vmem_limit_bytes=24 << 20),
        cost_estimate=pl.CostEstimate(flops=1, bytes_accessed=1, transcendentals=0),
        name="pack",
    )(chunks, *pieces)


def unpack_kernel(
    at_ref, left_own, left_other, right_own, right_other, qkv_ref, out_ref, bias_ref, side_ref
):
    z, y, core = at_ref[0], at_ref[1], at_ref[2]
    own = qkv_ref.shape[0]
    bias_ref[...] = jnp.zeros_like(bias_ref)
    for h in range(HEADS + 1):
        by_z, by_y = (h // 8 + 4 - z) % 4, ((h // 2) % 4 + 4 - y) % 4
        same = core == h % 2
        right_at = by_y * 4 + by_z
        right = jnp.where(same, right_own[right_at], right_other[right_at]).astype(F32)
        if h == HEADS:
            for q in range(HEADS):
                side_ref[:, q * HD : (q + 1) * HD] = right[q * 16 : q * 16 + 8, HD:]
            break
        left_at = by_z * 4 + by_y
        left = jnp.where(same, left_own[left_at], left_other[left_at]).astype(F32)
        for part, piece in enumerate((left[:, :HD], left[:, HD:], right[:, :HD])):
            at = (part * HEADS + h) * HD
            qkv_ref[:, at : at + HD] = piece[:own]
        bias_ref[0:1, h * HD : (h + 1) * HD] = left[own : own + 1, :HD]
        bias_ref[1:2, h * HD : (h + 1) * HD] = right[own : own + 1, :HD]
        for q in range(HEADS):
            out_ref[h * 16 : (h + 1) * 16, q * HD : (q + 1) * HD] = right[
                q * 16 : (q + 1) * 16, HD:
            ]


def unpack(at, left_own, left_other, right_own, right_other):
    rows = left_own.shape[1] - 16
    vmem = pl.BlockSpec(memory_space=pltpu.VMEM)
    return pl.pallas_call(
        unpack_kernel,
        in_specs=[pl.BlockSpec(memory_space=pltpu.SMEM)] + [vmem] * 4,
        out_specs=[vmem] * 4,
        out_shape=[
            jax.ShapeDtypeStruct((rows, 3 * HEADS * HD), F32),
            jax.ShapeDtypeStruct((rows, HEADS * HD), F32),
            jax.ShapeDtypeStruct((8, HEADS * HD), F32),
            jax.ShapeDtypeStruct((8, HEADS * HD), F32),
        ],
        compiler_params=pltpu.CompilerParams(vmem_limit_bytes=40 << 20),
        cost_estimate=pl.CostEstimate(flops=1, bytes_accessed=1, transcendentals=0),
        name="unpack",
    )(at, left_own, left_other, right_own, right_other)


def after(array, *others):
    return lax.optimization_barrier((array, *others))[0]


def on_device(
    layer_input,
    block_order,
    norm_gains,
    norm_shifts,
    qkv_weight,
    attn_bias,
    out_weight,
    out_bias,
    fc_weight,
    fc_bias,
    proj_weight,
    proj_bias,
    output_grad,
):
    seqs, rows, width = layer_input.shape
    tokens = seqs * rows
    n_ctx, n_w = lax.axis_size(CTX), lax.axis_size("wsh")
    ctx, wsh = lax.axis_index(CTX), lax.axis_index("wsh")
    z, y, core = (lax.axis_index(axis) for axis in CTX)
    own = width // n_w
    ff = fc_weight.shape[1] // n_w
    size, overlap = 208, 192
    at_x = jnp.stack([wsh, core])

    def shift(array, axis, k):
        size = lax.axis_size(axis)
        return lax.ppermute(array, axis, [((i + k) % size, i) for i in range(size)])

    def x_shift(array, k):
        return shift(array, "wsh", k)

    def partner(array):
        return shift(array, "core", 1)

    def around(array):
        return [array] + [x_shift(array, k) for k in range(1, n_w)]

    def deal(choose):
        return [choose(0)] + [x_shift(choose(k), k) for k in range(1, n_w)]

    def with_halves(whole, halves, *before):
        pieces = [whole]
        for k in range(1, n_w):
            mine = x_shift(halves[k - 1], k)
            pieces += [mine, partner(after(mine, *before))]
        return pieces

    def in_order(pieces):
        twice = jnp.stack(pieces + pieces)
        start = (n_w - wsh) % n_w
        return lax.dynamic_slice(twice, (start,) + (0,) * pieces[0].ndim, (n_w,) + pieces[0].shape)

    low = layer_input.reshape(tokens, width)
    gathered = lax.all_gather(low, CTX, axis=0, tiled=True)
    packed = jnp.concatenate(
        [norm_gains, norm_shifts, attn_bias, out_bias[None], proj_bias[None]], axis=0
    )
    vectors = in_order(around(packed)).transpose(1, 0, 2).reshape(8, width).astype(F32)
    gains, shifts, bias_pair = vectors[0:2], vectors[2:4], vectors[4:6]
    out_bias_row, proj_bias_row = vectors[6], vectors[7]

    head = jnp.minimum(ctx, HEADS - 1)
    head_cols = jnp.concatenate(
        [
            lax.dynamic_slice(qkv_weight, (0, part * width + head * HD), (own, HD))
            for part in range(3)
        ],
        axis=1,
    )
    head_weight = in_order(around(head_cols)).reshape(width, 3 * HD).T
    head_bias = lax.dynamic_slice(bias_pair, (0, head * HD), (2, HD))
    head_bias = jnp.concatenate([head_bias[:1], jnp.zeros((1, HD), F32), head_bias[1:]], axis=1)

    grad_low = output_grad.reshape(tokens, width)
    out_half = lax.dynamic_slice(
        after(out_weight, head_weight), (core * overlap, 0), (size, width)
    )
    out_pieces = with_halves(out_weight, [out_half] * (n_w - 1))
    out_all = join_rows(at_x, out_pieces, n_w, overlap)
    fc_own, *fc_halves = cut_columns(at_x, fc_weight, n_w, size, overlap)
    fc_halves = [after(half, *out_pieces[1::2]) for half in fc_halves]
    gathered = after(gathered, out_all)

    input_one, ordered, mixed_turned, mixed, logs = attend(
        block_order, gathered, gains[:1], shifts[:1], head_weight, head_bias, rows
    )
    grad_group = jnp.concatenate(around(after(grad_low, mixed_turned)), axis=0)
    grad_active = mm(grad_group, proj_weight, NT)
    attended = lax.all_to_all(mixed_turned, CTX, 0, 0).reshape(n_ctx * HD, tokens)[:width]
    weight_own = lax.all_gather(head_weight, ("z", "y"), axis=0, tiled=True)
    fc_pieces = with_halves(fc_own, fc_halves, mixed_turned)
    fc_cols = join_rows(at_x, [after(fc_pieces[0], attended), *fc_pieces[1:]], n_w, overlap)
    residual = low.astype(F32)
    middle = residual + mm(attended, out_all, TN) + out_bias_row
    normed_two, scaled_two, inverse_two = layer_norm(middle, gains[1], shifts[1])
    input_two = around(normed_two.astype(BF))
    *input_two, grad_active = lax.optimization_barrier((*input_two, grad_active))
    input_two = jnp.concatenate(input_two, axis=0)

    pre_gelu = mm(input_two, fc_cols) + fc_bias.astype(F32)
    activated, derivative = gelu_pair(pre_gelu)
    activated = activated.astype(BF)
    grad_pre = (grad_active * derivative).astype(BF)
    grad_two = mm(grad_pre, fc_cols, NT).reshape(n_w, tokens, width)
    parts = [grad_two[k].astype(BF) for k in range(1, n_w)]
    activated, grad_pre, *parts = lax.optimization_barrier((activated, grad_pre, *parts))
    came = [x_shift(part, n_w - k) for k, part in enumerate(parts, 1)]
    grad_proj = mm(activated, grad_group, TN).astype(BF)
    grad_fc = mm(input_two, grad_pre, TN).astype(BF)
    branch = mm(after(activated, came[0]), proj_weight).reshape(n_w, tokens, width)
    branch_own, branch_parts = branch[0], [branch[k].astype(BF) for k in range(1, n_w)]
    *came, branch_own = lax.optimization_barrier(
        (*came, branch_own, *branch_parts, grad_proj, grad_fc, weight_own)
    )[:n_w]
    grad_two = grad_two[0] + sum(piece.astype(F32) for piece in came)
    weight_other = partner(after(weight_own, grad_two))
    grad_fc_bias = jnp.sum(grad_pre.astype(F32), axis=0, keepdims=True)
    share_proj, share_fc = lax.psum((grad_proj, grad_fc), CTX)

    grad_norm_two, gain_two, shift_two = norm_back(grad_two, scaled_two, inverse_two, gains[1])
    grad_middle = grad_low.astype(F32) + grad_norm_two
    grad_branch = grad_middle.astype(BF)
    grad_attended = mm(out_all, grad_branch, NT).astype(BF)
    grad_heads = jnp.pad(grad_attended, ((0, (n_ctx - HEADS) * HD), (0, 0)))
    grad_heads = lax.all_to_all(grad_heads.reshape(n_ctx, HD, tokens), CTX, 0, 0)
    branch_group = jnp.concatenate(around(after(grad_branch, grad_attended)), axis=0)
    attended_rows = jnp.concatenate(
        deal(
            lambda k: lax.dynamic_slice(
                after(attended, came[0]), ((wsh + n_w - k) % n_w * own, 0), (own, tokens)
            )
        ),
        axis=1,
    )

    branch = branch_own + sum(
        x_shift(after(part, branch_group), n_w - k).astype(F32)
        for k, part in enumerate(branch_parts, 1)
    )
    layer_output = (middle + branch + proj_bias_row).astype(BF)

    chunks = out_grad(attended_rows, branch_group, grad_fc_bias, n_ctx, n_w)
    grad_heads = after(grad_heads, chunks)
    chunks = lax.all_to_all(chunks, CTX, 0, 0)

    grad_qkv, grad_bias = attend_back(block_order, ordered, mixed, logs, grad_heads, rows)
    grad_tokens = lax.all_to_all(grad_qkv, CTX, 0, 0)

    dealt = head_grad(at_x, grad_qkv, grad_bias, input_one, n_w)
    pieces = deal(lambda k: dealt[k])
    left, right = pack(chunks, pieces)
    left = jnp.stack([left] + [shift(left, "y", k) for k in range(1, 4)])
    right = jnp.stack([right] + [shift(right, "z", k) for k in range(1, 4)])
    left = jnp.concatenate([left] + [shift(left, "z", k) for k in range(1, 4)])
    right = jnp.concatenate([right] + [shift(right, "y", k) for k in range(1, 4)])
    side = jnp.stack(
        [
            gain_two,
            shift_two,
            jnp.sum(grad_low.astype(F32), axis=0),
            jnp.sum(grad_branch.astype(F32), axis=0),
        ]
    )
    side = jnp.pad(side, ((0, 4), (0, 0)))
    input_grad, blocks = finish(
        at_x, grad_tokens, weight_own, weight_other, low, gains[:1], shifts[:1], grad_middle, side, n_w
    )
    pieces = deal(
        lambda k: lax.dynamic_slice(blocks, ((wsh + n_w - k) % n_w, 0, 0), (1, 8, own))
    )
    vector_sum = (pieces[0] + pieces[1]) + (pieces[2] + pieces[3])
    everyone = lax.all_to_all(jnp.broadcast_to(vector_sum, (n_ctx, 8, own)), CTX, 0, 0)
    vector_out = jnp.sum(everyone, axis=0)

    qkv_out, out_out, bias_out, side_out = unpack(
        jnp.stack([z, y, core]), after(left, blocks), partner(left), right, partner(right)
    )
    bias_out = lax.dynamic_slice(bias_out, (0, wsh * own), (2, own))

    rows_for = lambda k, start, count: lax.dynamic_slice(
        share_fc, ((wsh + n_w - k) % n_w * own + start, 0), (count, ff)
    )
    fc_out = join_columns(
        at_x,
        with_halves(
            rows_for(0, 0, own),
            [rows_for(k, core * overlap, size) for k in range(1, n_w)],
            qkv_out,
        ),
        n_w,
        overlap,
    )
    return (
        layer_output.reshape(seqs, rows, width),
        input_grad.reshape(seqs, rows, width),
        vector_out[0:2],
        vector_out[2:4],
        qkv_out,
        bias_out,
        out_out,
        vector_out[5],
        fc_out,
        side_out[0],
        share_proj.astype(F32),
        vector_out[4],
    )


def solution(mesh):
    y, core = 4, 2
    split = Mesh(
        mesh.devices.reshape(mesh.shape["ctx"] // (y * core), y, core, mesh.shape["wsh"]),
        (*CTX, "wsh"),
    )
    return jax.shard_map(
        on_device,
        mesh=split,
        in_specs=(
            P("wsh", CTX, None),
            P("wsh", None),
            P(None, "wsh"),
            P(None, "wsh"),
            P("wsh", None),
            P(None, "wsh"),
            P("wsh", None),
            P("wsh"),
            P("wsh", None),
            P("wsh"),
            P("wsh", None),
            P("wsh"),
            P("wsh", CTX, None),
        ),
        out_specs=(
            P("wsh", CTX, None),
            P("wsh", CTX, None),
            P(None, "wsh"),
            P(None, "wsh"),
            P("wsh", None),
            P(None, "wsh"),
            P("wsh", None),
            P("wsh"),
            P("wsh", None),
            P("wsh"),
            P("wsh", None),
            P("wsh"),
        ),
        check_vma=False,
    )
```

```python
import functools

import jax
import jax.numpy as jnp
from jax import lax
from jax.experimental import pallas as pl
from jax.experimental.pallas import tpu as pltpu
from jax.sharding import Mesh
from jax.sharding import PartitionSpec as P

HEADS = 25
HD = 64
QB = 256
FB = 512
BF = jnp.bfloat16
F32 = jnp.float32
NN = (((1,), (0,)), ((), ()))
NT = (((1,), (1,)), ((), ()))
TN = (((0,), (0,)), ((), ()))
CTX = ("z", "y", "core")


def mm(left, right, dims=NN):
    return lax.dot_general(left, right, dims, preferred_element_type=F32)


def layer_norm(hidden, gain_row, shift_row):
    centered = hidden - jnp.mean(hidden, axis=-1, keepdims=True)
    inverse = lax.rsqrt(jnp.mean(centered * centered, axis=-1, keepdims=True) + 1e-05)
    scaled = centered * inverse
    return scaled * gain_row + shift_row, scaled, inverse


def norm_back(gradient, scaled, inverse, gain_row):
    weighted = gradient * gain_row
    first_mean = jnp.mean(weighted, axis=-1, keepdims=True)
    second_mean = jnp.mean(weighted * scaled, axis=-1, keepdims=True)
    result = inverse * (weighted - first_mean - scaled * second_mean)
    return result, jnp.sum(gradient * scaled, axis=0), jnp.sum(gradient, axis=0)


def gelu_pair(pre_gelu):
    squared = pre_gelu * pre_gelu
    tangent = jnp.tanh(0.7978845608028654 * (pre_gelu + 0.044715 * squared * pre_gelu))
    result = 0.5 * pre_gelu * (1.0 + tangent)
    derivative = 0.5 * (1.0 + tangent) + 0.5 * pre_gelu * (
        1.0 - tangent * tangent
    ) * 0.7978845608028654 * (1.0 + 3.0 * 0.044715 * squared)
    return result, derivative


def ordered_rows(order_ref, seq, block, half, length):
    return pl.multiple_of(seq * length + order_ref[seq, block] * half, half)


def below_mask(size):
    return lax.broadcasted_iota(jnp.int32, (size, size), 0) <= lax.broadcasted_iota(
        jnp.int32, (size, size), 1
    )


def attend_kernel(
    seqs, rows, half, order_ref, in_ref, gain_ref, shift_ref, weight_ref, bias_ref,
    normed_ref, sorted_ref, out_ref, mixed_ref, log_ref, rows_ref,
):
    step = pl.program_id(0)
    tokens = seqs * rows
    group = in_ref.shape[0] // tokens
    length = mixed_ref.shape[2]
    per = rows // half
    normed = layer_norm(in_ref[...].astype(F32), gain_ref[...], shift_ref[...])[0].astype(BF)
    normed_ref[...] = normed
    made = (mm(normed, weight_ref[...], NT) + bias_ref[...]).astype(BF)
    for g in range(group):
        for s in range(seqs):
            for b in range(per):
                at = ordered_rows(order_ref, s, (step * group + g) * per + b, half, length)
                first = g * tokens + s * rows + b * half
                sorted_ref[pl.ds(at, half), :] = made[first : first + half]

    @pl.when(step == pl.num_programs(0) - 1)
    def _():
        below = below_mask(FB)

        def one_seq(s, carry):
            base = pl.multiple_of(s * length, length)
            k_all = sorted_ref[pl.ds(base, length), HD : 2 * HD]
            v_turned = sorted_ref[pl.ds(base, length), 2 * HD :].T
            for i in range(length // FB):
                lo, hi = i * FB, (i + 1) * FB
                q_rows = sorted_ref[pl.ds(base + lo, FB), :HD] * 0.125
                scores = mm(k_all[:hi], q_rows, NT)
                last = jnp.where(below, scores[lo:], -1e30)
                best = jnp.max(last, axis=0, keepdims=True)
                if i:
                    best = jnp.maximum(best, jnp.max(scores[:lo], axis=0, keepdims=True))
                tail = jnp.exp(last - best)
                total = jnp.sum(tail, axis=0, keepdims=True)
                mixed = mm(v_turned[:, lo:hi], tail.astype(BF))
                if i:
                    head = jnp.exp(scores[:lo] - best)
                    total = total + jnp.sum(head, axis=0, keepdims=True)
                    mixed = mixed + mm(v_turned[:, :lo], head.astype(BF))
                mixed = mixed / total
                mixed_ref[s, :, lo:hi] = mixed
                log_ref[s, :, lo:hi] = best + jnp.log(total)
                rows_ref[pl.ds(base + lo, FB), :] = mixed.T
            return carry

        lax.fori_loop(0, seqs, one_seq, 0)

        def one_block(c, carry):
            parts = [
                rows_ref[pl.ds(ordered_rows(order_ref, s, c * per + b, half, length), half), :]
                for s in range(seqs)
                for b in range(per)
            ]
            out_ref[c] = jnp.concatenate(parts, axis=0).T.astype(BF)
            return carry

        lax.fori_loop(0, out_ref.shape[0], one_block, 0)


def attend(order, gathered, gain, shift, weight, bias, rows):
    seqs, halves = order.shape
    tokens, width = seqs * rows, gathered.shape[1]
    n_ctx = gathered.shape[0] // tokens
    length = rows * n_ctx
    half = length // halves
    group = 8
    whole = lambda *shape: pl.BlockSpec(shape, lambda i: (0,) * len(shape))
    return pl.pallas_call(
        functools.partial(attend_kernel, seqs, rows, half),
        grid=(n_ctx // group,),
        in_specs=[
            pl.BlockSpec(memory_space=pltpu.SMEM),
            pl.BlockSpec((group * tokens, width), lambda i: (i, 0)),
            whole(1, width),
            whole(1, width),
            whole(3 * HD, width),
            whole(1, 3 * HD),
        ],
        out_specs=[
            pl.BlockSpec((group * tokens, width), lambda i: (i, 0)),
            whole(seqs * length, 3 * HD),
            whole(n_ctx, HD, tokens),
            whole(seqs, HD, length),
            whole(seqs, 1, length),
        ],
        out_shape=[
            jax.ShapeDtypeStruct(gathered.shape, BF),
            jax.ShapeDtypeStruct((seqs * length, 3 * HD), BF),
            jax.ShapeDtypeStruct((n_ctx, HD, tokens), BF),
            jax.ShapeDtypeStruct((seqs, HD, length), F32),
            jax.ShapeDtypeStruct((seqs, 1, length), F32),
        ],
        scratch_shapes=[pltpu.VMEM((seqs * length, HD), F32)],
        compiler_params=pltpu.CompilerParams(vmem_limit_bytes=48 << 20),
        cost_estimate=pl.CostEstimate(
            flops=20_000_000_000, bytes_accessed=20_000_000, transcendentals=0
        ),
        name="attend",
    )(order, gathered, gain, shift, weight, bias)


def attend_back_kernel(
    seqs, rows, half, order_ref, sorted_ref, mixed_ref, log_ref, grad_ref, out_ref, bias_ref,
    rows_ref, key_ref, value_ref, all_ref,
):
    n_ctx, _, tokens = grad_ref.shape
    length = mixed_ref.shape[2]
    per = rows // half

    def spread(c, carry):
        block = grad_ref[c].T
        for s in range(seqs):
            for b in range(per):
                at = ordered_rows(order_ref, s, c * per + b, half, length)
                first = s * rows + b * half
                rows_ref[pl.ds(at, half), :] = block[first : first + half]
        return carry

    lax.fori_loop(0, n_ctx, spread, 0)
    below = below_mask(QB)

    def one_seq(s, carry):
        base = pl.multiple_of(s * length, length)
        k_all = sorted_ref[pl.ds(base, length), HD : 2 * HD]
        v_all = sorted_ref[pl.ds(base, length), 2 * HD :]
        k_turned = k_all.T
        g_turned = rows_ref[pl.ds(base, length), :].T
        delta = jnp.sum(g_turned.astype(F32) * mixed_ref[s], axis=0, keepdims=True)
        key_ref[...] = jnp.zeros_like(key_ref)
        value_ref[...] = jnp.zeros_like(value_ref)
        for i in range(length // QB):
            lo, hi = i * QB, (i + 1) * QB
            q_rows = sorted_ref[pl.ds(base + lo, QB), :HD] * 0.125
            g_rows = rows_ref[pl.ds(base + lo, QB), :]
            log_row = log_ref[s, :, lo:hi]
            delta_row = delta[:, lo:hi]
            query = jnp.zeros((HD, QB), F32)
            for first, end in ((0, lo), (lo, hi)):
                if first == end:
                    continue
                scores = mm(k_all[first:end], q_rows, NT)
                probs = jnp.exp(scores - log_row)
                if end == hi:
                    probs = jnp.where(below, probs, 0.0)
                slopes = mm(v_all[first:end], g_rows, NT)
                pulled = (probs * (slopes - delta_row)).astype(BF)
                value_ref[first:end, :] += mm(probs.astype(BF), g_rows)
                key_ref[first:end, :] += mm(pulled, q_rows)
                query = query + mm(k_turned[:, first:end], pulled)
            all_ref[pl.ds(base + lo, QB), :HD] = (query * 0.125).T
        all_ref[pl.ds(base, length), HD : 2 * HD] = key_ref[...]
        all_ref[pl.ds(base, length), 2 * HD :] = value_ref[...]
        return carry

    lax.fori_loop(0, seqs, one_seq, 0)

    def one_block(c, carry):
        parts = [
            all_ref[pl.ds(ordered_rows(order_ref, s, c * per + b, half, length), half), :]
            for s in range(seqs)
            for b in range(per)
        ]
        block = jnp.concatenate(parts, axis=0).astype(BF)
        out_ref[c] = block.T
        return carry + jnp.sum(block.astype(F32), axis=0, keepdims=True)

    bias_ref[...] = lax.fori_loop(0, n_ctx, one_block, jnp.zeros((1, 3 * HD), F32))


def attend_back(order, ordered, mixed, logs, grads, rows):
    n_ctx, _, tokens = grads.shape
    seqs, halves = order.shape
    length = rows * n_ctx
    half = length // halves
    vmem = pl.BlockSpec(memory_space=pltpu.VMEM)
    return pl.pallas_call(
        functools.partial(attend_back_kernel, seqs, rows, half),
        in_specs=[pl.BlockSpec(memory_space=pltpu.SMEM)] + [vmem] * 4,
        out_specs=[vmem] * 2,
        out_shape=[
            jax.ShapeDtypeStruct((n_ctx, 3 * HD, tokens), BF),
            jax.ShapeDtypeStruct((1, 3 * HD), F32),
        ],
        scratch_shapes=[
            pltpu.VMEM((seqs * length, HD), BF),
            pltpu.VMEM((length, HD), F32),
            pltpu.VMEM((length, HD), F32),
            pltpu.VMEM((seqs * length, 3 * HD), F32),
        ],
        compiler_params=pltpu.CompilerParams(vmem_limit_bytes=48 << 20),
        cost_estimate=pl.CostEstimate(flops=1, bytes_accessed=1, transcendentals=0),
        name="attend_back",
    )(order, ordered, mixed, logs, grads)


def head_grad_kernel(n_w, at_ref, grad_ref, bias_ref, in_ref, *refs):
    *out_refs, total_ref, turned_ref = refs
    step = pl.program_id(0)

    @pl.when(step == 0)
    def _():
        total_ref[...] = jnp.zeros_like(total_ref)

    turned = jnp.concatenate([grad_ref[g] for g in range(grad_ref.shape[0])], axis=1)
    total_ref[...] += mm(turned, in_ref[...])

    @pl.when(step == pl.num_programs(0) - 1)
    def _():
        turned_ref[...] = total_ref[...].T
        own = turned_ref.shape[0] // n_w
        for k, out_ref in enumerate(out_refs):
            at = pl.multiple_of((at_ref[0] + n_w - k) % n_w * own, 16)
            out_ref[:own] = turned_ref[pl.ds(at, own), :].astype(out_ref.dtype)
            out_ref[own:] = jnp.broadcast_to(
                bias_ref[...], (out_ref.shape[0] - own, out_ref.shape[1])
            ).astype(out_ref.dtype)


def head_grad(at, grads, bias, gathered, n_w):
    n_ctx, _, tokens = grads.shape
    width = gathered.shape[1]
    group = 4
    rows = width // n_w + 16
    return pl.pallas_call(
        functools.partial(head_grad_kernel, n_w),
        grid=(n_ctx // group,),
        in_specs=[
            pl.BlockSpec(memory_space=pltpu.SMEM),
            pl.BlockSpec((group, 3 * HD, tokens), lambda i: (i, 0, 0)),
            pl.BlockSpec((1, 3 * HD), lambda i: (0, 0)),
            pl.BlockSpec((group * tokens, width), lambda i: (i, 0)),
        ],
        out_specs=[pl.BlockSpec((rows, 3 * HD), lambda i: (0, 0))] * n_w,
        out_shape=[
            jax.ShapeDtypeStruct((rows, 3 * HD), BF if k else F32) for k in range(n_w)
        ],
        scratch_shapes=[pltpu.VMEM((3 * HD, width), F32), pltpu.VMEM((width, 3 * HD), F32)],
        compiler_params=pltpu.CompilerParams(vmem_limit_bytes=32 << 20),
        cost_estimate=pl.CostEstimate(flops=1, bytes_accessed=1, transcendentals=0),
        name="head_grad",
    )(at, grads, bias, gathered)


def finish_kernel(n_w, turned_ref, weight_ref, in_ref, gain_ref, shift_ref, middle_ref, side_ref, out_ref, block_ref, total_ref):
    step = pl.program_id(0)

    @pl.when(step == 0)
    def _():
        total_ref[...] = jnp.zeros_like(total_ref)

    total_ref[...] += mm(turned_ref[...].T, weight_ref[...])

    @pl.when(step == pl.num_programs(0) - 1)
    def _():
        grad = total_ref[...]
        _, scaled, inverse = layer_norm(in_ref[...].astype(F32), gain_ref[...], shift_ref[...])
        result, gain_grad, shift_grad = norm_back(grad, scaled, inverse, gain_ref[...])
        out_ref[...] = middle_ref[...] + result
        own = block_ref.shape[2]
        rows = (gain_grad.reshape(1, -1), side_ref[0:1], shift_grad.reshape(1, -1), side_ref[1:2])
        for w in range(n_w):
            at = slice(w * own, (w + 1) * own)
            for r, row in enumerate(rows):
                block_ref[w, r : r + 1] = row[:, at]
            block_ref[w, len(rows) :] = side_ref[2 : 2 + block_ref.shape[1] - len(rows), at]


def finish(turned, weight, low, gain, shift, middle, side, n_w):
    tokens, width = low.shape
    depth = HEADS * 3 * HD // 5
    whole = lambda *shape: pl.BlockSpec(shape, lambda i: (0,) * len(shape))
    return pl.pallas_call(
        functools.partial(finish_kernel, n_w),
        grid=(5,),
        in_specs=[
            pl.BlockSpec((depth, tokens), lambda i: (i, 0)),
            pl.BlockSpec((depth, width), lambda i: (i, 0)),
            whole(tokens, width),
            whole(1, width),
            whole(1, width),
            whole(tokens, width),
            whole(*side.shape),
        ],
        out_specs=[whole(tokens, width), whole(n_w, 8, width // n_w)],
        out_shape=[
            jax.ShapeDtypeStruct((tokens, width), F32),
            jax.ShapeDtypeStruct((n_w, 8, width // n_w), F32),
        ],
        scratch_shapes=[pltpu.VMEM((tokens, width), F32)],
        compiler_params=pltpu.CompilerParams(vmem_limit_bytes=32 << 20),
        cost_estimate=pl.CostEstimate(flops=1, bytes_accessed=1, transcendentals=0),
        name="finish",
    )(turned, weight, low, gain, shift, middle, side)


def join_rows_kernel(n_w, overlap, at_ref, *refs):
    *pieces, out_ref = refs
    wsh, core = at_ref[0], at_ref[1]
    own = pieces[0].shape[0]
    out_ref[pl.ds(pl.multiple_of(wsh * own, 16), own), :] = pieces[0][...]
    for k in range(1, n_w):
        base = (wsh + k) % n_w * own
        mine, other = pieces[2 * k - 1], pieces[2 * k]
        size = mine.shape[0]
        out_ref[pl.ds(pl.multiple_of(base + core * overlap, 16), size), :] = mine[...]
        out_ref[pl.ds(pl.multiple_of(base + (1 - core) * overlap, 16), size), :] = other[...]


def join_rows(at, pieces, n_w, overlap):
    own, width = pieces[0].shape
    vmem = pl.BlockSpec(memory_space=pltpu.VMEM)
    return pl.pallas_call(
        functools.partial(join_rows_kernel, n_w, overlap),
        in_specs=[pl.BlockSpec(memory_space=pltpu.SMEM)] + [vmem] * len(pieces),
        out_specs=vmem,
        out_shape=jax.ShapeDtypeStruct((n_w * own, width), BF),
        compiler_params=pltpu.CompilerParams(vmem_limit_bytes=32 << 20),
        cost_estimate=pl.CostEstimate(flops=1, bytes_accessed=1, transcendentals=0),
        name="join_rows",
    )(at, *pieces)


def cut_columns_kernel(n_w, overlap, at_ref, in_ref, *out_refs):
    wsh, core = at_ref[0], at_ref[1]
    cols = out_refs[0].shape[1]
    for k, out_ref in enumerate(out_refs):
        size = out_ref.shape[0]
        start = 0 if k == 0 else pl.multiple_of(core * overlap, 16)
        for b in range(n_w):

            @pl.when((wsh + n_w - k) % n_w == b)
            def _(out_ref=out_ref, start=start, size=size, b=b):
                out_ref[...] = in_ref[pl.ds(start, size), b * cols : (b + 1) * cols]


def cut_columns(at, array, n_w, size, overlap):
    own, cols = array.shape[0], array.shape[1] // n_w
    vmem = pl.BlockSpec(memory_space=pltpu.VMEM)
    return pl.pallas_call(
        functools.partial(cut_columns_kernel, n_w, overlap),
        in_specs=[pl.BlockSpec(memory_space=pltpu.SMEM), vmem],
        out_specs=[vmem] * n_w,
        out_shape=[
            jax.ShapeDtypeStruct((own if k == 0 else size, cols), BF) for k in range(n_w)
        ],
        compiler_params=pltpu.CompilerParams(vmem_limit_bytes=32 << 20),
        cost_estimate=pl.CostEstimate(flops=1, bytes_accessed=1, transcendentals=0),
        name="cut_columns",
    )(at, array)


def join_columns_kernel(n_w, overlap, at_ref, *refs):
    *pieces, out_ref = refs
    wsh, core = at_ref[0], at_ref[1]
    cols = pieces[0].shape[1]
    for k in range(n_w):
        for b in range(n_w):

            @pl.when((wsh + k) % n_w == b)
            def _(k=k, b=b):
                at = slice(b * cols, (b + 1) * cols)
                if k == 0:
                    out_ref[:, at] = pieces[0][...].astype(F32)
                    return
                mine, other = pieces[2 * k - 1], pieces[2 * k]
                size = mine.shape[0]
                out_ref[pl.ds(pl.multiple_of(core * overlap, 16), size), at] = mine[...].astype(F32)
                out_ref[pl.ds(pl.multiple_of((1 - core) * overlap, 16), size), at] = other[
                    ...
                ].astype(F32)


def join_columns(at, pieces, n_w, overlap):
    own, cols = pieces[0].shape
    vmem = pl.BlockSpec(memory_space=pltpu.VMEM)
    return pl.pallas_call(
        functools.partial(join_columns_kernel, n_w, overlap),
        in_specs=[pl.BlockSpec(memory_space=pltpu.SMEM)] + [vmem] * len(pieces),
        out_specs=vmem,
        out_shape=jax.ShapeDtypeStruct((own, n_w * cols), F32),
        compiler_params=pltpu.CompilerParams(vmem_limit_bytes=40 << 20),
        cost_estimate=pl.CostEstimate(flops=1, bytes_accessed=1, transcendentals=0),
        name="join_columns",
    )(at, *pieces)


def out_grad_kernel(n_w, in_ref, grad_ref, side_ref, out_ref):
    made = mm(in_ref[...], grad_ref[...])
    chunks = made.shape[0] // 16
    out_ref[...] = jnp.zeros_like(out_ref)
    for c in range(chunks):
        out_ref[c] = made[c * 16 : (c + 1) * 16].astype(BF)
    out_ref[chunks, :1] = side_ref[...].astype(BF)


def out_grad(rows, grads, side, n_ctx, n_w):
    vmem = pl.BlockSpec(memory_space=pltpu.VMEM)
    return pl.pallas_call(
        functools.partial(out_grad_kernel, n_w),
        in_specs=[vmem] * 3,
        out_specs=vmem,
        out_shape=jax.ShapeDtypeStruct((n_ctx, 16, grads.shape[1]), BF),
        compiler_params=pltpu.CompilerParams(vmem_limit_bytes=24 << 20),
        cost_estimate=pl.CostEstimate(flops=1, bytes_accessed=1, transcendentals=0),
        name="out_grad",
    )(rows, grads, side)


def pack_kernel(chunk_ref, *refs):
    *pieces, left_ref, right_ref = refs
    total = pieces[0][...]
    for piece in pieces[1:]:
        total = total + piece[...].astype(F32)
    left_ref[...] = total[:, : 2 * HD].astype(BF)
    chunk = chunk_ref[0].astype(F32)
    for c in range(1, chunk_ref.shape[0]):
        chunk = chunk + chunk_ref[c].astype(F32)
    turned = jnp.concatenate(
        [chunk[:, q * HD : (q + 1) * HD] for q in range(chunk.shape[1] // HD)], axis=0
    )
    turned = jnp.concatenate(
        [turned, jnp.zeros((total.shape[0] - turned.shape[0], HD), F32)], axis=0
    )
    right_ref[...] = jnp.concatenate([total[:, 2 * HD :], turned], axis=1).astype(BF)


def pack(chunks, pieces):
    rows = pieces[0].shape[0]
    vmem = pl.BlockSpec(memory_space=pltpu.VMEM)
    return pl.pallas_call(
        pack_kernel,
        in_specs=[vmem] * (1 + len(pieces)),
        out_specs=[vmem] * 2,
        out_shape=[jax.ShapeDtypeStruct((rows, 2 * HD), BF)] * 2,
        compiler_params=pltpu.CompilerParams(vmem_limit_bytes=24 << 20),
        cost_estimate=pl.CostEstimate(flops=1, bytes_accessed=1, transcendentals=0),
        name="pack",
    )(chunks, *pieces)


def unpack_kernel(
    at_ref, left_own, left_other, right_own, right_other, qkv_ref, out_ref, bias_ref, side_ref
):
    z, y, core = at_ref[0], at_ref[1], at_ref[2]
    own = qkv_ref.shape[0]
    bias_ref[...] = jnp.zeros_like(bias_ref)
    for h in range(HEADS + 1):
        by_z, by_y = (h // 8 + 4 - z) % 4, ((h // 2) % 4 + 4 - y) % 4
        same = core == h % 2
        right_at = by_y * 4 + by_z
        right = jnp.where(same, right_own[right_at], right_other[right_at]).astype(F32)
        if h == HEADS:
            for q in range(HEADS):
                side_ref[:, q * HD : (q + 1) * HD] = right[q * 16 : q * 16 + 8, HD:]
            break
        left_at = by_z * 4 + by_y
        left = jnp.where(same, left_own[left_at], left_other[left_at]).astype(F32)
        for part, piece in enumerate((left[:, :HD], left[:, HD:], right[:, :HD])):
            at = (part * HEADS + h) * HD
            qkv_ref[:, at : at + HD] = piece[:own]
        bias_ref[0:1, h * HD : (h + 1) * HD] = left[own : own + 1, :HD]
        bias_ref[1:2, h * HD : (h + 1) * HD] = right[own : own + 1, :HD]
        for q in range(HEADS):
            out_ref[h * 16 : (h + 1) * 16, q * HD : (q + 1) * HD] = right[
                q * 16 : (q + 1) * 16, HD:
            ]


def unpack(at, left_own, left_other, right_own, right_other):
    rows = left_own.shape[1] - 16
    vmem = pl.BlockSpec(memory_space=pltpu.VMEM)
    return pl.pallas_call(
        unpack_kernel,
        in_specs=[pl.BlockSpec(memory_space=pltpu.SMEM)] + [vmem] * 4,
        out_specs=[vmem] * 4,
        out_shape=[
            jax.ShapeDtypeStruct((rows, 3 * HEADS * HD), F32),
            jax.ShapeDtypeStruct((rows, HEADS * HD), F32),
            jax.ShapeDtypeStruct((8, HEADS * HD), F32),
            jax.ShapeDtypeStruct((8, HEADS * HD), F32),
        ],
        compiler_params=pltpu.CompilerParams(vmem_limit_bytes=40 << 20),
        cost_estimate=pl.CostEstimate(flops=1, bytes_accessed=1, transcendentals=0),
        name="unpack",
    )(at, left_own, left_other, right_own, right_other)


def after(array, *others):
    return lax.optimization_barrier((array, *others))[0]


def on_device(
    layer_input,
    block_order,
    norm_gains,
    norm_shifts,
    qkv_weight,
    attn_bias,
    out_weight,
    out_bias,
    fc_weight,
    fc_bias,
    proj_weight,
    proj_bias,
    output_grad,
):
    seqs, rows, width = layer_input.shape
    tokens = seqs * rows
    n_ctx, n_w = lax.axis_size(CTX), lax.axis_size("wsh")
    ctx, wsh = lax.axis_index(CTX), lax.axis_index("wsh")
    z, y, core = (lax.axis_index(axis) for axis in CTX)
    own = width // n_w
    ff = fc_weight.shape[1] // n_w
    size, overlap = 208, 192
    at_x = jnp.stack([wsh, core])

    def shift(array, axis, k):
        size = lax.axis_size(axis)
        return lax.ppermute(array, axis, [((i + k) % size, i) for i in range(size)])

    def x_shift(array, k):
        return shift(array, "wsh", k)

    def partner(array):
        return shift(array, "core", 1)

    def around(array):
        return [array] + [x_shift(array, k) for k in range(1, n_w)]

    def deal(choose):
        return [choose(0)] + [x_shift(choose(k), k) for k in range(1, n_w)]

    def with_halves(whole, halves, *before):
        pieces = [whole]
        for k in range(1, n_w):
            mine = x_shift(halves[k - 1], k)
            pieces += [mine, partner(after(mine, *before))]
        return pieces

    def in_order(pieces):
        twice = jnp.stack(pieces + pieces)
        start = (n_w - wsh) % n_w
        return lax.dynamic_slice(twice, (start,) + (0,) * pieces[0].ndim, (n_w,) + pieces[0].shape)

    low = layer_input.reshape(tokens, width)
    gathered = lax.all_gather(low, CTX, axis=0, tiled=True)
    packed = jnp.concatenate(
        [norm_gains, norm_shifts, attn_bias, out_bias[None], proj_bias[None]], axis=0
    )
    vectors = in_order(around(packed)).transpose(1, 0, 2).reshape(8, width).astype(F32)
    gains, shifts, bias_pair = vectors[0:2], vectors[2:4], vectors[4:6]
    out_bias_row, proj_bias_row = vectors[6], vectors[7]

    head = jnp.minimum(ctx, HEADS - 1)
    head_cols = jnp.concatenate(
        [
            lax.dynamic_slice(qkv_weight, (0, part * width + head * HD), (own, HD))
            for part in range(3)
        ],
        axis=1,
    )
    head_weight = in_order(around(head_cols)).reshape(width, 3 * HD).T
    head_bias = lax.dynamic_slice(bias_pair, (0, head * HD), (2, HD))
    head_bias = jnp.concatenate([head_bias[:1], jnp.zeros((1, HD), F32), head_bias[1:]], axis=1)

    grad_low = output_grad.reshape(tokens, width)
    out_half = lax.dynamic_slice(
        after(out_weight, head_weight), (core * overlap, 0), (size, width)
    )
    out_pieces = with_halves(out_weight, [out_half] * (n_w - 1))
    out_all = join_rows(at_x, out_pieces, n_w, overlap)
    fc_own, *fc_halves = cut_columns(at_x, fc_weight, n_w, size, overlap)
    fc_halves = [after(half, *out_pieces[1::2]) for half in fc_halves]
    gathered = after(gathered, out_all)

    input_one, ordered, mixed_turned, mixed, logs = attend(
        block_order, gathered, gains[:1], shifts[:1], head_weight, head_bias, rows
    )
    grad_group = jnp.concatenate(around(after(grad_low, mixed_turned)), axis=0)
    grad_active = mm(grad_group, proj_weight, NT)
    fc_pieces = with_halves(fc_own, fc_halves, mixed_turned)
    mixed_turned = after(mixed_turned, *fc_pieces[1::2])
    attended = lax.all_to_all(mixed_turned, CTX, 0, 0).reshape(n_ctx * HD, tokens)[:width]
    attended = after(attended, grad_group, *fc_pieces)
    fc_cols = join_rows(at_x, [after(fc_pieces[0], attended), *fc_pieces[1:]], n_w, overlap)
    residual = low.astype(F32)
    middle = residual + mm(attended, out_all, TN) + out_bias_row
    normed_two, scaled_two, inverse_two = layer_norm(middle, gains[1], shifts[1])
    normed_two = normed_two.astype(BF)
    weight_all = lax.all_gather(after(head_weight, normed_two), CTX, axis=0, tiled=True)
    input_two = around(normed_two)
    *input_two, grad_active = lax.optimization_barrier((*input_two, grad_active))
    input_two = jnp.concatenate(input_two, axis=0)

    pre_gelu = mm(input_two, fc_cols) + fc_bias.astype(F32)
    activated, derivative = gelu_pair(pre_gelu)
    activated = activated.astype(BF)
    grad_pre = (grad_active * derivative).astype(BF)
    grad_two = mm(grad_pre, fc_cols, NT).reshape(n_w, tokens, width)
    parts = [grad_two[k].astype(BF) for k in range(1, n_w)]
    activated, grad_pre, *parts = lax.optimization_barrier((activated, grad_pre, *parts))
    came = [x_shift(part, n_w - k) for k, part in enumerate(parts, 1)]
    grad_proj = mm(activated, grad_group, TN).astype(BF)
    grad_fc = mm(input_two, grad_pre, TN).astype(BF)
    branch = mm(after(activated, came[0]), proj_weight).reshape(n_w, tokens, width)
    branch_own, branch_parts = branch[0], [branch[k].astype(BF) for k in range(1, n_w)]
    *came, branch_own = lax.optimization_barrier(
        (*came, branch_own, *branch_parts, grad_proj, grad_fc, weight_all)
    )[:n_w]
    grad_two = grad_two[0] + sum(piece.astype(F32) for piece in came)
    grad_fc_bias = jnp.sum(grad_pre.astype(F32), axis=0, keepdims=True)
    share_proj, share_fc = lax.psum((grad_proj, grad_fc), CTX)

    grad_norm_two, gain_two, shift_two = norm_back(grad_two, scaled_two, inverse_two, gains[1])
    grad_middle = grad_low.astype(F32) + grad_norm_two
    grad_branch = grad_middle.astype(BF)
    grad_attended = mm(out_all, grad_branch, NT).astype(BF)
    grad_heads = jnp.pad(grad_attended, ((0, (n_ctx - HEADS) * HD), (0, 0)))
    grad_heads = lax.all_to_all(grad_heads.reshape(n_ctx, HD, tokens), CTX, 0, 0)
    branch_group = jnp.concatenate(around(after(grad_branch, grad_attended)), axis=0)
    attended_rows = jnp.concatenate(
        deal(
            lambda k: lax.dynamic_slice(
                after(attended, came[0]), ((wsh + n_w - k) % n_w * own, 0), (own, tokens)
            )
        ),
        axis=1,
    )

    branch = branch_own + sum(
        x_shift(after(part, branch_group), n_w - k).astype(F32)
        for k, part in enumerate(branch_parts, 1)
    )
    layer_output = (middle + branch + proj_bias_row).astype(BF)

    chunks = out_grad(attended_rows, branch_group, grad_fc_bias, n_ctx, n_w)
    grad_heads = after(grad_heads, chunks)
    chunks = lax.all_to_all(chunks, CTX, 0, 0)

    grad_qkv, grad_bias = attend_back(block_order, ordered, mixed, logs, grad_heads, rows)
    grad_tokens = lax.all_to_all(grad_qkv, CTX, 0, 0).reshape(n_ctx * 3 * HD, tokens)

    dealt = head_grad(at_x, grad_qkv, grad_bias, input_one, n_w)
    pieces = deal(lambda k: dealt[k])
    left, right = pack(chunks, pieces)
    left = jnp.stack([left] + [shift(left, "y", k) for k in range(1, 4)])
    right = jnp.stack([right] + [shift(right, "z", k) for k in range(1, 4)])
    left = jnp.concatenate([left] + [shift(left, "z", k) for k in range(1, 4)])
    right = jnp.concatenate([right] + [shift(right, "y", k) for k in range(1, 4)])
    side = jnp.stack(
        [
            gain_two,
            shift_two,
            jnp.sum(grad_low.astype(F32), axis=0),
            jnp.sum(grad_branch.astype(F32), axis=0),
        ]
    )
    side = jnp.pad(side, ((0, 4), (0, 0)))
    input_grad, blocks = finish(
        grad_tokens, weight_all, low, gains[:1], shifts[:1], grad_middle, side, n_w
    )
    pieces = deal(
        lambda k: lax.dynamic_slice(blocks, ((wsh + n_w - k) % n_w, 0, 0), (1, 8, own))
    )
    vector_sum = (pieces[0] + pieces[1]) + (pieces[2] + pieces[3])
    everyone = lax.all_to_all(jnp.broadcast_to(vector_sum, (n_ctx, 8, own)), CTX, 0, 0)
    vector_out = jnp.sum(everyone, axis=0)

    qkv_out, out_out, bias_out, side_out = unpack(
        jnp.stack([z, y, core]), after(left, blocks), partner(left), right, partner(right)
    )
    bias_out = lax.dynamic_slice(bias_out, (0, wsh * own), (2, own))

    rows_for = lambda k, start, count: lax.dynamic_slice(
        share_fc, ((wsh + n_w - k) % n_w * own + start, 0), (count, ff)
    )
    fc_out = join_columns(
        at_x,
        with_halves(
            rows_for(0, 0, own),
            [rows_for(k, core * overlap, size) for k in range(1, n_w)],
            qkv_out,
        ),
        n_w,
        overlap,
    )
    return (
        layer_output.reshape(seqs, rows, width),
        input_grad.reshape(seqs, rows, width),
        vector_out[0:2],
        vector_out[2:4],
        qkv_out,
        bias_out,
        out_out,
        vector_out[5],
        fc_out,
        side_out[0],
        share_proj.astype(F32),
        vector_out[4],
    )


def solution(mesh):
    y, core = 4, 2
    split = Mesh(
        mesh.devices.reshape(mesh.shape["ctx"] // (y * core), y, core, mesh.shape["wsh"]),
        (*CTX, "wsh"),
    )
    return jax.shard_map(
        on_device,
        mesh=split,
        in_specs=(
            P("wsh", CTX, None),
            P("wsh", None),
            P(None, "wsh"),
            P(None, "wsh"),
            P("wsh", None),
            P(None, "wsh"),
            P("wsh", None),
            P("wsh"),
            P("wsh", None),
            P("wsh"),
            P("wsh", None),
            P("wsh"),
            P("wsh", CTX, None),
        ),
        out_specs=(
            P("wsh", CTX, None),
            P("wsh", CTX, None),
            P(None, "wsh"),
            P(None, "wsh"),
            P("wsh", None),
            P(None, "wsh"),
            P("wsh", None),
            P("wsh"),
            P("wsh", None),
            P("wsh"),
            P("wsh", None),
            P("wsh"),
        ),
        check_vma=False,
    )
```

```python
import functools

import jax
import jax.numpy as jnp
from jax import lax
from jax.experimental import pallas as pl
from jax.experimental.pallas import tpu as pltpu
from jax.sharding import Mesh
from jax.sharding import PartitionSpec as P

HEADS = 25
HD = 64
QB = 256
FB = 512
BF = jnp.bfloat16
F32 = jnp.float32
NN = (((1,), (0,)), ((), ()))
NT = (((1,), (1,)), ((), ()))
TN = (((0,), (0,)), ((), ()))
CTX = ("z", "y", "core")


def mm(left, right, dims=NN):
    return lax.dot_general(left, right, dims, preferred_element_type=F32)


def layer_norm(hidden, gain_row, shift_row):
    centered = hidden - jnp.mean(hidden, axis=-1, keepdims=True)
    inverse = lax.rsqrt(jnp.mean(centered * centered, axis=-1, keepdims=True) + 1e-05)
    scaled = centered * inverse
    return scaled * gain_row + shift_row, scaled, inverse


def norm_back(gradient, scaled, inverse, gain_row):
    weighted = gradient * gain_row
    first_mean = jnp.mean(weighted, axis=-1, keepdims=True)
    second_mean = jnp.mean(weighted * scaled, axis=-1, keepdims=True)
    result = inverse * (weighted - first_mean - scaled * second_mean)
    return result, jnp.sum(gradient * scaled, axis=0), jnp.sum(gradient, axis=0)


def gelu_pair(pre_gelu):
    squared = pre_gelu * pre_gelu
    tangent = jnp.tanh(0.7978845608028654 * (pre_gelu + 0.044715 * squared * pre_gelu))
    result = 0.5 * pre_gelu * (1.0 + tangent)
    derivative = 0.5 * (1.0 + tangent) + 0.5 * pre_gelu * (
        1.0 - tangent * tangent
    ) * 0.7978845608028654 * (1.0 + 3.0 * 0.044715 * squared)
    return result, derivative


def ordered_rows(order_ref, seq, block, half, length):
    return pl.multiple_of(seq * length + order_ref[seq, block] * half, half)


def below_mask(size):
    return lax.broadcasted_iota(jnp.int32, (size, size), 0) <= lax.broadcasted_iota(
        jnp.int32, (size, size), 1
    )


def attend_kernel(
    seqs, rows, half, order_ref, in_ref, gain_ref, shift_ref, weight_ref, bias_ref,
    normed_ref, sorted_ref, out_ref, mixed_ref, log_ref, rows_ref,
):
    step = pl.program_id(0)
    tokens = seqs * rows
    group = in_ref.shape[0] // tokens
    length = mixed_ref.shape[2]
    per = rows // half
    normed = layer_norm(in_ref[...].astype(F32), gain_ref[...], shift_ref[...])[0].astype(BF)
    normed_ref[...] = normed
    made = (mm(normed, weight_ref[...], NT) + bias_ref[...]).astype(BF)
    for g in range(group):
        for s in range(seqs):
            for b in range(per):
                at = ordered_rows(order_ref, s, (step * group + g) * per + b, half, length)
                first = g * tokens + s * rows + b * half
                sorted_ref[pl.ds(at, half), :] = made[first : first + half]

    @pl.when(step == pl.num_programs(0) - 1)
    def _():
        below = below_mask(FB)

        def one_seq(s, carry):
            base = pl.multiple_of(s * length, length)
            k_all = sorted_ref[pl.ds(base, length), HD : 2 * HD]
            v_turned = sorted_ref[pl.ds(base, length), 2 * HD :].T
            for i in range(length // FB):
                lo, hi = i * FB, (i + 1) * FB
                q_rows = sorted_ref[pl.ds(base + lo, FB), :HD] * 0.125
                scores = mm(k_all[:hi], q_rows, NT)
                last = jnp.where(below, scores[lo:], -1e30)
                best = jnp.max(last, axis=0, keepdims=True)
                if i:
                    best = jnp.maximum(best, jnp.max(scores[:lo], axis=0, keepdims=True))
                tail = jnp.exp(last - best)
                total = jnp.sum(tail, axis=0, keepdims=True)
                mixed = mm(v_turned[:, lo:hi], tail.astype(BF))
                if i:
                    head = jnp.exp(scores[:lo] - best)
                    total = total + jnp.sum(head, axis=0, keepdims=True)
                    mixed = mixed + mm(v_turned[:, :lo], head.astype(BF))
                mixed = mixed / total
                mixed_ref[s, :, lo:hi] = mixed
                log_ref[s, :, lo:hi] = best + jnp.log(total)
                rows_ref[pl.ds(base + lo, FB), :] = mixed.T
            return carry

        lax.fori_loop(0, seqs, one_seq, 0)

        def one_block(c, carry):
            parts = [
                rows_ref[pl.ds(ordered_rows(order_ref, s, c * per + b, half, length), half), :]
                for s in range(seqs)
                for b in range(per)
            ]
            out_ref[c] = jnp.concatenate(parts, axis=0).T.astype(BF)
            return carry

        lax.fori_loop(0, out_ref.shape[0], one_block, 0)


def attend(order, gathered, gain, shift, weight, bias, rows):
    seqs, halves = order.shape
    tokens, width = seqs * rows, gathered.shape[1]
    n_ctx = gathered.shape[0] // tokens
    length = rows * n_ctx
    half = length // halves
    group = 8
    whole = lambda *shape: pl.BlockSpec(shape, lambda i: (0,) * len(shape))
    return pl.pallas_call(
        functools.partial(attend_kernel, seqs, rows, half),
        grid=(n_ctx // group,),
        in_specs=[
            pl.BlockSpec(memory_space=pltpu.SMEM),
            pl.BlockSpec((group * tokens, width), lambda i: (i, 0)),
            whole(1, width),
            whole(1, width),
            whole(3 * HD, width),
            whole(1, 3 * HD),
        ],
        out_specs=[
            pl.BlockSpec((group * tokens, width), lambda i: (i, 0)),
            whole(seqs * length, 3 * HD),
            whole(n_ctx, HD, tokens),
            whole(seqs, HD, length),
            whole(seqs, 1, length),
        ],
        out_shape=[
            jax.ShapeDtypeStruct(gathered.shape, BF),
            jax.ShapeDtypeStruct((seqs * length, 3 * HD), BF),
            jax.ShapeDtypeStruct((n_ctx, HD, tokens), BF),
            jax.ShapeDtypeStruct((seqs, HD, length), F32),
            jax.ShapeDtypeStruct((seqs, 1, length), F32),
        ],
        scratch_shapes=[pltpu.VMEM((seqs * length, HD), F32)],
        compiler_params=pltpu.CompilerParams(vmem_limit_bytes=48 << 20),
        cost_estimate=pl.CostEstimate(
            flops=20_000_000_000, bytes_accessed=20_000_000, transcendentals=0
        ),
        name="attend",
    )(order, gathered, gain, shift, weight, bias)


def attend_back_kernel(
    seqs, rows, half, order_ref, sorted_ref, mixed_ref, log_ref, grad_ref, out_ref, bias_ref,
    rows_ref, key_ref, value_ref, all_ref,
):
    n_ctx, _, tokens = grad_ref.shape
    length = mixed_ref.shape[2]
    per = rows // half

    def spread(c, carry):
        block = grad_ref[c].T
        for s in range(seqs):
            for b in range(per):
                at = ordered_rows(order_ref, s, c * per + b, half, length)
                first = s * rows + b * half
                rows_ref[pl.ds(at, half), :] = block[first : first + half]
        return carry

    lax.fori_loop(0, n_ctx, spread, 0)
    below = below_mask(QB)

    def one_seq(s, carry):
        base = pl.multiple_of(s * length, length)
        k_all = sorted_ref[pl.ds(base, length), HD : 2 * HD]
        v_all = sorted_ref[pl.ds(base, length), 2 * HD :]
        k_turned = k_all.T
        g_turned = rows_ref[pl.ds(base, length), :].T
        delta = jnp.sum(g_turned.astype(F32) * mixed_ref[s], axis=0, keepdims=True)
        key_ref[...] = jnp.zeros_like(key_ref)
        value_ref[...] = jnp.zeros_like(value_ref)
        for i in range(length // QB):
            lo, hi = i * QB, (i + 1) * QB
            q_rows = sorted_ref[pl.ds(base + lo, QB), :HD] * 0.125
            g_rows = rows_ref[pl.ds(base + lo, QB), :]
            log_row = log_ref[s, :, lo:hi]
            delta_row = delta[:, lo:hi]
            query = jnp.zeros((HD, QB), F32)
            for first, end in ((0, lo), (lo, hi)):
                if first == end:
                    continue
                scores = mm(k_all[first:end], q_rows, NT)
                probs = jnp.exp(scores - log_row)
                if end == hi:
                    probs = jnp.where(below, probs, 0.0)
                slopes = mm(v_all[first:end], g_rows, NT)
                pulled = (probs * (slopes - delta_row)).astype(BF)
                value_ref[first:end, :] += mm(probs.astype(BF), g_rows)
                key_ref[first:end, :] += mm(pulled, q_rows)
                query = query + mm(k_turned[:, first:end], pulled)
            all_ref[pl.ds(base + lo, QB), :HD] = (query * 0.125).T
        all_ref[pl.ds(base, length), HD : 2 * HD] = key_ref[...]
        all_ref[pl.ds(base, length), 2 * HD :] = value_ref[...]
        return carry

    lax.fori_loop(0, seqs, one_seq, 0)

    def one_block(c, carry):
        parts = [
            all_ref[pl.ds(ordered_rows(order_ref, s, c * per + b, half, length), half), :]
            for s in range(seqs)
            for b in range(per)
        ]
        block = jnp.concatenate(parts, axis=0).astype(BF)
        out_ref[c] = block.T
        return carry + jnp.sum(block.astype(F32), axis=0, keepdims=True)

    bias_ref[...] = lax.fori_loop(0, n_ctx, one_block, jnp.zeros((1, 3 * HD), F32))


def attend_back(order, ordered, mixed, logs, grads, rows):
    n_ctx, _, tokens = grads.shape
    seqs, halves = order.shape
    length = rows * n_ctx
    half = length // halves
    vmem = pl.BlockSpec(memory_space=pltpu.VMEM)
    return pl.pallas_call(
        functools.partial(attend_back_kernel, seqs, rows, half),
        in_specs=[pl.BlockSpec(memory_space=pltpu.SMEM)] + [vmem] * 4,
        out_specs=[vmem] * 2,
        out_shape=[
            jax.ShapeDtypeStruct((n_ctx, 3 * HD, tokens), BF),
            jax.ShapeDtypeStruct((1, 3 * HD), F32),
        ],
        scratch_shapes=[
            pltpu.VMEM((seqs * length, HD), BF),
            pltpu.VMEM((length, HD), F32),
            pltpu.VMEM((length, HD), F32),
            pltpu.VMEM((seqs * length, 3 * HD), F32),
        ],
        compiler_params=pltpu.CompilerParams(vmem_limit_bytes=48 << 20),
        cost_estimate=pl.CostEstimate(flops=1, bytes_accessed=1, transcendentals=0),
        name="attend_back",
    )(order, ordered, mixed, logs, grads)


def head_grad_kernel(n_w, at_ref, grad_ref, bias_ref, in_ref, *refs):
    *out_refs, total_ref, turned_ref = refs
    step = pl.program_id(0)

    @pl.when(step == 0)
    def _():
        total_ref[...] = jnp.zeros_like(total_ref)

    turned = jnp.concatenate([grad_ref[g] for g in range(grad_ref.shape[0])], axis=1)
    total_ref[...] += mm(turned, in_ref[...])

    @pl.when(step == pl.num_programs(0) - 1)
    def _():
        turned_ref[...] = total_ref[...].T
        own = turned_ref.shape[0] // n_w
        for k, out_ref in enumerate(out_refs):
            at = pl.multiple_of((at_ref[0] + n_w - k) % n_w * own, 16)
            out_ref[:own] = turned_ref[pl.ds(at, own), :].astype(out_ref.dtype)
            out_ref[own:] = jnp.broadcast_to(
                bias_ref[...], (out_ref.shape[0] - own, out_ref.shape[1])
            ).astype(out_ref.dtype)


def head_grad(at, grads, bias, gathered, n_w):
    n_ctx, _, tokens = grads.shape
    width = gathered.shape[1]
    group = 4
    rows = width // n_w + 16
    return pl.pallas_call(
        functools.partial(head_grad_kernel, n_w),
        grid=(n_ctx // group,),
        in_specs=[
            pl.BlockSpec(memory_space=pltpu.SMEM),
            pl.BlockSpec((group, 3 * HD, tokens), lambda i: (i, 0, 0)),
            pl.BlockSpec((1, 3 * HD), lambda i: (0, 0)),
            pl.BlockSpec((group * tokens, width), lambda i: (i, 0)),
        ],
        out_specs=[pl.BlockSpec((rows, 3 * HD), lambda i: (0, 0))] * n_w,
        out_shape=[
            jax.ShapeDtypeStruct((rows, 3 * HD), BF if k else F32) for k in range(n_w)
        ],
        scratch_shapes=[pltpu.VMEM((3 * HD, width), F32), pltpu.VMEM((width, 3 * HD), F32)],
        compiler_params=pltpu.CompilerParams(vmem_limit_bytes=32 << 20),
        cost_estimate=pl.CostEstimate(flops=1, bytes_accessed=1, transcendentals=0),
        name="head_grad",
    )(at, grads, bias, gathered)


def finish_kernel(n_w, turned_ref, weight_ref, in_ref, gain_ref, shift_ref, middle_ref, side_ref, out_ref, block_ref, total_ref):
    step = pl.program_id(0)

    @pl.when(step == 0)
    def _():
        total_ref[...] = jnp.zeros_like(total_ref)

    total_ref[...] += mm(turned_ref[...].T, weight_ref[...])

    @pl.when(step == pl.num_programs(0) - 1)
    def _():
        grad = total_ref[...]
        _, scaled, inverse = layer_norm(in_ref[...].astype(F32), gain_ref[...], shift_ref[...])
        result, gain_grad, shift_grad = norm_back(grad, scaled, inverse, gain_ref[...])
        out_ref[...] = middle_ref[...] + result
        own = block_ref.shape[2]
        rows = (gain_grad.reshape(1, -1), side_ref[0:1], shift_grad.reshape(1, -1), side_ref[1:2])
        for w in range(n_w):
            at = slice(w * own, (w + 1) * own)
            for r, row in enumerate(rows):
                block_ref[w, r : r + 1] = row[:, at]
            block_ref[w, len(rows) :] = side_ref[2 : 2 + block_ref.shape[1] - len(rows), at]


def finish(turned, weight, low, gain, shift, middle, side, n_w):
    tokens, width = low.shape
    depth = HEADS * 3 * HD // 5
    whole = lambda *shape: pl.BlockSpec(shape, lambda i: (0,) * len(shape))
    return pl.pallas_call(
        functools.partial(finish_kernel, n_w),
        grid=(5,),
        in_specs=[
            pl.BlockSpec((depth, tokens), lambda i: (i, 0)),
            pl.BlockSpec((depth, width), lambda i: (i, 0)),
            whole(tokens, width),
            whole(1, width),
            whole(1, width),
            whole(tokens, width),
            whole(*side.shape),
        ],
        out_specs=[whole(tokens, width), whole(n_w, 8, width // n_w)],
        out_shape=[
            jax.ShapeDtypeStruct((tokens, width), F32),
            jax.ShapeDtypeStruct((n_w, 8, width // n_w), F32),
        ],
        scratch_shapes=[pltpu.VMEM((tokens, width), F32)],
        compiler_params=pltpu.CompilerParams(vmem_limit_bytes=32 << 20),
        cost_estimate=pl.CostEstimate(flops=1, bytes_accessed=1, transcendentals=0),
        name="finish",
    )(turned, weight, low, gain, shift, middle, side)


def join_rows_kernel(n_w, overlap, at_ref, *refs):
    *pieces, out_ref = refs
    wsh, core = at_ref[0], at_ref[1]
    own = pieces[0].shape[0]
    out_ref[pl.ds(pl.multiple_of(wsh * own, 16), own), :] = pieces[0][...]
    for k in range(1, n_w):
        base = (wsh + k) % n_w * own
        mine, other = pieces[2 * k - 1], pieces[2 * k]
        size = mine.shape[0]
        out_ref[pl.ds(pl.multiple_of(base + core * overlap, 16), size), :] = mine[...]
        out_ref[pl.ds(pl.multiple_of(base + (1 - core) * overlap, 16), size), :] = other[...]


def join_rows(at, pieces, n_w, overlap):
    own, width = pieces[0].shape
    vmem = pl.BlockSpec(memory_space=pltpu.VMEM)
    return pl.pallas_call(
        functools.partial(join_rows_kernel, n_w, overlap),
        in_specs=[pl.BlockSpec(memory_space=pltpu.SMEM)] + [vmem] * len(pieces),
        out_specs=vmem,
        out_shape=jax.ShapeDtypeStruct((n_w * own, width), BF),
        compiler_params=pltpu.CompilerParams(vmem_limit_bytes=32 << 20),
        cost_estimate=pl.CostEstimate(flops=1, bytes_accessed=1, transcendentals=0),
        name="join_rows",
    )(at, *pieces)


def cut_columns_kernel(n_w, overlap, at_ref, in_ref, *out_refs):
    wsh, core = at_ref[0], at_ref[1]
    cols = out_refs[0].shape[1]
    for k, out_ref in enumerate(out_refs):
        size = out_ref.shape[0]
        start = 0 if k == 0 else pl.multiple_of(core * overlap, 16)
        for b in range(n_w):

            @pl.when((wsh + n_w - k) % n_w == b)
            def _(out_ref=out_ref, start=start, size=size, b=b):
                out_ref[...] = in_ref[pl.ds(start, size), b * cols : (b + 1) * cols]


def cut_columns(at, array, n_w, size, overlap):
    own, cols = array.shape[0], array.shape[1] // n_w
    vmem = pl.BlockSpec(memory_space=pltpu.VMEM)
    return pl.pallas_call(
        functools.partial(cut_columns_kernel, n_w, overlap),
        in_specs=[pl.BlockSpec(memory_space=pltpu.SMEM), vmem],
        out_specs=[vmem] * n_w,
        out_shape=[
            jax.ShapeDtypeStruct((own if k == 0 else size, cols), BF) for k in range(n_w)
        ],
        compiler_params=pltpu.CompilerParams(vmem_limit_bytes=32 << 20),
        cost_estimate=pl.CostEstimate(flops=1, bytes_accessed=1, transcendentals=0),
        name="cut_columns",
    )(at, array)


def join_columns_kernel(n_w, overlap, at_ref, *refs):
    *pieces, out_ref = refs
    wsh, core = at_ref[0], at_ref[1]
    cols = pieces[0].shape[1]
    for k in range(n_w):
        for b in range(n_w):

            @pl.when((wsh + k) % n_w == b)
            def _(k=k, b=b):
                at = slice(b * cols, (b + 1) * cols)
                if k == 0:
                    out_ref[:, at] = pieces[0][...].astype(F32)
                    return
                mine, other = pieces[2 * k - 1], pieces[2 * k]
                size = mine.shape[0]
                out_ref[pl.ds(pl.multiple_of(core * overlap, 16), size), at] = mine[...].astype(F32)
                out_ref[pl.ds(pl.multiple_of((1 - core) * overlap, 16), size), at] = other[
                    ...
                ].astype(F32)


def join_columns(at, pieces, n_w, overlap):
    own, cols = pieces[0].shape
    vmem = pl.BlockSpec(memory_space=pltpu.VMEM)
    return pl.pallas_call(
        functools.partial(join_columns_kernel, n_w, overlap),
        in_specs=[pl.BlockSpec(memory_space=pltpu.SMEM)] + [vmem] * len(pieces),
        out_specs=vmem,
        out_shape=jax.ShapeDtypeStruct((own, n_w * cols), F32),
        compiler_params=pltpu.CompilerParams(vmem_limit_bytes=40 << 20),
        cost_estimate=pl.CostEstimate(flops=1, bytes_accessed=1, transcendentals=0),
        name="join_columns",
    )(at, *pieces)


def out_grad_kernel(n_w, in_ref, grad_ref, side_ref, out_ref):
    made = mm(in_ref[...], grad_ref[...])
    chunks = made.shape[0] // 16
    out_ref[...] = jnp.zeros_like(out_ref)
    for c in range(chunks):
        out_ref[c] = made[c * 16 : (c + 1) * 16].astype(BF)
    out_ref[chunks, :1] = side_ref[...].astype(BF)


def out_grad(rows, grads, side, n_ctx, n_w):
    vmem = pl.BlockSpec(memory_space=pltpu.VMEM)
    return pl.pallas_call(
        functools.partial(out_grad_kernel, n_w),
        in_specs=[vmem] * 3,
        out_specs=vmem,
        out_shape=jax.ShapeDtypeStruct((n_ctx, 16, grads.shape[1]), BF),
        compiler_params=pltpu.CompilerParams(vmem_limit_bytes=24 << 20),
        cost_estimate=pl.CostEstimate(flops=1, bytes_accessed=1, transcendentals=0),
        name="out_grad",
    )(rows, grads, side)


def pack_kernel(chunk_ref, *refs):
    *pieces, left_ref, right_ref = refs
    total = pieces[0][...]
    for piece in pieces[1:]:
        total = total + piece[...].astype(F32)
    left_ref[...] = total[:, : 2 * HD].astype(BF)
    chunk = chunk_ref[0].astype(F32)
    for c in range(1, chunk_ref.shape[0]):
        chunk = chunk + chunk_ref[c].astype(F32)
    turned = jnp.concatenate(
        [chunk[:, q * HD : (q + 1) * HD] for q in range(chunk.shape[1] // HD)], axis=0
    )
    turned = jnp.concatenate(
        [turned, jnp.zeros((total.shape[0] - turned.shape[0], HD), F32)], axis=0
    )
    right_ref[...] = jnp.concatenate([total[:, 2 * HD :], turned], axis=1).astype(BF)


def pack(chunks, pieces):
    rows = pieces[0].shape[0]
    vmem = pl.BlockSpec(memory_space=pltpu.VMEM)
    return pl.pallas_call(
        pack_kernel,
        in_specs=[vmem] * (1 + len(pieces)),
        out_specs=[vmem] * 2,
        out_shape=[jax.ShapeDtypeStruct((rows, 2 * HD), BF)] * 2,
        compiler_params=pltpu.CompilerParams(vmem_limit_bytes=24 << 20),
        cost_estimate=pl.CostEstimate(flops=1, bytes_accessed=1, transcendentals=0),
        name="pack",
    )(chunks, *pieces)


def unpack_kernel(
    at_ref, left_own, left_other, right_own, right_other, qkv_ref, out_ref, bias_ref, side_ref
):
    z, y, core = at_ref[0], at_ref[1], at_ref[2]
    own = qkv_ref.shape[0]
    bias_ref[...] = jnp.zeros_like(bias_ref)
    for h in range(HEADS + 1):
        by_z, by_y = (h // 8 + 4 - z) % 4, ((h // 2) % 4 + 4 - y) % 4
        same = core == h % 2
        right_at = by_y * 4 + by_z
        right = jnp.where(same, right_own[right_at], right_other[right_at]).astype(F32)
        if h == HEADS:
            for q in range(HEADS):
                side_ref[:, q * HD : (q + 1) * HD] = right[q * 16 : q * 16 + 8, HD:]
            break
        left_at = by_z * 4 + by_y
        left = jnp.where(same, left_own[left_at], left_other[left_at]).astype(F32)
        for part, piece in enumerate((left[:, :HD], left[:, HD:], right[:, :HD])):
            at = (part * HEADS + h) * HD
            qkv_ref[:, at : at + HD] = piece[:own]
        bias_ref[0:1, h * HD : (h + 1) * HD] = left[own : own + 1, :HD]
        bias_ref[1:2, h * HD : (h + 1) * HD] = right[own : own + 1, :HD]
        for q in range(HEADS):
            out_ref[h * 16 : (h + 1) * 16, q * HD : (q + 1) * HD] = right[
                q * 16 : (q + 1) * 16, HD:
            ]


def unpack(at, left_own, left_other, right_own, right_other):
    rows = left_own.shape[1] - 16
    vmem = pl.BlockSpec(memory_space=pltpu.VMEM)
    return pl.pallas_call(
        unpack_kernel,
        in_specs=[pl.BlockSpec(memory_space=pltpu.SMEM)] + [vmem] * 4,
        out_specs=[vmem] * 4,
        out_shape=[
            jax.ShapeDtypeStruct((rows, 3 * HEADS * HD), F32),
            jax.ShapeDtypeStruct((rows, HEADS * HD), F32),
            jax.ShapeDtypeStruct((8, HEADS * HD), F32),
            jax.ShapeDtypeStruct((8, HEADS * HD), F32),
        ],
        compiler_params=pltpu.CompilerParams(vmem_limit_bytes=40 << 20),
        cost_estimate=pl.CostEstimate(flops=1, bytes_accessed=1, transcendentals=0),
        name="unpack",
    )(at, left_own, left_other, right_own, right_other)


def after(array, *others):
    return lax.optimization_barrier((array, *others))[0]


def on_device(
    layer_input,
    block_order,
    norm_gains,
    norm_shifts,
    qkv_weight,
    attn_bias,
    out_weight,
    out_bias,
    fc_weight,
    fc_bias,
    proj_weight,
    proj_bias,
    output_grad,
):
    seqs, rows, width = layer_input.shape
    tokens = seqs * rows
    n_ctx, n_w = lax.axis_size(CTX), lax.axis_size("wsh")
    ctx, wsh = lax.axis_index(CTX), lax.axis_index("wsh")
    z, y, core = (lax.axis_index(axis) for axis in CTX)
    own = width // n_w
    ff = fc_weight.shape[1] // n_w
    size, overlap = 208, 192
    at_x = jnp.stack([wsh, core])

    def shift(array, axis, k):
        size = lax.axis_size(axis)
        return lax.ppermute(array, axis, [((i + k) % size, i) for i in range(size)])

    def x_shift(array, k):
        return shift(array, "wsh", k)

    def partner(array):
        return shift(array, "core", 1)

    def around(array):
        return [array] + [x_shift(array, k) for k in range(1, n_w)]

    def deal(choose):
        return [choose(0)] + [x_shift(choose(k), k) for k in range(1, n_w)]

    def with_halves(whole, halves, *before):
        pieces = [whole]
        for k in range(1, n_w):
            mine = x_shift(halves[k - 1], k)
            pieces += [mine, partner(after(mine, *before))]
        return pieces

    def in_order(pieces):
        twice = jnp.stack(pieces + pieces)
        start = (n_w - wsh) % n_w
        return lax.dynamic_slice(twice, (start,) + (0,) * pieces[0].ndim, (n_w,) + pieces[0].shape)

    low = layer_input.reshape(tokens, width)
    gathered = lax.all_gather(low, CTX, axis=0, tiled=True)
    packed = jnp.concatenate(
        [norm_gains, norm_shifts, attn_bias, out_bias[None], proj_bias[None]], axis=0
    )
    vectors = in_order(around(packed)).transpose(1, 0, 2).reshape(8, width).astype(F32)
    gains, shifts, bias_pair = vectors[0:2], vectors[2:4], vectors[4:6]
    out_bias_row, proj_bias_row = vectors[6], vectors[7]

    head = jnp.minimum(ctx, HEADS - 1)
    head_cols = jnp.concatenate(
        [
            lax.dynamic_slice(qkv_weight, (0, part * width + head * HD), (own, HD))
            for part in range(3)
        ],
        axis=1,
    )
    head_weight = in_order(around(head_cols)).reshape(width, 3 * HD).T
    head_bias = lax.dynamic_slice(bias_pair, (0, head * HD), (2, HD))
    head_bias = jnp.concatenate([head_bias[:1], jnp.zeros((1, HD), F32), head_bias[1:]], axis=1)

    grad_low = output_grad.reshape(tokens, width)
    out_half = lax.dynamic_slice(
        after(out_weight, head_weight), (core * overlap, 0), (size, width)
    )
    out_pieces = with_halves(out_weight, [out_half] * (n_w - 1))
    out_all = join_rows(at_x, out_pieces, n_w, overlap)
    fc_own, *fc_halves = cut_columns(at_x, fc_weight, n_w, size, overlap)
    fc_halves = [after(half, *out_pieces[1::2]) for half in fc_halves]
    gathered = after(gathered, out_all)

    input_one, ordered, mixed_turned, mixed, logs = attend(
        block_order, gathered, gains[:1], shifts[:1], head_weight, head_bias, rows
    )
    grad_group = jnp.concatenate(around(after(grad_low, mixed_turned)), axis=0)
    grad_active = mm(grad_group, proj_weight, NT)
    fc_pieces = with_halves(fc_own, fc_halves, mixed_turned)
    mixed_turned = after(mixed_turned, *fc_pieces[1::2])
    attended = lax.all_to_all(mixed_turned, CTX, 0, 0).reshape(n_ctx * HD, tokens)[:width]
    attended = after(attended, grad_group, *fc_pieces)
    fc_cols = join_rows(at_x, [after(fc_pieces[0], attended), *fc_pieces[1:]], n_w, overlap)
    residual = low.astype(F32)
    middle = residual + mm(attended, out_all, TN) + out_bias_row
    normed_two, scaled_two, inverse_two = layer_norm(middle, gains[1], shifts[1])
    normed_two = normed_two.astype(BF)
    weight_all = lax.all_gather(head_weight, CTX, axis=0, tiled=True)
    input_two = around(normed_two)
    *input_two, grad_active = lax.optimization_barrier((*input_two, grad_active))
    input_two = jnp.concatenate(input_two, axis=0)

    pre_gelu = mm(input_two, fc_cols) + fc_bias.astype(F32)
    activated, derivative = gelu_pair(pre_gelu)
    activated = activated.astype(BF)
    grad_pre = (grad_active * derivative).astype(BF)
    grad_two = mm(grad_pre, fc_cols, NT).reshape(n_w, tokens, width)
    parts = [grad_two[k].astype(BF) for k in range(1, n_w)]
    activated, grad_pre, *parts = lax.optimization_barrier((activated, grad_pre, *parts))
    came = [x_shift(part, n_w - k) for k, part in enumerate(parts, 1)]
    grad_proj = mm(activated, grad_group, TN).astype(BF)
    grad_fc = mm(input_two, grad_pre, TN).astype(BF)
    branch = mm(after(activated, came[0]), proj_weight).reshape(n_w, tokens, width)
    branch_own, branch_parts = branch[0], [branch[k].astype(BF) for k in range(1, n_w)]
    *came, branch_own = lax.optimization_barrier(
        (*came, branch_own, *branch_parts, grad_proj, grad_fc, weight_all)
    )[:n_w]
    grad_two = grad_two[0] + sum(piece.astype(F32) for piece in came)
    grad_fc_bias = jnp.sum(grad_pre.astype(F32), axis=0, keepdims=True)
    share_proj, share_fc = lax.psum((grad_proj, grad_fc), CTX)

    grad_norm_two, gain_two, shift_two = norm_back(grad_two, scaled_two, inverse_two, gains[1])
    grad_middle = grad_low.astype(F32) + grad_norm_two
    grad_branch = grad_middle.astype(BF)
    grad_attended = mm(out_all, grad_branch, NT).astype(BF)
    grad_heads = jnp.pad(grad_attended, ((0, (n_ctx - HEADS) * HD), (0, 0)))
    grad_heads = lax.all_to_all(grad_heads.reshape(n_ctx, HD, tokens), CTX, 0, 0)
    branch_group = jnp.concatenate(around(after(grad_branch, grad_attended)), axis=0)
    attended_rows = jnp.concatenate(
        deal(
            lambda k: lax.dynamic_slice(
                after(attended, came[0]), ((wsh + n_w - k) % n_w * own, 0), (own, tokens)
            )
        ),
        axis=1,
    )

    branch_came = [
        x_shift(after(part, branch_group), n_w - k) for k, part in enumerate(branch_parts, 1)
    ]
    branch = branch_own + sum(piece.astype(F32) for piece in branch_came)
    layer_output = (middle + branch + proj_bias_row).astype(BF)

    chunks = out_grad(attended_rows, branch_group, grad_fc_bias, n_ctx, n_w)
    grad_heads = after(grad_heads, chunks)
    chunks = lax.all_to_all(chunks, CTX, 0, 0)

    grad_qkv, grad_bias = attend_back(block_order, ordered, mixed, logs, grad_heads, rows)
    grad_tokens = lax.all_to_all(grad_qkv, CTX, 0, 0).reshape(n_ctx * 3 * HD, tokens)

    dealt = head_grad(at_x, grad_qkv, grad_bias, after(input_one, *branch_came), n_w)
    pieces = deal(lambda k: dealt[k])
    left, right = pack(chunks, pieces)
    left = jnp.stack([left] + [shift(left, "y", k) for k in range(1, 4)])
    right = jnp.stack([right] + [shift(right, "z", k) for k in range(1, 4)])
    left = jnp.concatenate([left] + [shift(left, "z", k) for k in range(1, 4)])
    right = jnp.concatenate([right] + [shift(right, "y", k) for k in range(1, 4)])
    side = jnp.stack(
        [
            gain_two,
            shift_two,
            jnp.sum(grad_low.astype(F32), axis=0),
            jnp.sum(grad_branch.astype(F32), axis=0),
        ]
    )
    side = jnp.pad(side, ((0, 4), (0, 0)))
    input_grad, blocks = finish(
        grad_tokens, weight_all, low, gains[:1], shifts[:1], grad_middle, side, n_w
    )
    pieces = deal(
        lambda k: lax.dynamic_slice(blocks, ((wsh + n_w - k) % n_w, 0, 0), (1, 8, own))
    )
    vector_sum = (pieces[0] + pieces[1]) + (pieces[2] + pieces[3])
    everyone = lax.all_to_all(jnp.broadcast_to(vector_sum, (n_ctx, 8, own)), CTX, 0, 0)
    vector_out = jnp.sum(everyone, axis=0)

    qkv_out, out_out, bias_out, side_out = unpack(
        jnp.stack([z, y, core]), after(left, blocks), partner(left), right, partner(right)
    )
    bias_out = lax.dynamic_slice(bias_out, (0, wsh * own), (2, own))

    proj_out = share_proj.astype(F32)
    rows_for = lambda k, start, count: lax.dynamic_slice(
        share_fc, ((wsh + n_w - k) % n_w * own + start, 0), (count, ff)
    )
    fc_out = join_columns(
        at_x,
        with_halves(
            rows_for(0, 0, own),
            [rows_for(k, core * overlap, size) for k in range(1, n_w)],
            qkv_out,
            proj_out,
        ),
        n_w,
        overlap,
    )
    return (
        layer_output.reshape(seqs, rows, width),
        input_grad.reshape(seqs, rows, width),
        vector_out[0:2],
        vector_out[2:4],
        qkv_out,
        bias_out,
        out_out,
        vector_out[5],
        fc_out,
        side_out[0],
        proj_out,
        vector_out[4],
    )


def solution(mesh):
    y, core = 4, 2
    split = Mesh(
        mesh.devices.reshape(mesh.shape["ctx"] // (y * core), y, core, mesh.shape["wsh"]),
        (*CTX, "wsh"),
    )
    return jax.shard_map(
        on_device,
        mesh=split,
        in_specs=(
            P("wsh", CTX, None),
            P("wsh", None),
            P(None, "wsh"),
            P(None, "wsh"),
            P("wsh", None),
            P(None, "wsh"),
            P("wsh", None),
            P("wsh"),
            P("wsh", None),
            P("wsh"),
            P("wsh", None),
            P("wsh"),
            P("wsh", CTX, None),
        ),
        out_specs=(
            P("wsh", CTX, None),
            P("wsh", CTX, None),
            P(None, "wsh"),
            P(None, "wsh"),
            P("wsh", None),
            P(None, "wsh"),
            P("wsh", None),
            P("wsh"),
            P("wsh", None),
            P("wsh"),
            P("wsh", None),
            P("wsh"),
        ),
        check_vma=False,
    )
```

```python
import functools

import jax
import jax.numpy as jnp
from jax import lax
from jax.experimental import pallas as pl
from jax.experimental.pallas import tpu as pltpu
from jax.sharding import Mesh
from jax.sharding import PartitionSpec as P

HEADS = 25
HD = 64
QB = 256
FB = 512
BF = jnp.bfloat16
F32 = jnp.float32
NN = (((1,), (0,)), ((), ()))
NT = (((1,), (1,)), ((), ()))
TN = (((0,), (0,)), ((), ()))
CTX = ("z", "y", "core")


def mm(left, right, dims=NN):
    return lax.dot_general(left, right, dims, preferred_element_type=F32)


def layer_norm(hidden, gain_row, shift_row):
    centered = hidden - jnp.mean(hidden, axis=-1, keepdims=True)
    inverse = lax.rsqrt(jnp.mean(centered * centered, axis=-1, keepdims=True) + 1e-05)
    scaled = centered * inverse
    return scaled * gain_row + shift_row, scaled, inverse


def norm_back(gradient, scaled, inverse, gain_row):
    weighted = gradient * gain_row
    first_mean = jnp.mean(weighted, axis=-1, keepdims=True)
    second_mean = jnp.mean(weighted * scaled, axis=-1, keepdims=True)
    result = inverse * (weighted - first_mean - scaled * second_mean)
    return result, jnp.sum(gradient * scaled, axis=0), jnp.sum(gradient, axis=0)


def gelu_pair(pre_gelu):
    squared = pre_gelu * pre_gelu
    tangent = jnp.tanh(0.7978845608028654 * (pre_gelu + 0.044715 * squared * pre_gelu))
    result = 0.5 * pre_gelu * (1.0 + tangent)
    derivative = 0.5 * (1.0 + tangent) + 0.5 * pre_gelu * (
        1.0 - tangent * tangent
    ) * 0.7978845608028654 * (1.0 + 3.0 * 0.044715 * squared)
    return result, derivative


def ordered_rows(order_ref, seq, block, half, length):
    return pl.multiple_of(seq * length + order_ref[seq, block] * half, half)


def below_mask(size):
    return lax.broadcasted_iota(jnp.int32, (size, size), 0) <= lax.broadcasted_iota(
        jnp.int32, (size, size), 1
    )


def attend_kernel(
    seqs, rows, half, order_ref, in_ref, gain_ref, shift_ref, weight_ref, bias_ref,
    normed_ref, sorted_ref, out_ref, mixed_ref, log_ref, rows_ref,
):
    step = pl.program_id(0)
    tokens = seqs * rows
    group = in_ref.shape[0] // tokens
    length = mixed_ref.shape[2]
    per = rows // half
    normed = layer_norm(in_ref[...].astype(F32), gain_ref[...], shift_ref[...])[0].astype(BF)
    normed_ref[...] = normed
    made = (mm(normed, weight_ref[...], NT) + bias_ref[...]).astype(BF)
    for g in range(group):
        for s in range(seqs):
            for b in range(per):
                at = ordered_rows(order_ref, s, (step * group + g) * per + b, half, length)
                first = g * tokens + s * rows + b * half
                sorted_ref[pl.ds(at, half), :] = made[first : first + half]

    @pl.when(step == pl.num_programs(0) - 1)
    def _():
        below = below_mask(FB)

        def one_seq(s, carry):
            base = pl.multiple_of(s * length, length)
            k_all = sorted_ref[pl.ds(base, length), HD : 2 * HD]
            v_turned = sorted_ref[pl.ds(base, length), 2 * HD :].T
            for i in range(length // FB):
                lo, hi = i * FB, (i + 1) * FB
                q_rows = sorted_ref[pl.ds(base + lo, FB), :HD] * 0.125
                scores = mm(k_all[:hi], q_rows, NT)
                last = jnp.where(below, scores[lo:], -1e30)
                best = jnp.max(last, axis=0, keepdims=True)
                if i:
                    best = jnp.maximum(best, jnp.max(scores[:lo], axis=0, keepdims=True))
                tail = jnp.exp(last - best)
                total = jnp.sum(tail, axis=0, keepdims=True)
                mixed = mm(v_turned[:, lo:hi], tail.astype(BF))
                if i:
                    head = jnp.exp(scores[:lo] - best)
                    total = total + jnp.sum(head, axis=0, keepdims=True)
                    mixed = mixed + mm(v_turned[:, :lo], head.astype(BF))
                mixed = mixed / total
                mixed_ref[s, :, lo:hi] = mixed
                log_ref[s, :, lo:hi] = best + jnp.log(total)
                rows_ref[pl.ds(base + lo, FB), :] = mixed.T
            return carry

        lax.fori_loop(0, seqs, one_seq, 0)

        def one_block(c, carry):
            parts = [
                rows_ref[pl.ds(ordered_rows(order_ref, s, c * per + b, half, length), half), :]
                for s in range(seqs)
                for b in range(per)
            ]
            out_ref[c] = jnp.concatenate(parts, axis=0).T.astype(BF)
            return carry

        lax.fori_loop(0, out_ref.shape[0], one_block, 0)


def attend(order, gathered, gain, shift, weight, bias, rows):
    seqs, halves = order.shape
    tokens, width = seqs * rows, gathered.shape[1]
    n_ctx = gathered.shape[0] // tokens
    length = rows * n_ctx
    half = length // halves
    group = 8
    whole = lambda *shape: pl.BlockSpec(shape, lambda i: (0,) * len(shape))
    return pl.pallas_call(
        functools.partial(attend_kernel, seqs, rows, half),
        grid=(n_ctx // group,),
        in_specs=[
            pl.BlockSpec(memory_space=pltpu.SMEM),
            pl.BlockSpec((group * tokens, width), lambda i: (i, 0)),
            whole(1, width),
            whole(1, width),
            whole(3 * HD, width),
            whole(1, 3 * HD),
        ],
        out_specs=[
            pl.BlockSpec((group * tokens, width), lambda i: (i, 0)),
            whole(seqs * length, 3 * HD),
            whole(n_ctx, HD, tokens),
            whole(seqs, HD, length),
            whole(seqs, 1, length),
        ],
        out_shape=[
            jax.ShapeDtypeStruct(gathered.shape, BF),
            jax.ShapeDtypeStruct((seqs * length, 3 * HD), BF),
            jax.ShapeDtypeStruct((n_ctx, HD, tokens), BF),
            jax.ShapeDtypeStruct((seqs, HD, length), F32),
            jax.ShapeDtypeStruct((seqs, 1, length), F32),
        ],
        scratch_shapes=[pltpu.VMEM((seqs * length, HD), F32)],
        compiler_params=pltpu.CompilerParams(vmem_limit_bytes=48 << 20),
        cost_estimate=pl.CostEstimate(
            flops=20_000_000_000, bytes_accessed=20_000_000, transcendentals=0
        ),
        name="attend",
    )(order, gathered, gain, shift, weight, bias)


def attend_back_kernel(
    seqs, rows, half, order_ref, sorted_ref, mixed_ref, log_ref, grad_ref, out_ref, bias_ref,
    rows_ref, key_ref, value_ref, all_ref,
):
    n_ctx, _, tokens = grad_ref.shape
    length = mixed_ref.shape[2]
    per = rows // half

    def spread(c, carry):
        block = grad_ref[c].T
        for s in range(seqs):
            for b in range(per):
                at = ordered_rows(order_ref, s, c * per + b, half, length)
                first = s * rows + b * half
                rows_ref[pl.ds(at, half), :] = block[first : first + half]
        return carry

    lax.fori_loop(0, n_ctx, spread, 0)
    below = below_mask(QB)

    def one_seq(s, carry):
        base = pl.multiple_of(s * length, length)
        k_all = sorted_ref[pl.ds(base, length), HD : 2 * HD]
        v_all = sorted_ref[pl.ds(base, length), 2 * HD :]
        k_turned = k_all.T
        g_turned = rows_ref[pl.ds(base, length), :].T
        delta = jnp.sum(g_turned.astype(F32) * mixed_ref[s], axis=0, keepdims=True)
        key_ref[...] = jnp.zeros_like(key_ref)
        value_ref[...] = jnp.zeros_like(value_ref)
        for i in range(length // QB):
            lo, hi = i * QB, (i + 1) * QB
            q_rows = sorted_ref[pl.ds(base + lo, QB), :HD] * 0.125
            g_rows = rows_ref[pl.ds(base + lo, QB), :]
            log_row = log_ref[s, :, lo:hi]
            delta_row = delta[:, lo:hi]
            query = jnp.zeros((HD, QB), F32)
            for first, end in ((0, lo), (lo, hi)):
                if first == end:
                    continue
                scores = mm(k_all[first:end], q_rows, NT)
                probs = jnp.exp(scores - log_row)
                if end == hi:
                    probs = jnp.where(below, probs, 0.0)
                slopes = mm(v_all[first:end], g_rows, NT)
                pulled = (probs * (slopes - delta_row)).astype(BF)
                value_ref[first:end, :] += mm(probs.astype(BF), g_rows)
                key_ref[first:end, :] += mm(pulled, q_rows)
                query = query + mm(k_turned[:, first:end], pulled)
            all_ref[pl.ds(base + lo, QB), :HD] = (query * 0.125).T
        all_ref[pl.ds(base, length), HD : 2 * HD] = key_ref[...]
        all_ref[pl.ds(base, length), 2 * HD :] = value_ref[...]
        return carry

    lax.fori_loop(0, seqs, one_seq, 0)

    def one_block(c, carry):
        parts = [
            all_ref[pl.ds(ordered_rows(order_ref, s, c * per + b, half, length), half), :]
            for s in range(seqs)
            for b in range(per)
        ]
        block = jnp.concatenate(parts, axis=0).astype(BF)
        out_ref[c] = block.T
        return carry + jnp.sum(block.astype(F32), axis=0, keepdims=True)

    bias_ref[...] = lax.fori_loop(0, n_ctx, one_block, jnp.zeros((1, 3 * HD), F32))


def attend_back(order, ordered, mixed, logs, grads, rows):
    n_ctx, _, tokens = grads.shape
    seqs, halves = order.shape
    length = rows * n_ctx
    half = length // halves
    vmem = pl.BlockSpec(memory_space=pltpu.VMEM)
    return pl.pallas_call(
        functools.partial(attend_back_kernel, seqs, rows, half),
        in_specs=[pl.BlockSpec(memory_space=pltpu.SMEM)] + [vmem] * 4,
        out_specs=[vmem] * 2,
        out_shape=[
            jax.ShapeDtypeStruct((n_ctx, 3 * HD, tokens), BF),
            jax.ShapeDtypeStruct((1, 3 * HD), F32),
        ],
        scratch_shapes=[
            pltpu.VMEM((seqs * length, HD), BF),
            pltpu.VMEM((length, HD), F32),
            pltpu.VMEM((length, HD), F32),
            pltpu.VMEM((seqs * length, 3 * HD), F32),
        ],
        compiler_params=pltpu.CompilerParams(vmem_limit_bytes=48 << 20),
        cost_estimate=pl.CostEstimate(flops=1, bytes_accessed=1, transcendentals=0),
        name="attend_back",
    )(order, ordered, mixed, logs, grads)


def head_grad_kernel(n_w, at_ref, grad_ref, bias_ref, in_ref, *refs):
    *out_refs, total_ref, turned_ref = refs
    step = pl.program_id(0)

    @pl.when(step == 0)
    def _():
        total_ref[...] = jnp.zeros_like(total_ref)

    turned = jnp.concatenate([grad_ref[g] for g in range(grad_ref.shape[0])], axis=1)
    total_ref[...] += mm(turned, in_ref[...])

    @pl.when(step == pl.num_programs(0) - 1)
    def _():
        turned_ref[...] = total_ref[...].T
        own = turned_ref.shape[0] // n_w
        for k, out_ref in enumerate(out_refs):
            at = pl.multiple_of((at_ref[0] + n_w - k) % n_w * own, 16)
            out_ref[:own] = turned_ref[pl.ds(at, own), :].astype(out_ref.dtype)
            out_ref[own:] = jnp.broadcast_to(
                bias_ref[...], (out_ref.shape[0] - own, out_ref.shape[1])
            ).astype(out_ref.dtype)


def head_grad(at, grads, bias, gathered, n_w):
    n_ctx, _, tokens = grads.shape
    width = gathered.shape[1]
    group = 4
    rows = width // n_w + 16
    return pl.pallas_call(
        functools.partial(head_grad_kernel, n_w),
        grid=(n_ctx // group,),
        in_specs=[
            pl.BlockSpec(memory_space=pltpu.SMEM),
            pl.BlockSpec((group, 3 * HD, tokens), lambda i: (i, 0, 0)),
            pl.BlockSpec((1, 3 * HD), lambda i: (0, 0)),
            pl.BlockSpec((group * tokens, width), lambda i: (i, 0)),
        ],
        out_specs=[pl.BlockSpec((rows, 3 * HD), lambda i: (0, 0))] * n_w,
        out_shape=[
            jax.ShapeDtypeStruct((rows, 3 * HD), BF if k else F32) for k in range(n_w)
        ],
        scratch_shapes=[pltpu.VMEM((3 * HD, width), F32), pltpu.VMEM((width, 3 * HD), F32)],
        compiler_params=pltpu.CompilerParams(vmem_limit_bytes=32 << 20),
        cost_estimate=pl.CostEstimate(flops=1, bytes_accessed=1, transcendentals=0),
        name="head_grad",
    )(at, grads, bias, gathered)


def finish_kernel(n_w, turned_ref, weight_ref, in_ref, gain_ref, shift_ref, middle_ref, side_ref, out_ref, block_ref, total_ref):
    step = pl.program_id(0)

    @pl.when(step == 0)
    def _():
        total_ref[...] = jnp.zeros_like(total_ref)

    total_ref[...] += mm(turned_ref[...].T, weight_ref[...])

    @pl.when(step == pl.num_programs(0) - 1)
    def _():
        grad = total_ref[...]
        _, scaled, inverse = layer_norm(in_ref[...].astype(F32), gain_ref[...], shift_ref[...])
        result, gain_grad, shift_grad = norm_back(grad, scaled, inverse, gain_ref[...])
        out_ref[...] = middle_ref[...] + result
        own = block_ref.shape[2]
        rows = (gain_grad.reshape(1, -1), side_ref[0:1], shift_grad.reshape(1, -1), side_ref[1:2])
        for w in range(n_w):
            at = slice(w * own, (w + 1) * own)
            for r, row in enumerate(rows):
                block_ref[w, r : r + 1] = row[:, at]
            block_ref[w, len(rows) :] = side_ref[2 : 2 + block_ref.shape[1] - len(rows), at]


def finish(turned, weight, low, gain, shift, middle, side, n_w):
    tokens, width = low.shape
    depth = HEADS * 3 * HD // 5
    whole = lambda *shape: pl.BlockSpec(shape, lambda i: (0,) * len(shape))
    return pl.pallas_call(
        functools.partial(finish_kernel, n_w),
        grid=(5,),
        in_specs=[
            pl.BlockSpec((depth, tokens), lambda i: (i, 0)),
            pl.BlockSpec((depth, width), lambda i: (i, 0)),
            whole(tokens, width),
            whole(1, width),
            whole(1, width),
            whole(tokens, width),
            whole(*side.shape),
        ],
        out_specs=[whole(tokens, width), whole(n_w, 8, width // n_w)],
        out_shape=[
            jax.ShapeDtypeStruct((tokens, width), F32),
            jax.ShapeDtypeStruct((n_w, 8, width // n_w), F32),
        ],
        scratch_shapes=[pltpu.VMEM((tokens, width), F32)],
        compiler_params=pltpu.CompilerParams(vmem_limit_bytes=32 << 20),
        cost_estimate=pl.CostEstimate(flops=1, bytes_accessed=1, transcendentals=0),
        name="finish",
    )(turned, weight, low, gain, shift, middle, side)


def join_rows_kernel(n_w, overlap, at_ref, *refs):
    *pieces, out_ref = refs
    wsh, core = at_ref[0], at_ref[1]
    own = pieces[0].shape[0]
    out_ref[pl.ds(pl.multiple_of(wsh * own, 16), own), :] = pieces[0][...]
    for k in range(1, n_w):
        base = (wsh + k) % n_w * own
        mine, other = pieces[2 * k - 1], pieces[2 * k]
        size = mine.shape[0]
        out_ref[pl.ds(pl.multiple_of(base + core * overlap, 16), size), :] = mine[...]
        out_ref[pl.ds(pl.multiple_of(base + (1 - core) * overlap, 16), size), :] = other[...]


def join_rows(at, pieces, n_w, overlap):
    own, width = pieces[0].shape
    vmem = pl.BlockSpec(memory_space=pltpu.VMEM)
    return pl.pallas_call(
        functools.partial(join_rows_kernel, n_w, overlap),
        in_specs=[pl.BlockSpec(memory_space=pltpu.SMEM)] + [vmem] * len(pieces),
        out_specs=vmem,
        out_shape=jax.ShapeDtypeStruct((n_w * own, width), BF),
        compiler_params=pltpu.CompilerParams(vmem_limit_bytes=32 << 20),
        cost_estimate=pl.CostEstimate(flops=1, bytes_accessed=1, transcendentals=0),
        name="join_rows",
    )(at, *pieces)


def cut_columns_kernel(n_w, overlap, at_ref, in_ref, *out_refs):
    wsh, core = at_ref[0], at_ref[1]
    cols = out_refs[0].shape[1]
    for k, out_ref in enumerate(out_refs):
        size = out_ref.shape[0]
        start = 0 if k == 0 else pl.multiple_of(core * overlap, 16)
        for b in range(n_w):

            @pl.when((wsh + n_w - k) % n_w == b)
            def _(out_ref=out_ref, start=start, size=size, b=b):
                out_ref[...] = in_ref[pl.ds(start, size), b * cols : (b + 1) * cols]


def cut_columns(at, array, n_w, size, overlap):
    own, cols = array.shape[0], array.shape[1] // n_w
    vmem = pl.BlockSpec(memory_space=pltpu.VMEM)
    return pl.pallas_call(
        functools.partial(cut_columns_kernel, n_w, overlap),
        in_specs=[pl.BlockSpec(memory_space=pltpu.SMEM), vmem],
        out_specs=[vmem] * n_w,
        out_shape=[
            jax.ShapeDtypeStruct((own if k == 0 else size, cols), BF) for k in range(n_w)
        ],
        compiler_params=pltpu.CompilerParams(vmem_limit_bytes=32 << 20),
        cost_estimate=pl.CostEstimate(flops=1, bytes_accessed=1, transcendentals=0),
        name="cut_columns",
    )(at, array)


def join_halves_kernel(n_w, overlap, at_ref, fc_mine, fc_other, proj_mine, proj_other, fc_ref, proj_ref):
    wsh, core = at_ref[0], at_ref[1]
    size, cols = fc_mine.shape[0] // n_w, fc_mine.shape[1]
    for k in range(n_w):
        at = slice(k * size, (k + 1) * size)
        for b in range(n_w):

            @pl.when((wsh + k) % n_w == b)
            def _(at=at, b=b):
                to = slice(b * cols, (b + 1) * cols)
                for half, piece in ((core, fc_mine), (1 - core, fc_other)):
                    rows = pl.ds(pl.multiple_of(half * overlap, 16), size)
                    fc_ref[rows, to] = piece[at].astype(F32)

    size = proj_mine.shape[0]
    for half, piece in ((core, proj_mine), (1 - core, proj_other)):
        proj_ref[pl.ds(pl.multiple_of(half * size, 16), size), :] = piece[...].astype(F32)


def join_halves(at, fc_mine, fc_other, proj_mine, proj_other, n_w, own, overlap):
    vmem = pl.BlockSpec(memory_space=pltpu.VMEM)
    return pl.pallas_call(
        functools.partial(join_halves_kernel, n_w, overlap),
        in_specs=[pl.BlockSpec(memory_space=pltpu.SMEM)] + [vmem] * 4,
        out_specs=[vmem] * 2,
        out_shape=[
            jax.ShapeDtypeStruct((own, n_w * fc_mine.shape[1]), F32),
            jax.ShapeDtypeStruct((2 * proj_mine.shape[0], proj_mine.shape[1]), F32),
        ],
        compiler_params=pltpu.CompilerParams(vmem_limit_bytes=48 << 20),
        cost_estimate=pl.CostEstimate(flops=1, bytes_accessed=1, transcendentals=0),
        name="join_halves",
    )(at, fc_mine, fc_other, proj_mine, proj_other)


def half_grad_kernel(blocks, step, at_ref, left_mine, left_other, right_mine, right_other, out_ref):
    core = at_ref[1]
    size = out_ref.shape[0] // blocks
    stride = left_mine.shape[1] // blocks
    for c in range(2):

        @pl.when(core == c)
        def _(c=c):
            for b in range(blocks):
                cols = slice(b * stride + c * step, b * stride + c * step + size)
                total = mm(left_mine[:, cols], right_mine[...], TN)
                total = total + mm(left_other[:, cols], right_other[...], TN)
                out_ref[b * size : (b + 1) * size, :] = total.astype(BF)


def half_grad(at, left, right, blocks, step, size):
    vmem = pl.BlockSpec(memory_space=pltpu.VMEM)
    return pl.pallas_call(
        functools.partial(half_grad_kernel, blocks, step),
        in_specs=[pl.BlockSpec(memory_space=pltpu.SMEM)] + [vmem] * 4,
        out_specs=vmem,
        out_shape=jax.ShapeDtypeStruct((blocks * size, right[0].shape[1]), BF),
        compiler_params=pltpu.CompilerParams(vmem_limit_bytes=40 << 20),
        cost_estimate=pl.CostEstimate(flops=1, bytes_accessed=1, transcendentals=0),
        name="half_grad",
    )(at, *left, *right)


def out_grad_kernel(n_w, in_ref, grad_ref, side_ref, out_ref):
    made = mm(in_ref[...], grad_ref[...])
    chunks = made.shape[0] // 16
    out_ref[...] = jnp.zeros_like(out_ref)
    for c in range(chunks):
        out_ref[c] = made[c * 16 : (c + 1) * 16].astype(BF)
    out_ref[chunks, :1] = side_ref[...].astype(BF)


def out_grad(rows, grads, side, n_ctx, n_w):
    vmem = pl.BlockSpec(memory_space=pltpu.VMEM)
    return pl.pallas_call(
        functools.partial(out_grad_kernel, n_w),
        in_specs=[vmem] * 3,
        out_specs=vmem,
        out_shape=jax.ShapeDtypeStruct((n_ctx, 16, grads.shape[1]), BF),
        compiler_params=pltpu.CompilerParams(vmem_limit_bytes=24 << 20),
        cost_estimate=pl.CostEstimate(flops=1, bytes_accessed=1, transcendentals=0),
        name="out_grad",
    )(rows, grads, side)


def pack_kernel(chunk_ref, *refs):
    *pieces, left_ref, right_ref = refs
    total = pieces[0][...]
    for piece in pieces[1:]:
        total = total + piece[...].astype(F32)
    left_ref[...] = total[:, : 2 * HD].astype(BF)
    chunk = chunk_ref[0].astype(F32)
    for c in range(1, chunk_ref.shape[0]):
        chunk = chunk + chunk_ref[c].astype(F32)
    turned = jnp.concatenate(
        [chunk[:, q * HD : (q + 1) * HD] for q in range(chunk.shape[1] // HD)], axis=0
    )
    turned = jnp.concatenate(
        [turned, jnp.zeros((total.shape[0] - turned.shape[0], HD), F32)], axis=0
    )
    right_ref[...] = jnp.concatenate([total[:, 2 * HD :], turned], axis=1).astype(BF)


def pack(chunks, pieces):
    rows = pieces[0].shape[0]
    vmem = pl.BlockSpec(memory_space=pltpu.VMEM)
    return pl.pallas_call(
        pack_kernel,
        in_specs=[vmem] * (1 + len(pieces)),
        out_specs=[vmem] * 2,
        out_shape=[jax.ShapeDtypeStruct((rows, 2 * HD), BF)] * 2,
        compiler_params=pltpu.CompilerParams(vmem_limit_bytes=24 << 20),
        cost_estimate=pl.CostEstimate(flops=1, bytes_accessed=1, transcendentals=0),
        name="pack",
    )(chunks, *pieces)


def unpack_kernel(
    at_ref, left_own, left_other, right_own, right_other, qkv_ref, out_ref, bias_ref, side_ref
):
    z, y, core = at_ref[0], at_ref[1], at_ref[2]
    own = qkv_ref.shape[0]
    bias_ref[...] = jnp.zeros_like(bias_ref)
    for h in range(HEADS + 1):
        by_z, by_y = (h // 8 + 4 - z) % 4, ((h // 2) % 4 + 4 - y) % 4
        same = core == h % 2
        right_at = by_y * 4 + by_z
        right = jnp.where(same, right_own[right_at], right_other[right_at]).astype(F32)
        if h == HEADS:
            for q in range(HEADS):
                side_ref[:, q * HD : (q + 1) * HD] = right[q * 16 : q * 16 + 8, HD:]
            break
        left_at = by_z * 4 + by_y
        left = jnp.where(same, left_own[left_at], left_other[left_at]).astype(F32)
        for part, piece in enumerate((left[:, :HD], left[:, HD:], right[:, :HD])):
            at = (part * HEADS + h) * HD
            qkv_ref[:, at : at + HD] = piece[:own]
        bias_ref[0:1, h * HD : (h + 1) * HD] = left[own : own + 1, :HD]
        bias_ref[1:2, h * HD : (h + 1) * HD] = right[own : own + 1, :HD]
        for q in range(HEADS):
            out_ref[h * 16 : (h + 1) * 16, q * HD : (q + 1) * HD] = right[
                q * 16 : (q + 1) * 16, HD:
            ]


def unpack(at, left_own, left_other, right_own, right_other):
    rows = left_own.shape[1] - 16
    vmem = pl.BlockSpec(memory_space=pltpu.VMEM)
    return pl.pallas_call(
        unpack_kernel,
        in_specs=[pl.BlockSpec(memory_space=pltpu.SMEM)] + [vmem] * 4,
        out_specs=[vmem] * 4,
        out_shape=[
            jax.ShapeDtypeStruct((rows, 3 * HEADS * HD), F32),
            jax.ShapeDtypeStruct((rows, HEADS * HD), F32),
            jax.ShapeDtypeStruct((8, HEADS * HD), F32),
            jax.ShapeDtypeStruct((8, HEADS * HD), F32),
        ],
        compiler_params=pltpu.CompilerParams(vmem_limit_bytes=40 << 20),
        cost_estimate=pl.CostEstimate(flops=1, bytes_accessed=1, transcendentals=0),
        name="unpack",
    )(at, left_own, left_other, right_own, right_other)


def after(array, *others):
    return lax.optimization_barrier((array, *others))[0]


def on_device(
    layer_input,
    block_order,
    norm_gains,
    norm_shifts,
    qkv_weight,
    attn_bias,
    out_weight,
    out_bias,
    fc_weight,
    fc_bias,
    proj_weight,
    proj_bias,
    output_grad,
):
    seqs, rows, width = layer_input.shape
    tokens = seqs * rows
    n_ctx, n_w = lax.axis_size(CTX), lax.axis_size("wsh")
    ctx, wsh = lax.axis_index(CTX), lax.axis_index("wsh")
    z, y, core = (lax.axis_index(axis) for axis in CTX)
    own = width // n_w
    ff = fc_weight.shape[1] // n_w
    size, overlap = 208, 192
    at_x = jnp.stack([wsh, core])

    def shift(array, axis, k):
        size = lax.axis_size(axis)
        return lax.ppermute(array, axis, [((i + k) % size, i) for i in range(size)])

    def x_shift(array, k):
        return shift(array, "wsh", k)

    def partner(array):
        return shift(array, "core", 1)

    def around(array):
        return [array] + [x_shift(array, k) for k in range(1, n_w)]

    def deal(choose):
        return [choose(0)] + [x_shift(choose(k), k) for k in range(1, n_w)]

    def with_halves(whole, halves, *before):
        pieces = [whole]
        for k in range(1, n_w):
            mine = x_shift(halves[k - 1], k)
            pieces += [mine, partner(after(mine, *before))]
        return pieces

    def in_order(pieces):
        twice = jnp.stack(pieces + pieces)
        start = (n_w - wsh) % n_w
        return lax.dynamic_slice(twice, (start,) + (0,) * pieces[0].ndim, (n_w,) + pieces[0].shape)

    low = layer_input.reshape(tokens, width)
    gathered = lax.all_gather(low, CTX, axis=0, tiled=True)
    packed = jnp.concatenate(
        [norm_gains, norm_shifts, attn_bias, out_bias[None], proj_bias[None]], axis=0
    )
    vectors = in_order(around(packed)).transpose(1, 0, 2).reshape(8, width).astype(F32)
    gains, shifts, bias_pair = vectors[0:2], vectors[2:4], vectors[4:6]
    out_bias_row, proj_bias_row = vectors[6], vectors[7]

    head = jnp.minimum(ctx, HEADS - 1)
    head_cols = jnp.concatenate(
        [
            lax.dynamic_slice(qkv_weight, (0, part * width + head * HD), (own, HD))
            for part in range(3)
        ],
        axis=1,
    )
    head_weight = in_order(around(head_cols)).reshape(width, 3 * HD).T
    head_bias = lax.dynamic_slice(bias_pair, (0, head * HD), (2, HD))
    head_bias = jnp.concatenate([head_bias[:1], jnp.zeros((1, HD), F32), head_bias[1:]], axis=1)

    grad_low = output_grad.reshape(tokens, width)
    out_half = lax.dynamic_slice(
        after(out_weight, head_weight), (core * overlap, 0), (size, width)
    )
    out_pieces = with_halves(out_weight, [out_half] * (n_w - 1))
    out_all = join_rows(at_x, out_pieces, n_w, overlap)
    fc_own, *fc_halves = cut_columns(at_x, fc_weight, n_w, size, overlap)
    fc_halves = [after(half, *out_pieces[1::2]) for half in fc_halves]
    gathered = after(gathered, out_all)

    input_one, ordered, mixed_turned, mixed, logs = attend(
        block_order, gathered, gains[:1], shifts[:1], head_weight, head_bias, rows
    )
    grad_group = jnp.concatenate(around(after(grad_low, mixed_turned)), axis=0)
    grad_active = mm(grad_group, proj_weight, NT)
    fc_pieces = with_halves(fc_own, fc_halves, mixed_turned)
    mixed_turned = after(mixed_turned, *fc_pieces[1::2])
    attended = lax.all_to_all(mixed_turned, CTX, 0, 0).reshape(n_ctx * HD, tokens)[:width]
    attended = after(attended, grad_group, *fc_pieces)
    fc_cols = join_rows(at_x, [after(fc_pieces[0], attended), *fc_pieces[1:]], n_w, overlap)
    residual = low.astype(F32)
    middle = residual + mm(attended, out_all, TN) + out_bias_row
    normed_two, scaled_two, inverse_two = layer_norm(middle, gains[1], shifts[1])
    normed_two = normed_two.astype(BF)
    weight_all = lax.all_gather(head_weight, CTX, axis=0, tiled=True)
    input_two = around(normed_two)
    *input_two, grad_active = lax.optimization_barrier((*input_two, grad_active))
    input_two = jnp.concatenate(input_two, axis=0)

    attended_rows = jnp.concatenate(
        deal(
            lambda k: lax.dynamic_slice(
                after(attended, input_two), ((wsh + n_w - k) % n_w * own, 0), (own, tokens)
            )
        ),
        axis=1,
    )

    pre_gelu = mm(input_two, fc_cols) + fc_bias.astype(F32)
    activated, derivative = gelu_pair(pre_gelu)
    activated = activated.astype(BF)
    grad_pre = (grad_active * derivative).astype(BF)
    grad_two = mm(grad_pre, fc_cols, NT).reshape(n_w, tokens, width)
    parts = [grad_two[k].astype(BF) for k in range(1, n_w)]
    activated, grad_pre, *parts = lax.optimization_barrier(
        (activated, grad_pre, *parts, attended_rows)
    )[:-1]
    came = [x_shift(part, n_w - k) for k, part in enumerate(parts, 1)]
    pair = lambda array: (array, partner(array))
    grad_fc = half_grad(at_x, pair(input_two), pair(grad_pre), n_w, overlap, size)
    grad_fc = grad_fc.reshape(n_w, size, ff)
    grad_proj = half_grad(at_x, pair(activated), pair(grad_group), 1, ff // 2, ff // 2)
    *came, grad_fc = lax.optimization_barrier((*came, grad_fc, grad_proj, weight_all))[:n_w]
    grad_two = grad_two[0] + sum(piece.astype(F32) for piece in came)
    fc_parts = deal(
        lambda k: lax.dynamic_slice(grad_fc, ((wsh + n_w - k) % n_w, 0, 0), (1, size, ff))[0]
    )
    grad_fc_bias = jnp.sum(grad_pre.astype(F32), axis=0, keepdims=True)

    grad_norm_two, gain_two, shift_two = norm_back(grad_two, scaled_two, inverse_two, gains[1])
    grad_middle = grad_low.astype(F32) + grad_norm_two
    grad_branch = grad_middle.astype(BF)
    grad_attended = mm(out_all, grad_branch, NT).astype(BF)
    grad_heads = jnp.pad(grad_attended, ((0, (n_ctx - HEADS) * HD), (0, 0)))
    grad_heads = lax.all_to_all(grad_heads.reshape(n_ctx, HD, tokens), CTX, 0, 0)
    branch_group = jnp.concatenate(around(after(grad_branch, grad_attended)), axis=0)
    fc_parts[0] = after(fc_parts[0], grad_heads)
    share_fc, share_proj = lax.psum((jnp.concatenate(fc_parts, axis=0), grad_proj), ("z", "y"))
    branch = mm(after(activated, grad_attended), proj_weight).reshape(n_w, tokens, width)
    branch_own, branch_parts = branch[0], [branch[k].astype(BF) for k in range(1, n_w)]
    branch_group = after(branch_group, *branch_parts)
    branch_came = [
        x_shift(after(part, branch_group), n_w - k) for k, part in enumerate(branch_parts, 1)
    ]
    branch = branch_own + sum(piece.astype(F32) for piece in branch_came)
    layer_output = (middle + branch + proj_bias_row).astype(BF)

    chunks = out_grad(attended_rows, branch_group, grad_fc_bias, n_ctx, n_w)
    grad_heads = after(grad_heads, chunks)
    chunks = lax.all_to_all(chunks, CTX, 0, 0)

    grad_qkv, grad_bias = attend_back(block_order, ordered, mixed, logs, grad_heads, rows)
    grad_tokens = lax.all_to_all(grad_qkv, CTX, 0, 0).reshape(n_ctx * 3 * HD, tokens)

    dealt = head_grad(at_x, grad_qkv, grad_bias, after(input_one, chunks), n_w)
    pieces = deal(lambda k: dealt[k])
    left, right = pack(chunks, pieces)
    left = jnp.stack([left] + [shift(left, "y", k) for k in range(1, 4)])
    right = jnp.stack([right] + [shift(right, "z", k) for k in range(1, 4)])
    side = jnp.stack(
        [
            gain_two,
            shift_two,
            jnp.sum(grad_low.astype(F32), axis=0),
            jnp.sum(grad_branch.astype(F32), axis=0),
        ]
    )
    side = jnp.pad(side, ((0, 4), (0, 0)))
    input_grad, blocks = finish(
        grad_tokens, weight_all, low, gains[:1], shifts[:1], grad_middle, side, n_w
    )
    pieces = deal(
        lambda k: lax.dynamic_slice(blocks, ((wsh + n_w - k) % n_w, 0, 0), (1, 8, own))
    )
    vector_sum = (pieces[0] + pieces[1]) + (pieces[2] + pieces[3])
    everyone = lax.all_to_all(jnp.broadcast_to(vector_sum, (n_ctx, 8, own)), CTX, 0, 0)
    vector_out = jnp.sum(everyone, axis=0)

    left, right = lax.optimization_barrier((left, right, blocks))[:2]
    left = jnp.concatenate([left] + [shift(left, "z", k) for k in range(1, 4)])
    right = jnp.concatenate([right] + [shift(right, "y", k) for k in range(1, 4)])
    share_fc, share_proj, left, right = lax.optimization_barrier(
        (share_fc, share_proj, left, right, vector_out)
    )[:4]
    qkv_out, out_out, bias_out, side_out = unpack(
        jnp.stack([z, y, core]), left, partner(left), right, partner(right)
    )
    bias_out = lax.dynamic_slice(bias_out, (0, wsh * own), (2, own))

    fc_out, proj_out = join_halves(
        at_x, share_fc, partner(share_fc), share_proj, partner(share_proj), n_w, own, overlap
    )
    return (
        layer_output.reshape(seqs, rows, width),
        input_grad.reshape(seqs, rows, width),
        vector_out[0:2],
        vector_out[2:4],
        qkv_out,
        bias_out,
        out_out,
        vector_out[5],
        fc_out,
        side_out[0],
        proj_out,
        vector_out[4],
    )


def solution(mesh):
    y, core = 4, 2
    split = Mesh(
        mesh.devices.reshape(mesh.shape["ctx"] // (y * core), y, core, mesh.shape["wsh"]),
        (*CTX, "wsh"),
    )
    return jax.shard_map(
        on_device,
        mesh=split,
        in_specs=(
            P("wsh", CTX, None),
            P("wsh", None),
            P(None, "wsh"),
            P(None, "wsh"),
            P("wsh", None),
            P(None, "wsh"),
            P("wsh", None),
            P("wsh"),
            P("wsh", None),
            P("wsh"),
            P("wsh", None),
            P("wsh"),
            P("wsh", CTX, None),
        ),
        out_specs=(
            P("wsh", CTX, None),
            P("wsh", CTX, None),
            P(None, "wsh"),
            P(None, "wsh"),
            P("wsh", None),
            P(None, "wsh"),
            P("wsh", None),
            P("wsh"),
            P("wsh", None),
            P("wsh"),
            P("wsh", None),
            P("wsh"),
        ),
        check_vma=False,
    )
```

```python
import functools

import jax
import jax.numpy as jnp
from jax import lax
from jax.experimental import pallas as pl
from jax.experimental.pallas import tpu as pltpu
from jax.sharding import Mesh
from jax.sharding import PartitionSpec as P

HEADS = 25
HD = 64
QB = 256
FB = 512
BF = jnp.bfloat16
F32 = jnp.float32
NN = (((1,), (0,)), ((), ()))
NT = (((1,), (1,)), ((), ()))
TN = (((0,), (0,)), ((), ()))
CTX = ("z", "y", "core")


def mm(left, right, dims=NN):
    return lax.dot_general(left, right, dims, preferred_element_type=F32)


def layer_norm(hidden, gain_row, shift_row):
    centered = hidden - jnp.mean(hidden, axis=-1, keepdims=True)
    inverse = lax.rsqrt(jnp.mean(centered * centered, axis=-1, keepdims=True) + 1e-05)
    scaled = centered * inverse
    return scaled * gain_row + shift_row, scaled, inverse


def norm_back(gradient, scaled, inverse, gain_row):
    weighted = gradient * gain_row
    first_mean = jnp.mean(weighted, axis=-1, keepdims=True)
    second_mean = jnp.mean(weighted * scaled, axis=-1, keepdims=True)
    result = inverse * (weighted - first_mean - scaled * second_mean)
    return result, jnp.sum(gradient * scaled, axis=0), jnp.sum(gradient, axis=0)


def gelu_pair(pre_gelu):
    squared = pre_gelu * pre_gelu
    tangent = jnp.tanh(0.7978845608028654 * (pre_gelu + 0.044715 * squared * pre_gelu))
    result = 0.5 * pre_gelu * (1.0 + tangent)
    derivative = 0.5 * (1.0 + tangent) + 0.5 * pre_gelu * (
        1.0 - tangent * tangent
    ) * 0.7978845608028654 * (1.0 + 3.0 * 0.044715 * squared)
    return result, derivative


def ordered_rows(order_ref, seq, block, half, length):
    return pl.multiple_of(seq * length + order_ref[seq, block] * half, half)


def below_mask(size):
    return lax.broadcasted_iota(jnp.int32, (size, size), 0) <= lax.broadcasted_iota(
        jnp.int32, (size, size), 1
    )


def attend_kernel(
    seqs, rows, half, order_ref, in_ref, gain_ref, shift_ref, weight_ref, bias_ref,
    normed_ref, sorted_ref, out_ref, mixed_ref, log_ref, rows_ref,
):
    step = pl.program_id(0)
    tokens = seqs * rows
    group = in_ref.shape[0] // tokens
    length = mixed_ref.shape[2]
    per = rows // half
    normed = layer_norm(in_ref[...].astype(F32), gain_ref[...], shift_ref[...])[0].astype(BF)
    normed_ref[...] = normed
    made = (mm(normed, weight_ref[...], NT) + bias_ref[...]).astype(BF)
    for g in range(group):
        for s in range(seqs):
            for b in range(per):
                at = ordered_rows(order_ref, s, (step * group + g) * per + b, half, length)
                first = g * tokens + s * rows + b * half
                sorted_ref[pl.ds(at, half), :] = made[first : first + half]

    @pl.when(step == pl.num_programs(0) - 1)
    def _():
        below = below_mask(FB)

        def one_seq(s, carry):
            base = pl.multiple_of(s * length, length)
            k_all = sorted_ref[pl.ds(base, length), HD : 2 * HD]
            v_turned = sorted_ref[pl.ds(base, length), 2 * HD :].T
            for i in range(length // FB):
                lo, hi = i * FB, (i + 1) * FB
                q_rows = sorted_ref[pl.ds(base + lo, FB), :HD] * 0.125
                scores = mm(k_all[:hi], q_rows, NT)
                last = jnp.where(below, scores[lo:], -1e30)
                best = jnp.max(last, axis=0, keepdims=True)
                if i:
                    best = jnp.maximum(best, jnp.max(scores[:lo], axis=0, keepdims=True))
                tail = jnp.exp(last - best)
                total = jnp.sum(tail, axis=0, keepdims=True)
                mixed = mm(v_turned[:, lo:hi], tail.astype(BF))
                if i:
                    head = jnp.exp(scores[:lo] - best)
                    total = total + jnp.sum(head, axis=0, keepdims=True)
                    mixed = mixed + mm(v_turned[:, :lo], head.astype(BF))
                mixed = mixed / total
                mixed_ref[s, :, lo:hi] = mixed
                log_ref[s, :, lo:hi] = best + jnp.log(total)
                rows_ref[pl.ds(base + lo, FB), :] = mixed.T
            return carry

        lax.fori_loop(0, seqs, one_seq, 0)

        def one_block(c, carry):
            parts = [
                rows_ref[pl.ds(ordered_rows(order_ref, s, c * per + b, half, length), half), :]
                for s in range(seqs)
                for b in range(per)
            ]
            out_ref[c] = jnp.concatenate(parts, axis=0).T.astype(BF)
            return carry

        lax.fori_loop(0, out_ref.shape[0], one_block, 0)


def attend(order, gathered, gain, shift, weight, bias, rows):
    seqs, halves = order.shape
    tokens, width = seqs * rows, gathered.shape[1]
    n_ctx = gathered.shape[0] // tokens
    length = rows * n_ctx
    half = length // halves
    group = 8
    whole = lambda *shape: pl.BlockSpec(shape, lambda i: (0,) * len(shape))
    return pl.pallas_call(
        functools.partial(attend_kernel, seqs, rows, half),
        grid=(n_ctx // group,),
        in_specs=[
            pl.BlockSpec(memory_space=pltpu.SMEM),
            pl.BlockSpec((group * tokens, width), lambda i: (i, 0)),
            whole(1, width),
            whole(1, width),
            whole(3 * HD, width),
            whole(1, 3 * HD),
        ],
        out_specs=[
            pl.BlockSpec((group * tokens, width), lambda i: (i, 0)),
            whole(seqs * length, 3 * HD),
            whole(n_ctx, HD, tokens),
            whole(seqs, HD, length),
            whole(seqs, 1, length),
        ],
        out_shape=[
            jax.ShapeDtypeStruct(gathered.shape, BF),
            jax.ShapeDtypeStruct((seqs * length, 3 * HD), BF),
            jax.ShapeDtypeStruct((n_ctx, HD, tokens), BF),
            jax.ShapeDtypeStruct((seqs, HD, length), F32),
            jax.ShapeDtypeStruct((seqs, 1, length), F32),
        ],
        scratch_shapes=[pltpu.VMEM((seqs * length, HD), F32)],
        compiler_params=pltpu.CompilerParams(vmem_limit_bytes=48 << 20),
        cost_estimate=pl.CostEstimate(
            flops=20_000_000_000, bytes_accessed=20_000_000, transcendentals=0
        ),
        name="attend",
    )(order, gathered, gain, shift, weight, bias)


def attend_back_kernel(
    seqs, rows, half, order_ref, sorted_ref, mixed_ref, log_ref, grad_ref, out_ref, bias_ref,
    rows_ref, key_ref, value_ref, all_ref,
):
    n_ctx, _, tokens = grad_ref.shape
    length = mixed_ref.shape[2]
    per = rows // half

    def spread(c, carry):
        block = grad_ref[c].T
        for s in range(seqs):
            for b in range(per):
                at = ordered_rows(order_ref, s, c * per + b, half, length)
                first = s * rows + b * half
                rows_ref[pl.ds(at, half), :] = block[first : first + half]
        return carry

    lax.fori_loop(0, n_ctx, spread, 0)
    below = below_mask(QB)

    def one_seq(s, carry):
        base = pl.multiple_of(s * length, length)
        k_all = sorted_ref[pl.ds(base, length), HD : 2 * HD]
        v_all = sorted_ref[pl.ds(base, length), 2 * HD :]
        k_turned = k_all.T
        g_turned = rows_ref[pl.ds(base, length), :].T
        delta = jnp.sum(g_turned.astype(F32) * mixed_ref[s], axis=0, keepdims=True)
        key_ref[...] = jnp.zeros_like(key_ref)
        value_ref[...] = jnp.zeros_like(value_ref)
        for i in range(length // QB):
            lo, hi = i * QB, (i + 1) * QB
            q_rows = sorted_ref[pl.ds(base + lo, QB), :HD] * 0.125
            g_rows = rows_ref[pl.ds(base + lo, QB), :]
            log_row = log_ref[s, :, lo:hi]
            delta_row = delta[:, lo:hi]
            query = jnp.zeros((HD, QB), F32)
            for first, end in ((0, lo), (lo, hi)):
                if first == end:
                    continue
                scores = mm(k_all[first:end], q_rows, NT)
                probs = jnp.exp(scores - log_row)
                if end == hi:
                    probs = jnp.where(below, probs, 0.0)
                slopes = mm(v_all[first:end], g_rows, NT)
                pulled = (probs * (slopes - delta_row)).astype(BF)
                value_ref[first:end, :] += mm(probs.astype(BF), g_rows)
                key_ref[first:end, :] += mm(pulled, q_rows)
                query = query + mm(k_turned[:, first:end], pulled)
            all_ref[pl.ds(base + lo, QB), :HD] = (query * 0.125).T
        all_ref[pl.ds(base, length), HD : 2 * HD] = key_ref[...]
        all_ref[pl.ds(base, length), 2 * HD :] = value_ref[...]
        return carry

    lax.fori_loop(0, seqs, one_seq, 0)

    def one_block(c, carry):
        parts = [
            all_ref[pl.ds(ordered_rows(order_ref, s, c * per + b, half, length), half), :]
            for s in range(seqs)
            for b in range(per)
        ]
        block = jnp.concatenate(parts, axis=0).astype(BF)
        out_ref[c] = block.T
        return carry + jnp.sum(block.astype(F32), axis=0, keepdims=True)

    bias_ref[...] = lax.fori_loop(0, n_ctx, one_block, jnp.zeros((1, 3 * HD), F32))


def attend_back(order, ordered, mixed, logs, grads, rows):
    n_ctx, _, tokens = grads.shape
    seqs, halves = order.shape
    length = rows * n_ctx
    half = length // halves
    vmem = pl.BlockSpec(memory_space=pltpu.VMEM)
    return pl.pallas_call(
        functools.partial(attend_back_kernel, seqs, rows, half),
        in_specs=[pl.BlockSpec(memory_space=pltpu.SMEM)] + [vmem] * 4,
        out_specs=[vmem] * 2,
        out_shape=[
            jax.ShapeDtypeStruct((n_ctx, 3 * HD, tokens), BF),
            jax.ShapeDtypeStruct((1, 3 * HD), F32),
        ],
        scratch_shapes=[
            pltpu.VMEM((seqs * length, HD), BF),
            pltpu.VMEM((length, HD), F32),
            pltpu.VMEM((length, HD), F32),
            pltpu.VMEM((seqs * length, 3 * HD), F32),
        ],
        compiler_params=pltpu.CompilerParams(vmem_limit_bytes=48 << 20),
        cost_estimate=pl.CostEstimate(flops=23060000000, bytes_accessed=1, transcendentals=0),
        name="attend_back",
    )(order, ordered, mixed, logs, grads)


def head_grad_kernel(n_w, at_ref, grad_ref, bias_ref, in_ref, *refs):
    *out_refs, total_ref, turned_ref = refs
    step = pl.program_id(0)

    @pl.when(step == 0)
    def _():
        total_ref[...] = jnp.zeros_like(total_ref)

    turned = jnp.concatenate([grad_ref[g] for g in range(grad_ref.shape[0])], axis=1)
    total_ref[...] += mm(turned, in_ref[...])

    @pl.when(step == pl.num_programs(0) - 1)
    def _():
        turned_ref[...] = total_ref[...].T
        own = turned_ref.shape[0] // n_w
        for k, out_ref in enumerate(out_refs):
            at = pl.multiple_of((at_ref[0] + n_w - k) % n_w * own, 16)
            out_ref[:own] = turned_ref[pl.ds(at, own), :].astype(out_ref.dtype)
            out_ref[own:] = jnp.broadcast_to(
                bias_ref[...], (out_ref.shape[0] - own, out_ref.shape[1])
            ).astype(out_ref.dtype)


def head_grad(at, grads, bias, gathered, n_w):
    n_ctx, _, tokens = grads.shape
    width = gathered.shape[1]
    group = 4
    rows = width // n_w + 16
    return pl.pallas_call(
        functools.partial(head_grad_kernel, n_w),
        grid=(n_ctx // group,),
        in_specs=[
            pl.BlockSpec(memory_space=pltpu.SMEM),
            pl.BlockSpec((group, 3 * HD, tokens), lambda i: (i, 0, 0)),
            pl.BlockSpec((1, 3 * HD), lambda i: (0, 0)),
            pl.BlockSpec((group * tokens, width), lambda i: (i, 0)),
        ],
        out_specs=[pl.BlockSpec((rows, 3 * HD), lambda i: (0, 0))] * n_w,
        out_shape=[
            jax.ShapeDtypeStruct((rows, 3 * HD), BF if k else F32) for k in range(n_w)
        ],
        scratch_shapes=[pltpu.VMEM((3 * HD, width), F32), pltpu.VMEM((width, 3 * HD), F32)],
        compiler_params=pltpu.CompilerParams(vmem_limit_bytes=32 << 20),
        cost_estimate=pl.CostEstimate(flops=1, bytes_accessed=1, transcendentals=0),
        name="head_grad",
    )(at, grads, bias, gathered)


def finish_kernel(n_w, turned_ref, weight_ref, in_ref, gain_ref, shift_ref, middle_ref, side_ref, out_ref, block_ref, total_ref):
    step = pl.program_id(0)

    @pl.when(step == 0)
    def _():
        total_ref[...] = jnp.zeros_like(total_ref)

    total_ref[...] += mm(turned_ref[...].T, weight_ref[...])

    @pl.when(step == pl.num_programs(0) - 1)
    def _():
        grad = total_ref[...]
        _, scaled, inverse = layer_norm(in_ref[...].astype(F32), gain_ref[...], shift_ref[...])
        result, gain_grad, shift_grad = norm_back(grad, scaled, inverse, gain_ref[...])
        out_ref[...] = middle_ref[...] + result
        own = block_ref.shape[2]
        rows = (gain_grad.reshape(1, -1), side_ref[0:1], shift_grad.reshape(1, -1), side_ref[1:2])
        for w in range(n_w):
            at = slice(w * own, (w + 1) * own)
            for r, row in enumerate(rows):
                block_ref[w, r : r + 1] = row[:, at]
            block_ref[w, len(rows) :] = side_ref[2 : 2 + block_ref.shape[1] - len(rows), at]


def finish(turned, weight, low, gain, shift, middle, side, n_w):
    tokens, width = low.shape
    depth = HEADS * 3 * HD // 5
    whole = lambda *shape: pl.BlockSpec(shape, lambda i: (0,) * len(shape))
    return pl.pallas_call(
        functools.partial(finish_kernel, n_w),
        grid=(5,),
        in_specs=[
            pl.BlockSpec((depth, tokens), lambda i: (i, 0)),
            pl.BlockSpec((depth, width), lambda i: (i, 0)),
            whole(tokens, width),
            whole(1, width),
            whole(1, width),
            whole(tokens, width),
            whole(*side.shape),
        ],
        out_specs=[whole(tokens, width), whole(n_w, 8, width // n_w)],
        out_shape=[
            jax.ShapeDtypeStruct((tokens, width), F32),
            jax.ShapeDtypeStruct((n_w, 8, width // n_w), F32),
        ],
        scratch_shapes=[pltpu.VMEM((tokens, width), F32)],
        compiler_params=pltpu.CompilerParams(vmem_limit_bytes=32 << 20),
        cost_estimate=pl.CostEstimate(flops=1, bytes_accessed=1, transcendentals=0),
        name="finish",
    )(turned, weight, low, gain, shift, middle, side)


def join_rows_kernel(n_w, overlap, at_ref, *refs):
    *pieces, out_ref = refs
    wsh, core = at_ref[0], at_ref[1]
    own = pieces[0].shape[0]
    out_ref[pl.ds(pl.multiple_of(wsh * own, 16), own), :] = pieces[0][...]
    for k in range(1, n_w):
        base = (wsh + k) % n_w * own
        mine, other = pieces[2 * k - 1], pieces[2 * k]
        size = mine.shape[0]
        out_ref[pl.ds(pl.multiple_of(base + core * overlap, 16), size), :] = mine[...]
        out_ref[pl.ds(pl.multiple_of(base + (1 - core) * overlap, 16), size), :] = other[...]


def join_rows(at, pieces, n_w, overlap):
    own, width = pieces[0].shape
    vmem = pl.BlockSpec(memory_space=pltpu.VMEM)
    return pl.pallas_call(
        functools.partial(join_rows_kernel, n_w, overlap),
        in_specs=[pl.BlockSpec(memory_space=pltpu.SMEM)] + [vmem] * len(pieces),
        out_specs=vmem,
        out_shape=jax.ShapeDtypeStruct((n_w * own, width), BF),
        compiler_params=pltpu.CompilerParams(vmem_limit_bytes=32 << 20),
        cost_estimate=pl.CostEstimate(flops=1, bytes_accessed=1, transcendentals=0),
        name="join_rows",
    )(at, *pieces)


def cut_columns_kernel(n_w, overlap, at_ref, in_ref, *out_refs):
    wsh, core = at_ref[0], at_ref[1]
    cols = out_refs[0].shape[1]
    for k, out_ref in enumerate(out_refs):
        size = out_ref.shape[0]
        start = 0 if k == 0 else pl.multiple_of(core * overlap, 16)
        for b in range(n_w):

            @pl.when((wsh + n_w - k) % n_w == b)
            def _(out_ref=out_ref, start=start, size=size, b=b):
                out_ref[...] = in_ref[pl.ds(start, size), b * cols : (b + 1) * cols]


def cut_columns(at, array, n_w, size, overlap):
    own, cols = array.shape[0], array.shape[1] // n_w
    vmem = pl.BlockSpec(memory_space=pltpu.VMEM)
    return pl.pallas_call(
        functools.partial(cut_columns_kernel, n_w, overlap),
        in_specs=[pl.BlockSpec(memory_space=pltpu.SMEM), vmem],
        out_specs=[vmem] * n_w,
        out_shape=[
            jax.ShapeDtypeStruct((own if k == 0 else size, cols), BF) for k in range(n_w)
        ],
        compiler_params=pltpu.CompilerParams(vmem_limit_bytes=32 << 20),
        cost_estimate=pl.CostEstimate(flops=1, bytes_accessed=1, transcendentals=0),
        name="cut_columns",
    )(at, array)


def join_columns_kernel(n_w, overlap, at_ref, *refs):
    *pieces, out_ref = refs
    wsh, core = at_ref[0], at_ref[1]
    cols = pieces[0].shape[1]
    for k in range(n_w):
        for b in range(n_w):

            @pl.when((wsh + k) % n_w == b)
            def _(k=k, b=b):
                at = slice(b * cols, (b + 1) * cols)
                if k == 0:
                    out_ref[:, at] = pieces[0][...].astype(F32)
                    return
                mine, other = pieces[2 * k - 1], pieces[2 * k]
                size = mine.shape[0]
                out_ref[pl.ds(pl.multiple_of(core * overlap, 16), size), at] = mine[...].astype(F32)
                out_ref[pl.ds(pl.multiple_of((1 - core) * overlap, 16), size), at] = other[
                    ...
                ].astype(F32)


def join_columns(at, pieces, n_w, overlap):
    own, cols = pieces[0].shape
    vmem = pl.BlockSpec(memory_space=pltpu.VMEM)
    return pl.pallas_call(
        functools.partial(join_columns_kernel, n_w, overlap),
        in_specs=[pl.BlockSpec(memory_space=pltpu.SMEM)] + [vmem] * len(pieces),
        out_specs=vmem,
        out_shape=jax.ShapeDtypeStruct((own, n_w * cols), F32),
        compiler_params=pltpu.CompilerParams(vmem_limit_bytes=40 << 20),
        cost_estimate=pl.CostEstimate(flops=1, bytes_accessed=1, transcendentals=0),
        name="join_columns",
    )(at, *pieces)


def out_grad_kernel(n_w, in_ref, grad_ref, side_ref, out_ref):
    made = mm(in_ref[...], grad_ref[...])
    chunks = made.shape[0] // 16
    out_ref[...] = jnp.zeros_like(out_ref)
    for c in range(chunks):
        out_ref[c] = made[c * 16 : (c + 1) * 16].astype(BF)
    out_ref[chunks, :1] = side_ref[...].astype(BF)


def out_grad(rows, grads, side, n_ctx, n_w):
    vmem = pl.BlockSpec(memory_space=pltpu.VMEM)
    return pl.pallas_call(
        functools.partial(out_grad_kernel, n_w),
        in_specs=[vmem] * 3,
        out_specs=vmem,
        out_shape=jax.ShapeDtypeStruct((n_ctx, 16, grads.shape[1]), BF),
        compiler_params=pltpu.CompilerParams(vmem_limit_bytes=24 << 20),
        cost_estimate=pl.CostEstimate(flops=34590000001, bytes_accessed=1, transcendentals=0),
        name="out_grad",
    )(rows, grads, side)


def pack_kernel(chunk_ref, *refs):
    *pieces, left_ref, right_ref = refs
    total = pieces[0][...]
    for piece in pieces[1:]:
        total = total + piece[...].astype(F32)
    left_ref[...] = total[:, : 2 * HD].astype(BF)
    chunk = chunk_ref[0].astype(F32)
    for c in range(1, chunk_ref.shape[0]):
        chunk = chunk + chunk_ref[c].astype(F32)
    turned = jnp.concatenate(
        [chunk[:, q * HD : (q + 1) * HD] for q in range(chunk.shape[1] // HD)], axis=0
    )
    turned = jnp.concatenate(
        [turned, jnp.zeros((total.shape[0] - turned.shape[0], HD), F32)], axis=0
    )
    right_ref[...] = jnp.concatenate([total[:, 2 * HD :], turned], axis=1).astype(BF)


def pack(chunks, pieces):
    rows = pieces[0].shape[0]
    vmem = pl.BlockSpec(memory_space=pltpu.VMEM)
    return pl.pallas_call(
        pack_kernel,
        in_specs=[vmem] * (1 + len(pieces)),
        out_specs=[vmem] * 2,
        out_shape=[jax.ShapeDtypeStruct((rows, 2 * HD), BF)] * 2,
        compiler_params=pltpu.CompilerParams(vmem_limit_bytes=24 << 20),
        cost_estimate=pl.CostEstimate(flops=1, bytes_accessed=1, transcendentals=0),
        name="pack",
    )(chunks, *pieces)


def unpack_kernel(
    at_ref, left_own, left_other, right_own, right_other, qkv_ref, out_ref, bias_ref, side_ref
):
    z, y, core = at_ref[0], at_ref[1], at_ref[2]
    own = qkv_ref.shape[0]
    bias_ref[...] = jnp.zeros_like(bias_ref)
    for h in range(HEADS + 1):
        by_z, by_y = (h // 8 + 4 - z) % 4, ((h // 2) % 4 + 4 - y) % 4
        same = core == h % 2
        right_at = by_y * 4 + by_z
        right = jnp.where(same, right_own[right_at], right_other[right_at]).astype(F32)
        if h == HEADS:
            for q in range(HEADS):
                side_ref[:, q * HD : (q + 1) * HD] = right[q * 16 : q * 16 + 8, HD:]
            break
        left_at = by_z * 4 + by_y
        left = jnp.where(same, left_own[left_at], left_other[left_at]).astype(F32)
        for part, piece in enumerate((left[:, :HD], left[:, HD:], right[:, :HD])):
            at = (part * HEADS + h) * HD
            qkv_ref[:, at : at + HD] = piece[:own]
        bias_ref[0:1, h * HD : (h + 1) * HD] = left[own : own + 1, :HD]
        bias_ref[1:2, h * HD : (h + 1) * HD] = right[own : own + 1, :HD]
        for q in range(HEADS):
            out_ref[h * 16 : (h + 1) * 16, q * HD : (q + 1) * HD] = right[
                q * 16 : (q + 1) * 16, HD:
            ]


def unpack(at, left_own, left_other, right_own, right_other):
    rows = left_own.shape[1] - 16
    vmem = pl.BlockSpec(memory_space=pltpu.VMEM)
    return pl.pallas_call(
        unpack_kernel,
        in_specs=[pl.BlockSpec(memory_space=pltpu.SMEM)] + [vmem] * 4,
        out_specs=[vmem] * 4,
        out_shape=[
            jax.ShapeDtypeStruct((rows, 3 * HEADS * HD), F32),
            jax.ShapeDtypeStruct((rows, HEADS * HD), F32),
            jax.ShapeDtypeStruct((8, HEADS * HD), F32),
            jax.ShapeDtypeStruct((8, HEADS * HD), F32),
        ],
        compiler_params=pltpu.CompilerParams(vmem_limit_bytes=40 << 20),
        cost_estimate=pl.CostEstimate(flops=1, bytes_accessed=1, transcendentals=0),
        name="unpack",
    )(at, left_own, left_other, right_own, right_other)


def after(array, *others):
    return lax.optimization_barrier((array, *others))[0]


def on_device(
    layer_input,
    block_order,
    norm_gains,
    norm_shifts,
    qkv_weight,
    attn_bias,
    out_weight,
    out_bias,
    fc_weight,
    fc_bias,
    proj_weight,
    proj_bias,
    output_grad,
):
    seqs, rows, width = layer_input.shape
    tokens = seqs * rows
    n_ctx, n_w = lax.axis_size(CTX), lax.axis_size("wsh")
    ctx, wsh = lax.axis_index(CTX), lax.axis_index("wsh")
    z, y, core = (lax.axis_index(axis) for axis in CTX)
    own = width // n_w
    ff = fc_weight.shape[1] // n_w
    size, overlap = 208, 192
    at_x = jnp.stack([wsh, core])

    def shift(array, axis, k):
        size = lax.axis_size(axis)
        return lax.ppermute(array, axis, [((i + k) % size, i) for i in range(size)])

    def x_shift(array, k):
        return shift(array, "wsh", k)

    def partner(array):
        return shift(array, "core", 1)

    def around(array):
        return [array] + [x_shift(array, k) for k in range(1, n_w)]

    def deal(choose):
        return [choose(0)] + [x_shift(choose(k), k) for k in range(1, n_w)]

    def with_halves(whole, halves, *before):
        pieces = [whole]
        for k in range(1, n_w):
            mine = x_shift(halves[k - 1], k)
            pieces += [mine, partner(after(mine, *before))]
        return pieces

    def in_order(pieces):
        twice = jnp.stack(pieces + pieces)
        start = (n_w - wsh) % n_w
        return lax.dynamic_slice(twice, (start,) + (0,) * pieces[0].ndim, (n_w,) + pieces[0].shape)

    low = layer_input.reshape(tokens, width)
    gathered = lax.all_gather(low, CTX, axis=0, tiled=True)
    packed = jnp.concatenate(
        [norm_gains, norm_shifts, attn_bias, out_bias[None], proj_bias[None]], axis=0
    )
    vectors = in_order(around(packed)).transpose(1, 0, 2).reshape(8, width).astype(F32)
    gains, shifts, bias_pair = vectors[0:2], vectors[2:4], vectors[4:6]
    out_bias_row, proj_bias_row = vectors[6], vectors[7]

    head = jnp.minimum(ctx, HEADS - 1)
    head_cols = jnp.concatenate(
        [
            lax.dynamic_slice(qkv_weight, (0, part * width + head * HD), (own, HD))
            for part in range(3)
        ],
        axis=1,
    )
    head_weight = in_order(around(head_cols)).reshape(width, 3 * HD).T
    head_bias = lax.dynamic_slice(bias_pair, (0, head * HD), (2, HD))
    head_bias = jnp.concatenate([head_bias[:1], jnp.zeros((1, HD), F32), head_bias[1:]], axis=1)

    grad_low = output_grad.reshape(tokens, width)
    out_half = lax.dynamic_slice(
        after(out_weight, head_weight), (core * overlap, 0), (size, width)
    )
    out_pieces = with_halves(out_weight, [out_half] * (n_w - 1))
    out_all = join_rows(at_x, out_pieces, n_w, overlap)
    fc_own, *fc_halves = cut_columns(at_x, fc_weight, n_w, size, overlap)
    fc_halves = [after(half, *out_pieces[1::2]) for half in fc_halves]
    gathered = after(gathered, out_all)

    input_one, ordered, mixed_turned, mixed, logs = attend(
        block_order, gathered, gains[:1], shifts[:1], head_weight, head_bias, rows
    )
    grad_group = jnp.concatenate(around(after(grad_low, mixed_turned)), axis=0)
    grad_active = mm(grad_group, proj_weight, NT)
    fc_pieces = with_halves(fc_own, fc_halves, mixed_turned)
    mixed_turned = after(mixed_turned, *fc_pieces[1::2])
    attended = lax.all_to_all(mixed_turned, CTX, 0, 0).reshape(n_ctx * HD, tokens)[:width]
    attended = after(attended, grad_group, *fc_pieces)
    fc_cols = join_rows(at_x, [after(fc_pieces[0], attended), *fc_pieces[1:]], n_w, overlap)
    residual = low.astype(F32)
    middle = residual + mm(attended, out_all, TN) + out_bias_row
    normed_two, scaled_two, inverse_two = layer_norm(middle, gains[1], shifts[1])
    normed_two = normed_two.astype(BF)
    weight_all = lax.all_gather(head_weight, CTX, axis=0, tiled=True)
    input_two = around(normed_two)
    *input_two, grad_active = lax.optimization_barrier((*input_two, grad_active))
    input_two = jnp.concatenate(input_two, axis=0)

    pre_gelu = mm(input_two, fc_cols) + fc_bias.astype(F32)
    activated, derivative = gelu_pair(pre_gelu)
    activated = activated.astype(BF)
    grad_pre = (grad_active * derivative).astype(BF)
    grad_two = mm(grad_pre, fc_cols, NT).reshape(n_w, tokens, width)
    parts = [grad_two[k].astype(BF) for k in range(1, n_w)]
    activated, grad_pre, *parts = lax.optimization_barrier((activated, grad_pre, *parts))
    came = [x_shift(part, n_w - k) for k, part in enumerate(parts, 1)]
    grad_proj = mm(activated, grad_group, TN).astype(BF)
    grad_fc = mm(input_two, grad_pre, TN).astype(BF)
    branch = mm(after(activated, came[0]), proj_weight).reshape(n_w, tokens, width)
    branch_own, branch_parts = branch[0], [branch[k].astype(BF) for k in range(1, n_w)]
    attended_rows = jnp.concatenate(
        deal(
            lambda k: lax.dynamic_slice(
                after(attended, came[0]), ((wsh + n_w - k) % n_w * own, 0), (own, tokens)
            )
        ),
        axis=1,
    )
    *came, branch_own = lax.optimization_barrier(
        (*came, branch_own, *branch_parts, grad_proj, grad_fc, weight_all, attended_rows)
    )[:n_w]
    grad_two = grad_two[0] + sum(piece.astype(F32) for piece in came)
    grad_fc_bias = jnp.sum(grad_pre.astype(F32), axis=0, keepdims=True)
    share_proj, share_fc = lax.psum((grad_proj, grad_fc), CTX)

    grad_norm_two, gain_two, shift_two = norm_back(grad_two, scaled_two, inverse_two, gains[1])
    grad_middle = grad_low.astype(F32) + grad_norm_two
    grad_branch = grad_middle.astype(BF)
    grad_attended = mm(out_all, grad_branch, NT).astype(BF)
    grad_heads = jnp.pad(grad_attended, ((0, (n_ctx - HEADS) * HD), (0, 0)))
    grad_heads = lax.all_to_all(grad_heads.reshape(n_ctx, HD, tokens), CTX, 0, 0)
    branch_group = jnp.concatenate(around(after(grad_branch, grad_attended)), axis=0)
    branch_came = [
        x_shift(after(part, branch_group), n_w - k) for k, part in enumerate(branch_parts, 1)
    ]
    branch = branch_own + sum(piece.astype(F32) for piece in branch_came)
    layer_output = (middle + branch + proj_bias_row).astype(BF)

    chunks = out_grad(attended_rows, branch_group, grad_fc_bias, n_ctx, n_w)
    grad_heads = after(grad_heads, chunks)
    chunks = lax.all_to_all(chunks, CTX, 0, 0)

    grad_qkv, grad_bias = attend_back(block_order, ordered, mixed, logs, grad_heads, rows)
    grad_tokens = lax.all_to_all(grad_qkv, CTX, 0, 0).reshape(n_ctx * 3 * HD, tokens)

    dealt = head_grad(at_x, grad_qkv, grad_bias, after(input_one, chunks), n_w)
    pieces = deal(lambda k: dealt[k])
    left, right = pack(chunks, pieces)
    left = jnp.stack([left] + [shift(left, "y", k) for k in range(1, 4)])
    right = jnp.stack([right] + [shift(right, "z", k) for k in range(1, 4)])
    side = jnp.stack(
        [
            gain_two,
            shift_two,
            jnp.sum(grad_low.astype(F32), axis=0),
            jnp.sum(grad_branch.astype(F32), axis=0),
        ]
    )
    side = jnp.pad(side, ((0, 4), (0, 0)))
    input_grad, blocks = finish(
        grad_tokens, weight_all, low, gains[:1], shifts[:1], after(grad_middle, *branch_came), side, n_w
    )
    pieces = deal(
        lambda k: lax.dynamic_slice(blocks, ((wsh + n_w - k) % n_w, 0, 0), (1, 8, own))
    )
    vector_sum = (pieces[0] + pieces[1]) + (pieces[2] + pieces[3])
    everyone = lax.all_to_all(jnp.broadcast_to(vector_sum, (n_ctx, 8, own)), CTX, 0, 0)
    vector_out = jnp.sum(everyone, axis=0)

    left, right = lax.optimization_barrier((left, right, blocks))[:2]
    left = jnp.concatenate([left] + [shift(left, "z", k) for k in range(1, 4)])
    right = jnp.concatenate([right] + [shift(right, "y", k) for k in range(1, 4)])
    qkv_out, out_out, bias_out, side_out = unpack(
        jnp.stack([z, y, core]), left, partner(left), right, partner(right)
    )
    bias_out = lax.dynamic_slice(bias_out, (0, wsh * own), (2, own))

    share_proj, share_fc = lax.optimization_barrier((share_proj, share_fc, qkv_out))[:2]
    proj_out = share_proj.astype(F32)
    rows_for = lambda k, start, count: lax.dynamic_slice(
        share_fc, ((wsh + n_w - k) % n_w * own + start, 0), (count, ff)
    )
    fc_out = join_columns(
        at_x,
        with_halves(
            rows_for(0, 0, own),
            [rows_for(k, core * overlap, size) for k in range(1, n_w)],
            qkv_out,
            proj_out,
        ),
        n_w,
        overlap,
    )
    return (
        layer_output.reshape(seqs, rows, width),
        input_grad.reshape(seqs, rows, width),
        vector_out[0:2],
        vector_out[2:4],
        qkv_out,
        bias_out,
        out_out,
        vector_out[5],
        fc_out,
        side_out[0],
        proj_out,
        vector_out[4],
    )


def solution(mesh):
    y, core = 4, 2
    split = Mesh(
        mesh.devices.reshape(mesh.shape["ctx"] // (y * core), y, core, mesh.shape["wsh"]),
        (*CTX, "wsh"),
    )
    return jax.shard_map(
        on_device,
        mesh=split,
        in_specs=(
            P("wsh", CTX, None),
            P("wsh", None),
            P(None, "wsh"),
            P(None, "wsh"),
            P("wsh", None),
            P(None, "wsh"),
            P("wsh", None),
            P("wsh"),
            P("wsh", None),
            P("wsh"),
            P("wsh", None),
            P("wsh"),
            P("wsh", CTX, None),
        ),
        out_specs=(
            P("wsh", CTX, None),
            P("wsh", CTX, None),
            P(None, "wsh"),
            P(None, "wsh"),
            P("wsh", None),
            P(None, "wsh"),
            P("wsh", None),
            P("wsh"),
            P("wsh", None),
            P("wsh"),
            P("wsh", None),
            P("wsh"),
        ),
        check_vma=False,
    )
```

```python
import functools

import jax
import jax.numpy as jnp
from jax import lax
from jax.experimental import pallas as pl
from jax.experimental.pallas import tpu as pltpu
from jax.sharding import Mesh
from jax.sharding import PartitionSpec as P

HEADS = 25
HD = 64
QB = 256
FB = 512
BF = jnp.bfloat16
F32 = jnp.float32
NN = (((1,), (0,)), ((), ()))
NT = (((1,), (1,)), ((), ()))
TN = (((0,), (0,)), ((), ()))
CTX = ("z", "y", "core")


def mm(left, right, dims=NN):
    return lax.dot_general(left, right, dims, preferred_element_type=F32)


def layer_norm(hidden, gain_row, shift_row):
    centered = hidden - jnp.mean(hidden, axis=-1, keepdims=True)
    inverse = lax.rsqrt(jnp.mean(centered * centered, axis=-1, keepdims=True) + 1e-05)
    scaled = centered * inverse
    return scaled * gain_row + shift_row, scaled, inverse


def norm_back(gradient, scaled, inverse, gain_row):
    weighted = gradient * gain_row
    first_mean = jnp.mean(weighted, axis=-1, keepdims=True)
    second_mean = jnp.mean(weighted * scaled, axis=-1, keepdims=True)
    result = inverse * (weighted - first_mean - scaled * second_mean)
    return result, jnp.sum(gradient * scaled, axis=0), jnp.sum(gradient, axis=0)


def gelu_pair(pre_gelu):
    squared = pre_gelu * pre_gelu
    tangent = jnp.tanh(0.7978845608028654 * (pre_gelu + 0.044715 * squared * pre_gelu))
    result = 0.5 * pre_gelu * (1.0 + tangent)
    derivative = 0.5 * (1.0 + tangent) + 0.5 * pre_gelu * (
        1.0 - tangent * tangent
    ) * 0.7978845608028654 * (1.0 + 3.0 * 0.044715 * squared)
    return result, derivative


def ordered_rows(order_ref, seq, block, half, length):
    return pl.multiple_of(seq * length + order_ref[seq, block] * half, half)


def below_mask(size):
    return lax.broadcasted_iota(jnp.int32, (size, size), 0) <= lax.broadcasted_iota(
        jnp.int32, (size, size), 1
    )


def attend_kernel(
    seqs, rows, half, order_ref, in_ref, gain_ref, shift_ref, weight_ref, bias_ref,
    normed_ref, sorted_ref, out_ref, mixed_ref, log_ref, rows_ref,
):
    step = pl.program_id(0)
    tokens = seqs * rows
    group = in_ref.shape[0] // tokens
    length = mixed_ref.shape[2]
    per = rows // half
    normed = layer_norm(in_ref[...].astype(F32), gain_ref[...], shift_ref[...])[0].astype(BF)
    normed_ref[...] = normed
    made = (mm(normed, weight_ref[...], NT) + bias_ref[...]).astype(BF)
    for g in range(group):
        for s in range(seqs):
            for b in range(per):
                at = ordered_rows(order_ref, s, (step * group + g) * per + b, half, length)
                first = g * tokens + s * rows + b * half
                sorted_ref[pl.ds(at, half), :] = made[first : first + half]

    @pl.when(step == pl.num_programs(0) - 1)
    def _():
        below = below_mask(FB)

        def one_seq(s, carry):
            base = pl.multiple_of(s * length, length)
            k_all = sorted_ref[pl.ds(base, length), HD : 2 * HD]
            v_turned = sorted_ref[pl.ds(base, length), 2 * HD :].T
            for i in range(length // FB):
                lo, hi = i * FB, (i + 1) * FB
                q_rows = sorted_ref[pl.ds(base + lo, FB), :HD] * 0.125
                scores = mm(k_all[:hi], q_rows, NT)
                last = jnp.where(below, scores[lo:], -1e30)
                best = jnp.max(last, axis=0, keepdims=True)
                if i:
                    best = jnp.maximum(best, jnp.max(scores[:lo], axis=0, keepdims=True))
                tail = jnp.exp(last - best)
                total = jnp.sum(tail, axis=0, keepdims=True)
                mixed = mm(v_turned[:, lo:hi], tail.astype(BF))
                if i:
                    head = jnp.exp(scores[:lo] - best)
                    total = total + jnp.sum(head, axis=0, keepdims=True)
                    mixed = mixed + mm(v_turned[:, :lo], head.astype(BF))
                mixed = mixed / total
                mixed_ref[s, :, lo:hi] = mixed
                log_ref[s, :, lo:hi] = best + jnp.log(total)
                rows_ref[pl.ds(base + lo, FB), :] = mixed.T
            return carry

        lax.fori_loop(0, seqs, one_seq, 0)

        def one_block(c, carry):
            parts = [
                rows_ref[pl.ds(ordered_rows(order_ref, s, c * per + b, half, length), half), :]
                for s in range(seqs)
                for b in range(per)
            ]
            out_ref[c] = jnp.concatenate(parts, axis=0).T.astype(BF)
            return carry

        lax.fori_loop(0, out_ref.shape[0], one_block, 0)


def attend(order, gathered, gain, shift, weight, bias, rows):
    seqs, halves = order.shape
    tokens, width = seqs * rows, gathered.shape[1]
    n_ctx = gathered.shape[0] // tokens
    length = rows * n_ctx
    half = length // halves
    group = 8
    whole = lambda *shape: pl.BlockSpec(shape, lambda i: (0,) * len(shape))
    return pl.pallas_call(
        functools.partial(attend_kernel, seqs, rows, half),
        grid=(n_ctx // group,),
        in_specs=[
            pl.BlockSpec(memory_space=pltpu.SMEM),
            pl.BlockSpec((group * tokens, width), lambda i: (i, 0)),
            whole(1, width),
            whole(1, width),
            whole(3 * HD, width),
            whole(1, 3 * HD),
        ],
        out_specs=[
            pl.BlockSpec((group * tokens, width), lambda i: (i, 0)),
            whole(seqs * length, 3 * HD),
            whole(n_ctx, HD, tokens),
            whole(seqs, HD, length),
            whole(seqs, 1, length),
        ],
        out_shape=[
            jax.ShapeDtypeStruct(gathered.shape, BF),
            jax.ShapeDtypeStruct((seqs * length, 3 * HD), BF),
            jax.ShapeDtypeStruct((n_ctx, HD, tokens), BF),
            jax.ShapeDtypeStruct((seqs, HD, length), F32),
            jax.ShapeDtypeStruct((seqs, 1, length), F32),
        ],
        scratch_shapes=[pltpu.VMEM((seqs * length, HD), F32)],
        compiler_params=pltpu.CompilerParams(vmem_limit_bytes=48 << 20),
        cost_estimate=pl.CostEstimate(
            flops=20_000_000_000, bytes_accessed=20_000_000, transcendentals=0
        ),
        name="attend",
    )(order, gathered, gain, shift, weight, bias)


def attend_back_kernel(
    seqs, rows, half, order_ref, sorted_ref, mixed_ref, log_ref, grad_ref, out_ref, bias_ref,
    rows_ref, key_ref, value_ref, all_ref,
):
    n_ctx, _, tokens = grad_ref.shape
    length = mixed_ref.shape[2]
    per = rows // half

    def spread(c, carry):
        block = grad_ref[c].T
        for s in range(seqs):
            for b in range(per):
                at = ordered_rows(order_ref, s, c * per + b, half, length)
                first = s * rows + b * half
                rows_ref[pl.ds(at, half), :] = block[first : first + half]
        return carry

    lax.fori_loop(0, n_ctx, spread, 0)
    below = below_mask(QB)

    def one_seq(s, carry):
        base = pl.multiple_of(s * length, length)
        k_all = sorted_ref[pl.ds(base, length), HD : 2 * HD]
        v_all = sorted_ref[pl.ds(base, length), 2 * HD :]
        k_turned = k_all.T
        g_turned = rows_ref[pl.ds(base, length), :].T
        delta = jnp.sum(g_turned.astype(F32) * mixed_ref[s], axis=0, keepdims=True)
        key_ref[...] = jnp.zeros_like(key_ref)
        value_ref[...] = jnp.zeros_like(value_ref)
        for i in range(length // QB):
            lo, hi = i * QB, (i + 1) * QB
            q_rows = sorted_ref[pl.ds(base + lo, QB), :HD] * 0.125
            g_rows = rows_ref[pl.ds(base + lo, QB), :]
            log_row = log_ref[s, :, lo:hi]
            delta_row = delta[:, lo:hi]
            query = jnp.zeros((HD, QB), F32)
            for first, end in ((0, lo), (lo, hi)):
                if first == end:
                    continue
                scores = mm(k_all[first:end], q_rows, NT)
                probs = jnp.exp(scores - log_row)
                if end == hi:
                    probs = jnp.where(below, probs, 0.0)
                slopes = mm(v_all[first:end], g_rows, NT)
                pulled = (probs * (slopes - delta_row)).astype(BF)
                value_ref[first:end, :] += mm(probs.astype(BF), g_rows)
                key_ref[first:end, :] += mm(pulled, q_rows)
                query = query + mm(k_turned[:, first:end], pulled)
            all_ref[pl.ds(base + lo, QB), :HD] = (query * 0.125).T
        all_ref[pl.ds(base, length), HD : 2 * HD] = key_ref[...]
        all_ref[pl.ds(base, length), 2 * HD :] = value_ref[...]
        return carry

    lax.fori_loop(0, seqs, one_seq, 0)

    def one_block(c, carry):
        parts = [
            all_ref[pl.ds(ordered_rows(order_ref, s, c * per + b, half, length), half), :]
            for s in range(seqs)
            for b in range(per)
        ]
        block = jnp.concatenate(parts, axis=0).astype(BF)
        out_ref[c] = block.T
        return carry + jnp.sum(block.astype(F32), axis=0, keepdims=True)

    bias_ref[...] = lax.fori_loop(0, n_ctx, one_block, jnp.zeros((1, 3 * HD), F32))


def attend_back(order, ordered, mixed, logs, grads, rows):
    n_ctx, _, tokens = grads.shape
    seqs, halves = order.shape
    length = rows * n_ctx
    half = length // halves
    vmem = pl.BlockSpec(memory_space=pltpu.VMEM)
    return pl.pallas_call(
        functools.partial(attend_back_kernel, seqs, rows, half),
        in_specs=[pl.BlockSpec(memory_space=pltpu.SMEM)] + [vmem] * 4,
        out_specs=[vmem] * 2,
        out_shape=[
            jax.ShapeDtypeStruct((n_ctx, 3 * HD, tokens), BF),
            jax.ShapeDtypeStruct((1, 3 * HD), F32),
        ],
        scratch_shapes=[
            pltpu.VMEM((seqs * length, HD), BF),
            pltpu.VMEM((length, HD), F32),
            pltpu.VMEM((length, HD), F32),
            pltpu.VMEM((seqs * length, 3 * HD), F32),
        ],
        compiler_params=pltpu.CompilerParams(vmem_limit_bytes=48 << 20),
        cost_estimate=pl.CostEstimate(flops=1, bytes_accessed=1, transcendentals=0),
        name="attend_back",
    )(order, ordered, mixed, logs, grads)


def head_grad_kernel(n_w, at_ref, grad_ref, bias_ref, in_ref, *refs):
    *out_refs, total_ref, turned_ref = refs
    step = pl.program_id(0)

    @pl.when(step == 0)
    def _():
        total_ref[...] = jnp.zeros_like(total_ref)

    turned = jnp.concatenate([grad_ref[g] for g in range(grad_ref.shape[0])], axis=1)
    total_ref[...] += mm(turned, in_ref[...])

    @pl.when(step == pl.num_programs(0) - 1)
    def _():
        turned_ref[...] = total_ref[...].T
        own = turned_ref.shape[0] // n_w
        for k, out_ref in enumerate(out_refs):
            at = pl.multiple_of((at_ref[0] + n_w - k) % n_w * own, 16)
            out_ref[:own] = turned_ref[pl.ds(at, own), :].astype(out_ref.dtype)
            out_ref[own:] = jnp.broadcast_to(
                bias_ref[...], (out_ref.shape[0] - own, out_ref.shape[1])
            ).astype(out_ref.dtype)


def head_grad(at, grads, bias, gathered, n_w):
    n_ctx, _, tokens = grads.shape
    width = gathered.shape[1]
    group = 4
    rows = width // n_w + 16
    return pl.pallas_call(
        functools.partial(head_grad_kernel, n_w),
        grid=(n_ctx // group,),
        in_specs=[
            pl.BlockSpec(memory_space=pltpu.SMEM),
            pl.BlockSpec((group, 3 * HD, tokens), lambda i: (i, 0, 0)),
            pl.BlockSpec((1, 3 * HD), lambda i: (0, 0)),
            pl.BlockSpec((group * tokens, width), lambda i: (i, 0)),
        ],
        out_specs=[pl.BlockSpec((rows, 3 * HD), lambda i: (0, 0))] * n_w,
        out_shape=[
            jax.ShapeDtypeStruct((rows, 3 * HD), BF if k else F32) for k in range(n_w)
        ],
        scratch_shapes=[pltpu.VMEM((3 * HD, width), F32), pltpu.VMEM((width, 3 * HD), F32)],
        compiler_params=pltpu.CompilerParams(vmem_limit_bytes=32 << 20),
        cost_estimate=pl.CostEstimate(flops=1, bytes_accessed=1, transcendentals=0),
        name="head_grad",
    )(at, grads, bias, gathered)


def finish_kernel(n_w, turned_ref, weight_ref, in_ref, gain_ref, shift_ref, middle_ref, side_ref, out_ref, block_ref, total_ref):
    step = pl.program_id(0)

    @pl.when(step == 0)
    def _():
        total_ref[...] = jnp.zeros_like(total_ref)

    total_ref[...] += mm(turned_ref[...].T, weight_ref[...])

    @pl.when(step == pl.num_programs(0) - 1)
    def _():
        grad = total_ref[...]
        _, scaled, inverse = layer_norm(in_ref[...].astype(F32), gain_ref[...], shift_ref[...])
        result, gain_grad, shift_grad = norm_back(grad, scaled, inverse, gain_ref[...])
        out_ref[...] = middle_ref[...] + result
        own = block_ref.shape[2]
        rows = (gain_grad.reshape(1, -1), side_ref[0:1], shift_grad.reshape(1, -1), side_ref[1:2])
        for w in range(n_w):
            at = slice(w * own, (w + 1) * own)
            for r, row in enumerate(rows):
                block_ref[w, r : r + 1] = row[:, at]
            block_ref[w, len(rows) :] = side_ref[2 : 2 + block_ref.shape[1] - len(rows), at]


def finish(turned, weight, low, gain, shift, middle, side, n_w):
    tokens, width = low.shape
    depth = HEADS * 3 * HD // 5
    whole = lambda *shape: pl.BlockSpec(shape, lambda i: (0,) * len(shape))
    return pl.pallas_call(
        functools.partial(finish_kernel, n_w),
        grid=(5,),
        in_specs=[
            pl.BlockSpec((depth, tokens), lambda i: (i, 0)),
            pl.BlockSpec((depth, width), lambda i: (i, 0)),
            whole(tokens, width),
            whole(1, width),
            whole(1, width),
            whole(tokens, width),
            whole(*side.shape),
        ],
        out_specs=[whole(tokens, width), whole(n_w, 8, width // n_w)],
        out_shape=[
            jax.ShapeDtypeStruct((tokens, width), F32),
            jax.ShapeDtypeStruct((n_w, 8, width // n_w), F32),
        ],
        scratch_shapes=[pltpu.VMEM((tokens, width), F32)],
        compiler_params=pltpu.CompilerParams(vmem_limit_bytes=32 << 20),
        cost_estimate=pl.CostEstimate(flops=1, bytes_accessed=1, transcendentals=0),
        name="finish",
    )(turned, weight, low, gain, shift, middle, side)


def join_rows_kernel(n_w, overlap, at_ref, *refs):
    *pieces, out_ref = refs
    wsh, core = at_ref[0], at_ref[1]
    own = pieces[0].shape[0]
    out_ref[pl.ds(pl.multiple_of(wsh * own, 16), own), :] = pieces[0][...]
    for k in range(1, n_w):
        base = (wsh + k) % n_w * own
        mine, other = pieces[2 * k - 1], pieces[2 * k]
        size = mine.shape[0]
        out_ref[pl.ds(pl.multiple_of(base + core * overlap, 16), size), :] = mine[...]
        out_ref[pl.ds(pl.multiple_of(base + (1 - core) * overlap, 16), size), :] = other[...]


def join_rows(at, pieces, n_w, overlap):
    own, width = pieces[0].shape
    vmem = pl.BlockSpec(memory_space=pltpu.VMEM)
    return pl.pallas_call(
        functools.partial(join_rows_kernel, n_w, overlap),
        in_specs=[pl.BlockSpec(memory_space=pltpu.SMEM)] + [vmem] * len(pieces),
        out_specs=vmem,
        out_shape=jax.ShapeDtypeStruct((n_w * own, width), BF),
        compiler_params=pltpu.CompilerParams(vmem_limit_bytes=32 << 20),
        cost_estimate=pl.CostEstimate(flops=1, bytes_accessed=1, transcendentals=0),
        name="join_rows",
    )(at, *pieces)


def cut_columns_kernel(n_w, overlap, at_ref, in_ref, *out_refs):
    wsh, core = at_ref[0], at_ref[1]
    cols = out_refs[0].shape[1]
    for k, out_ref in enumerate(out_refs):
        size = out_ref.shape[0]
        start = 0 if k == 0 else pl.multiple_of(core * overlap, 16)
        for b in range(n_w):

            @pl.when((wsh + n_w - k) % n_w == b)
            def _(out_ref=out_ref, start=start, size=size, b=b):
                out_ref[...] = in_ref[pl.ds(start, size), b * cols : (b + 1) * cols]


def cut_columns(at, array, n_w, size, overlap):
    own, cols = array.shape[0], array.shape[1] // n_w
    vmem = pl.BlockSpec(memory_space=pltpu.VMEM)
    return pl.pallas_call(
        functools.partial(cut_columns_kernel, n_w, overlap),
        in_specs=[pl.BlockSpec(memory_space=pltpu.SMEM), vmem],
        out_specs=[vmem] * n_w,
        out_shape=[
            jax.ShapeDtypeStruct((own if k == 0 else size, cols), BF) for k in range(n_w)
        ],
        compiler_params=pltpu.CompilerParams(vmem_limit_bytes=32 << 20),
        cost_estimate=pl.CostEstimate(flops=1, bytes_accessed=1, transcendentals=0),
        name="cut_columns",
    )(at, array)


def join_columns_kernel(n_w, overlap, at_ref, *refs):
    *pieces, out_ref = refs
    wsh, core = at_ref[0], at_ref[1]
    cols = pieces[0].shape[1]
    for k in range(n_w):
        for b in range(n_w):

            @pl.when((wsh + k) % n_w == b)
            def _(k=k, b=b):
                at = slice(b * cols, (b + 1) * cols)
                if k == 0:
                    out_ref[:, at] = pieces[0][...].astype(F32)
                    return
                mine, other = pieces[2 * k - 1], pieces[2 * k]
                size = mine.shape[0]
                out_ref[pl.ds(pl.multiple_of(core * overlap, 16), size), at] = mine[...].astype(F32)
                out_ref[pl.ds(pl.multiple_of((1 - core) * overlap, 16), size), at] = other[
                    ...
                ].astype(F32)


def join_columns(at, pieces, n_w, overlap):
    own, cols = pieces[0].shape
    vmem = pl.BlockSpec(memory_space=pltpu.VMEM)
    return pl.pallas_call(
        functools.partial(join_columns_kernel, n_w, overlap),
        in_specs=[pl.BlockSpec(memory_space=pltpu.SMEM)] + [vmem] * len(pieces),
        out_specs=vmem,
        out_shape=jax.ShapeDtypeStruct((own, n_w * cols), F32),
        compiler_params=pltpu.CompilerParams(vmem_limit_bytes=40 << 20),
        cost_estimate=pl.CostEstimate(flops=1, bytes_accessed=1, transcendentals=0),
        name="join_columns",
    )(at, *pieces)


def out_grad_kernel(n_w, in_ref, grad_ref, side_ref, out_ref):
    made = mm(in_ref[...], grad_ref[...])
    chunks = made.shape[0] // 16
    out_ref[...] = jnp.zeros_like(out_ref)
    for c in range(chunks):
        out_ref[c] = made[c * 16 : (c + 1) * 16].astype(BF)
    out_ref[chunks, :1] = side_ref[...].astype(BF)


def out_grad(rows, grads, side, n_ctx, n_w):
    vmem = pl.BlockSpec(memory_space=pltpu.VMEM)
    return pl.pallas_call(
        functools.partial(out_grad_kernel, n_w),
        in_specs=[vmem] * 3,
        out_specs=vmem,
        out_shape=jax.ShapeDtypeStruct((n_ctx, 16, grads.shape[1]), BF),
        compiler_params=pltpu.CompilerParams(vmem_limit_bytes=24 << 20),
        cost_estimate=pl.CostEstimate(flops=1, bytes_accessed=1, transcendentals=0),
        name="out_grad",
    )(rows, grads, side)


def pack_kernel(chunk_ref, *refs):
    *pieces, left_ref, right_ref = refs
    total = pieces[0][...]
    for piece in pieces[1:]:
        total = total + piece[...].astype(F32)
    left_ref[...] = total[:, : 2 * HD].astype(BF)
    chunk = chunk_ref[0].astype(F32)
    for c in range(1, chunk_ref.shape[0]):
        chunk = chunk + chunk_ref[c].astype(F32)
    turned = jnp.concatenate(
        [chunk[:, q * HD : (q + 1) * HD] for q in range(chunk.shape[1] // HD)], axis=0
    )
    turned = jnp.concatenate(
        [turned, jnp.zeros((total.shape[0] - turned.shape[0], HD), F32)], axis=0
    )
    right_ref[...] = jnp.concatenate([total[:, 2 * HD :], turned], axis=1).astype(BF)


def pack(chunks, pieces):
    rows = pieces[0].shape[0]
    vmem = pl.BlockSpec(memory_space=pltpu.VMEM)
    return pl.pallas_call(
        pack_kernel,
        in_specs=[vmem] * (1 + len(pieces)),
        out_specs=[vmem] * 2,
        out_shape=[jax.ShapeDtypeStruct((rows, 2 * HD), BF)] * 2,
        compiler_params=pltpu.CompilerParams(vmem_limit_bytes=24 << 20),
        cost_estimate=pl.CostEstimate(flops=1, bytes_accessed=1, transcendentals=0),
        name="pack",
    )(chunks, *pieces)


def unpack_kernel(
    at_ref, left_own, left_other, right_own, right_other, qkv_ref, out_ref, bias_ref, side_ref
):
    z, y, core = at_ref[0], at_ref[1], at_ref[2]
    own = qkv_ref.shape[0]
    bias_ref[...] = jnp.zeros_like(bias_ref)
    for h in range(HEADS + 1):
        by_z, by_y = (h // 8 + 4 - z) % 4, ((h // 2) % 4 + 4 - y) % 4
        same = core == h % 2
        right_at = by_y * 4 + by_z
        right = jnp.where(same, right_own[right_at], right_other[right_at]).astype(F32)
        if h == HEADS:
            for q in range(HEADS):
                side_ref[:, q * HD : (q + 1) * HD] = right[q * 16 : q * 16 + 8, HD:]
            break
        left_at = by_z * 4 + by_y
        left = jnp.where(same, left_own[left_at], left_other[left_at]).astype(F32)
        for part, piece in enumerate((left[:, :HD], left[:, HD:], right[:, :HD])):
            at = (part * HEADS + h) * HD
            qkv_ref[:, at : at + HD] = piece[:own]
        bias_ref[0:1, h * HD : (h + 1) * HD] = left[own : own + 1, :HD]
        bias_ref[1:2, h * HD : (h + 1) * HD] = right[own : own + 1, :HD]
        for q in range(HEADS):
            out_ref[h * 16 : (h + 1) * 16, q * HD : (q + 1) * HD] = right[
                q * 16 : (q + 1) * 16, HD:
            ]


def unpack(at, left_own, left_other, right_own, right_other):
    rows = left_own.shape[1] - 16
    vmem = pl.BlockSpec(memory_space=pltpu.VMEM)
    return pl.pallas_call(
        unpack_kernel,
        in_specs=[pl.BlockSpec(memory_space=pltpu.SMEM)] + [vmem] * 4,
        out_specs=[vmem] * 4,
        out_shape=[
            jax.ShapeDtypeStruct((rows, 3 * HEADS * HD), F32),
            jax.ShapeDtypeStruct((rows, HEADS * HD), F32),
            jax.ShapeDtypeStruct((8, HEADS * HD), F32),
            jax.ShapeDtypeStruct((8, HEADS * HD), F32),
        ],
        compiler_params=pltpu.CompilerParams(vmem_limit_bytes=40 << 20),
        cost_estimate=pl.CostEstimate(flops=1, bytes_accessed=1, transcendentals=0),
        name="unpack",
    )(at, left_own, left_other, right_own, right_other)


def after(array, *others):
    return lax.optimization_barrier((array, *others))[0]


def on_device(
    layer_input,
    block_order,
    norm_gains,
    norm_shifts,
    qkv_weight,
    attn_bias,
    out_weight,
    out_bias,
    fc_weight,
    fc_bias,
    proj_weight,
    proj_bias,
    output_grad,
):
    seqs, rows, width = layer_input.shape
    tokens = seqs * rows
    n_ctx, n_w = lax.axis_size(CTX), lax.axis_size("wsh")
    ctx, wsh = lax.axis_index(CTX), lax.axis_index("wsh")
    z, y, core = (lax.axis_index(axis) for axis in CTX)
    own = width // n_w
    ff = fc_weight.shape[1] // n_w
    size, overlap = 208, 192
    at_x = jnp.stack([wsh, core])

    def shift(array, axis, k):
        size = lax.axis_size(axis)
        return lax.ppermute(array, axis, [((i + k) % size, i) for i in range(size)])

    def x_shift(array, k):
        return shift(array, "wsh", k)

    def partner(array):
        return shift(array, "core", 1)

    def around(array):
        return [array] + [x_shift(array, k) for k in range(1, n_w)]

    def deal(choose):
        return [choose(0)] + [x_shift(choose(k), k) for k in range(1, n_w)]

    def with_halves(whole, halves, *before):
        pieces = [whole]
        for k in range(1, n_w):
            mine = x_shift(halves[k - 1], k)
            pieces += [mine, partner(after(mine, *before))]
        return pieces

    def in_order(pieces):
        twice = jnp.stack(pieces + pieces)
        start = (n_w - wsh) % n_w
        return lax.dynamic_slice(twice, (start,) + (0,) * pieces[0].ndim, (n_w,) + pieces[0].shape)

    low = layer_input.reshape(tokens, width)
    gathered = lax.all_gather(low, CTX, axis=0, tiled=True)
    packed = jnp.concatenate(
        [norm_gains, norm_shifts, attn_bias, out_bias[None], proj_bias[None]], axis=0
    )
    vectors = in_order(around(packed)).transpose(1, 0, 2).reshape(8, width).astype(F32)
    gains, shifts, bias_pair = vectors[0:2], vectors[2:4], vectors[4:6]
    out_bias_row, proj_bias_row = vectors[6], vectors[7]

    head = jnp.minimum(ctx, HEADS - 1)
    head_cols = jnp.concatenate(
        [
            lax.dynamic_slice(qkv_weight, (0, part * width + head * HD), (own, HD))
            for part in range(3)
        ],
        axis=1,
    )
    head_weight = in_order(around(head_cols)).reshape(width, 3 * HD).T
    head_bias = lax.dynamic_slice(bias_pair, (0, head * HD), (2, HD))
    head_bias = jnp.concatenate([head_bias[:1], jnp.zeros((1, HD), F32), head_bias[1:]], axis=1)

    grad_low = output_grad.reshape(tokens, width)
    out_half = lax.dynamic_slice(
        after(out_weight, head_weight), (core * overlap, 0), (size, width)
    )
    out_pieces = with_halves(out_weight, [out_half] * (n_w - 1))
    out_all = join_rows(at_x, out_pieces, n_w, overlap)
    fc_own, *fc_halves = cut_columns(at_x, fc_weight, n_w, size, overlap)
    fc_halves = [after(half, *out_pieces[1::2]) for half in fc_halves]
    gathered = after(gathered, out_all)

    input_one, ordered, mixed_turned, mixed, logs = attend(
        block_order, gathered, gains[:1], shifts[:1], head_weight, head_bias, rows
    )
    grad_group = jnp.concatenate(around(after(grad_low, mixed_turned)), axis=0)
    grad_active = mm(grad_group, proj_weight, NT)
    fc_pieces = with_halves(fc_own, fc_halves, mixed_turned)
    mixed_turned = after(mixed_turned, *fc_pieces[1::2])
    attended = lax.all_to_all(mixed_turned, CTX, 0, 0).reshape(n_ctx * HD, tokens)[:width]
    attended = after(attended, grad_group, *fc_pieces)
    fc_cols = join_rows(at_x, [after(fc_pieces[0], attended), *fc_pieces[1:]], n_w, overlap)
    residual = low.astype(F32)
    middle = residual + mm(attended, out_all, TN) + out_bias_row
    normed_two, scaled_two, inverse_two = layer_norm(middle, gains[1], shifts[1])
    normed_two = normed_two.astype(BF)
    weight_all = lax.all_gather(head_weight, CTX, axis=0, tiled=True)
    input_two = around(normed_two)
    *input_two, grad_active = lax.optimization_barrier((*input_two, grad_active))
    input_two = jnp.concatenate(input_two, axis=0)

    pre_gelu = mm(input_two, fc_cols) + fc_bias.astype(F32)
    activated, derivative = gelu_pair(pre_gelu)
    activated = activated.astype(BF)
    grad_pre = (grad_active * derivative).astype(BF)
    grad_two = mm(grad_pre, fc_cols, NT).reshape(n_w, tokens, width)
    parts = [grad_two[k].astype(BF) for k in range(1, n_w)]
    activated, grad_pre, *parts = lax.optimization_barrier((activated, grad_pre, *parts))
    came = [x_shift(part, n_w - k) for k, part in enumerate(parts, 1)]
    grad_proj = mm(activated, grad_group, TN).astype(BF)
    grad_fc = mm(input_two, grad_pre, TN).astype(BF)
    branch = mm(after(activated, came[0]), proj_weight).reshape(n_w, tokens, width)
    branch_own, branch_parts = branch[0], [branch[k].astype(BF) for k in range(1, n_w)]
    *came, branch_own = lax.optimization_barrier(
        (*came, branch_own, *branch_parts, grad_proj, grad_fc, weight_all)
    )[:n_w]
    grad_two = grad_two[0] + sum(piece.astype(F32) for piece in came)
    grad_fc_bias = jnp.sum(grad_pre.astype(F32), axis=0, keepdims=True)
    share_proj, share_fc = lax.psum((grad_proj, grad_fc), CTX)

    grad_norm_two, gain_two, shift_two = norm_back(grad_two, scaled_two, inverse_two, gains[1])
    grad_middle = grad_low.astype(F32) + grad_norm_two
    grad_branch = grad_middle.astype(BF)
    grad_attended = mm(out_all, grad_branch, NT).astype(BF)
    grad_heads = jnp.pad(grad_attended, ((0, (n_ctx - HEADS) * HD), (0, 0)))
    grad_heads = lax.all_to_all(grad_heads.reshape(n_ctx, HD, tokens), CTX, 0, 0)
    branch_group = jnp.concatenate(around(after(grad_branch, grad_attended)), axis=0)
    attended_rows = jnp.concatenate(
        deal(
            lambda k: lax.dynamic_slice(
                after(attended, came[0]), ((wsh + n_w - k) % n_w * own, 0), (own, tokens)
            )
        ),
        axis=1,
    )

    branch_came = [
        x_shift(after(part, branch_group), n_w - k) for k, part in enumerate(branch_parts, 1)
    ]
    branch = branch_own + sum(piece.astype(F32) for piece in branch_came)
    layer_output = (middle + branch + proj_bias_row).astype(BF)

    chunks = out_grad(attended_rows, branch_group, grad_fc_bias, n_ctx, n_w)
    grad_heads = after(grad_heads, chunks)
    chunks = lax.all_to_all(chunks, CTX, 0, 0)

    grad_qkv, grad_bias = attend_back(block_order, ordered, mixed, logs, grad_heads, rows)
    grad_tokens = lax.all_to_all(grad_qkv, CTX, 0, 0).reshape(n_ctx * 3 * HD, tokens)

    dealt = head_grad(at_x, grad_qkv, grad_bias, after(input_one, *branch_came), n_w)
    pieces = deal(lambda k: dealt[k])
    left, right = pack(chunks, pieces)
    left = jnp.stack([left] + [shift(left, "y", k) for k in range(1, 4)])
    right = jnp.stack([right] + [shift(right, "z", k) for k in range(1, 4)])
    side = jnp.stack(
        [
            gain_two,
            shift_two,
            jnp.sum(grad_low.astype(F32), axis=0),
            jnp.sum(grad_branch.astype(F32), axis=0),
        ]
    )
    side = jnp.pad(side, ((0, 4), (0, 0)))
    input_grad, blocks = finish(
        grad_tokens, weight_all, low, gains[:1], shifts[:1], grad_middle, side, n_w
    )
    pieces = deal(
        lambda k: lax.dynamic_slice(blocks, ((wsh + n_w - k) % n_w, 0, 0), (1, 8, own))
    )
    vector_sum = (pieces[0] + pieces[1]) + (pieces[2] + pieces[3])
    everyone = lax.all_to_all(jnp.broadcast_to(vector_sum, (n_ctx, 8, own)), CTX, 0, 0)
    vector_out = jnp.sum(everyone, axis=0)

    left = [left] + [shift(left, "z", k) for k in range(1, 4)]
    right = [right] + [shift(right, "y", k) for k in range(1, 4)]
    *both, blocks = lax.optimization_barrier((*left, *right, blocks))
    left, right = jnp.concatenate(both[:4]), jnp.concatenate(both[4:])
    qkv_out, out_out, bias_out, side_out = unpack(
        jnp.stack([z, y, core]), left, partner(left), right, partner(right)
    )
    bias_out = lax.dynamic_slice(bias_out, (0, wsh * own), (2, own))

    proj_out = share_proj.astype(F32)
    rows_for = lambda k, start, count: lax.dynamic_slice(
        share_fc, ((wsh + n_w - k) % n_w * own + start, 0), (count, ff)
    )
    fc_out = join_columns(
        at_x,
        with_halves(
            rows_for(0, 0, own),
            [rows_for(k, core * overlap, size) for k in range(1, n_w)],
            qkv_out,
            proj_out,
        ),
        n_w,
        overlap,
    )
    return (
        layer_output.reshape(seqs, rows, width),
        input_grad.reshape(seqs, rows, width),
        vector_out[0:2],
        vector_out[2:4],
        qkv_out,
        bias_out,
        out_out,
        vector_out[5],
        fc_out,
        side_out[0],
        proj_out,
        vector_out[4],
    )


def solution(mesh):
    y, core = 4, 2
    split = Mesh(
        mesh.devices.reshape(mesh.shape["ctx"] // (y * core), y, core, mesh.shape["wsh"]),
        (*CTX, "wsh"),
    )
    return jax.shard_map(
        on_device,
        mesh=split,
        in_specs=(
            P("wsh", CTX, None),
            P("wsh", None),
            P(None, "wsh"),
            P(None, "wsh"),
            P("wsh", None),
            P(None, "wsh"),
            P("wsh", None),
            P("wsh"),
            P("wsh", None),
            P("wsh"),
            P("wsh", None),
            P("wsh"),
            P("wsh", CTX, None),
        ),
        out_specs=(
            P("wsh", CTX, None),
            P("wsh", CTX, None),
            P(None, "wsh"),
            P(None, "wsh"),
            P("wsh", None),
            P(None, "wsh"),
            P("wsh", None),
            P("wsh"),
            P("wsh", None),
            P("wsh"),
            P("wsh", None),
            P("wsh"),
        ),
        check_vma=False,
    )
```

```python
import functools

import jax
import jax.numpy as jnp
from jax import lax
from jax.experimental import pallas as pl
from jax.experimental.pallas import tpu as pltpu
from jax.sharding import Mesh
from jax.sharding import PartitionSpec as P

HEADS = 25
HD = 64
QB = 256
FB = 512
BF = jnp.bfloat16
F32 = jnp.float32
NN = (((1,), (0,)), ((), ()))
NT = (((1,), (1,)), ((), ()))
TN = (((0,), (0,)), ((), ()))
CTX = ("z", "y", "core")


def mm(left, right, dims=NN):
    return lax.dot_general(left, right, dims, preferred_element_type=F32)


def layer_norm(hidden, gain_row, shift_row):
    centered = hidden - jnp.mean(hidden, axis=-1, keepdims=True)
    inverse = lax.rsqrt(jnp.mean(centered * centered, axis=-1, keepdims=True) + 1e-05)
    scaled = centered * inverse
    return scaled * gain_row + shift_row, scaled, inverse


def norm_back(gradient, scaled, inverse, gain_row):
    weighted = gradient * gain_row
    first_mean = jnp.mean(weighted, axis=-1, keepdims=True)
    second_mean = jnp.mean(weighted * scaled, axis=-1, keepdims=True)
    result = inverse * (weighted - first_mean - scaled * second_mean)
    return result, jnp.sum(gradient * scaled, axis=0), jnp.sum(gradient, axis=0)


def gelu_pair(pre_gelu):
    squared = pre_gelu * pre_gelu
    tangent = jnp.tanh(0.7978845608028654 * (pre_gelu + 0.044715 * squared * pre_gelu))
    result = 0.5 * pre_gelu * (1.0 + tangent)
    derivative = 0.5 * (1.0 + tangent) + 0.5 * pre_gelu * (
        1.0 - tangent * tangent
    ) * 0.7978845608028654 * (1.0 + 3.0 * 0.044715 * squared)
    return result, derivative


def ordered_rows(order_ref, seq, block, half, length):
    return pl.multiple_of(seq * length + order_ref[seq, block] * half, half)


def below_mask(size):
    return lax.broadcasted_iota(jnp.int32, (size, size), 0) <= lax.broadcasted_iota(
        jnp.int32, (size, size), 1
    )


def attend_kernel(
    seqs, rows, half, order_ref, in_ref, gain_ref, shift_ref, weight_ref, bias_ref,
    normed_ref, sorted_ref, out_ref, mixed_ref, log_ref, rows_ref,
):
    step = pl.program_id(0)
    tokens = seqs * rows
    group = in_ref.shape[0] // tokens
    length = mixed_ref.shape[2]
    per = rows // half
    normed = layer_norm(in_ref[...].astype(F32), gain_ref[...], shift_ref[...])[0].astype(BF)
    normed_ref[...] = normed
    made = (mm(normed, weight_ref[...], NT) + bias_ref[...]).astype(BF)
    for g in range(group):
        for s in range(seqs):
            for b in range(per):
                at = ordered_rows(order_ref, s, (step * group + g) * per + b, half, length)
                first = g * tokens + s * rows + b * half
                sorted_ref[pl.ds(at, half), :] = made[first : first + half]

    @pl.when(step == pl.num_programs(0) - 1)
    def _():
        below = below_mask(FB)

        def one_seq(s, carry):
            base = pl.multiple_of(s * length, length)
            k_all = sorted_ref[pl.ds(base, length), HD : 2 * HD]
            v_turned = sorted_ref[pl.ds(base, length), 2 * HD :].T
            for i in range(length // FB):
                lo, hi = i * FB, (i + 1) * FB
                q_rows = sorted_ref[pl.ds(base + lo, FB), :HD] * 0.125
                scores = mm(k_all[:hi], q_rows, NT)
                last = jnp.where(below, scores[lo:], -1e30)
                best = jnp.max(last, axis=0, keepdims=True)
                if i:
                    best = jnp.maximum(best, jnp.max(scores[:lo], axis=0, keepdims=True))
                tail = jnp.exp(last - best)
                total = jnp.sum(tail, axis=0, keepdims=True)
                mixed = mm(v_turned[:, lo:hi], tail.astype(BF))
                if i:
                    head = jnp.exp(scores[:lo] - best)
                    total = total + jnp.sum(head, axis=0, keepdims=True)
                    mixed = mixed + mm(v_turned[:, :lo], head.astype(BF))
                mixed = mixed / total
                mixed_ref[s, :, lo:hi] = mixed
                log_ref[s, :, lo:hi] = best + jnp.log(total)
                rows_ref[pl.ds(base + lo, FB), :] = mixed.T
            return carry

        lax.fori_loop(0, seqs, one_seq, 0)

        def one_block(c, carry):
            parts = [
                rows_ref[pl.ds(ordered_rows(order_ref, s, c * per + b, half, length), half), :]
                for s in range(seqs)
                for b in range(per)
            ]
            out_ref[c] = jnp.concatenate(parts, axis=0).T.astype(BF)
            return carry

        lax.fori_loop(0, out_ref.shape[0], one_block, 0)


def attend(order, gathered, gain, shift, weight, bias, rows):
    seqs, halves = order.shape
    tokens, width = seqs * rows, gathered.shape[1]
    n_ctx = gathered.shape[0] // tokens
    length = rows * n_ctx
    half = length // halves
    group = 8
    whole = lambda *shape: pl.BlockSpec(shape, lambda i: (0,) * len(shape))
    return pl.pallas_call(
        functools.partial(attend_kernel, seqs, rows, half),
        grid=(n_ctx // group,),
        in_specs=[
            pl.BlockSpec(memory_space=pltpu.SMEM),
            pl.BlockSpec((group * tokens, width), lambda i: (i, 0)),
            whole(1, width),
            whole(1, width),
            whole(3 * HD, width),
            whole(1, 3 * HD),
        ],
        out_specs=[
            pl.BlockSpec((group * tokens, width), lambda i: (i, 0)),
            whole(seqs * length, 3 * HD),
            whole(n_ctx, HD, tokens),
            whole(seqs, HD, length),
            whole(seqs, 1, length),
        ],
        out_shape=[
            jax.ShapeDtypeStruct(gathered.shape, BF),
            jax.ShapeDtypeStruct((seqs * length, 3 * HD), BF),
            jax.ShapeDtypeStruct((n_ctx, HD, tokens), BF),
            jax.ShapeDtypeStruct((seqs, HD, length), F32),
            jax.ShapeDtypeStruct((seqs, 1, length), F32),
        ],
        scratch_shapes=[pltpu.VMEM((seqs * length, HD), F32)],
        compiler_params=pltpu.CompilerParams(vmem_limit_bytes=48 << 20),
        cost_estimate=pl.CostEstimate(
            flops=20_000_000_000, bytes_accessed=20_000_000, transcendentals=0
        ),
        name="attend",
    )(order, gathered, gain, shift, weight, bias)


def attend_back_kernel(
    seqs, rows, half, order_ref, sorted_ref, mixed_ref, log_ref, grad_ref, out_ref, bias_ref,
    rows_ref, key_ref, value_ref, all_ref,
):
    n_ctx, _, tokens = grad_ref.shape
    length = mixed_ref.shape[2]
    per = rows // half

    def spread(c, carry):
        block = grad_ref[c].T
        for s in range(seqs):
            for b in range(per):
                at = ordered_rows(order_ref, s, c * per + b, half, length)
                first = s * rows + b * half
                rows_ref[pl.ds(at, half), :] = block[first : first + half]
        return carry

    lax.fori_loop(0, n_ctx, spread, 0)
    below = below_mask(QB)

    def one_seq(s, carry):
        base = pl.multiple_of(s * length, length)
        k_all = sorted_ref[pl.ds(base, length), HD : 2 * HD]
        v_all = sorted_ref[pl.ds(base, length), 2 * HD :]
        k_turned = k_all.T
        g_turned = rows_ref[pl.ds(base, length), :].T
        delta = jnp.sum(g_turned.astype(F32) * mixed_ref[s], axis=0, keepdims=True)
        key_ref[...] = jnp.zeros_like(key_ref)
        value_ref[...] = jnp.zeros_like(value_ref)
        for i in range(length // QB):
            lo, hi = i * QB, (i + 1) * QB
            q_rows = sorted_ref[pl.ds(base + lo, QB), :HD] * 0.125
            g_rows = rows_ref[pl.ds(base + lo, QB), :]
            log_row = log_ref[s, :, lo:hi]
            delta_row = delta[:, lo:hi]
            query = jnp.zeros((HD, QB), F32)
            for first, end in ((0, lo), (lo, hi)):
                if first == end:
                    continue
                scores = mm(k_all[first:end], q_rows, NT)
                probs = jnp.exp(scores - log_row)
                if end == hi:
                    probs = jnp.where(below, probs, 0.0)
                slopes = mm(v_all[first:end], g_rows, NT)
                pulled = (probs * (slopes - delta_row)).astype(BF)
                value_ref[first:end, :] += mm(probs.astype(BF), g_rows)
                key_ref[first:end, :] += mm(pulled, q_rows)
                query = query + mm(k_turned[:, first:end], pulled)
            all_ref[pl.ds(base + lo, QB), :HD] = (query * 0.125).T
        all_ref[pl.ds(base, length), HD : 2 * HD] = key_ref[...]
        all_ref[pl.ds(base, length), 2 * HD :] = value_ref[...]
        return carry

    lax.fori_loop(0, seqs, one_seq, 0)

    def one_block(c, carry):
        parts = [
            all_ref[pl.ds(ordered_rows(order_ref, s, c * per + b, half, length), half), :]
            for s in range(seqs)
            for b in range(per)
        ]
        block = jnp.concatenate(parts, axis=0).astype(BF)
        out_ref[c] = block.T
        return carry + jnp.sum(block.astype(F32), axis=0, keepdims=True)

    bias_ref[...] = lax.fori_loop(0, n_ctx, one_block, jnp.zeros((1, 3 * HD), F32))


def attend_back(order, ordered, mixed, logs, grads, rows):
    n_ctx, _, tokens = grads.shape
    seqs, halves = order.shape
    length = rows * n_ctx
    half = length // halves
    vmem = pl.BlockSpec(memory_space=pltpu.VMEM)
    return pl.pallas_call(
        functools.partial(attend_back_kernel, seqs, rows, half),
        in_specs=[pl.BlockSpec(memory_space=pltpu.SMEM)] + [vmem] * 4,
        out_specs=[vmem] * 2,
        out_shape=[
            jax.ShapeDtypeStruct((n_ctx, 3 * HD, tokens), BF),
            jax.ShapeDtypeStruct((1, 3 * HD), F32),
        ],
        scratch_shapes=[
            pltpu.VMEM((seqs * length, HD), BF),
            pltpu.VMEM((length, HD), F32),
            pltpu.VMEM((length, HD), F32),
            pltpu.VMEM((seqs * length, 3 * HD), F32),
        ],
        compiler_params=pltpu.CompilerParams(vmem_limit_bytes=48 << 20),
        cost_estimate=pl.CostEstimate(flops=1, bytes_accessed=1, transcendentals=0),
        name="attend_back",
    )(order, ordered, mixed, logs, grads)


def head_grad_kernel(n_w, at_ref, grad_ref, bias_ref, in_ref, *refs):
    *out_refs, total_ref, turned_ref = refs
    step = pl.program_id(0)

    @pl.when(step == 0)
    def _():
        total_ref[...] = jnp.zeros_like(total_ref)

    turned = jnp.concatenate([grad_ref[g] for g in range(grad_ref.shape[0])], axis=1)
    total_ref[...] += mm(turned, in_ref[...])

    @pl.when(step == pl.num_programs(0) - 1)
    def _():
        turned_ref[...] = total_ref[...].T
        own = turned_ref.shape[0] // n_w
        for k, out_ref in enumerate(out_refs):
            at = pl.multiple_of((at_ref[0] + n_w - k) % n_w * own, 16)
            out_ref[:own] = turned_ref[pl.ds(at, own), :].astype(out_ref.dtype)
            out_ref[own:] = jnp.broadcast_to(
                bias_ref[...], (out_ref.shape[0] - own, out_ref.shape[1])
            ).astype(out_ref.dtype)


def head_grad(at, grads, bias, gathered, n_w):
    n_ctx, _, tokens = grads.shape
    width = gathered.shape[1]
    group = 4
    rows = width // n_w + 16
    return pl.pallas_call(
        functools.partial(head_grad_kernel, n_w),
        grid=(n_ctx // group,),
        in_specs=[
            pl.BlockSpec(memory_space=pltpu.SMEM),
            pl.BlockSpec((group, 3 * HD, tokens), lambda i: (i, 0, 0)),
            pl.BlockSpec((1, 3 * HD), lambda i: (0, 0)),
            pl.BlockSpec((group * tokens, width), lambda i: (i, 0)),
        ],
        out_specs=[pl.BlockSpec((rows, 3 * HD), lambda i: (0, 0))] * n_w,
        out_shape=[
            jax.ShapeDtypeStruct((rows, 3 * HD), BF if k else F32) for k in range(n_w)
        ],
        scratch_shapes=[pltpu.VMEM((3 * HD, width), F32), pltpu.VMEM((width, 3 * HD), F32)],
        compiler_params=pltpu.CompilerParams(vmem_limit_bytes=56 << 20),
        cost_estimate=pl.CostEstimate(flops=1, bytes_accessed=1, transcendentals=0),
        name="head_grad",
    )(at, grads, bias, gathered)


def finish_kernel(n_w, turned_ref, weight_ref, in_ref, gain_ref, shift_ref, middle_ref, side_ref, out_ref, block_ref, total_ref):
    step = pl.program_id(0)

    @pl.when(step == 0)
    def _():
        total_ref[...] = jnp.zeros_like(total_ref)

    total_ref[...] += mm(turned_ref[...].T, weight_ref[...])

    @pl.when(step == pl.num_programs(0) - 1)
    def _():
        grad = total_ref[...]
        _, scaled, inverse = layer_norm(in_ref[...].astype(F32), gain_ref[...], shift_ref[...])
        result, gain_grad, shift_grad = norm_back(grad, scaled, inverse, gain_ref[...])
        out_ref[...] = middle_ref[...] + result
        own = block_ref.shape[2]
        rows = (gain_grad.reshape(1, -1), side_ref[0:1], shift_grad.reshape(1, -1), side_ref[1:2])
        for w in range(n_w):
            at = slice(w * own, (w + 1) * own)
            for r, row in enumerate(rows):
                block_ref[w, r : r + 1] = row[:, at]
            block_ref[w, len(rows) :] = side_ref[2 : 2 + block_ref.shape[1] - len(rows), at]


def finish(turned, weight, low, gain, shift, middle, side, n_w):
    tokens, width = low.shape
    depth = HEADS * 3 * HD // 5
    whole = lambda *shape: pl.BlockSpec(shape, lambda i: (0,) * len(shape))
    return pl.pallas_call(
        functools.partial(finish_kernel, n_w),
        grid=(5,),
        in_specs=[
            pl.BlockSpec((depth, tokens), lambda i: (i, 0)),
            pl.BlockSpec((depth, width), lambda i: (i, 0)),
            whole(tokens, width),
            whole(1, width),
            whole(1, width),
            whole(tokens, width),
            whole(*side.shape),
        ],
        out_specs=[whole(tokens, width), whole(n_w, 8, width // n_w)],
        out_shape=[
            jax.ShapeDtypeStruct((tokens, width), F32),
            jax.ShapeDtypeStruct((n_w, 8, width // n_w), F32),
        ],
        scratch_shapes=[pltpu.VMEM((tokens, width), F32)],
        compiler_params=pltpu.CompilerParams(vmem_limit_bytes=32 << 20),
        cost_estimate=pl.CostEstimate(flops=1, bytes_accessed=1, transcendentals=0),
        name="finish",
    )(turned, weight, low, gain, shift, middle, side)


def join_rows_kernel(n_w, overlap, at_ref, *refs):
    *pieces, out_ref = refs
    wsh, core = at_ref[0], at_ref[1]
    own = pieces[0].shape[0]
    out_ref[pl.ds(pl.multiple_of(wsh * own, 16), own), :] = pieces[0][...]
    for k in range(1, n_w):
        base = (wsh + k) % n_w * own
        mine, other = pieces[2 * k - 1], pieces[2 * k]
        size = mine.shape[0]
        out_ref[pl.ds(pl.multiple_of(base + core * overlap, 16), size), :] = mine[...]
        out_ref[pl.ds(pl.multiple_of(base + (1 - core) * overlap, 16), size), :] = other[...]


def join_rows(at, pieces, n_w, overlap):
    own, width = pieces[0].shape
    vmem = pl.BlockSpec(memory_space=pltpu.VMEM)
    return pl.pallas_call(
        functools.partial(join_rows_kernel, n_w, overlap),
        in_specs=[pl.BlockSpec(memory_space=pltpu.SMEM)] + [vmem] * len(pieces),
        out_specs=vmem,
        out_shape=jax.ShapeDtypeStruct((n_w * own, width), BF),
        compiler_params=pltpu.CompilerParams(vmem_limit_bytes=32 << 20),
        cost_estimate=pl.CostEstimate(flops=1, bytes_accessed=1, transcendentals=0),
        name="join_rows",
    )(at, *pieces)


def cut_columns_kernel(n_w, overlap, at_ref, in_ref, *out_refs):
    wsh, core = at_ref[0], at_ref[1]
    cols = out_refs[0].shape[1]
    for k, out_ref in enumerate(out_refs):
        size = out_ref.shape[0]
        start = 0 if k == 0 else pl.multiple_of(core * overlap, 16)
        for b in range(n_w):

            @pl.when((wsh + n_w - k) % n_w == b)
            def _(out_ref=out_ref, start=start, size=size, b=b):
                out_ref[...] = in_ref[pl.ds(start, size), b * cols : (b + 1) * cols]


def cut_columns(at, array, n_w, size, overlap):
    own, cols = array.shape[0], array.shape[1] // n_w
    vmem = pl.BlockSpec(memory_space=pltpu.VMEM)
    return pl.pallas_call(
        functools.partial(cut_columns_kernel, n_w, overlap),
        in_specs=[pl.BlockSpec(memory_space=pltpu.SMEM), vmem],
        out_specs=[vmem] * n_w,
        out_shape=[
            jax.ShapeDtypeStruct((own if k == 0 else size, cols), BF) for k in range(n_w)
        ],
        compiler_params=pltpu.CompilerParams(vmem_limit_bytes=32 << 20),
        cost_estimate=pl.CostEstimate(flops=1, bytes_accessed=1, transcendentals=0),
        name="cut_columns",
    )(at, array)


def join_columns_kernel(n_w, overlap, at_ref, *refs):
    *pieces, out_ref = refs
    wsh, core = at_ref[0], at_ref[1]
    cols = pieces[0].shape[1]
    for k in range(n_w):
        for b in range(n_w):

            @pl.when((wsh + k) % n_w == b)
            def _(k=k, b=b):
                at = slice(b * cols, (b + 1) * cols)
                if k == 0:
                    out_ref[:, at] = pieces[0][...].astype(F32)
                    return
                mine, other = pieces[2 * k - 1], pieces[2 * k]
                size = mine.shape[0]
                out_ref[pl.ds(pl.multiple_of(core * overlap, 16), size), at] = mine[...].astype(F32)
                out_ref[pl.ds(pl.multiple_of((1 - core) * overlap, 16), size), at] = other[
                    ...
                ].astype(F32)


def join_columns(at, pieces, n_w, overlap):
    own, cols = pieces[0].shape
    vmem = pl.BlockSpec(memory_space=pltpu.VMEM)
    return pl.pallas_call(
        functools.partial(join_columns_kernel, n_w, overlap),
        in_specs=[pl.BlockSpec(memory_space=pltpu.SMEM)] + [vmem] * len(pieces),
        out_specs=vmem,
        out_shape=jax.ShapeDtypeStruct((own, n_w * cols), F32),
        compiler_params=pltpu.CompilerParams(vmem_limit_bytes=40 << 20),
        cost_estimate=pl.CostEstimate(flops=1, bytes_accessed=1, transcendentals=0),
        name="join_columns",
    )(at, *pieces)


def out_grad_kernel(n_w, in_ref, grad_ref, side_ref, out_ref):
    made = mm(in_ref[...], grad_ref[...])
    chunks = made.shape[0] // 16
    out_ref[...] = jnp.zeros_like(out_ref)
    for c in range(chunks):
        out_ref[c] = made[c * 16 : (c + 1) * 16].astype(BF)
    out_ref[chunks, :1] = side_ref[...].astype(BF)


def out_grad(rows, grads, side, n_ctx, n_w):
    vmem = pl.BlockSpec(memory_space=pltpu.VMEM)
    return pl.pallas_call(
        functools.partial(out_grad_kernel, n_w),
        in_specs=[vmem] * 3,
        out_specs=vmem,
        out_shape=jax.ShapeDtypeStruct((n_ctx, 16, grads.shape[1]), BF),
        compiler_params=pltpu.CompilerParams(vmem_limit_bytes=24 << 20),
        cost_estimate=pl.CostEstimate(flops=1, bytes_accessed=1, transcendentals=0),
        name="out_grad",
    )(rows, grads, side)


def pack_kernel(chunk_ref, *refs):
    *pieces, left_ref, right_ref = refs
    total = pieces[0][...]
    for piece in pieces[1:]:
        total = total + piece[...].astype(F32)
    left_ref[...] = total[:, : 2 * HD].astype(BF)
    chunk = chunk_ref[0].astype(F32)
    for c in range(1, chunk_ref.shape[0]):
        chunk = chunk + chunk_ref[c].astype(F32)
    turned = jnp.concatenate(
        [chunk[:, q * HD : (q + 1) * HD] for q in range(chunk.shape[1] // HD)], axis=0
    )
    turned = jnp.concatenate(
        [turned, jnp.zeros((total.shape[0] - turned.shape[0], HD), F32)], axis=0
    )
    right_ref[...] = jnp.concatenate([total[:, 2 * HD :], turned], axis=1).astype(BF)


def pack(chunks, pieces):
    rows = pieces[0].shape[0]
    vmem = pl.BlockSpec(memory_space=pltpu.VMEM)
    return pl.pallas_call(
        pack_kernel,
        in_specs=[vmem] * (1 + len(pieces)),
        out_specs=[vmem] * 2,
        out_shape=[jax.ShapeDtypeStruct((rows, 2 * HD), BF)] * 2,
        compiler_params=pltpu.CompilerParams(vmem_limit_bytes=24 << 20),
        cost_estimate=pl.CostEstimate(flops=1, bytes_accessed=1, transcendentals=0),
        name="pack",
    )(chunks, *pieces)


def unpack_kernel(
    at_ref, left_own, left_other, right_own, right_other, qkv_ref, out_ref, bias_ref, side_ref
):
    z, y, core = at_ref[0], at_ref[1], at_ref[2]
    own = qkv_ref.shape[0]
    bias_ref[...] = jnp.zeros_like(bias_ref)
    for h in range(HEADS + 1):
        by_z, by_y = (h // 8 + 4 - z) % 4, ((h // 2) % 4 + 4 - y) % 4
        same = core == h % 2
        right_at = by_y * 4 + by_z
        right = jnp.where(same, right_own[right_at], right_other[right_at]).astype(F32)
        if h == HEADS:
            for q in range(HEADS):
                side_ref[:, q * HD : (q + 1) * HD] = right[q * 16 : q * 16 + 8, HD:]
            break
        left_at = by_z * 4 + by_y
        left = jnp.where(same, left_own[left_at], left_other[left_at]).astype(F32)
        for part, piece in enumerate((left[:, :HD], left[:, HD:], right[:, :HD])):
            at = (part * HEADS + h) * HD
            qkv_ref[:, at : at + HD] = piece[:own]
        bias_ref[0:1, h * HD : (h + 1) * HD] = left[own : own + 1, :HD]
        bias_ref[1:2, h * HD : (h + 1) * HD] = right[own : own + 1, :HD]
        for q in range(HEADS):
            out_ref[h * 16 : (h + 1) * 16, q * HD : (q + 1) * HD] = right[
                q * 16 : (q + 1) * 16, HD:
            ]


def unpack(at, left_own, left_other, right_own, right_other):
    rows = left_own.shape[1] - 16
    vmem = pl.BlockSpec(memory_space=pltpu.VMEM)
    return pl.pallas_call(
        unpack_kernel,
        in_specs=[pl.BlockSpec(memory_space=pltpu.SMEM)] + [vmem] * 4,
        out_specs=[vmem] * 4,
        out_shape=[
            jax.ShapeDtypeStruct((rows, 3 * HEADS * HD), F32),
            jax.ShapeDtypeStruct((rows, HEADS * HD), F32),
            jax.ShapeDtypeStruct((8, HEADS * HD), F32),
            jax.ShapeDtypeStruct((8, HEADS * HD), F32),
        ],
        compiler_params=pltpu.CompilerParams(vmem_limit_bytes=40 << 20),
        cost_estimate=pl.CostEstimate(flops=1, bytes_accessed=1, transcendentals=0),
        name="unpack",
    )(at, left_own, left_other, right_own, right_other)


def after(array, *others):
    return lax.optimization_barrier((array, *others))[0]


def on_device(
    layer_input,
    block_order,
    norm_gains,
    norm_shifts,
    qkv_weight,
    attn_bias,
    out_weight,
    out_bias,
    fc_weight,
    fc_bias,
    proj_weight,
    proj_bias,
    output_grad,
):
    seqs, rows, width = layer_input.shape
    tokens = seqs * rows
    n_ctx, n_w = lax.axis_size(CTX), lax.axis_size("wsh")
    ctx, wsh = lax.axis_index(CTX), lax.axis_index("wsh")
    z, y, core = (lax.axis_index(axis) for axis in CTX)
    own = width // n_w
    ff = fc_weight.shape[1] // n_w
    size, overlap = 208, 192
    at_x = jnp.stack([wsh, core])

    def shift(array, axis, k):
        size = lax.axis_size(axis)
        return lax.ppermute(array, axis, [((i + k) % size, i) for i in range(size)])

    def x_shift(array, k):
        return shift(array, "wsh", k)

    def partner(array):
        return shift(array, "core", 1)

    def around(array):
        return [array] + [x_shift(array, k) for k in range(1, n_w)]

    def deal(choose):
        return [choose(0)] + [x_shift(choose(k), k) for k in range(1, n_w)]

    def with_halves(whole, halves, *before):
        pieces = [whole]
        for k in range(1, n_w):
            mine = x_shift(halves[k - 1], k)
            pieces += [mine, partner(after(mine, *before))]
        return pieces

    def in_order(pieces):
        twice = jnp.stack(pieces + pieces)
        start = (n_w - wsh) % n_w
        return lax.dynamic_slice(twice, (start,) + (0,) * pieces[0].ndim, (n_w,) + pieces[0].shape)

    low = layer_input.reshape(tokens, width)
    gathered = lax.all_gather(low, CTX, axis=0, tiled=True)
    packed = jnp.concatenate(
        [norm_gains, norm_shifts, attn_bias, out_bias[None], proj_bias[None]], axis=0
    )
    vectors = in_order(around(packed)).transpose(1, 0, 2).reshape(8, width).astype(F32)
    gains, shifts, bias_pair = vectors[0:2], vectors[2:4], vectors[4:6]
    out_bias_row, proj_bias_row = vectors[6], vectors[7]

    head = jnp.minimum(ctx, HEADS - 1)
    head_cols = jnp.concatenate(
        [
            lax.dynamic_slice(qkv_weight, (0, part * width + head * HD), (own, HD))
            for part in range(3)
        ],
        axis=1,
    )
    head_weight = in_order(around(head_cols)).reshape(width, 3 * HD).T
    head_bias = lax.dynamic_slice(bias_pair, (0, head * HD), (2, HD))
    head_bias = jnp.concatenate([head_bias[:1], jnp.zeros((1, HD), F32), head_bias[1:]], axis=1)

    grad_low = output_grad.reshape(tokens, width)
    out_half = lax.dynamic_slice(
        after(out_weight, head_weight), (core * overlap, 0), (size, width)
    )
    out_pieces = with_halves(out_weight, [out_half] * (n_w - 1))
    out_all = join_rows(at_x, out_pieces, n_w, overlap)
    fc_own, *fc_halves = cut_columns(at_x, fc_weight, n_w, size, overlap)
    fc_halves = [after(half, *out_pieces[1::2]) for half in fc_halves]
    gathered = after(gathered, out_all)

    input_one, ordered, mixed_turned, mixed, logs = attend(
        block_order, gathered, gains[:1], shifts[:1], head_weight, head_bias, rows
    )
    grad_group = jnp.concatenate(around(after(grad_low, mixed_turned)), axis=0)
    grad_active = mm(grad_group, proj_weight, NT)
    fc_pieces = with_halves(fc_own, fc_halves, mixed_turned)
    mixed_turned = after(mixed_turned, *fc_pieces[1::2])
    attended = lax.all_to_all(mixed_turned, CTX, 0, 0).reshape(n_ctx * HD, tokens)[:width]
    attended = after(attended, grad_group, *fc_pieces)
    fc_cols = join_rows(at_x, [after(fc_pieces[0], attended), *fc_pieces[1:]], n_w, overlap)
    residual = low.astype(F32)
    middle = residual + mm(attended, out_all, TN) + out_bias_row
    normed_two, scaled_two, inverse_two = layer_norm(middle, gains[1], shifts[1])
    normed_two = normed_two.astype(BF)
    weight_all = lax.all_gather(head_weight, CTX, axis=0, tiled=True)
    input_two = around(normed_two)
    *input_two, grad_active = lax.optimization_barrier((*input_two, grad_active))
    input_two = jnp.concatenate(input_two, axis=0)

    pre_gelu = mm(input_two, fc_cols) + fc_bias.astype(F32)
    activated, derivative = gelu_pair(pre_gelu)
    activated = activated.astype(BF)
    grad_pre = (grad_active * derivative).astype(BF)
    grad_two = mm(grad_pre, fc_cols, NT).reshape(n_w, tokens, width)
    parts = [grad_two[k].astype(BF) for k in range(1, n_w)]
    activated, grad_pre, *parts = lax.optimization_barrier((activated, grad_pre, *parts))
    came = [x_shift(part, n_w - k) for k, part in enumerate(parts, 1)]
    grad_proj = mm(activated, grad_group, TN).astype(BF)
    grad_fc = mm(input_two, grad_pre, TN).astype(BF)
    branch = mm(after(activated, came[0]), proj_weight).reshape(n_w, tokens, width)
    branch_own, branch_parts = branch[0], [branch[k].astype(BF) for k in range(1, n_w)]
    *came, branch_own = lax.optimization_barrier(
        (*came, branch_own, *branch_parts, grad_proj, grad_fc, weight_all)
    )[:n_w]
    grad_two = grad_two[0] + sum(piece.astype(F32) for piece in came)
    grad_fc_bias = jnp.sum(grad_pre.astype(F32), axis=0, keepdims=True)
    share_proj, share_fc = lax.psum((grad_proj, grad_fc), CTX)

    grad_norm_two, gain_two, shift_two = norm_back(grad_two, scaled_two, inverse_two, gains[1])
    grad_middle = grad_low.astype(F32) + grad_norm_two
    grad_branch = grad_middle.astype(BF)
    grad_attended = mm(out_all, grad_branch, NT).astype(BF)
    grad_heads = jnp.pad(grad_attended, ((0, (n_ctx - HEADS) * HD), (0, 0)))
    grad_heads = lax.all_to_all(grad_heads.reshape(n_ctx, HD, tokens), CTX, 0, 0)
    branch_group = jnp.concatenate(around(after(grad_branch, grad_attended)), axis=0)
    attended_rows = jnp.concatenate(
        deal(
            lambda k: lax.dynamic_slice(
                after(attended, came[0]), ((wsh + n_w - k) % n_w * own, 0), (own, tokens)
            )
        ),
        axis=1,
    )

    branch_came = [
        x_shift(after(part, branch_group), n_w - k) for k, part in enumerate(branch_parts, 1)
    ]
    branch = branch_own + sum(piece.astype(F32) for piece in branch_came)
    layer_output = (middle + branch + proj_bias_row).astype(BF)

    chunks = out_grad(attended_rows, branch_group, grad_fc_bias, n_ctx, n_w)
    grad_heads = after(grad_heads, chunks)
    chunks = lax.all_to_all(chunks, CTX, 0, 0)

    grad_qkv, grad_bias = attend_back(block_order, ordered, mixed, logs, grad_heads, rows)
    grad_tokens = lax.all_to_all(grad_qkv, CTX, 0, 0).reshape(n_ctx * 3 * HD, tokens)

    dealt = head_grad(at_x, grad_qkv, grad_bias, after(input_one, *branch_came), n_w)
    pieces = deal(lambda k: dealt[k])
    left, right = pack(chunks, pieces)
    left = jnp.stack([left] + [shift(left, "y", k) for k in range(1, 4)])
    right = jnp.stack([right] + [shift(right, "z", k) for k in range(1, 4)])
    left = jnp.concatenate([left] + [shift(left, "z", k) for k in range(1, 4)])
    right = jnp.concatenate([right] + [shift(right, "y", k) for k in range(1, 4)])
    side = jnp.stack(
        [
            gain_two,
            shift_two,
            jnp.sum(grad_low.astype(F32), axis=0),
            jnp.sum(grad_branch.astype(F32), axis=0),
        ]
    )
    side = jnp.pad(side, ((0, 4), (0, 0)))
    input_grad, blocks = finish(
        grad_tokens, weight_all, low, gains[:1], shifts[:1], grad_middle, side, n_w
    )
    pieces = deal(
        lambda k: lax.dynamic_slice(blocks, ((wsh + n_w - k) % n_w, 0, 0), (1, 8, own))
    )
    vector_sum = (pieces[0] + pieces[1]) + (pieces[2] + pieces[3])
    everyone = lax.all_to_all(jnp.broadcast_to(vector_sum, (n_ctx, 8, own)), CTX, 0, 0)
    vector_out = jnp.sum(everyone, axis=0)

    qkv_out, out_out, bias_out, side_out = unpack(
        jnp.stack([z, y, core]), after(left, blocks), partner(left), right, partner(right)
    )
    bias_out = lax.dynamic_slice(bias_out, (0, wsh * own), (2, own))

    proj_out = share_proj.astype(F32)
    rows_for = lambda k, start, count: lax.dynamic_slice(
        share_fc, ((wsh + n_w - k) % n_w * own + start, 0), (count, ff)
    )
    fc_out = join_columns(
        at_x,
        with_halves(
            rows_for(0, 0, own),
            [rows_for(k, core * overlap, size) for k in range(1, n_w)],
            qkv_out,
            proj_out,
        ),
        n_w,
        overlap,
    )
    return (
        layer_output.reshape(seqs, rows, width),
        input_grad.reshape(seqs, rows, width),
        vector_out[0:2],
        vector_out[2:4],
        qkv_out,
        bias_out,
        out_out,
        vector_out[5],
        fc_out,
        side_out[0],
        proj_out,
        vector_out[4],
    )


def solution(mesh):
    y, core = 4, 2
    split = Mesh(
        mesh.devices.reshape(mesh.shape["ctx"] // (y * core), y, core, mesh.shape["wsh"]),
        (*CTX, "wsh"),
    )
    return jax.shard_map(
        on_device,
        mesh=split,
        in_specs=(
            P("wsh", CTX, None),
            P("wsh", None),
            P(None, "wsh"),
            P(None, "wsh"),
            P("wsh", None),
            P(None, "wsh"),
            P("wsh", None),
            P("wsh"),
            P("wsh", None),
            P("wsh"),
            P("wsh", None),
            P("wsh"),
            P("wsh", CTX, None),
        ),
        out_specs=(
            P("wsh", CTX, None),
            P("wsh", CTX, None),
            P(None, "wsh"),
            P(None, "wsh"),
            P("wsh", None),
            P(None, "wsh"),
            P("wsh", None),
            P("wsh"),
            P("wsh", None),
            P("wsh"),
            P("wsh", None),
            P("wsh"),
        ),
        check_vma=False,
    )
```

```python
import functools

import jax
import jax.numpy as jnp
from jax import lax
from jax.experimental import pallas as pl
from jax.experimental.pallas import tpu as pltpu
from jax.sharding import Mesh
from jax.sharding import PartitionSpec as P

HEADS = 25
HD = 64
QB = 256
FB = 512
BF = jnp.bfloat16
F32 = jnp.float32
NN = (((1,), (0,)), ((), ()))
NT = (((1,), (1,)), ((), ()))
TN = (((0,), (0,)), ((), ()))
CTX = ("z", "y", "core")


def mm(left, right, dims=NN):
    return lax.dot_general(left, right, dims, preferred_element_type=F32)


def layer_norm(hidden, gain_row, shift_row):
    centered = hidden - jnp.mean(hidden, axis=-1, keepdims=True)
    inverse = lax.rsqrt(jnp.mean(centered * centered, axis=-1, keepdims=True) + 1e-05)
    scaled = centered * inverse
    return scaled * gain_row + shift_row, scaled, inverse


def norm_back(gradient, scaled, inverse, gain_row):
    weighted = gradient * gain_row
    first_mean = jnp.mean(weighted, axis=-1, keepdims=True)
    second_mean = jnp.mean(weighted * scaled, axis=-1, keepdims=True)
    result = inverse * (weighted - first_mean - scaled * second_mean)
    return result, jnp.sum(gradient * scaled, axis=0), jnp.sum(gradient, axis=0)


def gelu_pair(pre_gelu):
    squared = pre_gelu * pre_gelu
    tangent = jnp.tanh(0.7978845608028654 * (pre_gelu + 0.044715 * squared * pre_gelu))
    result = 0.5 * pre_gelu * (1.0 + tangent)
    derivative = 0.5 * (1.0 + tangent) + 0.5 * pre_gelu * (
        1.0 - tangent * tangent
    ) * 0.7978845608028654 * (1.0 + 3.0 * 0.044715 * squared)
    return result, derivative


def ordered_rows(order_ref, seq, block, half, length):
    return pl.multiple_of(seq * length + order_ref[seq, block] * half, half)


def below_mask(size):
    return lax.broadcasted_iota(jnp.int32, (size, size), 0) <= lax.broadcasted_iota(
        jnp.int32, (size, size), 1
    )


def attend_kernel(
    seqs, rows, half, order_ref, in_ref, gain_ref, shift_ref, weight_ref, bias_ref,
    normed_ref, sorted_ref, out_ref, mixed_ref, log_ref, rows_ref,
):
    step = pl.program_id(0)
    tokens = seqs * rows
    group = in_ref.shape[0] // tokens
    length = mixed_ref.shape[2]
    per = rows // half
    normed = layer_norm(in_ref[...].astype(F32), gain_ref[...], shift_ref[...])[0].astype(BF)
    normed_ref[...] = normed
    made = (mm(normed, weight_ref[...], NT) + bias_ref[...]).astype(BF)
    for g in range(group):
        for s in range(seqs):
            for b in range(per):
                at = ordered_rows(order_ref, s, (step * group + g) * per + b, half, length)
                first = g * tokens + s * rows + b * half
                sorted_ref[pl.ds(at, half), :] = made[first : first + half]

    @pl.when(step == pl.num_programs(0) - 1)
    def _():
        below = below_mask(FB)

        def one_seq(s, carry):
            base = pl.multiple_of(s * length, length)
            k_all = sorted_ref[pl.ds(base, length), HD : 2 * HD]
            v_turned = sorted_ref[pl.ds(base, length), 2 * HD :].T
            for i in range(length // FB):
                lo, hi = i * FB, (i + 1) * FB
                q_rows = sorted_ref[pl.ds(base + lo, FB), :HD] * 0.125
                scores = mm(k_all[:hi], q_rows, NT)
                last = jnp.where(below, scores[lo:], -1e30)
                best = jnp.max(last, axis=0, keepdims=True)
                if i:
                    best = jnp.maximum(best, jnp.max(scores[:lo], axis=0, keepdims=True))
                tail = jnp.exp(last - best)
                total = jnp.sum(tail, axis=0, keepdims=True)
                mixed = mm(v_turned[:, lo:hi], tail.astype(BF))
                if i:
                    head = jnp.exp(scores[:lo] - best)
                    total = total + jnp.sum(head, axis=0, keepdims=True)
                    mixed = mixed + mm(v_turned[:, :lo], head.astype(BF))
                mixed = mixed / total
                mixed_ref[s, :, lo:hi] = mixed
                log_ref[s, :, lo:hi] = best + jnp.log(total)
                rows_ref[pl.ds(base + lo, FB), :] = mixed.T
            return carry

        lax.fori_loop(0, seqs, one_seq, 0)

        def one_block(c, carry):
            parts = [
                rows_ref[pl.ds(ordered_rows(order_ref, s, c * per + b, half, length), half), :]
                for s in range(seqs)
                for b in range(per)
            ]
            out_ref[c] = jnp.concatenate(parts, axis=0).T.astype(BF)
            return carry

        lax.fori_loop(0, out_ref.shape[0], one_block, 0)


def attend(order, gathered, gain, shift, weight, bias, rows):
    seqs, halves = order.shape
    tokens, width = seqs * rows, gathered.shape[1]
    n_ctx = gathered.shape[0] // tokens
    length = rows * n_ctx
    half = length // halves
    group = 8
    whole = lambda *shape: pl.BlockSpec(shape, lambda i: (0,) * len(shape))
    return pl.pallas_call(
        functools.partial(attend_kernel, seqs, rows, half),
        grid=(n_ctx // group,),
        in_specs=[
            pl.BlockSpec(memory_space=pltpu.SMEM),
            pl.BlockSpec((group * tokens, width), lambda i: (i, 0)),
            whole(1, width),
            whole(1, width),
            whole(3 * HD, width),
            whole(1, 3 * HD),
        ],
        out_specs=[
            pl.BlockSpec((group * tokens, width), lambda i: (i, 0)),
            whole(seqs * length, 3 * HD),
            whole(n_ctx, HD, tokens),
            whole(seqs, HD, length),
            whole(seqs, 1, length),
        ],
        out_shape=[
            jax.ShapeDtypeStruct(gathered.shape, BF),
            jax.ShapeDtypeStruct((seqs * length, 3 * HD), BF),
            jax.ShapeDtypeStruct((n_ctx, HD, tokens), BF),
            jax.ShapeDtypeStruct((seqs, HD, length), F32),
            jax.ShapeDtypeStruct((seqs, 1, length), F32),
        ],
        scratch_shapes=[pltpu.VMEM((seqs * length, HD), F32)],
        compiler_params=pltpu.CompilerParams(vmem_limit_bytes=56 << 20),
        cost_estimate=pl.CostEstimate(
            flops=20_000_000_000, bytes_accessed=20_000_000, transcendentals=0
        ),
        name="attend",
    )(order, gathered, gain, shift, weight, bias)


def attend_back_kernel(
    seqs, rows, half, order_ref, sorted_ref, mixed_ref, log_ref, grad_ref, out_ref, bias_ref,
    rows_ref, key_ref, value_ref, all_ref,
):
    n_ctx, _, tokens = grad_ref.shape
    length = mixed_ref.shape[2]
    per = rows // half

    def spread(c, carry):
        block = grad_ref[c].T
        for s in range(seqs):
            for b in range(per):
                at = ordered_rows(order_ref, s, c * per + b, half, length)
                first = s * rows + b * half
                rows_ref[pl.ds(at, half), :] = block[first : first + half]
        return carry

    lax.fori_loop(0, n_ctx, spread, 0)
    below = below_mask(QB)

    def one_seq(s, carry):
        base = pl.multiple_of(s * length, length)
        k_all = sorted_ref[pl.ds(base, length), HD : 2 * HD]
        v_all = sorted_ref[pl.ds(base, length), 2 * HD :]
        k_turned = k_all.T
        g_turned = rows_ref[pl.ds(base, length), :].T
        delta = jnp.sum(g_turned.astype(F32) * mixed_ref[s], axis=0, keepdims=True)
        key_ref[...] = jnp.zeros_like(key_ref)
        value_ref[...] = jnp.zeros_like(value_ref)
        for i in range(length // QB):
            lo, hi = i * QB, (i + 1) * QB
            q_rows = sorted_ref[pl.ds(base + lo, QB), :HD] * 0.125
            g_rows = rows_ref[pl.ds(base + lo, QB), :]
            log_row = log_ref[s, :, lo:hi]
            delta_row = delta[:, lo:hi]
            query = jnp.zeros((HD, QB), F32)
            for first, end in ((0, lo), (lo, hi)):
                if first == end:
                    continue
                scores = mm(k_all[first:end], q_rows, NT)
                probs = jnp.exp(scores - log_row)
                if end == hi:
                    probs = jnp.where(below, probs, 0.0)
                slopes = mm(v_all[first:end], g_rows, NT)
                pulled = (probs * (slopes - delta_row)).astype(BF)
                value_ref[first:end, :] += mm(probs.astype(BF), g_rows)
                key_ref[first:end, :] += mm(pulled, q_rows)
                query = query + mm(k_turned[:, first:end], pulled)
            all_ref[pl.ds(base + lo, QB), :HD] = (query * 0.125).T
        all_ref[pl.ds(base, length), HD : 2 * HD] = key_ref[...]
        all_ref[pl.ds(base, length), 2 * HD :] = value_ref[...]
        return carry

    lax.fori_loop(0, seqs, one_seq, 0)

    def one_block(c, carry):
        parts = [
            all_ref[pl.ds(ordered_rows(order_ref, s, c * per + b, half, length), half), :]
            for s in range(seqs)
            for b in range(per)
        ]
        block = jnp.concatenate(parts, axis=0).astype(BF)
        out_ref[c] = block.T
        return carry + jnp.sum(block.astype(F32), axis=0, keepdims=True)

    bias_ref[...] = lax.fori_loop(0, n_ctx, one_block, jnp.zeros((1, 3 * HD), F32))


def attend_back(order, ordered, mixed, logs, grads, rows):
    n_ctx, _, tokens = grads.shape
    seqs, halves = order.shape
    length = rows * n_ctx
    half = length // halves
    vmem = pl.BlockSpec(memory_space=pltpu.VMEM)
    return pl.pallas_call(
        functools.partial(attend_back_kernel, seqs, rows, half),
        in_specs=[pl.BlockSpec(memory_space=pltpu.SMEM)] + [vmem] * 4,
        out_specs=[vmem] * 2,
        out_shape=[
            jax.ShapeDtypeStruct((n_ctx, 3 * HD, tokens), BF),
            jax.ShapeDtypeStruct((1, 3 * HD), F32),
        ],
        scratch_shapes=[
            pltpu.VMEM((seqs * length, HD), BF),
            pltpu.VMEM((length, HD), F32),
            pltpu.VMEM((length, HD), F32),
            pltpu.VMEM((seqs * length, 3 * HD), F32),
        ],
        compiler_params=pltpu.CompilerParams(vmem_limit_bytes=48 << 20),
        cost_estimate=pl.CostEstimate(flops=1, bytes_accessed=1, transcendentals=0),
        name="attend_back",
    )(order, ordered, mixed, logs, grads)


def head_grad_kernel(n_w, at_ref, grad_ref, bias_ref, in_ref, *refs):
    *out_refs, total_ref, turned_ref = refs
    step = pl.program_id(0)

    @pl.when(step == 0)
    def _():
        total_ref[...] = jnp.zeros_like(total_ref)

    turned = jnp.concatenate([grad_ref[g] for g in range(grad_ref.shape[0])], axis=1)
    total_ref[...] += mm(turned, in_ref[...])

    @pl.when(step == pl.num_programs(0) - 1)
    def _():
        turned_ref[...] = total_ref[...].T
        own = turned_ref.shape[0] // n_w
        for k, out_ref in enumerate(out_refs):
            at = pl.multiple_of((at_ref[0] + n_w - k) % n_w * own, 16)
            out_ref[:own] = turned_ref[pl.ds(at, own), :].astype(out_ref.dtype)
            out_ref[own:] = jnp.broadcast_to(
                bias_ref[...], (out_ref.shape[0] - own, out_ref.shape[1])
            ).astype(out_ref.dtype)


def head_grad(at, grads, bias, gathered, n_w):
    n_ctx, _, tokens = grads.shape
    width = gathered.shape[1]
    group = 4
    rows = width // n_w + 16
    return pl.pallas_call(
        functools.partial(head_grad_kernel, n_w),
        grid=(n_ctx // group,),
        in_specs=[
            pl.BlockSpec(memory_space=pltpu.SMEM),
            pl.BlockSpec((group, 3 * HD, tokens), lambda i: (i, 0, 0)),
            pl.BlockSpec((1, 3 * HD), lambda i: (0, 0)),
            pl.BlockSpec((group * tokens, width), lambda i: (i, 0)),
        ],
        out_specs=[pl.BlockSpec((rows, 3 * HD), lambda i: (0, 0))] * n_w,
        out_shape=[
            jax.ShapeDtypeStruct((rows, 3 * HD), BF if k else F32) for k in range(n_w)
        ],
        scratch_shapes=[pltpu.VMEM((3 * HD, width), F32), pltpu.VMEM((width, 3 * HD), F32)],
        compiler_params=pltpu.CompilerParams(vmem_limit_bytes=56 << 20),
        cost_estimate=pl.CostEstimate(flops=1, bytes_accessed=1, transcendentals=0),
        name="head_grad",
    )(at, grads, bias, gathered)


def finish_kernel(n_w, turned_ref, weight_ref, in_ref, gain_ref, shift_ref, middle_ref, side_ref, out_ref, block_ref, total_ref):
    step = pl.program_id(0)

    @pl.when(step == 0)
    def _():
        total_ref[...] = jnp.zeros_like(total_ref)

    total_ref[...] += mm(turned_ref[...].T, weight_ref[...])

    @pl.when(step == pl.num_programs(0) - 1)
    def _():
        grad = total_ref[...]
        _, scaled, inverse = layer_norm(in_ref[...].astype(F32), gain_ref[...], shift_ref[...])
        result, gain_grad, shift_grad = norm_back(grad, scaled, inverse, gain_ref[...])
        out_ref[...] = middle_ref[...] + result
        own = block_ref.shape[2]
        rows = (gain_grad.reshape(1, -1), side_ref[0:1], shift_grad.reshape(1, -1), side_ref[1:2])
        for w in range(n_w):
            at = slice(w * own, (w + 1) * own)
            for r, row in enumerate(rows):
                block_ref[w, r : r + 1] = row[:, at]
            block_ref[w, len(rows) :] = side_ref[2 : 2 + block_ref.shape[1] - len(rows), at]


def finish(turned, weight, low, gain, shift, middle, side, n_w):
    tokens, width = low.shape
    depth = HEADS * 3 * HD // 5
    whole = lambda *shape: pl.BlockSpec(shape, lambda i: (0,) * len(shape))
    return pl.pallas_call(
        functools.partial(finish_kernel, n_w),
        grid=(5,),
        in_specs=[
            pl.BlockSpec((depth, tokens), lambda i: (i, 0)),
            pl.BlockSpec((depth, width), lambda i: (i, 0)),
            whole(tokens, width),
            whole(1, width),
            whole(1, width),
            whole(tokens, width),
            whole(*side.shape),
        ],
        out_specs=[whole(tokens, width), whole(n_w, 8, width // n_w)],
        out_shape=[
            jax.ShapeDtypeStruct((tokens, width), F32),
            jax.ShapeDtypeStruct((n_w, 8, width // n_w), F32),
        ],
        scratch_shapes=[pltpu.VMEM((tokens, width), F32)],
        compiler_params=pltpu.CompilerParams(vmem_limit_bytes=32 << 20),
        cost_estimate=pl.CostEstimate(flops=1, bytes_accessed=1, transcendentals=0),
        name="finish",
    )(turned, weight, low, gain, shift, middle, side)


def join_rows_kernel(n_w, overlap, at_ref, *refs):
    *pieces, out_ref = refs
    wsh, core = at_ref[0], at_ref[1]
    own = pieces[0].shape[0]
    out_ref[pl.ds(pl.multiple_of(wsh * own, 16), own), :] = pieces[0][...]
    for k in range(1, n_w):
        base = (wsh + k) % n_w * own
        mine, other = pieces[2 * k - 1], pieces[2 * k]
        size = mine.shape[0]
        out_ref[pl.ds(pl.multiple_of(base + core * overlap, 16), size), :] = mine[...]
        out_ref[pl.ds(pl.multiple_of(base + (1 - core) * overlap, 16), size), :] = other[...]


def join_rows(at, pieces, n_w, overlap):
    own, width = pieces[0].shape
    vmem = pl.BlockSpec(memory_space=pltpu.VMEM)
    return pl.pallas_call(
        functools.partial(join_rows_kernel, n_w, overlap),
        in_specs=[pl.BlockSpec(memory_space=pltpu.SMEM)] + [vmem] * len(pieces),
        out_specs=vmem,
        out_shape=jax.ShapeDtypeStruct((n_w * own, width), BF),
        compiler_params=pltpu.CompilerParams(vmem_limit_bytes=56 << 20),
        cost_estimate=pl.CostEstimate(flops=1, bytes_accessed=1, transcendentals=0),
        name="join_rows",
    )(at, *pieces)


def cut_columns_kernel(n_w, overlap, at_ref, in_ref, *out_refs):
    wsh, core = at_ref[0], at_ref[1]
    cols = out_refs[0].shape[1]
    for k, out_ref in enumerate(out_refs):
        size = out_ref.shape[0]
        start = 0 if k == 0 else pl.multiple_of(core * overlap, 16)
        for b in range(n_w):

            @pl.when((wsh + n_w - k) % n_w == b)
            def _(out_ref=out_ref, start=start, size=size, b=b):
                out_ref[...] = in_ref[pl.ds(start, size), b * cols : (b + 1) * cols]


def cut_columns(at, array, n_w, size, overlap):
    own, cols = array.shape[0], array.shape[1] // n_w
    vmem = pl.BlockSpec(memory_space=pltpu.VMEM)
    return pl.pallas_call(
        functools.partial(cut_columns_kernel, n_w, overlap),
        in_specs=[pl.BlockSpec(memory_space=pltpu.SMEM), vmem],
        out_specs=[vmem] * n_w,
        out_shape=[
            jax.ShapeDtypeStruct((own if k == 0 else size, cols), BF) for k in range(n_w)
        ],
        compiler_params=pltpu.CompilerParams(vmem_limit_bytes=32 << 20),
        cost_estimate=pl.CostEstimate(flops=1, bytes_accessed=1, transcendentals=0),
        name="cut_columns",
    )(at, array)


def join_columns_kernel(n_w, overlap, at_ref, *refs):
    *pieces, out_ref = refs
    wsh, core = at_ref[0], at_ref[1]
    cols = pieces[0].shape[1]
    for k in range(n_w):
        for b in range(n_w):

            @pl.when((wsh + k) % n_w == b)
            def _(k=k, b=b):
                at = slice(b * cols, (b + 1) * cols)
                if k == 0:
                    out_ref[:, at] = pieces[0][...].astype(F32)
                    return
                mine, other = pieces[2 * k - 1], pieces[2 * k]
                size = mine.shape[0]
                out_ref[pl.ds(pl.multiple_of(core * overlap, 16), size), at] = mine[...].astype(F32)
                out_ref[pl.ds(pl.multiple_of((1 - core) * overlap, 16), size), at] = other[
                    ...
                ].astype(F32)


def join_columns(at, pieces, n_w, overlap):
    own, cols = pieces[0].shape
    vmem = pl.BlockSpec(memory_space=pltpu.VMEM)
    return pl.pallas_call(
        functools.partial(join_columns_kernel, n_w, overlap),
        in_specs=[pl.BlockSpec(memory_space=pltpu.SMEM)] + [vmem] * len(pieces),
        out_specs=vmem,
        out_shape=jax.ShapeDtypeStruct((own, n_w * cols), F32),
        compiler_params=pltpu.CompilerParams(vmem_limit_bytes=40 << 20),
        cost_estimate=pl.CostEstimate(flops=1, bytes_accessed=1, transcendentals=0),
        name="join_columns",
    )(at, *pieces)


def out_grad_kernel(n_w, in_ref, grad_ref, side_ref, out_ref):
    made = mm(in_ref[...], grad_ref[...])
    chunks = made.shape[0] // 16
    out_ref[...] = jnp.zeros_like(out_ref)
    for c in range(chunks):
        out_ref[c] = made[c * 16 : (c + 1) * 16].astype(BF)
    out_ref[chunks, :1] = side_ref[...].astype(BF)


def out_grad(rows, grads, side, n_ctx, n_w):
    vmem = pl.BlockSpec(memory_space=pltpu.VMEM)
    return pl.pallas_call(
        functools.partial(out_grad_kernel, n_w),
        in_specs=[vmem] * 3,
        out_specs=vmem,
        out_shape=jax.ShapeDtypeStruct((n_ctx, 16, grads.shape[1]), BF),
        compiler_params=pltpu.CompilerParams(vmem_limit_bytes=24 << 20),
        cost_estimate=pl.CostEstimate(flops=1, bytes_accessed=1, transcendentals=0),
        name="out_grad",
    )(rows, grads, side)


def pack_kernel(chunk_ref, *refs):
    *pieces, left_ref, right_ref = refs
    total = pieces[0][...]
    for piece in pieces[1:]:
        total = total + piece[...].astype(F32)
    left_ref[...] = total[:, : 2 * HD].astype(BF)
    chunk = chunk_ref[0].astype(F32)
    for c in range(1, chunk_ref.shape[0]):
        chunk = chunk + chunk_ref[c].astype(F32)
    turned = jnp.concatenate(
        [chunk[:, q * HD : (q + 1) * HD] for q in range(chunk.shape[1] // HD)], axis=0
    )
    turned = jnp.concatenate(
        [turned, jnp.zeros((total.shape[0] - turned.shape[0], HD), F32)], axis=0
    )
    right_ref[...] = jnp.concatenate([total[:, 2 * HD :], turned], axis=1).astype(BF)


def pack(chunks, pieces):
    rows = pieces[0].shape[0]
    vmem = pl.BlockSpec(memory_space=pltpu.VMEM)
    return pl.pallas_call(
        pack_kernel,
        in_specs=[vmem] * (1 + len(pieces)),
        out_specs=[vmem] * 2,
        out_shape=[jax.ShapeDtypeStruct((rows, 2 * HD), BF)] * 2,
        compiler_params=pltpu.CompilerParams(vmem_limit_bytes=24 << 20),
        cost_estimate=pl.CostEstimate(flops=1, bytes_accessed=1, transcendentals=0),
        name="pack",
    )(chunks, *pieces)


def unpack_kernel(
    at_ref, left_own, left_other, right_own, right_other, qkv_ref, out_ref, bias_ref, side_ref
):
    z, y, core = at_ref[0], at_ref[1], at_ref[2]
    own = qkv_ref.shape[0]
    bias_ref[...] = jnp.zeros_like(bias_ref)
    for h in range(HEADS + 1):
        by_z, by_y = (h // 8 + 4 - z) % 4, ((h // 2) % 4 + 4 - y) % 4
        same = core == h % 2
        right_at = by_y * 4 + by_z
        right = jnp.where(same, right_own[right_at], right_other[right_at]).astype(F32)
        if h == HEADS:
            for q in range(HEADS):
                side_ref[:, q * HD : (q + 1) * HD] = right[q * 16 : q * 16 + 8, HD:]
            break
        left_at = by_z * 4 + by_y
        left = jnp.where(same, left_own[left_at], left_other[left_at]).astype(F32)
        for part, piece in enumerate((left[:, :HD], left[:, HD:], right[:, :HD])):
            at = (part * HEADS + h) * HD
            qkv_ref[:, at : at + HD] = piece[:own]
        bias_ref[0:1, h * HD : (h + 1) * HD] = left[own : own + 1, :HD]
        bias_ref[1:2, h * HD : (h + 1) * HD] = right[own : own + 1, :HD]
        for q in range(HEADS):
            out_ref[h * 16 : (h + 1) * 16, q * HD : (q + 1) * HD] = right[
                q * 16 : (q + 1) * 16, HD:
            ]


def unpack(at, left_own, left_other, right_own, right_other):
    rows = left_own.shape[1] - 16
    vmem = pl.BlockSpec(memory_space=pltpu.VMEM)
    return pl.pallas_call(
        unpack_kernel,
        in_specs=[pl.BlockSpec(memory_space=pltpu.SMEM)] + [vmem] * 4,
        out_specs=[vmem] * 4,
        out_shape=[
            jax.ShapeDtypeStruct((rows, 3 * HEADS * HD), F32),
            jax.ShapeDtypeStruct((rows, HEADS * HD), F32),
            jax.ShapeDtypeStruct((8, HEADS * HD), F32),
            jax.ShapeDtypeStruct((8, HEADS * HD), F32),
        ],
        compiler_params=pltpu.CompilerParams(vmem_limit_bytes=40 << 20),
        cost_estimate=pl.CostEstimate(flops=1, bytes_accessed=1, transcendentals=0),
        name="unpack",
    )(at, left_own, left_other, right_own, right_other)


def after(array, *others):
    return lax.optimization_barrier((array, *others))[0]


def on_device(
    layer_input,
    block_order,
    norm_gains,
    norm_shifts,
    qkv_weight,
    attn_bias,
    out_weight,
    out_bias,
    fc_weight,
    fc_bias,
    proj_weight,
    proj_bias,
    output_grad,
):
    seqs, rows, width = layer_input.shape
    tokens = seqs * rows
    n_ctx, n_w = lax.axis_size(CTX), lax.axis_size("wsh")
    ctx, wsh = lax.axis_index(CTX), lax.axis_index("wsh")
    z, y, core = (lax.axis_index(axis) for axis in CTX)
    own = width // n_w
    ff = fc_weight.shape[1] // n_w
    size, overlap = 208, 192
    at_x = jnp.stack([wsh, core])

    def shift(array, axis, k):
        size = lax.axis_size(axis)
        return lax.ppermute(array, axis, [((i + k) % size, i) for i in range(size)])

    def x_shift(array, k):
        return shift(array, "wsh", k)

    def partner(array):
        return shift(array, "core", 1)

    def around(array):
        return [array] + [x_shift(array, k) for k in range(1, n_w)]

    def deal(choose):
        return [choose(0)] + [x_shift(choose(k), k) for k in range(1, n_w)]

    def with_halves(whole, halves, *before):
        pieces = [whole]
        for k in range(1, n_w):
            mine = x_shift(halves[k - 1], k)
            pieces += [mine, partner(after(mine, *before))]
        return pieces

    def in_order(pieces):
        twice = jnp.stack(pieces + pieces)
        start = (n_w - wsh) % n_w
        return lax.dynamic_slice(twice, (start,) + (0,) * pieces[0].ndim, (n_w,) + pieces[0].shape)

    low = layer_input.reshape(tokens, width)
    gathered = lax.all_gather(low, CTX, axis=0, tiled=True)
    packed = jnp.concatenate(
        [norm_gains, norm_shifts, attn_bias, out_bias[None], proj_bias[None]], axis=0
    )
    vectors = in_order(around(packed)).transpose(1, 0, 2).reshape(8, width).astype(F32)
    gains, shifts, bias_pair = vectors[0:2], vectors[2:4], vectors[4:6]
    out_bias_row, proj_bias_row = vectors[6], vectors[7]

    head = jnp.minimum(ctx, HEADS - 1)
    head_cols = jnp.concatenate(
        [
            lax.dynamic_slice(qkv_weight, (0, part * width + head * HD), (own, HD))
            for part in range(3)
        ],
        axis=1,
    )
    head_weight = in_order(around(head_cols)).reshape(width, 3 * HD).T
    head_bias = lax.dynamic_slice(bias_pair, (0, head * HD), (2, HD))
    head_bias = jnp.concatenate([head_bias[:1], jnp.zeros((1, HD), F32), head_bias[1:]], axis=1)

    grad_low = output_grad.reshape(tokens, width)
    out_half = lax.dynamic_slice(
        after(out_weight, head_weight), (core * overlap, 0), (size, width)
    )
    out_pieces = with_halves(out_weight, [out_half] * (n_w - 1))
    out_all = join_rows(at_x, out_pieces, n_w, overlap)
    fc_own, *fc_halves = cut_columns(at_x, fc_weight, n_w, size, overlap)
    fc_halves = [after(half, *out_pieces[1::2]) for half in fc_halves]
    gathered = after(gathered, out_all)

    input_one, ordered, mixed_turned, mixed, logs = attend(
        block_order, gathered, gains[:1], shifts[:1], head_weight, head_bias, rows
    )
    grad_group = jnp.concatenate(around(after(grad_low, mixed_turned)), axis=0)
    grad_active = mm(grad_group, proj_weight, NT)
    fc_pieces = with_halves(fc_own, fc_halves, mixed_turned)
    mixed_turned = after(mixed_turned, *fc_pieces[1::2])
    attended = lax.all_to_all(mixed_turned, CTX, 0, 0).reshape(n_ctx * HD, tokens)[:width]
    attended = after(attended, grad_group, *fc_pieces)
    fc_cols = join_rows(at_x, [after(fc_pieces[0], attended), *fc_pieces[1:]], n_w, overlap)
    residual = low.astype(F32)
    middle = residual + mm(attended, out_all, TN) + out_bias_row
    normed_two, scaled_two, inverse_two = layer_norm(middle, gains[1], shifts[1])
    normed_two = normed_two.astype(BF)
    weight_all = lax.all_gather(head_weight, CTX, axis=0, tiled=True)
    input_two = around(normed_two)
    *input_two, grad_active = lax.optimization_barrier((*input_two, grad_active))
    input_two = jnp.concatenate(input_two, axis=0)

    pre_gelu = mm(input_two, fc_cols) + fc_bias.astype(F32)
    activated, derivative = gelu_pair(pre_gelu)
    activated = activated.astype(BF)
    grad_pre = (grad_active * derivative).astype(BF)
    grad_two = mm(grad_pre, fc_cols, NT).reshape(n_w, tokens, width)
    parts = [grad_two[k].astype(BF) for k in range(1, n_w)]
    activated, grad_pre, *parts = lax.optimization_barrier((activated, grad_pre, *parts))
    came = [x_shift(part, n_w - k) for k, part in enumerate(parts, 1)]
    grad_proj = mm(activated, grad_group, TN).astype(BF)
    grad_fc = mm(input_two, grad_pre, TN).astype(BF)
    branch = mm(after(activated, came[0]), proj_weight).reshape(n_w, tokens, width)
    branch_own, branch_parts = branch[0], [branch[k].astype(BF) for k in range(1, n_w)]
    *came, branch_own = lax.optimization_barrier(
        (*came, branch_own, *branch_parts, grad_proj, grad_fc, weight_all)
    )[:n_w]
    grad_two = grad_two[0] + sum(piece.astype(F32) for piece in came)
    grad_fc_bias = jnp.sum(grad_pre.astype(F32), axis=0, keepdims=True)
    share_proj, share_fc = lax.psum((grad_proj, grad_fc), CTX)

    grad_norm_two, gain_two, shift_two = norm_back(grad_two, scaled_two, inverse_two, gains[1])
    grad_middle = grad_low.astype(F32) + grad_norm_two
    grad_branch = grad_middle.astype(BF)
    grad_attended = mm(out_all, grad_branch, NT).astype(BF)
    grad_heads = jnp.pad(grad_attended, ((0, (n_ctx - HEADS) * HD), (0, 0)))
    grad_heads = lax.all_to_all(grad_heads.reshape(n_ctx, HD, tokens), CTX, 0, 0)
    branch_group = jnp.concatenate(around(after(grad_branch, grad_attended)), axis=0)
    attended_rows = jnp.concatenate(
        deal(
            lambda k: lax.dynamic_slice(
                after(attended, came[0]), ((wsh + n_w - k) % n_w * own, 0), (own, tokens)
            )
        ),
        axis=1,
    )

    branch_came = [
        x_shift(after(part, branch_group), n_w - k) for k, part in enumerate(branch_parts, 1)
    ]
    branch = branch_own + sum(piece.astype(F32) for piece in branch_came)
    layer_output = (middle + branch + proj_bias_row).astype(BF)

    chunks = out_grad(attended_rows, branch_group, grad_fc_bias, n_ctx, n_w)
    grad_heads = after(grad_heads, chunks)
    chunks = lax.all_to_all(chunks, CTX, 0, 0)

    grad_qkv, grad_bias = attend_back(block_order, ordered, mixed, logs, grad_heads, rows)
    grad_tokens = lax.all_to_all(grad_qkv, CTX, 0, 0).reshape(n_ctx * 3 * HD, tokens)

    dealt = head_grad(at_x, grad_qkv, grad_bias, after(input_one, *branch_came), n_w)
    pieces = deal(lambda k: dealt[k])
    left, right = pack(chunks, pieces)
    left = jnp.stack([left] + [shift(left, "y", k) for k in range(1, 4)])
    right = jnp.stack([right] + [shift(right, "z", k) for k in range(1, 4)])
    left = jnp.concatenate([left] + [shift(left, "z", k) for k in range(1, 4)])
    right = jnp.concatenate([right] + [shift(right, "y", k) for k in range(1, 4)])
    side = jnp.stack(
        [
            gain_two,
            shift_two,
            jnp.sum(grad_low.astype(F32), axis=0),
            jnp.sum(grad_branch.astype(F32), axis=0),
        ]
    )
    side = jnp.pad(side, ((0, 4), (0, 0)))
    input_grad, blocks = finish(
        grad_tokens, weight_all, low, gains[:1], shifts[:1], grad_middle, side, n_w
    )
    pieces = deal(
        lambda k: lax.dynamic_slice(blocks, ((wsh + n_w - k) % n_w, 0, 0), (1, 8, own))
    )
    vector_sum = (pieces[0] + pieces[1]) + (pieces[2] + pieces[3])
    everyone = lax.all_to_all(jnp.broadcast_to(vector_sum, (n_ctx, 8, own)), CTX, 0, 0)
    vector_out = jnp.sum(everyone, axis=0)

    qkv_out, out_out, bias_out, side_out = unpack(
        jnp.stack([z, y, core]), after(left, blocks), partner(left), right, partner(right)
    )
    bias_out = lax.dynamic_slice(bias_out, (0, wsh * own), (2, own))

    proj_out = share_proj.astype(F32)
    rows_for = lambda k, start, count: lax.dynamic_slice(
        share_fc, ((wsh + n_w - k) % n_w * own + start, 0), (count, ff)
    )
    fc_out = join_columns(
        at_x,
        with_halves(
            rows_for(0, 0, own),
            [rows_for(k, core * overlap, size) for k in range(1, n_w)],
            qkv_out,
            proj_out,
        ),
        n_w,
        overlap,
    )
    return (
        layer_output.reshape(seqs, rows, width),
        input_grad.reshape(seqs, rows, width),
        vector_out[0:2],
        vector_out[2:4],
        qkv_out,
        bias_out,
        out_out,
        vector_out[5],
        fc_out,
        side_out[0],
        proj_out,
        vector_out[4],
    )


def solution(mesh):
    y, core = 4, 2
    split = Mesh(
        mesh.devices.reshape(mesh.shape["ctx"] // (y * core), y, core, mesh.shape["wsh"]),
        (*CTX, "wsh"),
    )
    return jax.shard_map(
        on_device,
        mesh=split,
        in_specs=(
            P("wsh", CTX, None),
            P("wsh", None),
            P(None, "wsh"),
            P(None, "wsh"),
            P("wsh", None),
            P(None, "wsh"),
            P("wsh", None),
            P("wsh"),
            P("wsh", None),
            P("wsh"),
            P("wsh", None),
            P("wsh"),
            P("wsh", CTX, None),
        ),
        out_specs=(
            P("wsh", CTX, None),
            P("wsh", CTX, None),
            P(None, "wsh"),
            P(None, "wsh"),
            P("wsh", None),
            P(None, "wsh"),
            P("wsh", None),
            P("wsh"),
            P("wsh", None),
            P("wsh"),
            P("wsh", None),
            P("wsh"),
        ),
        check_vma=False,
    )
```
